32 devices in a mesh: dp: 8 (over z, y), tensor: 4 (over x, core).
Axes of the slice: x: 2, y: 2, z: 4, core: 2. Of those that a mesh axis runs over, the one named last changes fastest.
Arguments:
- tokens: bfloat16 [16384, 768], P(('dp', 'tensor')), may hold values from -6 to 6
- query_weight: bfloat16 [768, 768], P('dp', 'tensor'), may hold values from -0.21875 to 0.21875
- w_key: bfloat16 [768, 768], P('dp', 'tensor'), may hold values from -0.21875 to 0.21875
- value_weight: bfloat16 [768, 768], P('dp', 'tensor'), may hold values from -0.21875 to 0.21875
- w_out: bfloat16 [768, 768], P('tensor', 'dp'), may hold values from -0.875 to 0.875
- w_in: bfloat16 [768, 3072], P('dp', 'tensor'), may hold values from -0.21875 to 0.21875
- w_down: bfloat16 [3072, 768], P('tensor', 'dp'), may hold values from -0.109375 to 0.109375
- gain_attn: float32 [768], replicated, may hold values from 0.5 to 1.5
- shift_attn: float32 [768], replicated, may hold values from -0.6 to 0.6
- gain_ffn: float32 [768], replicated, may hold values from 0.5 to 1.5
- shift_ffn: float32 [768], replicated, may hold values from -0.6 to 0.6
- query_down_factor: bfloat16 [768, 8], replicated, may hold values from -0.21875 to 0.21875
- query_up_factor: bfloat16 [8, 768], P(None, 'tensor'), may hold values from -1 to 1
- value_down_factor: bfloat16 [768, 8], replicated, may hold values from -0.21875 to 0.21875
- value_up_factor: bfloat16 [8, 768], P(None, 'tensor'), may hold values from -1 to 1
- lengths: int32 [8, 32], P('dp'), may hold values from 0 to 512, as said below
- cotangent: bfloat16 [16384, 768], P(('dp', 'tensor')), may hold values from -6 to 6
Outputs:
- mixed: bfloat16 [16384, 768], P(('dp', 'tensor'))
- grad_tokens: bfloat16 [16384, 768], P(('dp', 'tensor'))
- grad_a_query: float32 [768, 8], replicated
- query_up_gradient: float32 [8, 768], P(None, 'tensor')
- grad_a_value: float32 [768, 8], replicated
- value_up_gradient: float32 [8, 768], P(None, 'tensor')
The draws below stay inside these ranges and needn't reach their ends.
Inputs may be any that keep to these rules, and one draw needn't show every extreme that they name: `lengths`: row g lists the sequences of data group g, laid end to end from the group's first position; they cover at most 2048 positions and the rest is padding; 0 marks an empty slot; some group holds a document of 512 tokens.
All inputs are finite; a program needn't handle non-finite values.
Results may differ from the reference program's by a relative error of at most 0.019.
Values may be sent and summed in bfloat16 or wider, within the bound.
A program may use at most 128 MiB of HBM per device.

```python
import jax
import jax.numpy as jnp
from jax import lax

D = 768
HEADS = 12
HEAD_DIM = 64
FF = 3072
RANK = 8
MAXLEN = 512
SLOTS = 32
GROUP = 2048
TOKENS = 16384
N_DP = 8


def draw_lengths(key, part):
    key = jax.random.fold_in(key, 11)
    keys_split = jax.random.split(key, 4)
    short_lo = max(MAXLEN // 32, 1)
    short_hi = MAXLEN // 4 + 1
    short_len = jax.random.randint(keys_split[0], (N_DP, SLOTS), short_lo, short_hi)
    chance = jax.random.randint(keys_split[1], (N_DP, 1), 0, 8)
    long_count = jax.random.randint(keys_split[2], (N_DP, 1), 1, GROUP // MAXLEN + 1)
    forced = jax.random.randint(keys_split[3], (), 0, N_DP)
    groups = jnp.arange(N_DP)[:, None]
    long_count = jnp.where((chance == 0) | (groups == forced), long_count, 0)
    slot_ids = jnp.arange(SLOTS)[None, :]
    raw_len = jnp.where(slot_ids < long_count, MAXLEN, short_len)
    slot_ends = jnp.cumsum(raw_len, axis=1)
    starts = slot_ends - raw_len
    return jnp.minimum(raw_len, jnp.maximum(GROUP - starts, 0)).astype(jnp.int32)


def levels(own_key, dims, shards, low, high):
    factor_of = 1.0
    for axis_at, shards_of in shards:
        heights = jax.random.uniform(jax.random.fold_in(jax.random.fold_in(own_key, 6), axis_at), (shards_of,), jnp.float32, low / len(shards), high / len(shards))
        factor_of = factor_of * jnp.repeat(jnp.exp(heights), dims[axis_at] // shards_of).reshape((-1,) + (1,) * (len(dims) - 1 - axis_at))
    return factor_of


def bell_draw(stream_key, extent, scale, most, cuts=(), kind=jnp.bfloat16):
    loudness = levels(stream_key, extent, cuts, -0.22, 0.18) if cuts else 1.0
    result = jax.random.normal(stream_key, extent, jnp.float32) * scale * loudness
    return jnp.minimum(jnp.maximum(result, -most), most).astype(kind)


def setup_inputs(seed: int = 0) -> dict:
    streams_of = jax.random.split(jax.random.key(seed), 18)
    tokens = bell_draw(streams_of[0], (TOKENS, D), 1.0, 6.0, ((0, 32),))
    query_weight = bell_draw(streams_of[1], (D, D), D ** -0.5, 0.21875, ((0, 8), (1, 4)))
    w_key = bell_draw(streams_of[2], (D, D), D ** -0.5, 0.21875, ((0, 8), (1, 4)))
    value_weight = bell_draw(streams_of[3], (D, D), D ** -0.5, 0.21875, ((0, 8), (1, 4)))
    w_out = bell_draw(streams_of[4], (D, D), (D // 16) ** -0.5, 0.875, ((0, 4), (1, 8)))
    w_in = bell_draw(streams_of[5], (D, FF), D ** -0.5, 0.21875, ((0, 8), (1, 4)))
    w_down = bell_draw(streams_of[6], (FF, D), FF ** -0.5, 0.109375, ((0, 4), (1, 8)))
    gain_attn = jnp.clip(1.0 + 0.1 * jax.random.normal(streams_of[7], (D,), jnp.float32), 0.5, 1.5)
    shift_attn = bell_draw(streams_of[8], (D,), 0.1, 0.6, (), jnp.float32)
    gain_ffn = jnp.clip(1.0 + 0.1 * jax.random.normal(streams_of[9], (D,), jnp.float32), 0.5, 1.5)
    shift_ffn = bell_draw(streams_of[10], (D,), 0.1, 0.6, (), jnp.float32)
    query_down_factor = bell_draw(streams_of[11], (D, RANK), D ** -0.5, 0.21875)
    query_up_factor = bell_draw(streams_of[12], (RANK, D), (4 * RANK) ** -0.5, 1.0, ((1, 4),))
    value_down_factor = bell_draw(streams_of[13], (D, RANK), D ** -0.5, 0.21875)
    value_up_factor = bell_draw(streams_of[14], (RANK, D), (4 * RANK) ** -0.5, 1.0, ((1, 4),))
    lengths = draw_lengths(jax.random.fold_in(streams_of[17], 71), 0)
    cotangent = bell_draw(streams_of[16], (TOKENS, D), 1.0, 6.0, ((0, 32),))
    return {"tokens": tokens, "query_weight": query_weight, "w_key": w_key, "value_weight": value_weight, "w_out": w_out, "w_in": w_in, "w_down": w_down, "gain_attn": gain_attn, "shift_attn": shift_attn, "gain_ffn": gain_ffn, "shift_ffn": shift_ffn, "query_down_factor": query_down_factor, "query_up_factor": query_up_factor, "value_down_factor": value_down_factor, "value_up_factor": value_up_factor, "lengths": lengths, "cotangent": cotangent}


@jax.custom_vjp
def narrow_product(v):
    return lax.optimization_barrier(v.astype(jnp.bfloat16)).astype(jnp.float32)

@jax.custom_vjp
def narrow_backward(v):
    return v

def low_keep(v):
    return (narrow_product(v), None)

def low_pass(kept, grad):
    return (grad,)

def back_keep(v):
    return (v, None)

def back_low(kept, grad):
    return (narrow_product(grad),)
narrow_product.defvjp(low_keep, low_pass)
narrow_backward.defvjp(back_keep, back_low)
HIGH = lax.Precision.HIGHEST
ADAPTER_SCALE = 2.0
NEG_FILL = -1e+30
LN_EPS = 1e-05

def precise_multiply(left, right):
    return jnp.dot(left, right, precision=HIGH, preferred_element_type=jnp.float32)

def layer_norm(row_vals, gain_vals, offset):
    middle = lax.optimization_barrier(jnp.mean(row_vals, axis=-1, keepdims=True))
    centred = row_vals - middle
    spread = lax.optimization_barrier(jnp.mean(centred * centred, axis=-1, keepdims=True))
    return centred * lax.rsqrt(spread + LN_EPS) * gain_vals + offset

def segment_ids(length_row, total_rows):
    slot_ends = jnp.cumsum(length_row).astype(jnp.int32)
    places = jnp.arange(total_rows, dtype=jnp.int32)
    return lax.optimization_barrier(jnp.sum((slot_ends[None, :] <= places[:, None]).astype(jnp.int32), axis=1))

def attend_block(block_in, key_heads, value_heads, segments):
    q_blk, seg_blk = block_in
    raw_scores = jnp.einsum('qhe,khe->hqk', q_blk, key_heads, precision=HIGH) * HEAD_DIM ** (-0.5)
    allowed = seg_blk[:, None] == segments[None, :]
    scores = jnp.where(allowed[None], narrow_backward(raw_scores), NEG_FILL)
    row_top = lax.optimization_barrier(jnp.max(scores, axis=-1, keepdims=True))
    exp_scores = jnp.exp(scores - row_top)
    softmax_w = exp_scores / lax.optimization_barrier(jnp.sum(exp_scores, axis=-1, keepdims=True))
    return jnp.einsum('hqk,khe->qhe', narrow_product(softmax_w), value_heads, precision=HIGH)

def layer_forward(input_rows, query_down_factor, query_up_factor, value_down_factor, value_up_factor, frozen, segments):
    query_weight, w_key, value_weight, w_out, w_in, w_down, gain_attn, shift_attn, gain_ffn, shift_ffn = frozen
    total_rows = input_rows.shape[0]
    block_rows = min(512, total_rows)
    block_count = total_rows // block_rows
    query_lifted = narrow_product(precise_multiply(input_rows, query_down_factor))
    query_rows = narrow_backward(narrow_product(precise_multiply(input_rows, query_weight) + ADAPTER_SCALE * precise_multiply(query_lifted, query_up_factor)))
    keys_all = narrow_backward(narrow_product(precise_multiply(input_rows, w_key)))
    value_lifted = narrow_product(precise_multiply(input_rows, value_down_factor))
    value_rows_every = narrow_backward(narrow_product(precise_multiply(input_rows, value_weight) + ADAPTER_SCALE * precise_multiply(value_lifted, value_up_factor)))
    key_heads = keys_all.reshape(total_rows, HEADS, HEAD_DIM)
    value_heads = value_rows_every.reshape(total_rows, HEADS, HEAD_DIM)
    q_blocks = query_rows.reshape(block_count, block_rows, HEADS, HEAD_DIM)
    seg_blocks = segments.reshape(block_count, block_rows)
    block_fn = jax.checkpoint(attend_block)
    outputs = lax.map(lambda block_in: block_fn(block_in, key_heads, value_heads, segments), (q_blocks, seg_blocks))
    context = narrow_backward(narrow_product(outputs.reshape(total_rows, D)))
    attn_out = narrow_backward(precise_multiply(context, w_out))
    first = narrow_product(layer_norm(input_rows + attn_out, gain_attn, shift_attn))
    hidden = narrow_backward(precise_multiply(first, w_in))
    acted = narrow_product(jax.nn.gelu(hidden, approximate=False))
    ffn_out = narrow_backward(precise_multiply(acted, w_down))
    return layer_norm(first + ffn_out, gain_ffn, shift_ffn)

def reference(tokens, query_weight, w_key, value_weight, w_out, w_in, w_down, gain_attn, shift_attn, gain_ffn, shift_ffn, query_down_factor, query_up_factor, value_down_factor, value_up_factor, lengths, cotangent):
    frozen = tuple((weight_matrix.astype(jnp.float32) for weight_matrix in (query_weight, w_key, value_weight, w_out, w_in, w_down, gain_attn, shift_attn, gain_ffn, shift_ffn)))
    adapter_begin = tuple((weight_matrix.astype(jnp.float32) for weight_matrix in (query_down_factor, query_up_factor, value_down_factor, value_up_factor)))

    def one_group(running, group_in):
        input_rows, cot_rows, length_row = group_in
        segments = segment_ids(length_row, GROUP)

        def forward_pass(rows_val, aq_val, bq_val, av_val, bv_val):
            return layer_forward(rows_val, aq_val, bq_val, av_val, bv_val, frozen, segments)
        final_result, backward_map = jax.vjp(forward_pass, input_rows.astype(jnp.float32), *adapter_begin)
        grads = backward_map(cot_rows.astype(jnp.float32))
        running = tuple((acc_sum + grad_part for acc_sum, grad_part in zip(running, grads[1:])))
        return (running, (final_result.astype(jnp.bfloat16), grads[0].astype(jnp.bfloat16)))
    empty_gradients = tuple((jnp.zeros(weight_matrix.shape, jnp.float32) for weight_matrix in adapter_begin))
    group_data = (tokens.reshape(N_DP, GROUP, D), cotangent.reshape(N_DP, GROUP, D), lengths)
    totals, (mixed, grad_tokens) = lax.scan(one_group, empty_gradients, group_data)
    return (mixed.reshape(TOKENS, D), grad_tokens.reshape(TOKENS, D), totals[0], totals[1], totals[2], totals[3])
```

```python
import functools

import jax
import jax.numpy as jnp
from jax import lax
from jax.experimental import pallas as pl
from jax.experimental.pallas import tpu as pltpu
from jax.sharding import PartitionSpec as P

HEAD_DIM = 64
PAIR = 2 * HEAD_DIM
Q_BLOCK = 256
K_BLOCK = 512
ADAPTER_SCALE = 2.0
SCORE_SCALE = HEAD_DIM ** (-0.5)
LOG2_SCALE = SCORE_SCALE * 1.4426950408889634
NEG_FILL = -1e30
LN_EPS = 1e-05
VMEM_LIMIT = 56 * 1024 * 1024


def dot_nn(left, right):
    return jnp.dot(left, right, preferred_element_type=jnp.float32)


def dot_nt(left, right):
    return lax.dot_general(
        left, right, (((1,), (1,)), ((), ())), preferred_element_type=jnp.float32
    )


def dot_tn(left, right):
    return lax.dot_general(
        left, right, (((0,), (0,)), ((), ())), preferred_element_type=jnp.float32
    )


def norm_forward(row_vals, gain_vals, offset):
    middle = jnp.mean(row_vals, axis=-1, keepdims=True)
    centred = row_vals - middle
    inverse = lax.rsqrt(jnp.mean(centred * centred, axis=-1, keepdims=True) + LN_EPS)
    normed = centred * inverse
    return (normed * gain_vals + offset, normed, inverse)


def norm_backward(grad_out, normed, inverse, gain_vals):
    grad_n = grad_out * gain_vals
    return inverse * (
        grad_n
        - jnp.mean(grad_n, axis=-1, keepdims=True)
        - normed * jnp.mean(grad_n * normed, axis=-1, keepdims=True)
    )


def gelu_parts(hidden):
    cdf_part = 0.5 * (1.0 + lax.erf(hidden * 0.7071067811865476))
    density = jnp.exp(-0.5 * hidden * hidden) * 0.3989422804014327
    return (hidden * cdf_part, cdf_part + hidden * density)


def block_span(lengths_ref, first_row, rows, total_rows):
    low = jnp.int32(0)
    high = jnp.int32(total_rows)
    end = jnp.int32(0)
    for slot in range(lengths_ref.shape[1]):
        end = end + lengths_ref[0, slot]
        low = jnp.where(end <= first_row, jnp.maximum(low, end), low)
        high = jnp.where(end > first_row + rows - 1, jnp.minimum(high, end), high)
    return low, high


def row_bounds(lengths_ref, first_row, rows, total_rows):
    place = first_row + lax.broadcasted_iota(jnp.int32, (1, rows), 1)
    begin = jnp.zeros((1, rows), jnp.int32)
    finish = jnp.full((1, rows), total_rows, jnp.int32)
    end = jnp.int32(0)
    for slot in range(lengths_ref.shape[1]):
        end = end + lengths_ref[0, slot]
        done = place >= end
        begin = jnp.where(done, jnp.maximum(begin, end), begin)
        finish = jnp.where(done, finish, jnp.minimum(finish, end))
    return begin, finish


def stack_pair(block):
    lane = lax.broadcasted_iota(jnp.int32, block.shape, 1)
    zero = jnp.zeros_like(block)
    return jnp.concatenate(
        [jnp.where(lane < HEAD_DIM, block, zero), jnp.where(lane >= HEAD_DIM, block, zero)],
        axis=0,
    )


def unstack_pair(block, rows):
    joined = jnp.concatenate([block[:HEAD_DIM, :rows], block[HEAD_DIM:, rows:]], axis=0)
    return joined.T


def window_mask(step, low, begin, finish, total_rows):
    wanted = low + step * K_BLOCK
    start = pl.multiple_of(jnp.minimum(wanted, total_rows - K_BLOCK), 128)
    key_at = start + lax.broadcasted_iota(jnp.int32, (K_BLOCK, begin.shape[1]), 0)
    return start, (key_at >= jnp.maximum(begin, wanted)) & (key_at < finish)


def forward_kernel(lengths_ref, q_ref, k_ref, v_ref, out_ref, lse_ref):
    rows = q_ref.shape[0]
    total_rows = k_ref.shape[0]
    base = lax.axis_index("tensor") * rows
    for q_at in range(rows // Q_BLOCK):
        first_row = base + q_at * Q_BLOCK
        low, high = block_span(lengths_ref, first_row, Q_BLOCK, total_rows)
        low = (low // 128) * 128
        steps = (high - low + K_BLOCK - 1) // K_BLOCK
        begin, finish = row_bounds(lengths_ref, first_row, Q_BLOCK, total_rows)
        q_rows = slice(q_at * Q_BLOCK, (q_at + 1) * Q_BLOCK)
        for pair in range(q_ref.shape[1] // PAIR):
            lanes = slice(pair * PAIR, (pair + 1) * PAIR)
            q_two = stack_pair(q_ref[q_rows, lanes])

            def body(step, carry, q_two=q_two, lanes=lanes, low=low, begin=begin, finish=finish):
                top, total, acc = carry
                start, allowed = window_mask(step, low, begin, finish, total_rows)
                keys = k_ref[pl.ds(start, K_BLOCK), lanes]
                values = v_ref[pl.ds(start, K_BLOCK), lanes]
                both = jnp.concatenate([allowed, allowed], axis=1)
                scores = jnp.where(both, dot_nt(keys, q_two), NEG_FILL)
                new_top = jnp.maximum(top, jnp.max(scores, axis=0, keepdims=True))
                probs = jnp.exp2((scores - new_top) * LOG2_SCALE)
                shrink = jnp.exp2((top - new_top) * LOG2_SCALE)
                total = total * shrink + jnp.sum(probs, axis=0, keepdims=True)
                acc = acc * shrink + dot_tn(values, probs.astype(jnp.bfloat16))
                return new_top, total, acc

            top, total, acc = lax.fori_loop(
                0,
                steps,
                body,
                (
                    jnp.full((1, 2 * Q_BLOCK), NEG_FILL, jnp.float32),
                    jnp.zeros((1, 2 * Q_BLOCK), jnp.float32),
                    jnp.zeros((PAIR, 2 * Q_BLOCK), jnp.float32),
                ),
            )
            out_ref[q_rows, lanes] = unstack_pair(acc / total, Q_BLOCK).astype(jnp.bfloat16)
            lse = top * LOG2_SCALE + jnp.log2(total)
            lse_ref[2 * pair : 2 * pair + 1, q_rows] = lse[:, :Q_BLOCK]
            lse_ref[2 * pair + 1 : 2 * pair + 2, q_rows] = lse[:, Q_BLOCK:]


def backward_kernel(
    lengths_ref,
    q_ref,
    k_ref,
    v_ref,
    ctx_ref,
    lse_ref,
    grad_ref,
    gq_ref,
    gk_ref,
    gv_ref,
    gk_acc,
    gv_acc,
):
    rows = q_ref.shape[0]
    total_rows = k_ref.shape[0]
    base = lax.axis_index("tensor") * rows
    gk_acc[...] = jnp.zeros_like(gk_acc)
    gv_acc[...] = jnp.zeros_like(gv_acc)
    for q_at in range(rows // Q_BLOCK):
        first_row = base + q_at * Q_BLOCK
        low, high = block_span(lengths_ref, first_row, Q_BLOCK, total_rows)
        low = (low // 128) * 128
        steps = (high - low + K_BLOCK - 1) // K_BLOCK
        begin, finish = row_bounds(lengths_ref, first_row, Q_BLOCK, total_rows)
        q_rows = slice(q_at * Q_BLOCK, (q_at + 1) * Q_BLOCK)
        for pair in range(q_ref.shape[1] // PAIR):
            lanes = slice(pair * PAIR, (pair + 1) * PAIR)
            q_two = stack_pair(q_ref[q_rows, lanes])
            grad_blk = grad_ref[q_rows, lanes]
            grad_two = stack_pair(grad_blk)
            product = (grad_blk.astype(jnp.float32) * ctx_ref[q_rows, lanes].astype(jnp.float32)).T
            row_dot = jnp.concatenate(
                [
                    jnp.sum(product[:HEAD_DIM], axis=0, keepdims=True),
                    jnp.sum(product[HEAD_DIM:], axis=0, keepdims=True),
                ],
                axis=1,
            )
            lse = jnp.concatenate(
                [
                    lse_ref[2 * pair : 2 * pair + 1, q_rows],
                    lse_ref[2 * pair + 1 : 2 * pair + 2, q_rows],
                ],
                axis=1,
            )

            def body(
                step,
                acc,
                q_two=q_two,
                grad_two=grad_two,
                row_dot=row_dot,
                lse=lse,
                lanes=lanes,
                low=low,
                begin=begin,
                finish=finish,
            ):
                start, allowed = window_mask(step, low, begin, finish, total_rows)
                window = pl.ds(start, K_BLOCK)
                keys = k_ref[window, lanes]
                values = v_ref[window, lanes]
                both = jnp.concatenate([allowed, allowed], axis=1)
                scores = jnp.where(both, dot_nt(keys, q_two), NEG_FILL)
                probs = jnp.exp2(scores * LOG2_SCALE - lse)
                grad_probs = dot_nt(values, grad_two)
                grad_scores = (probs * (grad_probs - row_dot)).astype(jnp.bfloat16)
                gk_acc[window, lanes] += dot_nn(grad_scores, q_two)
                gv_acc[window, lanes] += dot_nn(probs.astype(jnp.bfloat16), grad_two)
                return acc + dot_tn(keys, grad_scores)

            acc = lax.fori_loop(0, steps, body, jnp.zeros((PAIR, 2 * Q_BLOCK), jnp.float32))
            gq_ref[q_rows, lanes] = (unstack_pair(acc, Q_BLOCK) * SCORE_SCALE).astype(jnp.bfloat16)
    gk_ref[...] = (gk_acc[...] * SCORE_SCALE).astype(jnp.bfloat16)
    gv_ref[...] = gv_acc[...].astype(jnp.bfloat16)


VMEM_SPEC = pl.BlockSpec(memory_space=pltpu.VMEM)
SMEM_SPEC = pl.BlockSpec(memory_space=pltpu.SMEM)


def attend_forward(lengths, q_own, k_all, v_all):
    rows, width = q_own.shape
    heads = width // HEAD_DIM
    return pl.pallas_call(
        forward_kernel,
        out_shape=(
            jax.ShapeDtypeStruct((rows, width), jnp.bfloat16),
            jax.ShapeDtypeStruct((-(-heads // 8) * 8, rows), jnp.float32),
        ),
        in_specs=[SMEM_SPEC] + [VMEM_SPEC] * 3,
        out_specs=(VMEM_SPEC, VMEM_SPEC),
        compiler_params=pltpu.CompilerParams(vmem_limit_bytes=VMEM_LIMIT),
        name="attend_forward",
    )(lengths, q_own, k_all, v_all)


def attend_backward(lengths, q_own, k_all, v_all, context, lse, grad_context):
    rows, width = q_own.shape
    total_rows = k_all.shape[0]
    return pl.pallas_call(
        backward_kernel,
        out_shape=(
            jax.ShapeDtypeStruct((rows, width), jnp.bfloat16),
            jax.ShapeDtypeStruct((total_rows, width), jnp.bfloat16),
            jax.ShapeDtypeStruct((total_rows, width), jnp.bfloat16),
        ),
        in_specs=[SMEM_SPEC] + [VMEM_SPEC] * 6,
        out_specs=(VMEM_SPEC,) * 3,
        scratch_shapes=[
            pltpu.VMEM((total_rows, width), jnp.float32),
            pltpu.VMEM((total_rows, width), jnp.float32),
        ],
        compiler_params=pltpu.CompilerParams(vmem_limit_bytes=VMEM_LIMIT),
        name="attend_backward",
    )(lengths, q_own, k_all, v_all, context, lse, grad_context)


def local(
    tokens,
    query_weight,
    w_key,
    value_weight,
    w_out,
    w_in,
    w_down,
    gain_attn,
    shift_attn,
    gain_ffn,
    shift_ffn,
    query_down_factor,
    query_up_factor,
    value_down_factor,
    value_up_factor,
    lengths,
    cotangent,
):
    slim = query_weight.shape[1]
    attn_pack = jnp.concatenate([query_weight, w_key, value_weight, w_out.T], axis=1)
    packed = jnp.stack([attn_pack, w_in, w_down.T])
    packed = lax.all_gather(packed, "dp", axis=1, tiled=True)
    packed = lax.all_gather(packed, "tensor", axis=0)
    width = packed.shape[2]
    attn_full = packed[:, 0].reshape(-1, width, 4, slim).transpose(2, 1, 0, 3)
    attn_full = attn_full.reshape(4, width, width)
    w_q, w_k, w_v, w_o_t = (attn_full[i] for i in range(4))
    full_in = packed[:, 1].transpose(1, 0, 2).reshape(width, -1)
    full_down_t = packed[:, 2].transpose(1, 0, 2).reshape(width, -1)
    query_up = lax.all_gather(query_up_factor, "tensor", axis=1, tiled=True)
    value_up = lax.all_gather(value_up_factor, "tensor", axis=1, tiled=True)
    rows_all = lax.all_gather(tokens, "tensor", axis=0, tiled=True)

    u_query = dot_nn(tokens, query_down_factor).astype(jnp.bfloat16)
    q_own = (dot_nn(tokens, w_q) + ADAPTER_SCALE * dot_nn(u_query, query_up)).astype(jnp.bfloat16)
    k_all = dot_nn(rows_all, w_k).astype(jnp.bfloat16)
    u_value = dot_nn(rows_all, value_down_factor).astype(jnp.bfloat16)
    v_all = (dot_nn(rows_all, w_v) + ADAPTER_SCALE * dot_nn(u_value, value_up)).astype(jnp.bfloat16)

    context, lse = attend_forward(lengths, q_own, k_all, v_all)

    first_f, normed_one, inverse_one = norm_forward(
        tokens.astype(jnp.float32) + dot_nt(context, w_o_t), gain_attn, shift_attn
    )
    first = first_f.astype(jnp.bfloat16)
    hidden = dot_nn(first, full_in)
    acted_f, slope = gelu_parts(hidden)
    ffn_out = dot_nt(acted_f.astype(jnp.bfloat16), full_down_t)
    mixed_f, normed_two, inverse_two = norm_forward(
        first.astype(jnp.float32) + ffn_out, gain_ffn, shift_ffn
    )
    mixed = mixed_f.astype(jnp.bfloat16)
    grad_two = norm_backward(cotangent.astype(jnp.float32), normed_two, inverse_two, gain_ffn)
    grad_hidden = (dot_nn(grad_two.astype(jnp.bfloat16), full_down_t) * slope).astype(jnp.bfloat16)
    grad_first = grad_two + dot_nt(grad_hidden, full_in)
    grad_one = norm_backward(grad_first, normed_one, inverse_one, gain_attn)
    grad_context = dot_nn(grad_one.astype(jnp.bfloat16), w_o_t).astype(jnp.bfloat16)

    grad_q, grad_k, grad_v = attend_backward(
        lengths, q_own, k_all, v_all, context, lse, grad_context
    )
    rows = tokens.shape[0]
    grad_uq = ADAPTER_SCALE * dot_nt(grad_q, query_up)
    grad_uv = ADAPTER_SCALE * dot_nt(grad_v, value_up)
    grad_bq = ADAPTER_SCALE * dot_tn(u_query, grad_q)
    grad_bv = ADAPTER_SCALE * dot_tn(u_value, grad_v)
    grad_aq = dot_tn(tokens, grad_uq.astype(jnp.bfloat16))
    grad_av = dot_tn(rows_all, grad_uv.astype(jnp.bfloat16))
    grad_rows = (
        dot_nt(grad_k, w_k)
        + dot_nt(grad_v, w_v)
        + dot_nt(grad_uv.astype(jnp.bfloat16), value_down_factor)
    )
    own_rows = dot_nt(grad_q, w_q) + dot_nt(grad_uq.astype(jnp.bfloat16), query_down_factor)
    shared = lax.psum_scatter(
        grad_rows.astype(jnp.bfloat16), "tensor", scatter_dimension=0, tiled=True
    )
    grad_tokens = (grad_one + own_rows + shared.astype(jnp.float32)).astype(jnp.bfloat16)
    grad_aq, grad_av, grad_bq, grad_bv = lax.psum(
        (grad_aq, grad_av, grad_bq, grad_bv), ("dp", "tensor")
    )
    at = lax.axis_index("tensor") * slim
    grad_bq = lax.dynamic_slice_in_dim(grad_bq, at, slim, 1)
    grad_bv = lax.dynamic_slice_in_dim(grad_bv, at, slim, 1)
    return (mixed, grad_tokens, grad_aq, grad_bq, grad_av, grad_bv)


def solution(mesh):
    return jax.shard_map(
        local,
        mesh=mesh,
        in_specs=(
            P(("dp", "tensor"), None),
            P("dp", "tensor"),
            P("dp", "tensor"),
            P("dp", "tensor"),
            P("tensor", "dp"),
            P("dp", "tensor"),
            P("tensor", "dp"),
            P(),
            P(),
            P(),
            P(),
            P(),
            P(None, "tensor"),
            P(),
            P(None, "tensor"),
            P("dp", None),
            P(("dp", "tensor"), None),
        ),
        out_specs=(
            P(("dp", "tensor"), None),
            P(("dp", "tensor"), None),
            P(),
            P(None, "tensor"),
            P(),
            P(None, "tensor"),
        ),
        check_vma=False,
    )
```

```python
import functools
import heapq

import jax
import jax.numpy as jnp
from jax import lax
from jax.experimental import pallas as pl
from jax.experimental.pallas import tpu as pltpu
from jax.sharding import PartitionSpec as P

HEAD_DIM = 64
PAIR = 2 * HEAD_DIM
Q_BLOCK = 256
K_BLOCK = 512
ADAPTER_SCALE = 2.0
SCORE_SCALE = HEAD_DIM ** (-0.5)
LOG2_SCALE = SCORE_SCALE * 1.4426950408889634
NEG_FILL = -1e30
LN_EPS = 1e-05
VMEM_LIMIT = 56 * 1024 * 1024


def dot_nn(left, right):
    return jnp.dot(left, right, preferred_element_type=jnp.float32)


def dot_nt(left, right):
    return lax.dot_general(
        left, right, (((1,), (1,)), ((), ())), preferred_element_type=jnp.float32
    )


def dot_tn(left, right):
    return lax.dot_general(
        left, right, (((0,), (0,)), ((), ())), preferred_element_type=jnp.float32
    )


def norm_forward(row_vals, gain_vals, offset):
    middle = jnp.mean(row_vals, axis=-1, keepdims=True)
    centred = row_vals - middle
    inverse = lax.rsqrt(jnp.mean(centred * centred, axis=-1, keepdims=True) + LN_EPS)
    normed = centred * inverse
    return (normed * gain_vals + offset, normed, inverse)


def norm_backward(grad_out, normed, inverse, gain_vals):
    grad_n = grad_out * gain_vals
    return inverse * (
        grad_n
        - jnp.mean(grad_n, axis=-1, keepdims=True)
        - normed * jnp.mean(grad_n * normed, axis=-1, keepdims=True)
    )


def gelu_parts(hidden):
    cdf_part = 0.5 * (1.0 + lax.erf(hidden * 0.7071067811865476))
    density = jnp.exp(-0.5 * hidden * hidden) * 0.3989422804014327
    return (hidden * cdf_part, cdf_part + hidden * density)


def block_span(lengths_ref, first_row, rows, total_rows):
    low = jnp.int32(0)
    high = jnp.int32(total_rows)
    end = jnp.int32(0)
    for slot in range(lengths_ref.shape[1]):
        end = end + lengths_ref[0, slot]
        low = jnp.where(end <= first_row, jnp.maximum(low, end), low)
        high = jnp.where(end > first_row + rows - 1, jnp.minimum(high, end), high)
    return low, high


def row_bounds(lengths_ref, first_row, rows, total_rows):
    place = first_row + lax.broadcasted_iota(jnp.int32, (1, rows), 1)
    begin = jnp.zeros((1, rows), jnp.int32)
    finish = jnp.full((1, rows), total_rows, jnp.int32)
    end = jnp.int32(0)
    for slot in range(lengths_ref.shape[1]):
        end = end + lengths_ref[0, slot]
        done = place >= end
        begin = jnp.where(done, jnp.maximum(begin, end), begin)
        finish = jnp.where(done, finish, jnp.minimum(finish, end))
    return begin, finish


def stack_pair(block):
    lane = lax.broadcasted_iota(jnp.int32, block.shape, 1)
    zero = jnp.zeros_like(block)
    return jnp.concatenate(
        [jnp.where(lane < HEAD_DIM, block, zero), jnp.where(lane >= HEAD_DIM, block, zero)],
        axis=0,
    )


def unstack_pair(block, rows):
    joined = jnp.concatenate([block[:HEAD_DIM, :rows], block[HEAD_DIM:, rows:]], axis=0)
    return joined.T


def window_mask(step, low, begin, finish, total_rows):
    wanted = low + step * K_BLOCK
    start = pl.multiple_of(jnp.minimum(wanted, total_rows - K_BLOCK), 128)
    key_at = start + lax.broadcasted_iota(jnp.int32, (K_BLOCK, begin.shape[1]), 0)
    return start, (key_at >= jnp.maximum(begin, wanted)) & (key_at < finish)


def forward_kernel(lengths_ref, q_ref, k_ref, v_ref, out_ref, lse_ref):
    rows = q_ref.shape[0]
    total_rows = k_ref.shape[0]
    base = lax.axis_index("tensor") * rows
    for q_at in range(rows // Q_BLOCK):
        first_row = base + q_at * Q_BLOCK
        low, high = block_span(lengths_ref, first_row, Q_BLOCK, total_rows)
        low = (low // 128) * 128
        steps = (high - low + K_BLOCK - 1) // K_BLOCK
        begin, finish = row_bounds(lengths_ref, first_row, Q_BLOCK, total_rows)
        q_rows = slice(q_at * Q_BLOCK, (q_at + 1) * Q_BLOCK)
        for pair in range(q_ref.shape[1] // PAIR):
            lanes = slice(pair * PAIR, (pair + 1) * PAIR)
            q_two = stack_pair(q_ref[q_rows, lanes])

            def body(step, carry, q_two=q_two, lanes=lanes, low=low, begin=begin, finish=finish):
                top, total, acc = carry
                start, allowed = window_mask(step, low, begin, finish, total_rows)
                keys = k_ref[pl.ds(start, K_BLOCK), lanes]
                values = v_ref[pl.ds(start, K_BLOCK), lanes]
                both = jnp.concatenate([allowed, allowed], axis=1)
                scores = jnp.where(both, dot_nt(keys, q_two), NEG_FILL)
                new_top = jnp.maximum(top, jnp.max(scores, axis=0, keepdims=True))
                probs = jnp.exp2((scores - new_top) * LOG2_SCALE)
                shrink = jnp.exp2((top - new_top) * LOG2_SCALE)
                total = total * shrink + jnp.sum(probs, axis=0, keepdims=True)
                acc = acc * shrink + dot_tn(values, probs.astype(jnp.bfloat16))
                return new_top, total, acc

            top, total, acc = lax.fori_loop(
                0,
                steps,
                body,
                (
                    jnp.full((1, 2 * Q_BLOCK), NEG_FILL, jnp.float32),
                    jnp.zeros((1, 2 * Q_BLOCK), jnp.float32),
                    jnp.zeros((PAIR, 2 * Q_BLOCK), jnp.float32),
                ),
            )
            out_ref[q_rows, lanes] = unstack_pair(acc / total, Q_BLOCK).astype(jnp.bfloat16)
            lse = top * LOG2_SCALE + jnp.log2(total)
            lse_ref[2 * pair : 2 * pair + 1, q_rows] = lse[:, :Q_BLOCK]
            lse_ref[2 * pair + 1 : 2 * pair + 2, q_rows] = lse[:, Q_BLOCK:]


def backward_kernel(
    lengths_ref,
    q_ref,
    k_ref,
    v_ref,
    ctx_ref,
    lse_ref,
    grad_ref,
    gq_ref,
    gk_ref,
    gv_ref,
    gk_acc,
    gv_acc,
):
    rows = q_ref.shape[0]
    total_rows = k_ref.shape[0]
    base = lax.axis_index("tensor") * rows
    gk_acc[...] = jnp.zeros_like(gk_acc)
    gv_acc[...] = jnp.zeros_like(gv_acc)
    for q_at in range(rows // Q_BLOCK):
        first_row = base + q_at * Q_BLOCK
        low, high = block_span(lengths_ref, first_row, Q_BLOCK, total_rows)
        low = (low // 128) * 128
        steps = (high - low + K_BLOCK - 1) // K_BLOCK
        begin, finish = row_bounds(lengths_ref, first_row, Q_BLOCK, total_rows)
        q_rows = slice(q_at * Q_BLOCK, (q_at + 1) * Q_BLOCK)
        for pair in range(q_ref.shape[1] // PAIR):
            lanes = slice(pair * PAIR, (pair + 1) * PAIR)
            q_two = stack_pair(q_ref[q_rows, lanes])
            grad_blk = grad_ref[q_rows, lanes]
            grad_two = stack_pair(grad_blk)
            product = (grad_blk.astype(jnp.float32) * ctx_ref[q_rows, lanes].astype(jnp.float32)).T
            row_dot = jnp.concatenate(
                [
                    jnp.sum(product[:HEAD_DIM], axis=0, keepdims=True),
                    jnp.sum(product[HEAD_DIM:], axis=0, keepdims=True),
                ],
                axis=1,
            )
            lse = jnp.concatenate(
                [
                    lse_ref[2 * pair : 2 * pair + 1, q_rows],
                    lse_ref[2 * pair + 1 : 2 * pair + 2, q_rows],
                ],
                axis=1,
            )

            def body(
                step,
                acc,
                q_two=q_two,
                grad_two=grad_two,
                row_dot=row_dot,
                lse=lse,
                lanes=lanes,
                low=low,
                begin=begin,
                finish=finish,
            ):
                start, allowed = window_mask(step, low, begin, finish, total_rows)
                window = pl.ds(start, K_BLOCK)
                keys = k_ref[window, lanes]
                values = v_ref[window, lanes]
                both = jnp.concatenate([allowed, allowed], axis=1)
                scores = jnp.where(both, dot_nt(keys, q_two), NEG_FILL)
                probs = jnp.exp2(scores * LOG2_SCALE - lse)
                grad_probs = dot_nt(values, grad_two)
                grad_scores = (probs * (grad_probs - row_dot)).astype(jnp.bfloat16)
                gk_acc[window, lanes] += dot_nn(grad_scores, q_two)
                gv_acc[window, lanes] += dot_nn(probs.astype(jnp.bfloat16), grad_two)
                return acc + dot_tn(keys, grad_scores)

            acc = lax.fori_loop(0, steps, body, jnp.zeros((PAIR, 2 * Q_BLOCK), jnp.float32))
            gq_ref[q_rows, lanes] = (unstack_pair(acc, Q_BLOCK) * SCORE_SCALE).astype(jnp.bfloat16)
    gk_ref[...] = (gk_acc[...] * SCORE_SCALE).astype(jnp.bfloat16)
    gv_ref[...] = gv_acc[...].astype(jnp.bfloat16)


VMEM_SPEC = pl.BlockSpec(memory_space=pltpu.VMEM)
HBM_SPEC = pl.BlockSpec(memory_space=pltpu.HBM)
SMEM_SPEC = pl.BlockSpec(memory_space=pltpu.SMEM)


def attend_forward(lengths, q_own, k_all, v_all):
    rows, width = q_own.shape
    heads = width // HEAD_DIM
    return pl.pallas_call(
        forward_kernel,
        out_shape=(
            jax.ShapeDtypeStruct((rows, width), jnp.bfloat16),
            jax.ShapeDtypeStruct((-(-heads // 8) * 8, rows), jnp.float32),
        ),
        in_specs=[SMEM_SPEC] + [VMEM_SPEC] * 3,
        out_specs=(VMEM_SPEC, VMEM_SPEC),
        compiler_params=pltpu.CompilerParams(vmem_limit_bytes=VMEM_LIMIT),
        name="attend_forward",
    )(lengths, q_own, k_all, v_all)


def attend_backward(lengths, q_own, k_all, v_all, context, lse, grad_context):
    rows, width = q_own.shape
    total_rows = k_all.shape[0]
    return pl.pallas_call(
        backward_kernel,
        out_shape=(
            jax.ShapeDtypeStruct((rows, width), jnp.bfloat16),
            jax.ShapeDtypeStruct((total_rows, width), jnp.bfloat16),
            jax.ShapeDtypeStruct((total_rows, width), jnp.bfloat16),
        ),
        in_specs=[SMEM_SPEC] + [VMEM_SPEC] * 6,
        out_specs=(VMEM_SPEC,) * 3,
        scratch_shapes=[
            pltpu.VMEM((total_rows, width), jnp.float32),
            pltpu.VMEM((total_rows, width), jnp.float32),
        ],
        compiler_params=pltpu.CompilerParams(vmem_limit_bytes=VMEM_LIMIT),
        name="attend_backward",
    )(lengths, q_own, k_all, v_all, context, lse, grad_context)


MESH_ID = pl.DeviceIdType.MESH
DEPTH = 4
FULL_ROWS = 96

FLOWS = (
    (0, 0, "zxy", 0.0),
    (0, 1, "xzy", 0.0),
    (1, 0, "xyz", 0.0),
    (1, 1, "xzy", 0.0),
    (2, 0, "zyx", 0.0),
    (2, 1, "zyx", 0.0),
)
OWN = (0, 0, 0)


def forwards(order, piece):
    used = [axis for axis in order if piece["xyz".index(axis)] != 0]
    at = order.index(used[-1]) if used else -1
    steps = []
    if used and used[-1] == "z":
        steps.append(("z", 1 if piece[2] < 0 else -1))
    for axis in order[at + 1 :]:
        steps += [("z", 1), ("z", -1)] if axis == "z" else [(axis, 1)]
    return steps


def passed(piece, axis, sign):
    x, y, z = piece
    if axis == "x":
        return (1 - x, y, z)
    return (x, 1 - y, z) if axis == "y" else (x, y, z - sign)


def event_order(token_time):
    per_piece = 1.75
    links, heap, times, count = {}, [], {}, 0
    for z in range(DEPTH):
        links[z, "x", 1] = token_time
        for flow, (_, _, _, start) in enumerate(FLOWS):
            heapq.heappush(heap, (start + 0.01 * flow, count, z, flow, OWN))
            count += 1
    while heap:
        now, _, z, flow, piece = heapq.heappop(heap)
        times.setdefault((flow, piece), []).append(now)
        for axis, sign in forwards(FLOWS[flow][2], piece):
            there = z + sign if axis == "z" else z
            if not 0 <= there < DEPTH:
                continue
            end = max(links.get((z, axis, sign), 0.0), now) + per_piece
            links[z, axis, sign] = end
            heapq.heappush(heap, (end + 3.0, count, there, flow, passed(piece, axis, sign)))
            count += 1
    return [key for _, key in sorted((sum(v) / len(v), key) for key, v in times.items())]


class Place:
    def __init__(self):
        dp, tensor = lax.axis_index("dp"), lax.axis_index("tensor")
        self.z, self.y = dp // 2, lax.rem(dp, 2)
        self.x, self.core = tensor // 2, lax.rem(tensor, 2)

    def device(self, x=None, y=None, z=None, core=None):
        x = self.x if x is None else x
        y = self.y if y is None else y
        z = self.z if z is None else z
        core = self.core if core is None else core
        return (z * 2 + y, x * 2 + core)

    def step(self, axis, sign):
        if axis == "x":
            return self.device(x=1 - self.x)
        return self.device(y=1 - self.y) if axis == "y" else self.device(z=self.z + sign)

    def sibling(self):
        return self.device(core=1 - self.core)


def gather_kernel(
    pack_ref,
    tokens_ref,
    ups_ref,
    full_ref,
    rows_ref,
    ups_all_ref,
    piece_recv,
    send_sem,
    sib_send,
    sib_recv,
    own_sem,
    rows_send,
    rows_recv,
    ups_send,
    ups_recv,
):
    place = Place()
    x, y, z, core = place.x, place.y, place.z, place.core
    token_rows = tokens_ref.shape[0]
    part_rows = FULL_ROWS // 2
    half_rows = token_rows // 2

    barrier = pltpu.get_barrier_semaphore()
    others = (
        place.sibling(),
        place.step("x", 1),
        place.device(x=1 - x, core=1 - core),
        place.step("y", 1),
    )
    for target in others:
        pl.semaphore_signal(barrier, inc=1, device_id=target, device_id_type=MESH_ID)
    for sign, there in ((1, z < DEPTH - 1), (-1, z > 0)):

        @pl.when(there)
        def _(sign=sign):
            pl.semaphore_signal(
                barrier, inc=1, device_id=place.step("z", sign), device_id_type=MESH_ID
            )

    inner = ((z > 0) & (z < DEPTH - 1)).astype(jnp.int32)
    pl.semaphore_wait(barrier, len(others) + 1 + inner)

    def remote(source, target, send, recv, device):
        return pltpu.make_async_remote_copy(
            src_ref=source,
            dst_ref=target,
            send_sem=send,
            recv_sem=recv,
            device_id=device,
            device_id_type=MESH_ID,
        )

    def rows_at(owner_x, owner_core, half):
        return rows_ref.at[owner_x * 2 + owner_core, pl.ds(half * half_rows, half_rows)]

    own_copies = [
        pltpu.make_async_copy(pack_ref, full_ref.at[:, core, x, z, y], own_sem.at[0]),
        pltpu.make_async_copy(tokens_ref, rows_ref.at[x * 2 + core], own_sem.at[1]),
        pltpu.make_async_copy(ups_ref, ups_all_ref.at[x * 2 + core], own_sem.at[2]),
    ]
    row_copies = []
    for half in range(2):
        source = tokens_ref.at[pl.ds(half * half_rows, half_rows)]
        for slot, device in ((0, place.step("x", 1)), (1, place.sibling())):
            row_copies.append(
                remote(
                    source,
                    rows_at(x, core, half),
                    rows_send.at[slot, half],
                    rows_recv.at[slot, half],
                    device,
                )
            )
    up_copies = [
        remote(ups_ref, ups_all_ref.at[x * 2 + core], ups_send.at[i], ups_recv.at[i], device)
        for i, device in enumerate(others[:3])
    ]

    sends = {}

    def piece_at(flow, piece):
        kind, part, _, _ = FLOWS[flow]
        px, py = lax.rem(x + piece[0], 2), lax.rem(y + piece[1], 2)
        return full_ref.at[
            kind, core, px, z + piece[2], py, pl.ds(part * part_rows, part_rows)
        ], (px * 2 + py) * DEPTH + z + piece[2]

    def handle(flow, piece):
        kind, part, order, _ = FLOWS[flow]
        landed, index = piece_at(flow, piece)
        source = landed
        if piece == OWN:
            source = pack_ref.at[kind, pl.ds(part * part_rows, part_rows)]
        else:
            remote(landed, landed, send_sem.at[flow, 0], piece_recv.at[flow, index], place.sibling()).wait_recv()
        for axis, sign in forwards(order, piece):
            slot = {"x": 0, "y": 1, "z": 2 if sign > 0 else 3}[axis]
            copy = remote(
                source,
                landed,
                send_sem.at[flow, slot],
                piece_recv.at[flow, index],
                place.step(axis, sign),
            )
            if axis == "z":
                pl.when((z + sign >= 0) & (z + sign < DEPTH))(copy.start)
            else:
                copy.start()
                sends[flow, slot] = sends.get((flow, slot), 0) + 1
        remote(source, landed, sib_send.at[flow], sib_recv.at[flow], place.sibling()).start()

    def block_of(flow, pieces, plane):
        kind, part, _, _ = FLOWS[flow]
        nx = 2 if pieces % 2 == 0 else 1
        ny = 2 if pieces % 4 == 0 else 1
        return full_ref.at[
            kind,
            plane,
            pl.ds(0, nx),
            pl.ds(0, pieces // (nx * ny)),
            pl.ds(0, ny),
            pl.ds(part * part_rows, part_rows),
        ]

    def finish_flow(flow):
        order = FLOWS[flow][2]
        everything = block_of(flow, 4 * DEPTH, 1 - core)
        remote(everything, everything, sib_send.at[flow], sib_recv.at[flow], place.sibling()).wait()

    def finish_sends(flow):
        order = FLOWS[flow][2]
        for axis, slot in (("x", 0), ("y", 1)):
            block = block_of(flow, 2 ** order.index(axis) * (DEPTH // 2 if "z" in order[: order.index(axis)] else 1), core)
            remote(block, block, send_sem.at[flow, slot], sib_recv.at[flow], place.sibling()).wait_send()
        each = 2 ** order.index("z")
        for at in range(DEPTH):
            for slot, sets in ((2, at + 1 if at < DEPTH - 1 else 0), (3, DEPTH - at if at > 0 else 0)):
                if sets:

                    @pl.when(z == at)
                    def _(slot=slot, sets=sets):
                        nx = 2 if each > 1 else 1
                        ny = 2 if each > 2 else 1
                        kind, part, _, _ = FLOWS[flow]
                        block = full_ref.at[
                            kind,
                            core,
                            pl.ds(0, nx),
                            pl.ds(0, sets),
                            pl.ds(0, ny),
                            pl.ds(part * part_rows, part_rows),
                        ]
                        remote(
                            block, block, send_sem.at[flow, slot], sib_recv.at[flow], place.sibling()
                        ).wait_send()

    for copy in row_copies + up_copies + own_copies:
        copy.start()

    def pass_rows(half):
        row_copies[2 * half].wait_recv()
        landed = rows_at(1 - x, core, half)
        copy = remote(landed, landed, rows_send.at[2, half], rows_recv.at[2, half], place.sibling())
        copy.start()
        return copy

    passed_rows = []
    events = event_order(17.0)
    arrivals = 0
    for flow, piece in events:
        if piece[2] == 0:
            handle(flow, piece)
        else:
            pl.when((z + piece[2] >= 0) & (z + piece[2] < DEPTH))(
                functools.partial(handle, flow, piece)
            )
        if piece != OWN:
            arrivals += 1
            if arrivals in (8, 16):
                passed_rows.append(pass_rows(len(passed_rows)))

    for half in range(2):
        row_copies[2 * half].wait_send()
        row_copies[2 * half + 1].wait()
        passed_rows[half].wait()
    for copy in up_copies + own_copies:
        copy.wait()
    for flow in range(len(FLOWS)):
        finish_flow(flow)
        finish_sends(flow)


def gather_all(pack, tokens, ups):
    kinds, shard_rows, width = pack.shape
    token_rows = tokens.shape[0]
    hbm = pl.BlockSpec(memory_space=pltpu.HBM)
    flows = len(FLOWS)
    dma = pltpu.SemaphoreType.DMA
    return pl.pallas_call(
        gather_kernel,
        out_shape=(
            jax.ShapeDtypeStruct((kinds, 2, 2, DEPTH, 2, shard_rows, width), pack.dtype),
            jax.ShapeDtypeStruct((4, token_rows, width), tokens.dtype),
            jax.ShapeDtypeStruct((4,) + ups.shape, ups.dtype),
        ),
        in_specs=[hbm] * 3,
        out_specs=(hbm,) * 3,
        scratch_shapes=[
            dma((flows, 4 * DEPTH)),
            dma((flows, 4)),
            dma((flows,)),
            dma((flows,)),
            dma((3,)),
            dma((3, 2)),
            dma((3, 2)),
            dma((3,)),
            dma((3,)),
        ],
        compiler_params=pltpu.CompilerParams(
            collective_id=1, has_side_effects=True, vmem_limit_bytes=VMEM_LIMIT
        ),
        name="gather_all",
    )(pack, tokens, ups)


def project_kernel(
    order,
    full_hbm,
    rows_ref,
    ups_ref,
    down_q_ref,
    down_v_ref,
    weights_ref,
    q_ref,
    k_ref,
    v_ref,
    packs_ref,
    sems,
):
    token_rows = q_ref.shape[0]
    slim = packs_ref.shape[2] // 4
    tensor = lax.axis_index("tensor")
    copies = [
        pltpu.make_async_copy(full_hbm.at[0, i], packs_ref.at[i], sems.at[i])
        for i in range(len(order))
    ]
    for copy in copies:
        copy.start()
    for i, t in enumerate(order):
        copies[i].wait()
        lanes = slice(t * slim, (t + 1) * slim)
        for kind, down_ref, first in ((0, down_q_ref, 0), (1, None, 0), (2, down_v_ref, 8), (3, None, 0)):
            part = packs_ref[i, :, kind * slim : (kind + 1) * slim]
            if down_ref is not None:
                up = ups_ref[t, first : first + 8, :slim]
                part = (
                    part.astype(jnp.float32) + ADAPTER_SCALE * dot_nn(down_ref[...], up)
                ).astype(jnp.bfloat16)
            weights_ref[kind, :, lanes] = part
    own = rows_ref[pl.ds(pl.multiple_of(tensor * token_rows, token_rows), token_rows), :]
    q_ref[...] = dot_nn(own, weights_ref[0]).astype(jnp.bfloat16)

    @pl.loop(0, rows_ref.shape[0] // token_rows)
    def _(at):
        window = pl.ds(pl.multiple_of(at * token_rows, token_rows), token_rows)
        block = rows_ref[window, :]
        k_ref[window, :] = dot_nn(block, weights_ref[1]).astype(jnp.bfloat16)
        v_ref[window, :] = dot_nn(block, weights_ref[2]).astype(jnp.bfloat16)


def project(order, full, rows_all, ups_all, down_q, down_v, token_rows):
    total_rows, width = rows_all.shape
    bf16 = jnp.bfloat16
    return pl.pallas_call(
        functools.partial(project_kernel, order),
        out_shape=(
            jax.ShapeDtypeStruct((4, width, width), bf16),
            jax.ShapeDtypeStruct((token_rows, width), bf16),
            jax.ShapeDtypeStruct((total_rows, width), bf16),
            jax.ShapeDtypeStruct((total_rows, width), bf16),
        ),
        in_specs=[HBM_SPEC] + [VMEM_SPEC] * 4,
        out_specs=(VMEM_SPEC,) * 4,
        scratch_shapes=[
            pltpu.VMEM(full.shape[1:], bf16),
            pltpu.SemaphoreType.DMA((len(order),)),
        ],
        compiler_params=pltpu.CompilerParams(vmem_limit_bytes=VMEM_LIMIT),
        name="project",
    )(full, rows_all, ups_all, down_q, down_v)


def ffn_kernel(
    tokens_ref,
    ctx_ref,
    cot_ref,
    norms_ref,
    weights_hbm,
    full_hbm,
    mixed_ref,
    grad_one_ref,
    grad_ctx_ref,
    out_buf,
    in_buf,
    down_buf,
    slope_buf,
    sems,
):
    parts = in_buf.shape[0]
    copies = [pltpu.make_async_copy(weights_hbm.at[3], out_buf, sems.at[0])]
    for part in range(parts):
        copies.append(
            pltpu.make_async_copy(full_hbm.at[1, part], in_buf.at[part], sems.at[1 + 2 * part])
        )
        copies.append(
            pltpu.make_async_copy(full_hbm.at[2, part], down_buf.at[part], sems.at[2 + 2 * part])
        )
    for copy in copies:
        copy.start()
    gain_attn, shift_attn, gain_ffn, shift_ffn = (norms_ref[i : i + 1, :] for i in range(4))
    copies[0].wait()
    first_f, normed_one, inverse_one = norm_forward(
        tokens_ref[...].astype(jnp.float32) + dot_nt(ctx_ref[...], out_buf[...]),
        gain_attn,
        shift_attn,
    )
    first = first_f.astype(jnp.bfloat16)
    ffn_out = first.astype(jnp.float32)
    for part in range(parts):
        copies[1 + 2 * part].wait()
        acted, slope = gelu_parts(dot_nn(first, in_buf[part]))
        slope_buf[part] = slope
        copies[2 + 2 * part].wait()
        ffn_out = ffn_out + dot_nt(acted.astype(jnp.bfloat16), down_buf[part])
    mixed_f, normed_two, inverse_two = norm_forward(ffn_out, gain_ffn, shift_ffn)
    mixed_ref[...] = mixed_f.astype(jnp.bfloat16)
    grad_two = norm_backward(cot_ref[...].astype(jnp.float32), normed_two, inverse_two, gain_ffn)
    grad_ffn = grad_two.astype(jnp.bfloat16)
    grad_first = grad_two
    for part in range(parts):
        grad_hidden = dot_nn(grad_ffn, down_buf[part]) * slope_buf[part]
        grad_first = grad_first + dot_nt(grad_hidden.astype(jnp.bfloat16), in_buf[part])
    grad_one = norm_backward(grad_first, normed_one, inverse_one, gain_attn)
    grad_one_ref[...] = grad_one
    grad_ctx_ref[...] = dot_nn(grad_one.astype(jnp.bfloat16), out_buf[...]).astype(jnp.bfloat16)


def feed_forward(tokens, context, cotangent, norms, weights, full):
    rows, width = tokens.shape
    parts = full.shape[1]
    part_shape = full.shape[1:]
    return pl.pallas_call(
        ffn_kernel,
        out_shape=(
            jax.ShapeDtypeStruct((rows, width), jnp.bfloat16),
            jax.ShapeDtypeStruct((rows, width), jnp.float32),
            jax.ShapeDtypeStruct((rows, width), jnp.bfloat16),
        ),
        in_specs=[VMEM_SPEC] * 4 + [HBM_SPEC] * 2,
        out_specs=(VMEM_SPEC,) * 3,
        scratch_shapes=[
            pltpu.VMEM((width, width), jnp.bfloat16),
            pltpu.VMEM(part_shape, jnp.bfloat16),
            pltpu.VMEM(part_shape, jnp.bfloat16),
            pltpu.VMEM((parts, rows, part_shape[2]), jnp.float32),
            pltpu.SemaphoreType.DMA((1 + 2 * parts,)),
        ],
        compiler_params=pltpu.CompilerParams(vmem_limit_bytes=VMEM_LIMIT),
        name="feed_forward",
    )(tokens, context, cotangent, norms, weights, full)


def local(
    fast,
    tokens,
    query_weight,
    w_key,
    value_weight,
    w_out,
    w_in,
    w_down,
    gain_attn,
    shift_attn,
    gain_ffn,
    shift_ffn,
    query_down_factor,
    query_up_factor,
    value_down_factor,
    value_up_factor,
    lengths,
    cotangent,
):
    slim = query_weight.shape[1]
    width = tokens.shape[1]
    token_rows = tokens.shape[0]
    attn_pack = jnp.concatenate([query_weight, w_key, value_weight, w_out.T], axis=1)
    packed = jnp.stack([attn_pack, w_in, w_down.T])
    ups = jnp.concatenate([query_up_factor, value_up_factor], axis=0)
    ups = jnp.pad(ups, ((0, 0), (0, -slim % 128)))
    if fast:
        full, rows_all, ups_all = gather_all(packed, tokens, ups)
        full = full.reshape(3, 4, width, width)
        order = (0, 2, 1, 3)
    else:
        full = lax.all_gather(packed, "dp", axis=1, tiled=True)
        full = lax.all_gather(full, "tensor", axis=1)
        order = tuple(range(full.shape[1]))
        rows_all = lax.all_gather(tokens, "tensor")
        ups_all = lax.all_gather(ups, "tensor")
    rows_all = rows_all.reshape(-1, width)
    query_up = ups_all[:, :8, :slim].transpose(1, 0, 2).reshape(8, width)
    value_up = ups_all[:, 8:, :slim].transpose(1, 0, 2).reshape(8, width)
    weights, q_own, k_all, v_all = project(
        order, full, rows_all, ups_all, query_down_factor, value_down_factor, token_rows
    )
    w_q, w_k, w_v = weights[0], weights[1], weights[2]
    u_query = dot_nn(tokens, query_down_factor).astype(jnp.bfloat16)
    u_value = dot_nn(rows_all, value_down_factor).astype(jnp.bfloat16)

    context, lse = attend_forward(lengths, q_own, k_all, v_all)
    norms = jnp.stack([gain_attn, shift_attn, gain_ffn, shift_ffn])
    mixed, grad_one, grad_context = feed_forward(
        tokens, context, cotangent, norms, weights, full
    )

    grad_q, grad_k, grad_v = attend_backward(
        lengths, q_own, k_all, v_all, context, lse, grad_context
    )
    grad_uq = ADAPTER_SCALE * dot_nt(grad_q, query_up)
    grad_uv = ADAPTER_SCALE * dot_nt(grad_v, value_up)
    grad_bq = ADAPTER_SCALE * dot_tn(u_query, grad_q)
    grad_bv = ADAPTER_SCALE * dot_tn(u_value, grad_v)
    grad_aq = dot_tn(tokens, grad_uq.astype(jnp.bfloat16))
    grad_av = dot_tn(rows_all, grad_uv.astype(jnp.bfloat16))
    grad_rows = dot_nt(grad_k, w_k) + dot_nt(grad_v, w_v)
    own_rows = dot_nt(grad_q, w_q)
    shared = lax.psum_scatter(
        grad_rows.astype(jnp.bfloat16), "tensor", scatter_dimension=0, tiled=True
    )
    grad_tokens = (grad_one + own_rows + shared.astype(jnp.float32)).astype(jnp.bfloat16)
    grad_aq, grad_av, grad_bq, grad_bv = lax.psum(
        (grad_aq, grad_av, grad_bq, grad_bv), ("dp", "tensor")
    )
    at = lax.axis_index("tensor") * slim
    grad_bq = lax.dynamic_slice_in_dim(grad_bq, at, slim, 1)
    grad_bv = lax.dynamic_slice_in_dim(grad_bv, at, slim, 1)
    return (mixed, grad_tokens, grad_aq, grad_bq, grad_av, grad_bv)


def solution(mesh):
    fast = dict(mesh.shape) == {"dp": 2 * DEPTH, "tensor": 4}
    return jax.shard_map(
        functools.partial(local, fast),
        mesh=mesh,
        in_specs=(
            P(("dp", "tensor"), None),
            P("dp", "tensor"),
            P("dp", "tensor"),
            P("dp", "tensor"),
            P("tensor", "dp"),
            P("dp", "tensor"),
            P("tensor", "dp"),
            P(),
            P(),
            P(),
            P(),
            P(),
            P(None, "tensor"),
            P(),
            P(None, "tensor"),
            P("dp", None),
            P(("dp", "tensor"), None),
        ),
        out_specs=(
            P(("dp", "tensor"), None),
            P(("dp", "tensor"), None),
            P(),
            P(None, "tensor"),
            P(),
            P(None, "tensor"),
        ),
        check_vma=False,
    )
```

```python
import functools
import heapq

import jax
import jax.numpy as jnp
from jax import lax
from jax.experimental import pallas as pl
from jax.experimental.pallas import tpu as pltpu
from jax.sharding import PartitionSpec as P

HEAD_DIM = 64
PAIR = 2 * HEAD_DIM
Q_BLOCK = 256
K_BLOCK = 512
ADAPTER_SCALE = 2.0
SCORE_SCALE = HEAD_DIM ** (-0.5)
LOG2_SCALE = SCORE_SCALE * 1.4426950408889634
NEG_FILL = -1e30
LN_EPS = 1e-05
VMEM_LIMIT = 56 * 1024 * 1024


def dot_nn(left, right):
    return jnp.dot(left, right, preferred_element_type=jnp.float32)


def dot_nt(left, right):
    return lax.dot_general(
        left, right, (((1,), (1,)), ((), ())), preferred_element_type=jnp.float32
    )


def dot_tn(left, right):
    return lax.dot_general(
        left, right, (((0,), (0,)), ((), ())), preferred_element_type=jnp.float32
    )


def norm_forward(row_vals, gain_vals, offset):
    middle = jnp.mean(row_vals, axis=-1, keepdims=True)
    centred = row_vals - middle
    inverse = lax.rsqrt(jnp.mean(centred * centred, axis=-1, keepdims=True) + LN_EPS)
    normed = centred * inverse
    return (normed * gain_vals + offset, normed, inverse)


def norm_backward(grad_out, normed, inverse, gain_vals):
    grad_n = grad_out * gain_vals
    return inverse * (
        grad_n
        - jnp.mean(grad_n, axis=-1, keepdims=True)
        - normed * jnp.mean(grad_n * normed, axis=-1, keepdims=True)
    )


def gelu_parts(hidden):
    cdf_part = 0.5 * (1.0 + lax.erf(hidden * 0.7071067811865476))
    density = jnp.exp(-0.5 * hidden * hidden) * 0.3989422804014327
    return (hidden * cdf_part, cdf_part + hidden * density)


def block_span(lengths_ref, first_row, rows, total_rows):
    low = jnp.int32(0)
    high = jnp.int32(total_rows)
    end = jnp.int32(0)
    for slot in range(lengths_ref.shape[1]):
        end = end + lengths_ref[0, slot]
        low = jnp.where(end <= first_row, jnp.maximum(low, end), low)
        high = jnp.where(end > first_row + rows - 1, jnp.minimum(high, end), high)
    return low, high


def row_bounds(lengths_ref, first_row, rows, total_rows):
    place = first_row + lax.broadcasted_iota(jnp.int32, (1, rows), 1)
    begin = jnp.zeros((1, rows), jnp.int32)
    finish = jnp.full((1, rows), total_rows, jnp.int32)
    end = jnp.int32(0)
    for slot in range(lengths_ref.shape[1]):
        end = end + lengths_ref[0, slot]
        done = place >= end
        begin = jnp.where(done, jnp.maximum(begin, end), begin)
        finish = jnp.where(done, finish, jnp.minimum(finish, end))
    return begin, finish


def stack_pair(block):
    lane = lax.broadcasted_iota(jnp.int32, block.shape, 1)
    zero = jnp.zeros_like(block)
    return jnp.concatenate(
        [jnp.where(lane < HEAD_DIM, block, zero), jnp.where(lane >= HEAD_DIM, block, zero)],
        axis=0,
    )


def unstack_pair(block, rows):
    joined = jnp.concatenate([block[:HEAD_DIM, :rows], block[HEAD_DIM:, rows:]], axis=0)
    return joined.T


def window_mask(step, low, begin, finish, total_rows):
    wanted = low + step * K_BLOCK
    start = pl.multiple_of(jnp.minimum(wanted, total_rows - K_BLOCK), 128)
    key_at = start + lax.broadcasted_iota(jnp.int32, (K_BLOCK, begin.shape[1]), 0)
    return start, (key_at >= jnp.maximum(begin, wanted)) & (key_at < finish)


def forward_kernel(lengths_ref, q_ref, k_ref, v_ref, out_ref, lse_ref):
    rows = q_ref.shape[0]
    total_rows = k_ref.shape[0]
    base = lax.axis_index("tensor") * rows
    for q_at in range(rows // Q_BLOCK):
        first_row = base + q_at * Q_BLOCK
        low, high = block_span(lengths_ref, first_row, Q_BLOCK, total_rows)
        low = (low // 128) * 128
        steps = (high - low + K_BLOCK - 1) // K_BLOCK
        begin, finish = row_bounds(lengths_ref, first_row, Q_BLOCK, total_rows)
        q_rows = slice(q_at * Q_BLOCK, (q_at + 1) * Q_BLOCK)
        for pair in range(q_ref.shape[1] // PAIR):
            lanes = slice(pair * PAIR, (pair + 1) * PAIR)
            q_two = stack_pair(q_ref[q_rows, lanes])

            def body(step, carry, q_two=q_two, lanes=lanes, low=low, begin=begin, finish=finish):
                top, total, acc = carry
                start, allowed = window_mask(step, low, begin, finish, total_rows)
                keys = k_ref[pl.ds(start, K_BLOCK), lanes]
                values = v_ref[pl.ds(start, K_BLOCK), lanes]
                both = jnp.concatenate([allowed, allowed], axis=1)
                scores = jnp.where(both, dot_nt(keys, q_two), NEG_FILL)
                new_top = jnp.maximum(top, jnp.max(scores, axis=0, keepdims=True))
                probs = jnp.exp2((scores - new_top) * LOG2_SCALE)
                shrink = jnp.exp2((top - new_top) * LOG2_SCALE)
                total = total * shrink + jnp.sum(probs, axis=0, keepdims=True)
                acc = acc * shrink + dot_tn(values, probs.astype(jnp.bfloat16))
                return new_top, total, acc

            top, total, acc = lax.fori_loop(
                0,
                steps,
                body,
                (
                    jnp.full((1, 2 * Q_BLOCK), NEG_FILL, jnp.float32),
                    jnp.zeros((1, 2 * Q_BLOCK), jnp.float32),
                    jnp.zeros((PAIR, 2 * Q_BLOCK), jnp.float32),
                ),
            )
            out_ref[q_rows, lanes] = unstack_pair(acc / total, Q_BLOCK).astype(jnp.bfloat16)
            lse = top * LOG2_SCALE + jnp.log2(total)
            lse_ref[2 * pair : 2 * pair + 1, q_rows] = lse[:, :Q_BLOCK]
            lse_ref[2 * pair + 1 : 2 * pair + 2, q_rows] = lse[:, Q_BLOCK:]


def backward_kernel(
    lengths_ref,
    q_ref,
    k_ref,
    v_ref,
    ctx_ref,
    lse_ref,
    grad_ref,
    gq_ref,
    gk_ref,
    gv_ref,
    gk_acc,
    gv_acc,
):
    rows = q_ref.shape[0]
    total_rows = k_ref.shape[0]
    base = lax.axis_index("tensor") * rows
    gk_acc[...] = jnp.zeros_like(gk_acc)
    gv_acc[...] = jnp.zeros_like(gv_acc)
    for q_at in range(rows // Q_BLOCK):
        first_row = base + q_at * Q_BLOCK
        low, high = block_span(lengths_ref, first_row, Q_BLOCK, total_rows)
        low = (low // 128) * 128
        steps = (high - low + K_BLOCK - 1) // K_BLOCK
        begin, finish = row_bounds(lengths_ref, first_row, Q_BLOCK, total_rows)
        q_rows = slice(q_at * Q_BLOCK, (q_at + 1) * Q_BLOCK)
        for pair in range(q_ref.shape[1] // PAIR):
            lanes = slice(pair * PAIR, (pair + 1) * PAIR)
            q_two = stack_pair(q_ref[q_rows, lanes])
            grad_blk = grad_ref[q_rows, lanes]
            grad_two = stack_pair(grad_blk)
            product = (grad_blk.astype(jnp.float32) * ctx_ref[q_rows, lanes].astype(jnp.float32)).T
            row_dot = jnp.concatenate(
                [
                    jnp.sum(product[:HEAD_DIM], axis=0, keepdims=True),
                    jnp.sum(product[HEAD_DIM:], axis=0, keepdims=True),
                ],
                axis=1,
            )
            lse = jnp.concatenate(
                [
                    lse_ref[2 * pair : 2 * pair + 1, q_rows],
                    lse_ref[2 * pair + 1 : 2 * pair + 2, q_rows],
                ],
                axis=1,
            )

            def body(
                step,
                acc,
                q_two=q_two,
                grad_two=grad_two,
                row_dot=row_dot,
                lse=lse,
                lanes=lanes,
                low=low,
                begin=begin,
                finish=finish,
            ):
                start, allowed = window_mask(step, low, begin, finish, total_rows)
                window = pl.ds(start, K_BLOCK)
                keys = k_ref[window, lanes]
                values = v_ref[window, lanes]
                both = jnp.concatenate([allowed, allowed], axis=1)
                scores = jnp.where(both, dot_nt(keys, q_two), NEG_FILL)
                probs = jnp.exp2(scores * LOG2_SCALE - lse)
                grad_probs = dot_nt(values, grad_two)
                grad_scores = (probs * (grad_probs - row_dot)).astype(jnp.bfloat16)
                gk_acc[window, lanes] += dot_nn(grad_scores, q_two)
                gv_acc[window, lanes] += dot_nn(probs.astype(jnp.bfloat16), grad_two)
                return acc + dot_tn(keys, grad_scores)

            acc = lax.fori_loop(0, steps, body, jnp.zeros((PAIR, 2 * Q_BLOCK), jnp.float32))
            gq_ref[q_rows, lanes] = (unstack_pair(acc, Q_BLOCK) * SCORE_SCALE).astype(jnp.bfloat16)
    gk_ref[...] = (gk_acc[...] * SCORE_SCALE).astype(jnp.bfloat16)
    gv_ref[...] = gv_acc[...].astype(jnp.bfloat16)


VMEM_SPEC = pl.BlockSpec(memory_space=pltpu.VMEM)
HBM_SPEC = pl.BlockSpec(memory_space=pltpu.HBM)
SMEM_SPEC = pl.BlockSpec(memory_space=pltpu.SMEM)


def attend_forward(lengths, q_own, k_all, v_all):
    rows, width = q_own.shape
    heads = width // HEAD_DIM
    return pl.pallas_call(
        forward_kernel,
        out_shape=(
            jax.ShapeDtypeStruct((rows, width), jnp.bfloat16),
            jax.ShapeDtypeStruct((-(-heads // 8) * 8, rows), jnp.float32),
        ),
        in_specs=[SMEM_SPEC] + [VMEM_SPEC] * 3,
        out_specs=(VMEM_SPEC, VMEM_SPEC),
        compiler_params=pltpu.CompilerParams(vmem_limit_bytes=VMEM_LIMIT),
        name="attend_forward",
    )(lengths, q_own, k_all, v_all)


def attend_backward(lengths, q_own, k_all, v_all, context, lse, grad_context):
    rows, width = q_own.shape
    total_rows = k_all.shape[0]
    return pl.pallas_call(
        backward_kernel,
        out_shape=(
            jax.ShapeDtypeStruct((rows, width), jnp.bfloat16),
            jax.ShapeDtypeStruct((total_rows, width), jnp.bfloat16),
            jax.ShapeDtypeStruct((total_rows, width), jnp.bfloat16),
        ),
        in_specs=[SMEM_SPEC] + [VMEM_SPEC] * 6,
        out_specs=(VMEM_SPEC,) * 3,
        scratch_shapes=[
            pltpu.VMEM((total_rows, width), jnp.float32),
            pltpu.VMEM((total_rows, width), jnp.float32),
        ],
        compiler_params=pltpu.CompilerParams(vmem_limit_bytes=VMEM_LIMIT),
        name="attend_backward",
    )(lengths, q_own, k_all, v_all, context, lse, grad_context)


MESH_ID = pl.DeviceIdType.MESH
DEPTH = 4
FULL_ROWS = 96

FLOWS = (
    (0, 0, "zxy", 0.0),
    (0, 1, "xzy", 0.0),
    (1, 0, "xyz", 0.0),
    (1, 1, "xzy", 0.0),
    (2, 0, "zyx", 0.0),
    (2, 1, "zyx", 0.0),
)
OWN = (0, 0, 0)


def forwards(order, piece):
    used = [axis for axis in order if piece["xyz".index(axis)] != 0]
    at = order.index(used[-1]) if used else -1
    steps = []
    if used and used[-1] == "z":
        steps.append(("z", 1 if piece[2] < 0 else -1))
    for axis in order[at + 1 :]:
        steps += [("z", 1), ("z", -1)] if axis == "z" else [(axis, 1)]
    return steps


def passed(piece, axis, sign):
    x, y, z = piece
    if axis == "x":
        return (1 - x, y, z)
    return (x, 1 - y, z) if axis == "y" else (x, y, z - sign)


def event_order(token_time):
    per_piece = 1.75
    links, heap, times, count = {}, [], {}, 0
    for z in range(DEPTH):
        links[z, "x", 1] = token_time
        for flow, (_, _, _, start) in enumerate(FLOWS):
            heapq.heappush(heap, (start + 0.01 * flow, count, z, flow, OWN))
            count += 1
    while heap:
        now, _, z, flow, piece = heapq.heappop(heap)
        times.setdefault((flow, piece), []).append(now)
        for axis, sign in forwards(FLOWS[flow][2], piece):
            there = z + sign if axis == "z" else z
            if not 0 <= there < DEPTH:
                continue
            end = max(links.get((z, axis, sign), 0.0), now) + per_piece
            links[z, axis, sign] = end
            heapq.heappush(heap, (end + 3.0, count, there, flow, passed(piece, axis, sign)))
            count += 1
    return [key for _, key in sorted((sum(v) / len(v), key) for key, v in times.items())]


class Place:
    def __init__(self):
        dp, tensor = lax.axis_index("dp"), lax.axis_index("tensor")
        self.z, self.y = dp // 2, lax.rem(dp, 2)
        self.x, self.core = tensor // 2, lax.rem(tensor, 2)

    def device(self, x=None, y=None, z=None, core=None):
        x = self.x if x is None else x
        y = self.y if y is None else y
        z = self.z if z is None else z
        core = self.core if core is None else core
        return (z * 2 + y, x * 2 + core)

    def step(self, axis, sign):
        if axis == "x":
            return self.device(x=1 - self.x)
        return self.device(y=1 - self.y) if axis == "y" else self.device(z=self.z + sign)

    def sibling(self):
        return self.device(core=1 - self.core)


def gather_kernel(
    pack_ref,
    tokens_ref,
    ups_ref,
    full_ref,
    rows_ref,
    ups_all_ref,
    piece_recv,
    send_sem,
    sib_send,
    sib_recv,
    own_sem,
    rows_send,
    rows_recv,
    ups_send,
    ups_recv,
):
    place = Place()
    x, y, z, core = place.x, place.y, place.z, place.core
    token_rows = tokens_ref.shape[0]
    part_rows = FULL_ROWS // 2
    half_rows = token_rows // 2

    barrier = pltpu.get_barrier_semaphore()
    others = (
        place.sibling(),
        place.step("x", 1),
        place.device(x=1 - x, core=1 - core),
        place.step("y", 1),
    )
    for target in others:
        pl.semaphore_signal(barrier, inc=1, device_id=target, device_id_type=MESH_ID)
    for sign, there in ((1, z < DEPTH - 1), (-1, z > 0)):

        @pl.when(there)
        def _(sign=sign):
            pl.semaphore_signal(
                barrier, inc=1, device_id=place.step("z", sign), device_id_type=MESH_ID
            )

    inner = ((z > 0) & (z < DEPTH - 1)).astype(jnp.int32)
    pl.semaphore_wait(barrier, len(others) + 1 + inner)

    def remote(source, target, send, recv, device):
        return pltpu.make_async_remote_copy(
            src_ref=source,
            dst_ref=target,
            send_sem=send,
            recv_sem=recv,
            device_id=device,
            device_id_type=MESH_ID,
        )

    def rows_at(owner_x, owner_core, half):
        return rows_ref.at[owner_x * 2 + owner_core, pl.ds(half * half_rows, half_rows)]

    own_copies = [
        pltpu.make_async_copy(pack_ref, full_ref.at[:, core, x, z, y], own_sem.at[0]),
        pltpu.make_async_copy(tokens_ref, rows_ref.at[x * 2 + core], own_sem.at[1]),
        pltpu.make_async_copy(ups_ref, ups_all_ref.at[x * 2 + core], own_sem.at[2]),
    ]
    row_copies = []
    for half in range(2):
        source = tokens_ref.at[pl.ds(half * half_rows, half_rows)]
        for slot, device in ((0, place.step("x", 1)), (1, place.sibling())):
            row_copies.append(
                remote(
                    source,
                    rows_at(x, core, half),
                    rows_send.at[slot, half],
                    rows_recv.at[slot, half],
                    device,
                )
            )
    up_copies = [
        remote(ups_ref, ups_all_ref.at[x * 2 + core], ups_send.at[i], ups_recv.at[i], device)
        for i, device in enumerate(others[:3])
    ]

    sends = {}

    def piece_at(flow, piece):
        kind, part, _, _ = FLOWS[flow]
        px, py = lax.rem(x + piece[0], 2), lax.rem(y + piece[1], 2)
        return full_ref.at[
            kind, core, px, z + piece[2], py, pl.ds(part * part_rows, part_rows)
        ], (px * 2 + py) * DEPTH + z + piece[2]

    def handle(flow, piece):
        kind, part, order, _ = FLOWS[flow]
        landed, index = piece_at(flow, piece)
        source = landed
        if piece == OWN:
            source = pack_ref.at[kind, pl.ds(part * part_rows, part_rows)]
        else:
            remote(landed, landed, send_sem.at[flow, 0], piece_recv.at[flow, index], place.sibling()).wait_recv()
        for axis, sign in forwards(order, piece):
            slot = {"x": 0, "y": 1, "z": 2 if sign > 0 else 3}[axis]
            copy = remote(
                source,
                landed,
                send_sem.at[flow, slot],
                piece_recv.at[flow, index],
                place.step(axis, sign),
            )
            if axis == "z":
                pl.when((z + sign >= 0) & (z + sign < DEPTH))(copy.start)
            else:
                copy.start()
                sends[flow, slot] = sends.get((flow, slot), 0) + 1
        remote(source, landed, sib_send.at[flow], sib_recv.at[flow], place.sibling()).start()

    def block_of(flow, pieces, plane):
        kind, part, _, _ = FLOWS[flow]
        nx = 2 if pieces % 2 == 0 else 1
        ny = 2 if pieces % 4 == 0 else 1
        return full_ref.at[
            kind,
            plane,
            pl.ds(0, nx),
            pl.ds(0, pieces // (nx * ny)),
            pl.ds(0, ny),
            pl.ds(part * part_rows, part_rows),
        ]

    def finish_flow(flow):
        order = FLOWS[flow][2]
        everything = block_of(flow, 4 * DEPTH, 1 - core)
        remote(everything, everything, sib_send.at[flow], sib_recv.at[flow], place.sibling()).wait()

    def finish_sends(flow):
        order = FLOWS[flow][2]
        for axis, slot in (("x", 0), ("y", 1)):
            block = block_of(flow, 2 ** order.index(axis) * (DEPTH // 2 if "z" in order[: order.index(axis)] else 1), core)
            remote(block, block, send_sem.at[flow, slot], sib_recv.at[flow], place.sibling()).wait_send()
        each = 2 ** order.index("z")
        for at in range(DEPTH):
            for slot, sets in ((2, at + 1 if at < DEPTH - 1 else 0), (3, DEPTH - at if at > 0 else 0)):
                if sets:

                    @pl.when(z == at)
                    def _(slot=slot, sets=sets):
                        nx = 2 if each > 1 else 1
                        ny = 2 if each > 2 else 1
                        kind, part, _, _ = FLOWS[flow]
                        block = full_ref.at[
                            kind,
                            core,
                            pl.ds(0, nx),
                            pl.ds(0, sets),
                            pl.ds(0, ny),
                            pl.ds(part * part_rows, part_rows),
                        ]
                        remote(
                            block, block, send_sem.at[flow, slot], sib_recv.at[flow], place.sibling()
                        ).wait_send()

    for copy in row_copies + up_copies + own_copies:
        copy.start()

    def pass_rows(half):
        row_copies[2 * half].wait_recv()
        landed = rows_at(1 - x, core, half)
        copy = remote(landed, landed, rows_send.at[2, half], rows_recv.at[2, half], place.sibling())
        copy.start()
        return copy

    passed_rows = []
    events = event_order(17.0)
    arrivals = 0
    for flow, piece in events:
        if piece[2] == 0:
            handle(flow, piece)
        else:
            pl.when((z + piece[2] >= 0) & (z + piece[2] < DEPTH))(
                functools.partial(handle, flow, piece)
            )
        if piece != OWN:
            arrivals += 1
            if arrivals in (8, 16):
                passed_rows.append(pass_rows(len(passed_rows)))

    for half in range(2):
        row_copies[2 * half].wait_send()
        row_copies[2 * half + 1].wait()
        passed_rows[half].wait()
    for copy in up_copies + own_copies:
        copy.wait()
    for flow in range(len(FLOWS)):
        finish_flow(flow)
        finish_sends(flow)


def gather_all(pack, tokens, ups):
    kinds, shard_rows, width = pack.shape
    token_rows = tokens.shape[0]
    hbm = pl.BlockSpec(memory_space=pltpu.HBM)
    flows = len(FLOWS)
    dma = pltpu.SemaphoreType.DMA
    return pl.pallas_call(
        gather_kernel,
        out_shape=(
            jax.ShapeDtypeStruct((kinds, 2, 2, DEPTH, 2, shard_rows, width), pack.dtype),
            jax.ShapeDtypeStruct((4, token_rows, width), tokens.dtype),
            jax.ShapeDtypeStruct((4,) + ups.shape, ups.dtype),
        ),
        in_specs=[hbm] * 3,
        out_specs=(hbm,) * 3,
        scratch_shapes=[
            dma((flows, 4 * DEPTH)),
            dma((flows, 4)),
            dma((flows,)),
            dma((flows,)),
            dma((3,)),
            dma((3, 2)),
            dma((3, 2)),
            dma((3,)),
            dma((3,)),
        ],
        compiler_params=pltpu.CompilerParams(
            collective_id=1, has_side_effects=True, vmem_limit_bytes=VMEM_LIMIT
        ),
        name="gather_all",
    )(pack, tokens, ups)


def project_kernel(
    order,
    full_hbm,
    rows_ref,
    ups_ref,
    downs_ref,
    weights_ref,
    q_ref,
    k_ref,
    v_ref,
    packs_ref,
    sems,
):
    token_rows = q_ref.shape[0]
    slim = packs_ref.shape[2] // 4
    tensor = lax.axis_index("tensor")
    copies = [
        pltpu.make_async_copy(full_hbm.at[0, i], packs_ref.at[i], sems.at[i])
        for i in range(len(order))
    ]
    for copy in copies:
        copy.start()
    for i, t in enumerate(order):
        copies[i].wait()
        lanes = slice(t * slim, (t + 1) * slim)
        for kind, first in ((0, 0), (1, None), (2, 8), (3, None)):
            part = packs_ref[i, :, kind * slim : (kind + 1) * slim]
            if first is not None:
                up = ups_ref[t, first : first + 8, :slim]
                product = dot_tn(downs_ref[first : first + 8, :], up)
                part = (part.astype(jnp.float32) + ADAPTER_SCALE * product).astype(jnp.bfloat16)
            weights_ref[kind, :, lanes] = part
    own = rows_ref[pl.ds(pl.multiple_of(tensor * token_rows, token_rows), token_rows), :]
    q_ref[...] = dot_nn(own, weights_ref[0]).astype(jnp.bfloat16)

    @pl.loop(0, rows_ref.shape[0] // token_rows)
    def _(at):
        window = pl.ds(pl.multiple_of(at * token_rows, token_rows), token_rows)
        block = rows_ref[window, :]
        k_ref[window, :] = dot_nn(block, weights_ref[1]).astype(jnp.bfloat16)
        v_ref[window, :] = dot_nn(block, weights_ref[2]).astype(jnp.bfloat16)


def project(order, full, rows_all, ups_all, downs, token_rows):
    total_rows, width = rows_all.shape
    bf16 = jnp.bfloat16
    return pl.pallas_call(
        functools.partial(project_kernel, order),
        out_shape=(
            jax.ShapeDtypeStruct((4, width, width), bf16),
            jax.ShapeDtypeStruct((token_rows, width), bf16),
            jax.ShapeDtypeStruct((total_rows, width), bf16),
            jax.ShapeDtypeStruct((total_rows, width), bf16),
        ),
        in_specs=[HBM_SPEC] + [VMEM_SPEC] * 3,
        out_specs=(VMEM_SPEC,) * 4,
        scratch_shapes=[
            pltpu.VMEM(full.shape[1:], bf16),
            pltpu.SemaphoreType.DMA((len(order),)),
        ],
        compiler_params=pltpu.CompilerParams(vmem_limit_bytes=VMEM_LIMIT),
        name="project",
    )(full, rows_all, ups_all, downs)


def ffn_kernel(
    tokens_ref,
    ctx_ref,
    cot_ref,
    norms_ref,
    weights_hbm,
    full_hbm,
    mixed_ref,
    grad_one_ref,
    grad_ctx_ref,
    out_buf,
    in_buf,
    down_buf,
    slope_buf,
    sems,
):
    parts = in_buf.shape[0]
    copies = [pltpu.make_async_copy(weights_hbm.at[3], out_buf, sems.at[0])]
    for part in range(parts):
        copies.append(
            pltpu.make_async_copy(full_hbm.at[1, part], in_buf.at[part], sems.at[1 + 2 * part])
        )
        copies.append(
            pltpu.make_async_copy(full_hbm.at[2, part], down_buf.at[part], sems.at[2 + 2 * part])
        )
    for copy in copies:
        copy.start()
    gain_attn, shift_attn, gain_ffn, shift_ffn = (norms_ref[i : i + 1, :] for i in range(4))
    copies[0].wait()
    first_f, normed_one, inverse_one = norm_forward(
        tokens_ref[...].astype(jnp.float32) + dot_nt(ctx_ref[...], out_buf[...]),
        gain_attn,
        shift_attn,
    )
    first = first_f.astype(jnp.bfloat16)
    ffn_out = first.astype(jnp.float32)
    for part in range(parts):
        copies[1 + 2 * part].wait()
        acted, slope = gelu_parts(dot_nn(first, in_buf[part]))
        slope_buf[part] = slope
        copies[2 + 2 * part].wait()
        ffn_out = ffn_out + dot_nt(acted.astype(jnp.bfloat16), down_buf[part])
    mixed_f, normed_two, inverse_two = norm_forward(ffn_out, gain_ffn, shift_ffn)
    mixed_ref[...] = mixed_f.astype(jnp.bfloat16)
    grad_two = norm_backward(cot_ref[...].astype(jnp.float32), normed_two, inverse_two, gain_ffn)
    grad_ffn = grad_two.astype(jnp.bfloat16)
    grad_first = grad_two
    for part in range(parts):
        grad_hidden = dot_nn(grad_ffn, down_buf[part]) * slope_buf[part]
        grad_first = grad_first + dot_nt(grad_hidden.astype(jnp.bfloat16), in_buf[part])
    grad_one = norm_backward(grad_first, normed_one, inverse_one, gain_attn)
    grad_one_ref[...] = grad_one
    grad_ctx_ref[...] = dot_nn(grad_one.astype(jnp.bfloat16), out_buf[...]).astype(jnp.bfloat16)


def feed_forward(tokens, context, cotangent, norms, weights, full):
    rows, width = tokens.shape
    parts = full.shape[1]
    part_shape = full.shape[1:]
    return pl.pallas_call(
        ffn_kernel,
        out_shape=(
            jax.ShapeDtypeStruct((rows, width), jnp.bfloat16),
            jax.ShapeDtypeStruct((rows, width), jnp.float32),
            jax.ShapeDtypeStruct((rows, width), jnp.bfloat16),
        ),
        in_specs=[VMEM_SPEC] * 4 + [HBM_SPEC] * 2,
        out_specs=(VMEM_SPEC,) * 3,
        scratch_shapes=[
            pltpu.VMEM((width, width), jnp.bfloat16),
            pltpu.VMEM(part_shape, jnp.bfloat16),
            pltpu.VMEM(part_shape, jnp.bfloat16),
            pltpu.VMEM((parts, rows, part_shape[2]), jnp.float32),
            pltpu.SemaphoreType.DMA((1 + 2 * parts,)),
        ],
        compiler_params=pltpu.CompilerParams(vmem_limit_bytes=VMEM_LIMIT),
        name="feed_forward",
    )(tokens, context, cotangent, norms, weights, full)


def adapter_parts(rows_ref, grad_ref, down_t, up, total_ref, down_at, up_at):
    block = 512
    first = jnp.zeros(down_t.shape, jnp.float32)
    second = jnp.zeros(down_t.shape, jnp.float32)
    for at in range(rows_ref.shape[0] // block):
        window = pl.ds(at * block, block)
        rows, grads = rows_ref[window, :], grad_ref[window, :]
        lifted = (ADAPTER_SCALE * dot_nt(rows, down_t)).astype(jnp.bfloat16)
        grad_lifted = (ADAPTER_SCALE * dot_nt(grads, up)).astype(jnp.bfloat16)
        second = second + dot_tn(lifted, grads)
        first = first + dot_tn(grad_lifted, rows)
    total_ref[down_at : down_at + 8, :] = first
    total_ref[up_at : up_at + 8, :] = second


def final_kernel(
    gq_hbm,
    gk_hbm,
    gv_hbm,
    weights_hbm,
    rows_hbm,
    grad_one_hbm,
    ups_ref,
    downs_ref,
    grad_tokens_ref,
    aq_ref,
    av_ref,
    bq_ref,
    bv_ref,
    gq_ref,
    gk_ref,
    gv_ref,
    weights_ref,
    rows_ref,
    grad_one_ref,
    ups_full,
    to_sib,
    from_sib,
    to_x,
    from_x,
    home_to,
    home_from,
    sums,
    sums_in,
    step_out,
    step_in,
    z_slots,
    final_in,
    load_sem,
    block_send,
    block_recv,
    sum_send,
    sum_recv,
):
    place = Place()
    x, y, z, core = place.x, place.y, place.z, place.core
    token_rows = gq_ref.shape[0]
    half_rows = token_rows // 2
    tensor = x * 2 + core

    def rows_of(block):
        return pl.ds(pl.multiple_of(block * token_rows, token_rows), token_rows)

    far_sib, far_same = (1 - x) * 2 + 1 - core, (1 - x) * 2 + core
    near_sib = x * 2 + 1 - core
    loads = {}

    def load(name, source, target):
        copy = pltpu.make_async_copy(source, target, load_sem.at[len(loads)])
        copy.start()
        loads[name] = copy

    for kind in (1, 2):
        load(("w", kind), weights_hbm.at[kind], weights_ref.at[kind])
    for block in range(4):
        owner = (far_sib, far_same, near_sib, tensor)[block]
        load(("k", block), gk_hbm.at[rows_of(owner)], gk_ref.at[rows_of(owner)])
        load(("v", block), gv_hbm.at[rows_of(owner)], gv_ref.at[rows_of(owner)])
    load("rows", rows_hbm, rows_ref)
    load("q", gq_hbm, gq_ref)
    load(("w", 0), weights_hbm.at[0], weights_ref.at[0])
    load("one", grad_one_hbm, grad_one_ref)

    barrier = pltpu.get_barrier_semaphore()
    others = [place.sibling(), place.step("x", 1), place.step("y", 1)]
    others += [place.device(z=lax.rem(z + i, DEPTH)) for i in range(1, DEPTH)]
    for target in others:
        pl.semaphore_signal(barrier, inc=1, device_id=target, device_id_type=MESH_ID)
    pl.semaphore_wait(barrier, len(others))

    def remote(source, target, send, recv, device):
        copy = pltpu.make_async_remote_copy(
            src_ref=source,
            dst_ref=target,
            send_sem=send,
            recv_sem=recv,
            device_id=device,
            device_id_type=MESH_ID,
        )
        copy.start()
        return copy

    slim = bq_ref.shape[1]
    for t in range(ups_ref.shape[0]):
        ups_full[:, t * slim : (t + 1) * slim] = ups_ref[t, :, :slim]

    def partial(owner, half):
        window = pl.ds(pl.multiple_of(owner * token_rows + half * half_rows, half_rows), half_rows)
        return dot_nt(gk_ref[window, :], weights_ref[1]) + dot_nt(gv_ref[window, :], weights_ref[2])

    def await_loads(*names):
        for name in names:
            loads[name].wait()

    await_loads(("w", 1), ("w", 2), ("k", 0), ("v", 0))
    sib_copies, x_copies, home_copies = [], [], []
    for half in range(2):
        to_sib[half] = partial(far_sib, half).astype(jnp.bfloat16)
        sib_copies.append(
            remote(
                to_sib.at[half],
                from_sib.at[half],
                block_send.at[0, half],
                block_recv.at[0, half],
                place.sibling(),
            )
        )
    await_loads(("k", 1), ("v", 1))
    for half in range(2):
        mine = partial(far_same, half)
        sib_copies[half].wait_recv()
        to_x[half] = (mine + from_sib[half].astype(jnp.float32)).astype(jnp.bfloat16)
        x_copies.append(
            remote(
                to_x.at[half],
                from_x.at[half],
                block_send.at[1, half],
                block_recv.at[1, half],
                place.step("x", 1),
            )
        )

    await_loads(("k", 2), ("v", 2), ("k", 3), ("v", 3), "rows", "q")
    own_rows = rows_ref.at[rows_of(tensor)]
    adapter_parts(own_rows, gq_ref, downs_ref[0:8, :], ups_full[0:8, :], sums, 0, 16)
    adapter_parts(rows_ref, gv_ref, downs_ref[8:16, :], ups_full[8:16, :], sums, 8, 24)
    kept = pl.ds(pl.multiple_of(core * 16, 16), 16)
    given = pl.ds(pl.multiple_of((1 - core) * 16, 16), 16)
    sum_copies = [
        remote(sums.at[given], sums_in, sum_send.at[0], sum_recv.at[0], place.sibling())
    ]
    for half in range(2):
        home_to[half] = partial(near_sib, half).astype(jnp.bfloat16)
        home_copies.append(
            remote(
                home_to.at[half],
                home_from.at[half],
                block_send.at[2, half],
                block_recv.at[2, half],
                place.sibling(),
            )
        )
    sum_copies[0].wait_recv()
    step_out[0] = sums[kept, :] + sums_in[...]
    sum_copies.append(
        remote(step_out.at[0], step_in.at[0], sum_send.at[1], sum_recv.at[1], place.step("y", 1))
    )
    await_loads(("w", 0), "one")
    for half in range(2):
        window = pl.ds(half * half_rows, half_rows)
        grad_one_ref[window, :] += partial(tensor, half) + dot_nt(gq_ref[window, :], weights_ref[0])
    sum_copies[1].wait_recv()
    z_slots[z] = step_out[0] + step_in[0]
    for i in range(1, DEPTH):
        there = lax.rem(z + i, DEPTH)
        sum_copies.append(
            remote(
                z_slots.at[z],
                z_slots.at[z],
                sum_send.at[1 + i],
                sum_recv.at[1 + i],
                place.device(z=there),
            )
        )
    for i in range(1, DEPTH):
        sum_copies[1 + i].wait_recv()
    column = z_slots[0]
    for i in range(1, DEPTH):
        column = column + z_slots[i]
    step_out[1] = column
    sum_copies.append(
        remote(
            step_out.at[1],
            step_in.at[1],
            sum_send.at[DEPTH + 1],
            sum_recv.at[DEPTH + 1],
            place.step("x", 1),
        )
    )
    sum_copies[-1].wait_recv()
    step_out[2] = step_out[1] + step_in[1]
    sum_copies.append(
        remote(
            step_out.at[2],
            final_in,
            sum_send.at[DEPTH + 2],
            sum_recv.at[DEPTH + 2],
            place.sibling(),
        )
    )

    for half in range(2):
        home_copies[half].wait_recv()
        x_copies[half].wait_recv()
        window = pl.ds(half * half_rows, half_rows)
        grad_tokens_ref[window, :] = (
            grad_one_ref[window, :]
            + home_from[half].astype(jnp.float32)
            + from_x[half].astype(jnp.float32)
        ).astype(jnp.bfloat16)
    sum_copies[-1].wait_recv()

    def give(first_half, second_half):
        aq_ref[...] = first_half[0:8, :]
        av_ref[...] = first_half[8:16, :]
        for t in range(ups_ref.shape[0]):

            @pl.when(tensor == t)
            def _(t=t):
                bq_ref[...] = second_half[0:8, t * slim : (t + 1) * slim]
                bv_ref[...] = second_half[8:16, t * slim : (t + 1) * slim]

    @pl.when(core == 0)
    def _():
        give(step_out.at[2], final_in)

    @pl.when(core == 1)
    def _():
        give(final_in, step_out.at[2])

    for copy in sib_copies + x_copies + home_copies + sum_copies:
        copy.wait_send()


def final_sums(grad_q, grad_k, grad_v, weights, rows_all, grad_one, ups_all, downs, slim):
    token_rows, width = grad_q.shape
    total_rows = grad_k.shape[0]
    bf16, f32 = jnp.bfloat16, jnp.float32
    half = (2, token_rows // 2, width)
    dma = pltpu.SemaphoreType.DMA
    return pl.pallas_call(
        final_kernel,
        out_shape=(
            jax.ShapeDtypeStruct((token_rows, width), bf16),
            jax.ShapeDtypeStruct((8, width), f32),
            jax.ShapeDtypeStruct((8, width), f32),
            jax.ShapeDtypeStruct((8, slim), f32),
            jax.ShapeDtypeStruct((8, slim), f32),
        ),
        in_specs=[HBM_SPEC] * 6 + [VMEM_SPEC] * 2,
        out_specs=(VMEM_SPEC,) * 5,
        scratch_shapes=[
            pltpu.VMEM((token_rows, width), bf16),
            pltpu.VMEM((total_rows, width), bf16),
            pltpu.VMEM((total_rows, width), bf16),
            pltpu.VMEM((3, width, width), bf16),
            pltpu.VMEM((total_rows, width), bf16),
            pltpu.VMEM((token_rows, width), f32),
            pltpu.VMEM((16, width), bf16),
        ]
        + [pltpu.VMEM(half, bf16)] * 6
        + [
            pltpu.VMEM((32, width), f32),
            pltpu.VMEM((16, width), f32),
            pltpu.VMEM((3, 16, width), f32),
            pltpu.VMEM((2, 16, width), f32),
            pltpu.VMEM((DEPTH, 16, width), f32),
            pltpu.VMEM((16, width), f32),
            dma((14,)),
            dma((3, 2)),
            dma((3, 2)),
            dma((DEPTH + 3,)),
            dma((DEPTH + 3,)),
        ],
        compiler_params=pltpu.CompilerParams(
            collective_id=2, has_side_effects=True, vmem_limit_bytes=VMEM_LIMIT
        ),
        name="final_sums",
    )(grad_q, grad_k, grad_v, weights, rows_all, grad_one, ups_all, downs)


def local(
    fast,
    tokens,
    query_weight,
    w_key,
    value_weight,
    w_out,
    w_in,
    w_down,
    gain_attn,
    shift_attn,
    gain_ffn,
    shift_ffn,
    query_down_factor,
    query_up_factor,
    value_down_factor,
    value_up_factor,
    lengths,
    cotangent,
):
    slim = query_weight.shape[1]
    width = tokens.shape[1]
    token_rows = tokens.shape[0]
    attn_pack = jnp.concatenate([query_weight, w_key, value_weight, w_out.T], axis=1)
    packed = jnp.stack([attn_pack, w_in, w_down.T])
    ups = jnp.concatenate([query_up_factor, value_up_factor], axis=0)
    ups = jnp.pad(ups, ((0, 0), (0, -slim % 128)))
    downs = jnp.concatenate([query_down_factor.T, value_down_factor.T], axis=0)
    if fast:
        full, rows_all, ups_all = gather_all(packed, tokens, ups)
        full = full.reshape(3, 4, width, width)
        order = (0, 2, 1, 3)
    else:
        full = lax.all_gather(packed, "dp", axis=1, tiled=True)
        full = lax.all_gather(full, "tensor", axis=1)
        order = tuple(range(full.shape[1]))
        rows_all = lax.all_gather(tokens, "tensor")
        ups_all = lax.all_gather(ups, "tensor")
    rows_all = rows_all.reshape(-1, width)
    weights, q_own, k_all, v_all = project(order, full, rows_all, ups_all, downs, token_rows)

    context, lse = attend_forward(lengths, q_own, k_all, v_all)
    norms = jnp.stack([gain_attn, shift_attn, gain_ffn, shift_ffn])
    mixed, grad_one, grad_context = feed_forward(
        tokens, context, cotangent, norms, weights, full
    )

    grad_q, grad_k, grad_v = attend_backward(
        lengths, q_own, k_all, v_all, context, lse, grad_context
    )
    if fast:
        grad_tokens, grad_aq, grad_av, grad_bq, grad_bv = final_sums(
            grad_q, grad_k, grad_v, weights, rows_all, grad_one, ups_all, downs, slim
        )
        return (mixed, grad_tokens, grad_aq.T, grad_bq, grad_av.T, grad_bv)

    query_up = ups_all[:, :8, :slim].transpose(1, 0, 2).reshape(8, width)
    value_up = ups_all[:, 8:, :slim].transpose(1, 0, 2).reshape(8, width)
    w_q, w_k, w_v = weights[0], weights[1], weights[2]
    u_query = dot_nn(tokens, query_down_factor).astype(jnp.bfloat16)
    u_value = dot_nn(rows_all, value_down_factor).astype(jnp.bfloat16)
    grad_uq = ADAPTER_SCALE * dot_nt(grad_q, query_up)
    grad_uv = ADAPTER_SCALE * dot_nt(grad_v, value_up)
    grad_bq = ADAPTER_SCALE * dot_tn(u_query, grad_q)
    grad_bv = ADAPTER_SCALE * dot_tn(u_value, grad_v)
    grad_aq = dot_tn(tokens, grad_uq.astype(jnp.bfloat16))
    grad_av = dot_tn(rows_all, grad_uv.astype(jnp.bfloat16))
    grad_rows = dot_nt(grad_k, w_k) + dot_nt(grad_v, w_v)
    own_rows = dot_nt(grad_q, w_q)
    shared = lax.psum_scatter(
        grad_rows.astype(jnp.bfloat16), "tensor", scatter_dimension=0, tiled=True
    )
    grad_tokens = (grad_one + own_rows + shared.astype(jnp.float32)).astype(jnp.bfloat16)
    grad_aq, grad_av, grad_bq, grad_bv = lax.psum(
        (grad_aq, grad_av, grad_bq, grad_bv), ("dp", "tensor")
    )
    at = lax.axis_index("tensor") * slim
    grad_bq = lax.dynamic_slice_in_dim(grad_bq, at, slim, 1)
    grad_bv = lax.dynamic_slice_in_dim(grad_bv, at, slim, 1)
    return (mixed, grad_tokens, grad_aq, grad_bq, grad_av, grad_bv)


def solution(mesh):
    fast = dict(mesh.shape) == {"dp": 2 * DEPTH, "tensor": 4}
    return jax.shard_map(
        functools.partial(local, fast),
        mesh=mesh,
        in_specs=(
            P(("dp", "tensor"), None),
            P("dp", "tensor"),
            P("dp", "tensor"),
            P("dp", "tensor"),
            P("tensor", "dp"),
            P("dp", "tensor"),
            P("tensor", "dp"),
            P(),
            P(),
            P(),
            P(),
            P(),
            P(None, "tensor"),
            P(),
            P(None, "tensor"),
            P("dp", None),
            P(("dp", "tensor"), None),
        ),
        out_specs=(
            P(("dp", "tensor"), None),
            P(("dp", "tensor"), None),
            P(),
            P(None, "tensor"),
            P(),
            P(None, "tensor"),
        ),
        check_vma=False,
    )
```

```python
import functools
import heapq

import jax
import jax.numpy as jnp
from jax import lax
from jax.experimental import pallas as pl
from jax.experimental.pallas import tpu as pltpu
from jax.sharding import PartitionSpec as P

HEAD_DIM = 64
PAIR = 2 * HEAD_DIM
Q_BLOCK = 256
K_BLOCK = 512
FFN_BLOCK = 256
FORWARD_GROUP = 3
BACKWARD_GROUP = 3
ADAPTER_SCALE = 2.0
SCORE_SCALE = HEAD_DIM ** (-0.5)
LOG2_SCALE = SCORE_SCALE * 1.4426950408889634
NEG_FILL = -1e30
LN_EPS = 1e-05
VMEM_LIMIT = 56 * 1024 * 1024


def dot_nn(left, right):
    return jnp.dot(left, right, preferred_element_type=jnp.float32)


def dot_nt(left, right):
    return lax.dot_general(
        left, right, (((1,), (1,)), ((), ())), preferred_element_type=jnp.float32
    )


def dot_tn(left, right):
    return lax.dot_general(
        left, right, (((0,), (0,)), ((), ())), preferred_element_type=jnp.float32
    )


def norm_forward(row_vals, gain_vals, offset):
    middle = jnp.mean(row_vals, axis=-1, keepdims=True)
    centred = row_vals - middle
    inverse = lax.rsqrt(jnp.mean(centred * centred, axis=-1, keepdims=True) + LN_EPS)
    normed = centred * inverse
    return (normed * gain_vals + offset, normed, inverse)


def norm_backward(grad_out, normed, inverse, gain_vals):
    grad_n = grad_out * gain_vals
    return inverse * (
        grad_n
        - jnp.mean(grad_n, axis=-1, keepdims=True)
        - normed * jnp.mean(grad_n * normed, axis=-1, keepdims=True)
    )


def gelu_parts(hidden):
    cdf_part = 0.5 * (1.0 + lax.erf(hidden * 0.7071067811865476))
    density = jnp.exp(-0.5 * hidden * hidden) * 0.3989422804014327
    return (hidden * cdf_part, cdf_part + hidden * density)


def block_span(lengths_ref, first_row, rows, total_rows):
    last_row = first_row + rows - 1

    def slot_step(slot, carry):
        end, low, high = carry
        end = end + lengths_ref[0, slot]
        low = jnp.where(end <= first_row, jnp.maximum(low, end), low)
        high = jnp.where(end > last_row, jnp.minimum(high, end), high)
        return end, low, high

    start = (jnp.int32(0), jnp.int32(0), jnp.int32(total_rows))
    _, low, high = lax.fori_loop(0, lengths_ref.shape[1], slot_step, start, unroll=8)
    return low, high


def row_bounds(lengths_ref, first_row, rows, total_rows):
    place = first_row + lax.broadcasted_iota(jnp.int32, (1, rows), 1)

    def slot_step(slot, carry):
        end, begin, finish = carry
        end = end + lengths_ref[0, slot]
        done = place >= end
        begin = jnp.where(done, jnp.maximum(begin, end), begin)
        finish = jnp.where(done, finish, jnp.minimum(finish, end))
        return end, begin, finish

    start = (
        jnp.int32(0),
        jnp.zeros((1, rows), jnp.int32),
        jnp.full((1, rows), total_rows, jnp.int32),
    )
    _, begin, finish = lax.fori_loop(0, lengths_ref.shape[1], slot_step, start, unroll=8)
    return begin, finish


def stack_pair(block):
    lane = lax.broadcasted_iota(jnp.int32, block.shape, 1)
    zero = jnp.zeros_like(block)
    return jnp.concatenate(
        [jnp.where(lane < HEAD_DIM, block, zero), jnp.where(lane >= HEAD_DIM, block, zero)],
        axis=0,
    )


def unstack_pair(block, rows):
    joined = jnp.concatenate([block[:HEAD_DIM, :rows], block[HEAD_DIM:, rows:]], axis=0)
    return joined.T


def window_mask(step, low, begin, finish, total_rows):
    wanted = low + step * K_BLOCK
    start = pl.multiple_of(jnp.minimum(wanted, total_rows - K_BLOCK), 16)
    key_at = start + lax.broadcasted_iota(jnp.int32, (K_BLOCK, begin.shape[1]), 0)
    return start, (key_at >= jnp.maximum(begin, wanted)) & (key_at < finish)


def each_q_block(lengths_ref, rows, total_rows, group, heads_width, block_step):
    base = lax.axis_index("tensor") * rows

    @pl.loop(0, rows // Q_BLOCK)
    def _(q_at):
        first_row = base + q_at * Q_BLOCK
        low, high = block_span(lengths_ref, first_row, Q_BLOCK, total_rows)
        low = (low // 16) * 16
        steps = (high - low + K_BLOCK - 1) // K_BLOCK
        begin, finish = row_bounds(lengths_ref, first_row, Q_BLOCK, total_rows)
        q_rows = pl.ds(pl.multiple_of(q_at * Q_BLOCK, Q_BLOCK), Q_BLOCK)

        @pl.loop(0, heads_width // PAIR // group)
        def _(at):
            pairs = [at * group + i for i in range(group)]
            lanes = [pl.ds(pl.multiple_of(pair * PAIR, PAIR), PAIR) for pair in pairs]
            slots = [q_at * (heads_width // PAIR) + pair for pair in pairs]
            block_step(q_rows, lanes, slots, low, steps, begin, finish)


def forward_kernel(lengths_ref, q_ref, k_ref, v_ref, out_ref, lse_ref):
    total_rows = k_ref.shape[0]

    def block_step(q_rows, lanes, slots, low, steps, begin, finish):
        q_two = [stack_pair(q_ref[q_rows, lane]) for lane in lanes]

        def body(step, carry):
            start, allowed = window_mask(step, low, begin, finish, total_rows)
            window = pl.ds(start, K_BLOCK)
            both = jnp.concatenate([allowed, allowed], axis=1)
            result = []
            for (top, total, acc), q_pair, lane in zip(carry, q_two, lanes):
                scores = jnp.where(both, dot_nt(k_ref[window, lane], q_pair), NEG_FILL)
                new_top = jnp.maximum(top, jnp.max(scores, axis=0, keepdims=True))
                probs = jnp.exp2((scores - new_top) * LOG2_SCALE)
                shrink = jnp.exp2((top - new_top) * LOG2_SCALE)
                total = total * shrink + jnp.sum(probs, axis=0, keepdims=True)
                acc = acc * shrink + dot_tn(v_ref[window, lane], probs.astype(jnp.bfloat16))
                result.append((new_top, total, acc))
            return tuple(result)

        empty = (
            jnp.full((1, 2 * Q_BLOCK), NEG_FILL, jnp.float32),
            jnp.zeros((1, 2 * Q_BLOCK), jnp.float32),
            jnp.zeros((PAIR, 2 * Q_BLOCK), jnp.float32),
        )
        final = lax.fori_loop(0, steps, body, (empty,) * len(lanes))
        for (top, total, acc), lane, slot in zip(final, lanes, slots):
            out_ref[q_rows, lane] = unstack_pair(acc / total, Q_BLOCK).astype(jnp.bfloat16)
            lse_ref[slot] = top * LOG2_SCALE + jnp.log2(total)

    each_q_block(
        lengths_ref, q_ref.shape[0], total_rows, FORWARD_GROUP, q_ref.shape[1], block_step
    )


def backward_kernel(
    lengths_ref,
    q_ref,
    k_ref,
    v_ref,
    ctx_ref,
    lse_ref,
    grad_ref,
    gq_ref,
    gk_ref,
    gv_ref,
    gk_acc,
    gv_acc,
):
    total_rows = k_ref.shape[0]
    gk_acc[...] = jnp.zeros_like(gk_acc)
    gv_acc[...] = jnp.zeros_like(gv_acc)

    def block_step(q_rows, lanes, slots, low, steps, begin, finish):
        ready = []
        for lane, slot in zip(lanes, slots):
            grads = grad_ref[q_rows, lane]
            product = (grads.astype(jnp.float32) * ctx_ref[q_rows, lane].astype(jnp.float32)).T
            row_dot = jnp.concatenate(
                [
                    jnp.sum(product[:HEAD_DIM], axis=0, keepdims=True),
                    jnp.sum(product[HEAD_DIM:], axis=0, keepdims=True),
                ],
                axis=1,
            )
            ready.append((stack_pair(q_ref[q_rows, lane]), stack_pair(grads), row_dot, lse_ref[slot]))

        def body(step, carry):
            start, allowed = window_mask(step, low, begin, finish, total_rows)
            window = pl.ds(start, K_BLOCK)
            both = jnp.concatenate([allowed, allowed], axis=1)
            result = []
            for acc, (q_pair, grad_pair, row_dot, lse), lane in zip(carry, ready, lanes):
                keys = k_ref[window, lane]
                scores = jnp.where(both, dot_nt(keys, q_pair), NEG_FILL)
                probs = jnp.exp2(scores * LOG2_SCALE - lse)
                grad_probs = dot_nt(v_ref[window, lane], grad_pair)
                grad_scores = (probs * (grad_probs - row_dot)).astype(jnp.bfloat16)
                gk_acc[window, lane] += dot_nn(grad_scores, q_pair)
                gv_acc[window, lane] += dot_nn(probs.astype(jnp.bfloat16), grad_pair)
                result.append(acc + dot_tn(keys, grad_scores))
            return tuple(result)

        zero = jnp.zeros((PAIR, 2 * Q_BLOCK), jnp.float32)
        final = lax.fori_loop(0, steps, body, (zero,) * len(lanes))
        for acc, lane in zip(final, lanes):
            gq_ref[q_rows, lane] = (unstack_pair(acc, Q_BLOCK) * SCORE_SCALE).astype(jnp.bfloat16)

    each_q_block(
        lengths_ref, q_ref.shape[0], total_rows, BACKWARD_GROUP, q_ref.shape[1], block_step
    )

    @pl.loop(0, total_rows // K_BLOCK)
    def _(at):
        window = pl.ds(pl.multiple_of(at * K_BLOCK, K_BLOCK), K_BLOCK)
        gk_ref[window, :] = (gk_acc[window, :] * SCORE_SCALE).astype(jnp.bfloat16)
        gv_ref[window, :] = gv_acc[window, :].astype(jnp.bfloat16)


VMEM_SPEC = pl.BlockSpec(memory_space=pltpu.VMEM)
HBM_SPEC = pl.BlockSpec(memory_space=pltpu.HBM)
SMEM_SPEC = pl.BlockSpec(memory_space=pltpu.SMEM)


def attend_forward(lengths, q_own, k_all, v_all):
    rows, width = q_own.shape
    heads = width // HEAD_DIM
    return pl.pallas_call(
        forward_kernel,
        out_shape=(
            jax.ShapeDtypeStruct((rows, width), jnp.bfloat16),
            jax.ShapeDtypeStruct((rows // Q_BLOCK * heads // 2, 1, 2 * Q_BLOCK), jnp.float32),
        ),
        in_specs=[SMEM_SPEC] + [VMEM_SPEC] * 3,
        out_specs=(VMEM_SPEC, VMEM_SPEC),
        compiler_params=pltpu.CompilerParams(vmem_limit_bytes=VMEM_LIMIT),
        name="attend_forward",
    )(lengths, q_own, k_all, v_all)


def attend_backward(lengths, q_own, k_all, v_all, context, lse, grad_context):
    rows, width = q_own.shape
    total_rows = k_all.shape[0]
    return pl.pallas_call(
        backward_kernel,
        out_shape=(
            jax.ShapeDtypeStruct((rows, width), jnp.bfloat16),
            jax.ShapeDtypeStruct((total_rows, width), jnp.bfloat16),
            jax.ShapeDtypeStruct((total_rows, width), jnp.bfloat16),
        ),
        in_specs=[SMEM_SPEC] + [VMEM_SPEC] * 6,
        out_specs=(VMEM_SPEC,) * 3,
        scratch_shapes=[
            pltpu.VMEM((total_rows, width), jnp.float32),
            pltpu.VMEM((total_rows, width), jnp.float32),
        ],
        compiler_params=pltpu.CompilerParams(vmem_limit_bytes=VMEM_LIMIT),
        name="attend_backward",
    )(lengths, q_own, k_all, v_all, context, lse, grad_context)


MESH_ID = pl.DeviceIdType.MESH
DEPTH = 4
FULL_ROWS = 96

FLOWS = (
    (0, 0, "zxy", 0.0),
    (0, 1, "zyx", 0.0),
    (1, 0, "xzy", 12.0),
    (1, 1, "zyx", 24.0),
    (2, 0, "xzy", 12.0),
    (2, 1, "yxz", 12.0),
)
OWN = (0, 0, 0)


def forwards(order, piece):
    used = [axis for axis in order if piece["xyz".index(axis)] != 0]
    at = order.index(used[-1]) if used else -1
    steps = []
    if used and used[-1] == "z":
        steps.append(("z", 1 if piece[2] < 0 else -1))
    for axis in order[at + 1 :]:
        steps += [("z", 1), ("z", -1)] if axis == "z" else [(axis, 1)]
    return steps


def passed(piece, axis, sign):
    x, y, z = piece
    if axis == "x":
        return (1 - x, y, z)
    return (x, 1 - y, z) if axis == "y" else (x, y, z - sign)


def event_order(token_time):
    per_piece = 1.7
    links, heap, times, count = {}, [], {}, 0
    for z in range(DEPTH):
        links[z, "x", 1] = token_time
        for flow, (_, _, _, start) in enumerate(FLOWS):
            heapq.heappush(heap, (start + 0.01 * flow, count, z, flow, OWN))
            count += 1
    while heap:
        now, _, z, flow, piece = heapq.heappop(heap)
        times.setdefault((flow, piece), []).append(now)
        for axis, sign in forwards(FLOWS[flow][2], piece):
            there = z + sign if axis == "z" else z
            if not 0 <= there < DEPTH:
                continue
            end = max(links.get((z, axis, sign), 0.0), now) + per_piece
            links[z, axis, sign] = end
            heapq.heappush(heap, (end + 3.0, count, there, flow, passed(piece, axis, sign)))
            count += 1
    return [key for _, key in sorted((sum(v) / len(v), key) for key, v in times.items())]


class Place:
    def __init__(self):
        dp, tensor = lax.axis_index("dp"), lax.axis_index("tensor")
        self.z, self.y = dp // 2, lax.rem(dp, 2)
        self.x, self.core = tensor // 2, lax.rem(tensor, 2)

    def device(self, x=None, y=None, z=None, core=None):
        x = self.x if x is None else x
        y = self.y if y is None else y
        z = self.z if z is None else z
        core = self.core if core is None else core
        return (z * 2 + y, x * 2 + core)

    def step(self, axis, sign):
        if axis == "x":
            return self.device(x=1 - self.x)
        return self.device(y=1 - self.y) if axis == "y" else self.device(z=self.z + sign)

    def sibling(self):
        return self.device(core=1 - self.core)


def gather_kernel(
    wq_ref,
    wk_ref,
    wv_ref,
    wo_ref,
    w_in_ref,
    w_down_ref,
    tokens_ref,
    up_q_ref,
    up_v_ref,
    down_q_ref,
    down_v_ref,
    full_ref,
    weights_hbm,
    rows_hbm,
    q_hbm,
    k_hbm,
    v_hbm,
    ups_full,
    pack_ref,
    packs_ref,
    rows_ref,
    ups_ref,
    ups_all_ref,
    weights_ref,
    q_ref,
    k_ref,
    v_ref,
    piece_recv,
    send_sem,
    sib_send,
    sib_recv,
    own_sem,
    rows_send,
    rows_recv,
    ups_send,
    ups_recv,
    out_sem,
):
    place = Place()
    x, y, z, core = place.x, place.y, place.z, place.core
    token_rows = tokens_ref.shape[0]
    part_rows = FULL_ROWS // 2
    half_rows = token_rows // 2

    barrier = pltpu.get_barrier_semaphore()
    others = (
        place.sibling(),
        place.step("x", 1),
        place.device(x=1 - x, core=1 - core),
        place.step("y", 1),
    )
    for target in others:
        pl.semaphore_signal(barrier, inc=1, device_id=target, device_id_type=MESH_ID)
    for sign, there in ((1, z < DEPTH - 1), (-1, z > 0)):

        @pl.when(there)
        def _(sign=sign):
            pl.semaphore_signal(
                barrier, inc=1, device_id=place.step("z", sign), device_id_type=MESH_ID
            )

    slim = wq_ref.shape[1]
    for kind, ref in enumerate((wq_ref, wk_ref, wv_ref)):
        pack_ref[:, kind * slim : (kind + 1) * slim] = ref[...]
    pack_ref[:, 3 * slim : 4 * slim] = wo_ref[...].astype(jnp.float32).T.astype(jnp.bfloat16)
    ups_ref[...] = jnp.zeros_like(ups_ref)
    ups_ref[0:8, :slim] = up_q_ref[...].astype(jnp.float32)
    ups_ref[8:16, :slim] = up_v_ref[...].astype(jnp.float32)
    shards = (pack_ref, w_in_ref, w_down_ref)
    inner = ((z > 0) & (z < DEPTH - 1)).astype(jnp.int32)
    pl.semaphore_wait(barrier, len(others) + 1 + inner)

    def remote(source, target, send, recv, device):
        return pltpu.make_async_remote_copy(
            src_ref=source,
            dst_ref=target,
            send_sem=send,
            recv_sem=recv,
            device_id=device,
            device_id_type=MESH_ID,
        )

    def rows_at(owner_x, owner_core, half):
        return rows_ref.at[owner_x * 2 + owner_core, pl.ds(half * half_rows, half_rows)]

    own_copies = [
        pltpu.make_async_copy(pack_ref, packs_ref.at[core, x, z, y], own_sem.at[0]),
        pltpu.make_async_copy(tokens_ref, rows_ref.at[x * 2 + core], own_sem.at[1]),
        pltpu.make_async_copy(ups_ref, ups_all_ref.at[x * 2 + core], own_sem.at[2]),
        pltpu.make_async_copy(w_in_ref, full_ref.at[0, core, x, z, y], own_sem.at[3]),
        pltpu.make_async_copy(w_down_ref, full_ref.at[1, core, x, z, y], own_sem.at[4]),
    ]
    row_copies = []
    for half in range(2):
        source = tokens_ref.at[pl.ds(half * half_rows, half_rows)]
        for slot, device in ((0, place.step("x", 1)), (1, place.sibling())):
            row_copies.append(
                remote(
                    source,
                    rows_at(x, core, half),
                    rows_send.at[slot, half],
                    rows_recv.at[slot, half],
                    device,
                )
            )
    up_copies = [
        remote(ups_ref, ups_all_ref.at[x * 2 + core], ups_send.at[i], ups_recv.at[i], device)
        for i, device in enumerate(others[:3])
    ]

    sends = {}

    def gathered(kind):
        return packs_ref if kind == 0 else full_ref.at[kind - 1]

    def piece_at(flow, piece):
        kind, part, _, _ = FLOWS[flow]
        px, py = lax.rem(x + piece[0], 2), lax.rem(y + piece[1], 2)
        return gathered(kind).at[
            core, px, z + piece[2], py, pl.ds(part * part_rows, part_rows)
        ], (px * 2 + py) * DEPTH + z + piece[2]

    def handle(flow, piece):
        kind, part, order, _ = FLOWS[flow]
        landed, index = piece_at(flow, piece)
        source = landed
        if piece == OWN:
            source = shards[kind].at[pl.ds(part * part_rows, part_rows)]
        else:
            remote(landed, landed, send_sem.at[flow, 0], piece_recv.at[flow, index], place.sibling()).wait_recv()
        for axis, sign in forwards(order, piece):
            slot = {"x": 0, "y": 1, "z": 2 if sign > 0 else 3}[axis]
            copy = remote(
                source,
                landed,
                send_sem.at[flow, slot],
                piece_recv.at[flow, index],
                place.step(axis, sign),
            )
            if axis == "z":
                pl.when((z + sign >= 0) & (z + sign < DEPTH))(copy.start)
            else:
                copy.start()
                sends[flow, slot] = sends.get((flow, slot), 0) + 1
        remote(source, landed, sib_send.at[flow], sib_recv.at[flow], place.sibling()).start()

    def block_of(flow, pieces, plane):
        kind, part, _, _ = FLOWS[flow]
        nx = 2 if pieces % 2 == 0 else 1
        ny = 2 if pieces % 4 == 0 else 1
        return gathered(kind).at[
            plane,
            pl.ds(0, nx),
            pl.ds(0, pieces // (nx * ny)),
            pl.ds(0, ny),
            pl.ds(part * part_rows, part_rows),
        ]

    def finish_flow(flow):
        order = FLOWS[flow][2]
        everything = block_of(flow, 4 * DEPTH, 1 - core)
        remote(everything, everything, sib_send.at[flow], sib_recv.at[flow], place.sibling()).wait()

    def finish_sends(flow):
        order = FLOWS[flow][2]
        for axis, slot in (("x", 0), ("y", 1)):
            block = block_of(flow, 2 ** order.index(axis) * (DEPTH // 2 if "z" in order[: order.index(axis)] else 1), core)
            remote(block, block, send_sem.at[flow, slot], sib_recv.at[flow], place.sibling()).wait_send()
        each = 2 ** order.index("z")
        for at in range(DEPTH):
            for slot, sets in ((2, at + 1 if at < DEPTH - 1 else 0), (3, DEPTH - at if at > 0 else 0)):
                if sets:

                    @pl.when(z == at)
                    def _(slot=slot, sets=sets):
                        nx = 2 if each > 1 else 1
                        ny = 2 if each > 2 else 1
                        kind, part, _, _ = FLOWS[flow]
                        block = gathered(kind).at[
                            core,
                            pl.ds(0, nx),
                            pl.ds(0, sets),
                            pl.ds(0, ny),
                            pl.ds(part * part_rows, part_rows),
                        ]
                        remote(
                            block, block, send_sem.at[flow, slot], sib_recv.at[flow], place.sibling()
                        ).wait_send()

    for copy in row_copies + up_copies + own_copies:
        copy.start()

    def pass_rows(half):
        row_copies[2 * half].wait_recv()
        landed = rows_at(1 - x, core, half)
        copy = remote(landed, landed, rows_send.at[2, half], rows_recv.at[2, half], place.sibling())
        copy.start()
        return copy

    outs = []

    def write(source, target):
        copy = pltpu.make_async_copy(source, target, out_sem.at[len(outs)])
        copy.start()
        outs.append(copy)

    def assemble(t):
        if t == 0:
            for copy in up_copies + own_copies[:3]:
                copy.wait()
            for half in range(2):
                row_copies[2 * half + 1].wait_recv()
                passed_rows[half].wait_recv()
            for owner in range(4):
                write(rows_ref.at[owner], rows_hbm.at[pl.ds(owner * token_rows, token_rows)])
            finish_flow(0)
            finish_flow(1)
            for owner in range(4):
                ups_full[:, owner * slim : (owner + 1) * slim] = ups_all_ref[owner, :, :slim].astype(jnp.bfloat16)
        lanes = slice(t * slim, (t + 1) * slim)
        source = packs_ref.at[t % 2, t // 2]
        for kind, down_ref, first in ((0, down_q_ref, 0), (1, None, 0), (2, down_v_ref, 8), (3, None, 0)):
            part = source[:, :, :, kind * slim : (kind + 1) * slim].reshape(-1, slim)
            if down_ref is not None:
                up = ups_all_ref[t, first : first + 8, :slim].astype(jnp.bfloat16)
                product = dot_tn(down_ref[...], up)
                part = (part.astype(jnp.float32) + ADAPTER_SCALE * product).astype(jnp.bfloat16)
            weights_ref[kind, :, lanes] = part
        if t == 3:
            write(weights_ref, weights_hbm)

    def own_queries():
        q_ref[...] = dot_nn(rows_ref[x * 2 + core], weights_ref[0]).astype(jnp.bfloat16)
        write(q_ref, q_hbm)

    def keys_values(ref, hbm, kind, owner):
        ref[owner] = dot_nn(rows_ref[owner], weights_ref[kind]).astype(jnp.bfloat16)
        write(ref.at[owner], hbm.at[pl.ds(owner * token_rows, token_rows)])

    steps = [functools.partial(assemble, t) for t in range(4)] + [own_queries]
    for owner in range(4):
        steps.append(functools.partial(keys_values, k_ref, k_hbm, 1, owner))
        steps.append(functools.partial(keys_values, v_ref, v_hbm, 2, owner))

    passed_rows = []
    events = event_order(17.0)
    last_pack = max(i for i, (flow, _) in enumerate(events) if FLOWS[flow][0] == 0)
    between = max(1, (len(events) - last_pack) // (len(steps) + 1))
    arrivals = 0
    for at, (flow, piece) in enumerate(events):
        if piece[2] == 0:
            handle(flow, piece)
        else:
            pl.when((z + piece[2] >= 0) & (z + piece[2] < DEPTH))(
                functools.partial(handle, flow, piece)
            )
        if piece != OWN:
            arrivals += 1
            if arrivals in (8, 16):
                passed_rows.append(pass_rows(len(passed_rows)))
        if at >= last_pack and (at - last_pack) % between == between - 1 and steps:
            steps.pop(0)()
    for step in steps:
        step()

    for half in range(2):
        row_copies[2 * half].wait_send()
        row_copies[2 * half + 1].wait_send()
        passed_rows[half].wait_send()
    for copy in own_copies[3:] + outs:
        copy.wait()
    for flow in range(len(FLOWS)):
        if flow > 1:
            finish_flow(flow)
        finish_sends(flow)


def gather_all(w_q, w_k, w_v, w_out, w_in, w_down_t, tokens, up_q, up_v, down_q_t, down_v_t):
    shard_rows, width = w_in.shape
    token_rows = tokens.shape[0]
    bf16, f32 = jnp.bfloat16, jnp.float32
    slim = w_q.shape[1]
    padded = slim + -slim % 128
    flows = len(FLOWS)
    dma = pltpu.SemaphoreType.DMA
    grid = (2, 2, DEPTH, 2, shard_rows, width)
    return pl.pallas_call(
        gather_kernel,
        out_shape=(
            jax.ShapeDtypeStruct((2,) + grid, bf16),
            jax.ShapeDtypeStruct((4, width, width), bf16),
            jax.ShapeDtypeStruct((4 * token_rows, width), bf16),
            jax.ShapeDtypeStruct((token_rows, width), bf16),
            jax.ShapeDtypeStruct((4 * token_rows, width), bf16),
            jax.ShapeDtypeStruct((4 * token_rows, width), bf16),
            jax.ShapeDtypeStruct((16, width), bf16),
        ),
        in_specs=[VMEM_SPEC] * 4 + [HBM_SPEC] * 3 + [VMEM_SPEC] * 4,
        out_specs=(HBM_SPEC,) * 6 + (VMEM_SPEC,),
        scratch_shapes=[
            pltpu.VMEM((shard_rows, width), bf16),
            pltpu.VMEM(grid, bf16),
            pltpu.VMEM((4, token_rows, width), bf16),
            pltpu.VMEM((16, padded), f32),
            pltpu.VMEM((4, 16, padded), f32),
            pltpu.VMEM((4, width, width), bf16),
            pltpu.VMEM((token_rows, width), bf16),
            pltpu.VMEM((4, token_rows, width), bf16),
            pltpu.VMEM((4, token_rows, width), bf16),
            dma((flows, 4 * DEPTH)),
            dma((flows, 4)),
            dma((flows,)),
            dma((flows,)),
            dma((5,)),
            dma((3, 2)),
            dma((3, 2)),
            dma((3,)),
            dma((3,)),
            dma((14,)),
        ],
        compiler_params=pltpu.CompilerParams(
            collective_id=1, has_side_effects=True, vmem_limit_bytes=VMEM_LIMIT
        ),
        name="gather_all",
    )(w_q, w_k, w_v, w_out, w_in, w_down_t, tokens, up_q, up_v, down_q_t, down_v_t)


def project_kernel(
    order,
    full_hbm,
    rows_ref,
    ups_ref,
    downs_ref,
    weights_ref,
    q_ref,
    k_ref,
    v_ref,
    packs_ref,
    sems,
):
    token_rows = q_ref.shape[0]
    slim = packs_ref.shape[2] // 4
    tensor = lax.axis_index("tensor")
    copies = [
        pltpu.make_async_copy(full_hbm.at[0, i], packs_ref.at[i], sems.at[i])
        for i in range(len(order))
    ]
    for copy in copies:
        copy.start()
    for i, t in enumerate(order):
        copies[i].wait()
        lanes = slice(t * slim, (t + 1) * slim)
        for kind, first in ((0, 0), (1, None), (2, 8), (3, None)):
            part = packs_ref[i, :, kind * slim : (kind + 1) * slim]
            if first is not None:
                up = ups_ref[t, first : first + 8, :slim]
                product = dot_tn(downs_ref[first : first + 8, :], up)
                part = (part.astype(jnp.float32) + ADAPTER_SCALE * product).astype(jnp.bfloat16)
            weights_ref[kind, :, lanes] = part
    own = rows_ref[pl.ds(pl.multiple_of(tensor * token_rows, token_rows), token_rows), :]
    q_ref[...] = dot_nn(own, weights_ref[0]).astype(jnp.bfloat16)

    @pl.loop(0, rows_ref.shape[0] // token_rows)
    def _(at):
        window = pl.ds(pl.multiple_of(at * token_rows, token_rows), token_rows)
        block = rows_ref[window, :]
        k_ref[window, :] = dot_nn(block, weights_ref[1]).astype(jnp.bfloat16)
        v_ref[window, :] = dot_nn(block, weights_ref[2]).astype(jnp.bfloat16)


def project(order, full, rows_all, ups_all, downs, token_rows):
    total_rows, width = rows_all.shape
    bf16 = jnp.bfloat16
    return pl.pallas_call(
        functools.partial(project_kernel, order),
        out_shape=(
            jax.ShapeDtypeStruct((4, width, width), bf16),
            jax.ShapeDtypeStruct((token_rows, width), bf16),
            jax.ShapeDtypeStruct((total_rows, width), bf16),
            jax.ShapeDtypeStruct((total_rows, width), bf16),
        ),
        in_specs=[HBM_SPEC] + [VMEM_SPEC] * 3,
        out_specs=(VMEM_SPEC,) * 4,
        scratch_shapes=[
            pltpu.VMEM(full.shape[1:], bf16),
            pltpu.SemaphoreType.DMA((len(order),)),
        ],
        compiler_params=pltpu.CompilerParams(vmem_limit_bytes=VMEM_LIMIT),
        name="project",
    )(full, rows_all, ups_all, downs)


def ffn_kernel(
    tokens_ref,
    ctx_ref,
    cot_ref,
    gain_attn_ref,
    shift_attn_ref,
    gain_ffn_ref,
    shift_ffn_ref,
    weights_hbm,
    full_hbm,
    mixed_ref,
    grad_one_ref,
    grad_ctx_ref,
    out_buf,
    in_buf,
    down_buf,
    slope_buf,
    first_buf,
    sum_buf,
    normed_buf,
    inverse_buf,
    sems,
):
    parts, kinds = in_buf.shape[0], full_hbm.shape[0]
    blocks = tokens_ref.shape[0] // FFN_BLOCK
    gain_attn, shift_attn, gain_ffn, shift_ffn = (
        ref[...].reshape(1, -1) for ref in (gain_attn_ref, shift_attn_ref, gain_ffn_ref, shift_ffn_ref)
    )

    def out_copy():
        return pltpu.make_async_copy(weights_hbm.at[3], out_buf, sems.at[2 * parts])

    def in_copy(part):
        return pltpu.make_async_copy(full_hbm.at[kinds - 2, part], in_buf.at[part], sems.at[part])

    def down_copy(part):
        return pltpu.make_async_copy(
            full_hbm.at[kinds - 1, part], down_buf.at[part], sems.at[parts + part]
        )

    def block_rows(at):
        return pl.ds(pl.multiple_of(at * FFN_BLOCK, FFN_BLOCK), FFN_BLOCK)

    out_copy().start()
    for part in range(parts):
        in_copy(part).start()
        down_copy(part).start()
    out_copy().wait()

    @pl.loop(0, blocks)
    def _(at):
        rows = block_rows(at)
        residual = tokens_ref[rows, :].astype(jnp.float32) + dot_nt(ctx_ref[rows, :], out_buf[...])
        first, normed, inverse = norm_forward(residual, gain_attn, shift_attn)
        first_buf[rows, :] = first.astype(jnp.bfloat16)
        sum_buf[rows, :] = first.astype(jnp.bfloat16).astype(jnp.float32)
        normed_buf[rows, :] = normed
        inverse_buf[rows, :] = inverse

    @pl.loop(0, parts)
    def _(part):
        in_copy(part).wait()
        down_copy(part).wait()

        @pl.loop(0, blocks)
        def _(at):
            rows = block_rows(at)
            acted, slope = gelu_parts(dot_nn(first_buf[rows, :], in_buf[part]))
            slope_buf[part, rows, :] = slope
            sum_buf[rows, :] += dot_nt(acted.astype(jnp.bfloat16), down_buf[part])

    @pl.loop(0, blocks)
    def _(at):
        rows = block_rows(at)
        mixed, normed, inverse = norm_forward(sum_buf[rows, :], gain_ffn, shift_ffn)
        mixed_ref[rows, :] = mixed.astype(jnp.bfloat16)
        grad_two = norm_backward(cot_ref[rows, :].astype(jnp.float32), normed, inverse, gain_ffn)
        first_buf[rows, :] = grad_two.astype(jnp.bfloat16)
        sum_buf[rows, :] = grad_two

    @pl.loop(0, parts * blocks)
    def _(step):
        part, rows = step // blocks, block_rows(lax.rem(step, blocks))
        grad_hidden = dot_nn(first_buf[rows, :], down_buf[part]) * slope_buf[part, rows, :]
        sum_buf[rows, :] += dot_nt(grad_hidden.astype(jnp.bfloat16), in_buf[part])

    @pl.loop(0, blocks)
    def _(at):
        rows = block_rows(at)
        grad_one = norm_backward(
            sum_buf[rows, :], normed_buf[rows, :], inverse_buf[rows, :], gain_attn
        )
        grad_one_ref[rows, :] = grad_one
        grad_ctx_ref[rows, :] = dot_nn(grad_one.astype(jnp.bfloat16), out_buf[...]).astype(
            jnp.bfloat16
        )


def feed_forward(tokens, context, cotangent, norms, weights, full):
    rows, width = tokens.shape
    parts = full.shape[1]
    part_shape = full.shape[1:]
    return pl.pallas_call(
        ffn_kernel,
        out_shape=(
            jax.ShapeDtypeStruct((rows, width), jnp.bfloat16),
            jax.ShapeDtypeStruct((rows, width), jnp.float32),
            jax.ShapeDtypeStruct((rows, width), jnp.bfloat16),
        ),
        in_specs=[VMEM_SPEC] * 7 + [HBM_SPEC] * 2,
        out_specs=(VMEM_SPEC,) * 3,
        scratch_shapes=[
            pltpu.VMEM((width, width), jnp.bfloat16),
            pltpu.VMEM(part_shape, jnp.bfloat16),
            pltpu.VMEM(part_shape, jnp.bfloat16),
            pltpu.VMEM((parts, rows, part_shape[2]), jnp.float32),
            pltpu.VMEM((rows, width), jnp.bfloat16),
            pltpu.VMEM((rows, width), jnp.float32),
            pltpu.VMEM((rows, width), jnp.float32),
            pltpu.VMEM((rows, 1), jnp.float32),
            pltpu.SemaphoreType.DMA((1 + 2 * parts,)),
        ],
        compiler_params=pltpu.CompilerParams(vmem_limit_bytes=VMEM_LIMIT),
        name="feed_forward",
    )(tokens, context, cotangent, *norms, weights, full)


def adapter_parts(rows_ref, grad_ref, down_t, up, total_ref, down_at, up_at):
    block = 512
    first = jnp.zeros(down_t.shape, jnp.float32)
    second = jnp.zeros(down_t.shape, jnp.float32)
    for at in range(rows_ref.shape[0] // block):
        window = pl.ds(at * block, block)
        rows, grads = rows_ref[window, :], grad_ref[window, :]
        lifted = (ADAPTER_SCALE * dot_nt(rows, down_t)).astype(jnp.bfloat16)
        grad_lifted = (ADAPTER_SCALE * dot_nt(grads, up)).astype(jnp.bfloat16)
        second = second + dot_tn(lifted, grads)
        first = first + dot_tn(grad_lifted, rows)
    total_ref[down_at : down_at + 8, :] = first
    total_ref[up_at : up_at + 8, :] = second


def final_kernel(
    gq_hbm,
    gk_hbm,
    gv_hbm,
    weights_hbm,
    rows_hbm,
    grad_one_hbm,
    ups_full,
    down_q_ref,
    down_v_ref,
    grad_tokens_ref,
    aq_ref,
    av_ref,
    bq_ref,
    bv_ref,
    gq_ref,
    gk_ref,
    gv_ref,
    weights_ref,
    rows_ref,
    grad_one_ref,
    to_sib,
    from_sib,
    to_x,
    from_x,
    home_to,
    home_from,
    sums,
    sums_in,
    step_out,
    step_in,
    z_slots,
    final_in,
    load_sem,
    block_send,
    block_recv,
    sum_send,
    sum_recv,
):
    place = Place()
    x, y, z, core = place.x, place.y, place.z, place.core
    token_rows = gq_ref.shape[0]
    half_rows = token_rows // 2
    tensor = x * 2 + core

    def rows_of(block):
        return pl.ds(pl.multiple_of(block * token_rows, token_rows), token_rows)

    far_sib, far_same = (1 - x) * 2 + 1 - core, (1 - x) * 2 + core
    near_sib = x * 2 + 1 - core
    loads = {}

    def load(name, source, target):
        copy = pltpu.make_async_copy(source, target, load_sem.at[len(loads)])
        copy.start()
        loads[name] = copy

    for kind in (1, 2):
        load(("w", kind), weights_hbm.at[kind], weights_ref.at[kind])
    for block in range(4):
        owner = (far_sib, far_same, near_sib, tensor)[block]
        load(("k", block), gk_hbm.at[rows_of(owner)], gk_ref.at[rows_of(owner)])
        load(("v", block), gv_hbm.at[rows_of(owner)], gv_ref.at[rows_of(owner)])
    load("rows", rows_hbm, rows_ref)
    load("q", gq_hbm, gq_ref)
    load(("w", 0), weights_hbm.at[0], weights_ref.at[0])
    load("one", grad_one_hbm, grad_one_ref)

    barrier = pltpu.get_barrier_semaphore()
    others = [place.sibling(), place.step("x", 1), place.step("y", 1)]
    others += [place.device(z=lax.rem(z + i, DEPTH)) for i in range(1, DEPTH)]
    for target in others:
        pl.semaphore_signal(barrier, inc=1, device_id=target, device_id_type=MESH_ID)
    pl.semaphore_wait(barrier, len(others))

    def remote(source, target, send, recv, device):
        copy = pltpu.make_async_remote_copy(
            src_ref=source,
            dst_ref=target,
            send_sem=send,
            recv_sem=recv,
            device_id=device,
            device_id_type=MESH_ID,
        )
        copy.start()
        return copy

    slim = bq_ref.shape[1]

    def partial(owner, half):
        window = pl.ds(pl.multiple_of(owner * token_rows + half * half_rows, half_rows), half_rows)
        return dot_nt(gk_ref[window, :], weights_ref[1]) + dot_nt(gv_ref[window, :], weights_ref[2])

    def await_loads(*names):
        for name in names:
            loads[name].wait()

    await_loads(("w", 1), ("w", 2), ("k", 0), ("v", 0))
    sib_copies, x_copies, home_copies = [], [], []
    for half in range(2):
        to_sib[half] = partial(far_sib, half).astype(jnp.bfloat16)
        sib_copies.append(
            remote(
                to_sib.at[half],
                from_sib.at[half],
                block_send.at[0, half],
                block_recv.at[0, half],
                place.sibling(),
            )
        )
    await_loads(("k", 1), ("v", 1))
    for half in range(2):
        mine = partial(far_same, half)
        sib_copies[half].wait_recv()
        to_x[half] = (mine + from_sib[half].astype(jnp.float32)).astype(jnp.bfloat16)
        x_copies.append(
            remote(
                to_x.at[half],
                from_x.at[half],
                block_send.at[1, half],
                block_recv.at[1, half],
                place.step("x", 1),
            )
        )

    await_loads(("k", 2), ("v", 2), ("k", 3), ("v", 3), "rows", "q")
    own_rows = rows_ref.at[rows_of(tensor)]
    adapter_parts(own_rows, gq_ref, down_q_ref[...], ups_full[0:8, :], sums, 0, 16)
    adapter_parts(rows_ref, gv_ref, down_v_ref[...], ups_full[8:16, :], sums, 8, 24)
    kept = pl.ds(pl.multiple_of(core * 16, 16), 16)
    given = pl.ds(pl.multiple_of((1 - core) * 16, 16), 16)
    sum_copies = [
        remote(sums.at[given], sums_in, sum_send.at[0], sum_recv.at[0], place.sibling())
    ]
    for half in range(2):
        home_to[half] = partial(near_sib, half).astype(jnp.bfloat16)
        home_copies.append(
            remote(
                home_to.at[half],
                home_from.at[half],
                block_send.at[2, half],
                block_recv.at[2, half],
                place.sibling(),
            )
        )
    sum_copies[0].wait_recv()
    step_out[0] = sums[kept, :] + sums_in[...]
    sum_copies.append(
        remote(step_out.at[0], step_in.at[0], sum_send.at[1], sum_recv.at[1], place.step("y", 1))
    )
    await_loads(("w", 0), "one")
    for half in range(2):
        window = pl.ds(half * half_rows, half_rows)
        grad_one_ref[window, :] += partial(tensor, half) + dot_nt(gq_ref[window, :], weights_ref[0])
    sum_copies[1].wait_recv()
    z_slots[z] = step_out[0] + step_in[0]
    for i in range(1, DEPTH):
        there = lax.rem(z + i, DEPTH)
        sum_copies.append(
            remote(
                z_slots.at[z],
                z_slots.at[z],
                sum_send.at[1 + i],
                sum_recv.at[1 + i],
                place.device(z=there),
            )
        )
    for i in range(1, DEPTH):
        sum_copies[1 + i].wait_recv()
    column = z_slots[0]
    for i in range(1, DEPTH):
        column = column + z_slots[i]
    step_out[1] = column
    sum_copies.append(
        remote(
            step_out.at[1],
            step_in.at[1],
            sum_send.at[DEPTH + 1],
            sum_recv.at[DEPTH + 1],
            place.step("x", 1),
        )
    )
    sum_copies[-1].wait_recv()
    step_out[2] = step_out[1] + step_in[1]
    sum_copies.append(
        remote(
            step_out.at[2],
            final_in,
            sum_send.at[DEPTH + 2],
            sum_recv.at[DEPTH + 2],
            place.sibling(),
        )
    )

    for half in range(2):
        home_copies[half].wait_recv()
        x_copies[half].wait_recv()
        window = pl.ds(half * half_rows, half_rows)
        grad_tokens_ref[window, :] = (
            grad_one_ref[window, :]
            + home_from[half].astype(jnp.float32)
            + from_x[half].astype(jnp.float32)
        ).astype(jnp.bfloat16)
    sum_copies[-1].wait_recv()

    def give(first_half, second_half):
        aq_ref[...] = first_half[0:8, :]
        av_ref[...] = first_half[8:16, :]
        for t in range(4):

            @pl.when(tensor == t)
            def _(t=t):
                bq_ref[...] = second_half[0:8, t * slim : (t + 1) * slim]
                bv_ref[...] = second_half[8:16, t * slim : (t + 1) * slim]

    @pl.when(core == 0)
    def _():
        give(step_out.at[2], final_in)

    @pl.when(core == 1)
    def _():
        give(final_in, step_out.at[2])

    for copy in sib_copies + x_copies + home_copies + sum_copies:
        copy.wait_send()


def final_sums(
    grad_q, grad_k, grad_v, weights, rows_all, grad_one, ups_full, down_q_t, down_v_t, slim
):
    token_rows, width = grad_q.shape
    total_rows = grad_k.shape[0]
    bf16, f32 = jnp.bfloat16, jnp.float32
    half = (2, token_rows // 2, width)
    dma = pltpu.SemaphoreType.DMA
    return pl.pallas_call(
        final_kernel,
        out_shape=(
            jax.ShapeDtypeStruct((token_rows, width), bf16),
            jax.ShapeDtypeStruct((8, width), f32),
            jax.ShapeDtypeStruct((8, width), f32),
            jax.ShapeDtypeStruct((8, slim), f32),
            jax.ShapeDtypeStruct((8, slim), f32),
        ),
        in_specs=[HBM_SPEC] * 6 + [VMEM_SPEC] * 3,
        out_specs=(VMEM_SPEC,) * 5,
        scratch_shapes=[
            pltpu.VMEM((token_rows, width), bf16),
            pltpu.VMEM((total_rows, width), bf16),
            pltpu.VMEM((total_rows, width), bf16),
            pltpu.VMEM((3, width, width), bf16),
            pltpu.VMEM((total_rows, width), bf16),
            pltpu.VMEM((token_rows, width), f32),
        ]
        + [pltpu.VMEM(half, bf16)] * 6
        + [
            pltpu.VMEM((32, width), f32),
            pltpu.VMEM((16, width), f32),
            pltpu.VMEM((3, 16, width), f32),
            pltpu.VMEM((2, 16, width), f32),
            pltpu.VMEM((DEPTH, 16, width), f32),
            pltpu.VMEM((16, width), f32),
            dma((14,)),
            dma((3, 2)),
            dma((3, 2)),
            dma((DEPTH + 3,)),
            dma((DEPTH + 3,)),
        ],
        compiler_params=pltpu.CompilerParams(
            collective_id=2, has_side_effects=True, vmem_limit_bytes=VMEM_LIMIT
        ),
        name="final_sums",
    )(grad_q, grad_k, grad_v, weights, rows_all, grad_one, ups_full, down_q_t, down_v_t)


def local(
    fast,
    tokens,
    query_weight,
    w_key,
    value_weight,
    w_out,
    w_in,
    w_down,
    gain_attn,
    shift_attn,
    gain_ffn,
    shift_ffn,
    query_down_factor,
    query_up_factor,
    value_down_factor,
    value_up_factor,
    lengths,
    cotangent,
):
    slim = query_weight.shape[1]
    width = tokens.shape[1]
    token_rows = tokens.shape[0]
    down_q_t, down_v_t = query_down_factor.T, value_down_factor.T
    if fast:
        full, weights, rows_all, q_own, k_all, v_all, ups_full = gather_all(
            query_weight,
            w_key,
            value_weight,
            w_out,
            w_in,
            w_down.T,
            tokens,
            query_up_factor,
            value_up_factor,
            down_q_t,
            down_v_t,
        )
        full = full.reshape(2, 4, width, width)
    else:
        attn_pack = jnp.concatenate([query_weight, w_key, value_weight, w_out.T], axis=1)
        full = jnp.stack([attn_pack, w_in, w_down.T])
        full = lax.all_gather(full, "dp", axis=1, tiled=True)
        full = lax.all_gather(full, "tensor", axis=1)
        rows_all = lax.all_gather(tokens, "tensor").reshape(-1, width)
        ups = jnp.concatenate([query_up_factor, value_up_factor], axis=0)
        ups = jnp.pad(ups, ((0, 0), (0, -slim % 128)))
        ups_all = lax.all_gather(ups, "tensor")
        downs = jnp.concatenate([down_q_t, down_v_t], axis=0)
        order = tuple(range(full.shape[1]))
        weights, q_own, k_all, v_all = project(order, full, rows_all, ups_all, downs, token_rows)

    context, lse = attend_forward(lengths, q_own, k_all, v_all)
    norms = (gain_attn, shift_attn, gain_ffn, shift_ffn)
    mixed, grad_one, grad_context = feed_forward(
        tokens, context, cotangent, norms, weights, full
    )

    grad_q, grad_k, grad_v = attend_backward(
        lengths, q_own, k_all, v_all, context, lse, grad_context
    )
    if fast:
        grad_tokens, grad_aq, grad_av, grad_bq, grad_bv = final_sums(
            grad_q,
            grad_k,
            grad_v,
            weights,
            rows_all,
            grad_one,
            ups_full,
            down_q_t,
            down_v_t,
            slim,
        )
        return (mixed, grad_tokens, grad_aq.T, grad_bq, grad_av.T, grad_bv)

    query_up = ups_all[:, :8, :slim].transpose(1, 0, 2).reshape(8, width)
    value_up = ups_all[:, 8:, :slim].transpose(1, 0, 2).reshape(8, width)
    w_q, w_k, w_v = weights[0], weights[1], weights[2]
    u_query = dot_nn(tokens, query_down_factor).astype(jnp.bfloat16)
    u_value = dot_nn(rows_all, value_down_factor).astype(jnp.bfloat16)
    grad_uq = ADAPTER_SCALE * dot_nt(grad_q, query_up)
    grad_uv = ADAPTER_SCALE * dot_nt(grad_v, value_up)
    grad_bq = ADAPTER_SCALE * dot_tn(u_query, grad_q)
    grad_bv = ADAPTER_SCALE * dot_tn(u_value, grad_v)
    grad_aq = dot_tn(tokens, grad_uq.astype(jnp.bfloat16))
    grad_av = dot_tn(rows_all, grad_uv.astype(jnp.bfloat16))
    grad_rows = dot_nt(grad_k, w_k) + dot_nt(grad_v, w_v)
    own_rows = dot_nt(grad_q, w_q)
    shared = lax.psum_scatter(
        grad_rows.astype(jnp.bfloat16), "tensor", scatter_dimension=0, tiled=True
    )
    grad_tokens = (grad_one + own_rows + shared.astype(jnp.float32)).astype(jnp.bfloat16)
    grad_aq, grad_av, grad_bq, grad_bv = lax.psum(
        (grad_aq, grad_av, grad_bq, grad_bv), ("dp", "tensor")
    )
    at = lax.axis_index("tensor") * slim
    grad_bq = lax.dynamic_slice_in_dim(grad_bq, at, slim, 1)
    grad_bv = lax.dynamic_slice_in_dim(grad_bv, at, slim, 1)
    return (mixed, grad_tokens, grad_aq, grad_bq, grad_av, grad_bv)


def solution(mesh):
    fast = dict(mesh.shape) == {"dp": 2 * DEPTH, "tensor": 4}
    return jax.shard_map(
        functools.partial(local, fast),
        mesh=mesh,
        in_specs=(
            P(("dp", "tensor"), None),
            P("dp", "tensor"),
            P("dp", "tensor"),
            P("dp", "tensor"),
            P("tensor", "dp"),
            P("dp", "tensor"),
            P("tensor", "dp"),
            P(),
            P(),
            P(),
            P(),
            P(),
            P(None, "tensor"),
            P(),
            P(None, "tensor"),
            P("dp", None),
            P(("dp", "tensor"), None),
        ),
        out_specs=(
            P(("dp", "tensor"), None),
            P(("dp", "tensor"), None),
            P(),
            P(None, "tensor"),
            P(),
            P(None, "tensor"),
        ),
        check_vma=False,
    )
```

```python
import functools
import heapq

import jax
import jax.numpy as jnp
from jax import lax
from jax.experimental import pallas as pl
from jax.experimental.pallas import tpu as pltpu
from jax.sharding import PartitionSpec as P

HEAD_DIM = 64
PAIR = 2 * HEAD_DIM
Q_BLOCK = 256
K_BLOCK = 512
KV_BLOCK = 256
FORWARD_GROUP = 3
BACKWARD_GROUP = 3
ADAPTER_SCALE = 2.0
SCORE_SCALE = HEAD_DIM ** (-0.5)
LOG2_SCALE = SCORE_SCALE * 1.4426950408889634
NEG_FILL = -1e30
LN_EPS = 1e-05
VMEM_LIMIT = 60 * 1024 * 1024


def dot_nn(left, right):
    return jnp.dot(left, right, preferred_element_type=jnp.float32)


def dot_nt(left, right):
    return lax.dot_general(
        left, right, (((1,), (1,)), ((), ())), preferred_element_type=jnp.float32
    )


def dot_tn(left, right):
    return lax.dot_general(
        left, right, (((0,), (0,)), ((), ())), preferred_element_type=jnp.float32
    )


def norm_forward(row_vals, gain_vals, offset):
    middle = jnp.mean(row_vals, axis=-1, keepdims=True)
    centred = row_vals - middle
    inverse = lax.rsqrt(jnp.mean(centred * centred, axis=-1, keepdims=True) + LN_EPS)
    normed = centred * inverse
    return (normed * gain_vals + offset, normed, inverse)


def norm_backward(grad_out, normed, inverse, gain_vals):
    grad_n = grad_out * gain_vals
    return inverse * (
        grad_n
        - jnp.mean(grad_n, axis=-1, keepdims=True)
        - normed * jnp.mean(grad_n * normed, axis=-1, keepdims=True)
    )


def gelu_parts(hidden):
    cdf_part = 0.5 * (1.0 + lax.erf(hidden * 0.7071067811865476))
    density = jnp.exp(-0.5 * hidden * hidden) * 0.3989422804014327
    return (hidden * cdf_part, cdf_part + hidden * density)


def block_span(lengths_ref, first_row, rows, total_rows):
    last_row = first_row + rows - 1

    def slot_step(slot, carry):
        end, low, high = carry
        end = end + lengths_ref[0, slot]
        low = jnp.where(end <= first_row, jnp.maximum(low, end), low)
        high = jnp.where(end > last_row, jnp.minimum(high, end), high)
        return end, low, high

    start = (jnp.int32(0), jnp.int32(0), jnp.int32(total_rows))
    _, low, high = lax.fori_loop(0, lengths_ref.shape[1], slot_step, start, unroll=8)
    return low, high


def row_bounds(lengths_ref, first_row, rows, total_rows):
    place = first_row + lax.broadcasted_iota(jnp.int32, (1, rows), 1)

    def slot_step(slot, carry):
        end, begin, finish = carry
        end = end + lengths_ref[0, slot]
        done = place >= end
        begin = jnp.where(done, jnp.maximum(begin, end), begin)
        finish = jnp.where(done, finish, jnp.minimum(finish, end))
        return end, begin, finish

    start = (
        jnp.int32(0),
        jnp.zeros((1, rows), jnp.int32),
        jnp.full((1, rows), total_rows, jnp.int32),
    )
    _, begin, finish = lax.fori_loop(0, lengths_ref.shape[1], slot_step, start, unroll=8)
    return begin, finish


def stack_pair(block):
    lane = lax.broadcasted_iota(jnp.int32, block.shape, 1)
    zero = jnp.zeros_like(block)
    return jnp.concatenate(
        [jnp.where(lane < HEAD_DIM, block, zero), jnp.where(lane >= HEAD_DIM, block, zero)],
        axis=0,
    )


def unstack_pair(block, rows):
    joined = jnp.concatenate([block[:HEAD_DIM, :rows], block[HEAD_DIM:, rows:]], axis=0)
    return joined.T


def window_mask(step, low, begin, finish, total_rows):
    wanted = low + step * K_BLOCK
    start = pl.multiple_of(jnp.minimum(wanted, total_rows - K_BLOCK), 16)
    key_at = start + lax.broadcasted_iota(jnp.int32, (K_BLOCK, begin.shape[1]), 0)
    return start, (key_at >= jnp.maximum(begin, wanted)) & (key_at < finish)


def query_span(lengths_ref, first_row, total_rows):
    low, high = block_span(lengths_ref, first_row, Q_BLOCK, total_rows)
    low = (low // 16) * 16
    return low, (high - low + K_BLOCK - 1) // K_BLOCK


def each_q_block(lengths_ref, rows, total_rows, group, heads_width, block_step):
    base = lax.axis_index("tensor") * rows

    @pl.loop(0, rows // Q_BLOCK)
    def _(q_at):
        first_row = base + q_at * Q_BLOCK
        low, steps = query_span(lengths_ref, first_row, total_rows)
        begin, finish = row_bounds(lengths_ref, first_row, Q_BLOCK, total_rows)
        q_rows = pl.ds(pl.multiple_of(q_at * Q_BLOCK, Q_BLOCK), Q_BLOCK)

        @pl.loop(0, heads_width // PAIR // group)
        def _(at):
            pairs = [at * group + i for i in range(group)]
            lanes = [pl.ds(pl.multiple_of(pair * PAIR, PAIR), PAIR) for pair in pairs]
            slots = [q_at * (heads_width // PAIR) + pair for pair in pairs]
            block_step(q_rows, lanes, slots, low, steps, begin, finish)


def attend_forward(lengths_ref, q_ref, k_ref, v_ref, out_ref, lse_ref):
    total_rows = k_ref.shape[0]

    def block_step(q_rows, lanes, slots, low, steps, begin, finish):
        q_two = [stack_pair(q_ref[q_rows, lane]) for lane in lanes]

        def body(step, carry):
            start, allowed = window_mask(step, low, begin, finish, total_rows)
            window = pl.ds(start, K_BLOCK)
            both = jnp.concatenate([allowed, allowed], axis=1)
            result = []
            for (top, total, acc), q_pair, lane in zip(carry, q_two, lanes):
                scores = jnp.where(both, dot_nt(k_ref[window, lane], q_pair), NEG_FILL)
                new_top = jnp.maximum(top, jnp.max(scores, axis=0, keepdims=True))
                probs = jnp.exp2((scores - new_top) * LOG2_SCALE)
                shrink = jnp.exp2((top - new_top) * LOG2_SCALE)
                total = total * shrink + jnp.sum(probs, axis=0, keepdims=True)
                acc = acc * shrink + dot_tn(v_ref[window, lane], probs.astype(jnp.bfloat16))
                result.append((new_top, total, acc))
            return tuple(result)

        empty = (
            jnp.full((1, 2 * Q_BLOCK), NEG_FILL, jnp.float32),
            jnp.zeros((1, 2 * Q_BLOCK), jnp.float32),
            jnp.zeros((PAIR, 2 * Q_BLOCK), jnp.float32),
        )
        final = lax.fori_loop(0, steps, body, (empty,) * len(lanes))
        for (top, total, acc), lane, slot in zip(final, lanes, slots):
            out_ref[q_rows, lane] = unstack_pair(acc / total, Q_BLOCK).astype(jnp.bfloat16)
            lse_ref[slot] = top * LOG2_SCALE + jnp.log2(total)

    each_q_block(
        lengths_ref, q_ref.shape[0], total_rows, FORWARD_GROUP, q_ref.shape[1], block_step
    )


def attend_backward(
    lengths_ref, q_ref, k_ref, v_ref, ctx_ref, lse_ref, grad_ref, gq_ref, gk_acc, gv_acc
):
    total_rows = k_ref.shape[0]

    def block_step(q_rows, lanes, slots, low, steps, begin, finish):
        ready = []
        for lane, slot in zip(lanes, slots):
            grads = grad_ref[q_rows, lane]
            product = (grads.astype(jnp.float32) * ctx_ref[q_rows, lane].astype(jnp.float32)).T
            row_dot = jnp.concatenate(
                [
                    jnp.sum(product[:HEAD_DIM], axis=0, keepdims=True),
                    jnp.sum(product[HEAD_DIM:], axis=0, keepdims=True),
                ],
                axis=1,
            )
            ready.append((stack_pair(q_ref[q_rows, lane]), stack_pair(grads), row_dot, lse_ref[slot]))

        def body(step, carry):
            start, allowed = window_mask(step, low, begin, finish, total_rows)
            window = pl.ds(start, K_BLOCK)
            both = jnp.concatenate([allowed, allowed], axis=1)
            result = []
            for acc, (q_pair, grad_pair, row_dot, lse), lane in zip(carry, ready, lanes):
                keys = k_ref[window, lane]
                scores = jnp.where(both, dot_nt(keys, q_pair), NEG_FILL)
                probs = jnp.exp2(scores * LOG2_SCALE - lse)
                grad_probs = dot_nt(v_ref[window, lane], grad_pair)
                grad_scores = (probs * (grad_probs - row_dot)).astype(jnp.bfloat16)
                gk_acc[window, lane] += dot_nn(grad_scores, q_pair)
                gv_acc[window, lane] += dot_nn(probs.astype(jnp.bfloat16), grad_pair)
                result.append(acc + dot_tn(keys, grad_scores))
            return tuple(result)

        zero = jnp.zeros((PAIR, 2 * Q_BLOCK), jnp.float32)
        final = lax.fori_loop(0, steps, body, (zero,) * len(lanes))
        for acc, lane in zip(final, lanes):
            gq_ref[q_rows, lane] = (unstack_pair(acc, Q_BLOCK) * SCORE_SCALE).astype(jnp.bfloat16)

    each_q_block(
        lengths_ref, q_ref.shape[0], total_rows, BACKWARD_GROUP, q_ref.shape[1], block_step
    )


VMEM_SPEC = pl.BlockSpec(memory_space=pltpu.VMEM)
HBM_SPEC = pl.BlockSpec(memory_space=pltpu.HBM)
SMEM_SPEC = pl.BlockSpec(memory_space=pltpu.SMEM)


MESH_ID = pl.DeviceIdType.MESH
DEPTH = 4
FULL_ROWS = 96

FLOWS = (
    (0, 0, "zxy", 0.0),
    (0, 1, "zyx", 0.0),
    (1, 0, "xzy", 12.0),
    (1, 1, "zyx", 24.0),
    (2, 0, "xzy", 12.0),
    (2, 1, "yxz", 12.0),
)
OWN = (0, 0, 0)


def forwards(order, piece):
    used = [axis for axis in order if piece["xyz".index(axis)] != 0]
    at = order.index(used[-1]) if used else -1
    steps = []
    if used and used[-1] == "z":
        steps.append(("z", 1 if piece[2] < 0 else -1))
    for axis in order[at + 1 :]:
        steps += [("z", 1), ("z", -1)] if axis == "z" else [(axis, 1)]
    return steps


def passed(piece, axis, sign):
    x, y, z = piece
    if axis == "x":
        return (1 - x, y, z)
    return (x, 1 - y, z) if axis == "y" else (x, y, z - sign)


def event_order(token_time):
    per_piece = 1.7
    links, heap, times, count = {}, [], {}, 0
    for z in range(DEPTH):
        links[z, "x", 1] = token_time
        for flow, (_, _, _, start) in enumerate(FLOWS):
            heapq.heappush(heap, (start + 0.01 * flow, count, z, flow, OWN))
            count += 1
    while heap:
        now, _, z, flow, piece = heapq.heappop(heap)
        times.setdefault((flow, piece), []).append(now)
        for axis, sign in forwards(FLOWS[flow][2], piece):
            there = z + sign if axis == "z" else z
            if not 0 <= there < DEPTH:
                continue
            end = max(links.get((z, axis, sign), 0.0), now) + per_piece
            links[z, axis, sign] = end
            heapq.heappush(heap, (end + 3.0, count, there, flow, passed(piece, axis, sign)))
            count += 1
    return [key for _, key in sorted((sum(v) / len(v), key) for key, v in times.items())]


class Place:
    def __init__(self):
        dp, tensor = lax.axis_index("dp"), lax.axis_index("tensor")
        self.z, self.y = dp // 2, lax.rem(dp, 2)
        self.x, self.core = tensor // 2, lax.rem(tensor, 2)

    def device(self, x=None, y=None, z=None, core=None):
        x = self.x if x is None else x
        y = self.y if y is None else y
        z = self.z if z is None else z
        core = self.core if core is None else core
        return (z * 2 + y, x * 2 + core)

    def step(self, axis, sign):
        if axis == "x":
            return self.device(x=1 - self.x)
        return self.device(y=1 - self.y) if axis == "y" else self.device(z=self.z + sign)

    def sibling(self):
        return self.device(core=1 - self.core)


def gather_kernel(
    wq_ref,
    wk_ref,
    wv_ref,
    wo_ref,
    w_in_ref,
    w_down_ref,
    tokens_ref,
    up_q_ref,
    up_v_ref,
    down_q_ref,
    down_v_ref,
    full_ref,
    weights_hbm,
    rows_hbm,
    q_hbm,
    k_hbm,
    v_hbm,
    ups_full,
    pack_ref,
    packs_ref,
    rows_ref,
    ups_ref,
    ups_all_ref,
    weights_ref,
    q_ref,
    k_ref,
    v_ref,
    piece_recv,
    send_sem,
    sib_send,
    sib_recv,
    own_sem,
    rows_send,
    rows_recv,
    ups_send,
    ups_recv,
    out_sem,
):
    place = Place()
    x, y, z, core = place.x, place.y, place.z, place.core
    token_rows = tokens_ref.shape[0]
    part_rows = FULL_ROWS // 2
    half_rows = token_rows // 2

    barrier = pltpu.get_barrier_semaphore()
    others = (
        place.sibling(),
        place.step("x", 1),
        place.device(x=1 - x, core=1 - core),
        place.step("y", 1),
    )
    for target in others:
        pl.semaphore_signal(barrier, inc=1, device_id=target, device_id_type=MESH_ID)
    for sign, there in ((1, z < DEPTH - 1), (-1, z > 0)):

        @pl.when(there)
        def _(sign=sign):
            pl.semaphore_signal(
                barrier, inc=1, device_id=place.step("z", sign), device_id_type=MESH_ID
            )

    slim = wq_ref.shape[1]
    for kind, ref in enumerate((wq_ref, wk_ref, wv_ref)):
        pack_ref[:, kind * slim : (kind + 1) * slim] = ref[...]
    pack_ref[:, 3 * slim : 4 * slim] = wo_ref[...].astype(jnp.float32).T.astype(jnp.bfloat16)
    ups_ref[...] = jnp.zeros_like(ups_ref)
    ups_ref[0:8, :slim] = up_q_ref[...].astype(jnp.float32)
    ups_ref[8:16, :slim] = up_v_ref[...].astype(jnp.float32)
    shards = (pack_ref, w_in_ref, w_down_ref)
    inner = ((z > 0) & (z < DEPTH - 1)).astype(jnp.int32)
    pl.semaphore_wait(barrier, len(others) + 1 + inner)

    def remote(source, target, send, recv, device):
        return pltpu.make_async_remote_copy(
            src_ref=source,
            dst_ref=target,
            send_sem=send,
            recv_sem=recv,
            device_id=device,
            device_id_type=MESH_ID,
        )

    def rows_at(owner_x, owner_core, half):
        return rows_ref.at[owner_x * 2 + owner_core, pl.ds(half * half_rows, half_rows)]

    own_copies = [
        pltpu.make_async_copy(pack_ref, packs_ref.at[core, x, z, y], own_sem.at[0]),
        pltpu.make_async_copy(tokens_ref, rows_ref.at[x * 2 + core], own_sem.at[1]),
        pltpu.make_async_copy(ups_ref, ups_all_ref.at[x * 2 + core], own_sem.at[2]),
        pltpu.make_async_copy(w_in_ref, full_ref.at[0, core, x, z, y], own_sem.at[3]),
        pltpu.make_async_copy(w_down_ref, full_ref.at[1, core, x, z, y], own_sem.at[4]),
    ]
    row_copies = []
    for half in range(2):
        source = tokens_ref.at[pl.ds(half * half_rows, half_rows)]
        for slot, device in ((0, place.step("x", 1)), (1, place.sibling())):
            row_copies.append(
                remote(
                    source,
                    rows_at(x, core, half),
                    rows_send.at[slot, half],
                    rows_recv.at[slot, half],
                    device,
                )
            )
    up_copies = [
        remote(ups_ref, ups_all_ref.at[x * 2 + core], ups_send.at[i], ups_recv.at[i], device)
        for i, device in enumerate(others[:3])
    ]

    sends = {}

    def gathered(kind):
        return packs_ref if kind == 0 else full_ref.at[kind - 1]

    def piece_at(flow, piece):
        kind, part, _, _ = FLOWS[flow]
        px, py = lax.rem(x + piece[0], 2), lax.rem(y + piece[1], 2)
        return gathered(kind).at[
            core, px, z + piece[2], py, pl.ds(part * part_rows, part_rows)
        ], (px * 2 + py) * DEPTH + z + piece[2]

    def handle(flow, piece):
        kind, part, order, _ = FLOWS[flow]
        landed, index = piece_at(flow, piece)
        source = landed
        if piece == OWN:
            source = shards[kind].at[pl.ds(part * part_rows, part_rows)]
        else:
            remote(landed, landed, send_sem.at[flow, 0], piece_recv.at[flow, index], place.sibling()).wait_recv()
        for axis, sign in forwards(order, piece):
            slot = {"x": 0, "y": 1, "z": 2 if sign > 0 else 3}[axis]
            copy = remote(
                source,
                landed,
                send_sem.at[flow, slot],
                piece_recv.at[flow, index],
                place.step(axis, sign),
            )
            if axis == "z":
                pl.when((z + sign >= 0) & (z + sign < DEPTH))(copy.start)
            else:
                copy.start()
                sends[flow, slot] = sends.get((flow, slot), 0) + 1
        remote(source, landed, sib_send.at[flow], sib_recv.at[flow], place.sibling()).start()

    def block_of(flow, pieces, plane):
        kind, part, _, _ = FLOWS[flow]
        nx = 2 if pieces % 2 == 0 else 1
        ny = 2 if pieces % 4 == 0 else 1
        return gathered(kind).at[
            plane,
            pl.ds(0, nx),
            pl.ds(0, pieces // (nx * ny)),
            pl.ds(0, ny),
            pl.ds(part * part_rows, part_rows),
        ]

    def finish_flow(flow):
        order = FLOWS[flow][2]
        everything = block_of(flow, 4 * DEPTH, 1 - core)
        remote(everything, everything, sib_send.at[flow], sib_recv.at[flow], place.sibling()).wait()

    def finish_sends(flow):
        order = FLOWS[flow][2]
        for axis, slot in (("x", 0), ("y", 1)):
            block = block_of(flow, 2 ** order.index(axis) * (DEPTH // 2 if "z" in order[: order.index(axis)] else 1), core)
            remote(block, block, send_sem.at[flow, slot], sib_recv.at[flow], place.sibling()).wait_send()
        each = 2 ** order.index("z")
        for at in range(DEPTH):
            for slot, sets in ((2, at + 1 if at < DEPTH - 1 else 0), (3, DEPTH - at if at > 0 else 0)):
                if sets:

                    @pl.when(z == at)
                    def _(slot=slot, sets=sets):
                        nx = 2 if each > 1 else 1
                        ny = 2 if each > 2 else 1
                        kind, part, _, _ = FLOWS[flow]
                        block = gathered(kind).at[
                            core,
                            pl.ds(0, nx),
                            pl.ds(0, sets),
                            pl.ds(0, ny),
                            pl.ds(part * part_rows, part_rows),
                        ]
                        remote(
                            block, block, send_sem.at[flow, slot], sib_recv.at[flow], place.sibling()
                        ).wait_send()

    for copy in row_copies + up_copies + own_copies:
        copy.start()

    def pass_rows(half):
        row_copies[2 * half].wait_recv()
        landed = rows_at(1 - x, core, half)
        copy = remote(landed, landed, rows_send.at[2, half], rows_recv.at[2, half], place.sibling())
        copy.start()
        return copy

    outs = []

    def write(source, target):
        copy = pltpu.make_async_copy(source, target, out_sem.at[len(outs)])
        copy.start()
        outs.append(copy)

    def assemble(t):
        if t == 0:
            for copy in up_copies + own_copies[:3]:
                copy.wait()
            for half in range(2):
                row_copies[2 * half + 1].wait_recv()
                passed_rows[half].wait_recv()
            for owner in range(4):
                write(rows_ref.at[owner], rows_hbm.at[pl.ds(owner * token_rows, token_rows)])
            finish_flow(0)
            finish_flow(1)
            for owner in range(4):
                ups_full[:, owner * slim : (owner + 1) * slim] = ups_all_ref[owner, :, :slim].astype(jnp.bfloat16)
        lanes = slice(t * slim, (t + 1) * slim)
        source = packs_ref.at[t % 2, t // 2]
        for kind, down_ref, first in ((0, down_q_ref, 0), (1, None, 0), (2, down_v_ref, 8), (3, None, 0)):
            part = source[:, :, :, kind * slim : (kind + 1) * slim].reshape(-1, slim)
            if down_ref is not None:
                up = ups_all_ref[t, first : first + 8, :slim].astype(jnp.bfloat16)
                product = dot_tn(down_ref[...], up)
                part = (part.astype(jnp.float32) + ADAPTER_SCALE * product).astype(jnp.bfloat16)
            weights_ref[kind, :, lanes] = part
        if t == 3:
            write(weights_ref, weights_hbm)

    def own_queries():
        q_ref[...] = dot_nn(rows_ref[x * 2 + core], weights_ref[0]).astype(jnp.bfloat16)
        write(q_ref, q_hbm)

    def keys_values(ref, hbm, kind, owner):
        ref[owner] = dot_nn(rows_ref[owner], weights_ref[kind]).astype(jnp.bfloat16)
        write(ref.at[owner], hbm.at[pl.ds(owner * token_rows, token_rows)])

    steps = [functools.partial(assemble, t) for t in range(4)] + [own_queries]
    for owner in range(4):
        steps.append(functools.partial(keys_values, k_ref, k_hbm, 1, owner))
        steps.append(functools.partial(keys_values, v_ref, v_hbm, 2, owner))

    passed_rows = []
    events = event_order(17.0)
    last_pack = max(i for i, (flow, _) in enumerate(events) if FLOWS[flow][0] == 0)
    between = max(1, (len(events) - last_pack) // (len(steps) + 1))
    arrivals = 0
    for at, (flow, piece) in enumerate(events):
        if piece[2] == 0:
            handle(flow, piece)
        else:
            pl.when((z + piece[2] >= 0) & (z + piece[2] < DEPTH))(
                functools.partial(handle, flow, piece)
            )
        if piece != OWN:
            arrivals += 1
            if arrivals in (8, 16):
                passed_rows.append(pass_rows(len(passed_rows)))
        if at >= last_pack and (at - last_pack) % between == between - 1 and steps:
            steps.pop(0)()
    for step in steps:
        step()

    for half in range(2):
        row_copies[2 * half].wait_send()
        row_copies[2 * half + 1].wait_send()
        passed_rows[half].wait_send()
    for copy in own_copies[3:] + outs:
        copy.wait()
    for flow in range(len(FLOWS)):
        if flow > 1:
            finish_flow(flow)
        finish_sends(flow)


def gather_all(w_q, w_k, w_v, w_out, w_in, w_down_t, tokens, up_q, up_v, down_q_t, down_v_t):
    shard_rows, width = w_in.shape
    token_rows = tokens.shape[0]
    bf16, f32 = jnp.bfloat16, jnp.float32
    slim = w_q.shape[1]
    padded = slim + -slim % 128
    flows = len(FLOWS)
    dma = pltpu.SemaphoreType.DMA
    grid = (2, 2, DEPTH, 2, shard_rows, width)
    return pl.pallas_call(
        gather_kernel,
        out_shape=(
            jax.ShapeDtypeStruct((2,) + grid, bf16),
            jax.ShapeDtypeStruct((4, width, width), bf16),
            jax.ShapeDtypeStruct((4 * token_rows, width), bf16),
            jax.ShapeDtypeStruct((token_rows, width), bf16),
            jax.ShapeDtypeStruct((4 * token_rows, width), bf16),
            jax.ShapeDtypeStruct((4 * token_rows, width), bf16),
            jax.ShapeDtypeStruct((16, width), bf16),
        ),
        in_specs=[VMEM_SPEC] * 4 + [HBM_SPEC] * 3 + [VMEM_SPEC] * 4,
        out_specs=(HBM_SPEC,) * 6 + (VMEM_SPEC,),
        scratch_shapes=[
            pltpu.VMEM((shard_rows, width), bf16),
            pltpu.VMEM(grid, bf16),
            pltpu.VMEM((4, token_rows, width), bf16),
            pltpu.VMEM((16, padded), f32),
            pltpu.VMEM((4, 16, padded), f32),
            pltpu.VMEM((4, width, width), bf16),
            pltpu.VMEM((token_rows, width), bf16),
            pltpu.VMEM((4, token_rows, width), bf16),
            pltpu.VMEM((4, token_rows, width), bf16),
            dma((flows, 4 * DEPTH)),
            dma((flows, 4)),
            dma((flows,)),
            dma((flows,)),
            dma((5,)),
            dma((3, 2)),
            dma((3, 2)),
            dma((3,)),
            dma((3,)),
            dma((14,)),
        ],
        compiler_params=pltpu.CompilerParams(
            collective_id=1, has_side_effects=True, vmem_limit_bytes=VMEM_LIMIT
        ),
        name="gather_all",
    )(w_q, w_k, w_v, w_out, w_in, w_down_t, tokens, up_q, up_v, down_q_t, down_v_t)


def project_kernel(
    order,
    full_hbm,
    rows_ref,
    ups_ref,
    downs_ref,
    weights_ref,
    q_ref,
    k_ref,
    v_ref,
    packs_ref,
    sems,
):
    token_rows = q_ref.shape[0]
    slim = packs_ref.shape[2] // 4
    tensor = lax.axis_index("tensor")
    copies = [
        pltpu.make_async_copy(full_hbm.at[0, i], packs_ref.at[i], sems.at[i])
        for i in range(len(order))
    ]
    for copy in copies:
        copy.start()
    for i, t in enumerate(order):
        copies[i].wait()
        lanes = slice(t * slim, (t + 1) * slim)
        for kind, first in ((0, 0), (1, None), (2, 8), (3, None)):
            part = packs_ref[i, :, kind * slim : (kind + 1) * slim]
            if first is not None:
                up = ups_ref[t, first : first + 8, :slim]
                product = dot_tn(downs_ref[first : first + 8, :], up)
                part = (part.astype(jnp.float32) + ADAPTER_SCALE * product).astype(jnp.bfloat16)
            weights_ref[kind, :, lanes] = part
    own = rows_ref[pl.ds(pl.multiple_of(tensor * token_rows, token_rows), token_rows), :]
    q_ref[...] = dot_nn(own, weights_ref[0]).astype(jnp.bfloat16)

    @pl.loop(0, rows_ref.shape[0] // token_rows)
    def _(at):
        window = pl.ds(pl.multiple_of(at * token_rows, token_rows), token_rows)
        block = rows_ref[window, :]
        k_ref[window, :] = dot_nn(block, weights_ref[1]).astype(jnp.bfloat16)
        v_ref[window, :] = dot_nn(block, weights_ref[2]).astype(jnp.bfloat16)


def project(order, full, rows_all, ups_all, downs, token_rows):
    total_rows, width = rows_all.shape
    bf16 = jnp.bfloat16
    return pl.pallas_call(
        functools.partial(project_kernel, order),
        out_shape=(
            jax.ShapeDtypeStruct((4, width, width), bf16),
            jax.ShapeDtypeStruct((token_rows, width), bf16),
            jax.ShapeDtypeStruct((total_rows, width), bf16),
            jax.ShapeDtypeStruct((total_rows, width), bf16),
        ),
        in_specs=[HBM_SPEC] + [VMEM_SPEC] * 3,
        out_specs=(VMEM_SPEC,) * 4,
        scratch_shapes=[
            pltpu.VMEM(full.shape[1:], bf16),
            pltpu.SemaphoreType.DMA((len(order),)),
        ],
        compiler_params=pltpu.CompilerParams(vmem_limit_bytes=VMEM_LIMIT),
        name="project",
    )(full, rows_all, ups_all, downs)


def middle_kernel(
    lengths_ref,
    gain_attn_ref,
    shift_attn_ref,
    gain_ffn_ref,
    shift_ffn_ref,
    q_hbm,
    k_hbm,
    v_hbm,
    tokens_hbm,
    cot_hbm,
    weights_hbm,
    full_hbm,
    mixed_hbm,
    grad_one_hbm,
    gq_hbm,
    gk_hbm,
    gv_hbm,
    q_ref,
    k_ref,
    v_ref,
    tokens_ref,
    cot_ref,
    out_buf,
    in_buf,
    down_buf,
    slope_buf,
    first_buf,
    sum_buf,
    normed_buf,
    inverse_buf,
    ctx_ref,
    lse_ref,
    grad_ref,
    gk_acc,
    gv_acc,
    gk_out,
    gv_out,
    load_sem,
    part_sem,
    kv_sem,
    store_sem,
    grad_sem,
):
    rows, width = q_ref.shape
    total_rows = k_ref.shape[0]
    parts, kinds = in_buf.shape[0], full_hbm.shape[0]
    kv_blocks = total_rows // KV_BLOCK
    base = lax.axis_index("tensor") * rows

    span_low, span_high = jnp.int32(total_rows), jnp.int32(0)
    for at in range(rows // Q_BLOCK):
        low, steps = query_span(lengths_ref, base + at * Q_BLOCK, total_rows)
        span_low = jnp.minimum(span_low, jnp.minimum(low, total_rows - K_BLOCK))
        span_high = jnp.maximum(span_high, jnp.minimum(low + steps * K_BLOCK, total_rows))

    def kv_rows(block):
        return pl.ds(pl.multiple_of(block * KV_BLOCK, KV_BLOCK), KV_BLOCK)

    def touched(block):
        return (block * KV_BLOCK < span_high) & ((block + 1) * KV_BLOCK > span_low)

    def kv_copies(block):
        window = kv_rows(block)
        return (
            pltpu.make_async_copy(k_hbm.at[window], k_ref.at[window], kv_sem.at[0, block]),
            pltpu.make_async_copy(v_hbm.at[window], v_ref.at[window], kv_sem.at[1, block]),
        )

    def part_copies(part):
        return (
            pltpu.make_async_copy(
                full_hbm.at[kinds - 2, part], in_buf.at[part], part_sem.at[0, part]
            ),
            pltpu.make_async_copy(
                full_hbm.at[kinds - 1, part], down_buf.at[part], part_sem.at[1, part]
            ),
        )

    q_copy = pltpu.make_async_copy(q_hbm, q_ref, load_sem.at[0])
    tokens_copy = pltpu.make_async_copy(tokens_hbm, tokens_ref, load_sem.at[1])
    out_copy = pltpu.make_async_copy(weights_hbm.at[3], out_buf, load_sem.at[2])
    cot_copy = pltpu.make_async_copy(cot_hbm, cot_ref, load_sem.at[3])
    q_copy.start()

    @pl.loop(0, kv_blocks)
    def _(block):
        @pl.when(touched(block))
        def _():
            for copy in kv_copies(block):
                copy.start()

    tokens_copy.start()
    out_copy.start()
    cot_copy.start()
    for part in range(parts):
        for copy in part_copies(part):
            copy.start()

    gk_acc[...] = jnp.zeros_like(gk_acc)
    gv_acc[...] = jnp.zeros_like(gv_acc)
    q_copy.wait()

    @pl.loop(0, kv_blocks)
    def _(block):
        @pl.when(touched(block))
        def _():
            for copy in kv_copies(block):
                copy.wait()

    attend_forward(lengths_ref, q_ref, k_ref, v_ref, ctx_ref, lse_ref)

    gain_attn, shift_attn, gain_ffn, shift_ffn = (
        ref[...].reshape(1, -1) for ref in (gain_attn_ref, shift_attn_ref, gain_ffn_ref, shift_ffn_ref)
    )
    tokens_copy.wait()
    out_copy.wait()
    residual = tokens_ref[...].astype(jnp.float32) + dot_nt(ctx_ref[...], out_buf[...])
    first, normed, inverse = norm_forward(residual, gain_attn, shift_attn)
    first_buf[...] = first.astype(jnp.bfloat16)
    sum_buf[...] = first.astype(jnp.bfloat16).astype(jnp.float32)
    normed_buf[...] = normed
    inverse_buf[...] = inverse

    @pl.loop(0, parts)
    def _(part):
        for copy in part_copies(part):
            copy.wait()
        acted, slope = gelu_parts(dot_nn(first_buf[...], in_buf[part]))
        slope_buf[part] = slope
        sum_buf[...] += dot_nt(acted.astype(jnp.bfloat16), down_buf[part])

    cot_copy.wait()
    mixed, normed, inverse = norm_forward(sum_buf[...], gain_ffn, shift_ffn)
    tokens_ref[...] = mixed.astype(jnp.bfloat16)
    mixed_copy = pltpu.make_async_copy(tokens_ref, mixed_hbm, store_sem.at[0])
    mixed_copy.start()
    grad_two = norm_backward(cot_ref[...].astype(jnp.float32), normed, inverse, gain_ffn)
    first_buf[...] = grad_two.astype(jnp.bfloat16)
    sum_buf[...] = grad_two

    @pl.loop(0, parts)
    def _(part):
        grad_hidden = dot_nn(first_buf[...], down_buf[part]) * slope_buf[part]
        sum_buf[...] += dot_nt(grad_hidden.astype(jnp.bfloat16), in_buf[part])

    grad_one = norm_backward(sum_buf[...], normed_buf[...], inverse_buf[...], gain_attn)
    normed_buf[...] = grad_one
    grad_one_copy = pltpu.make_async_copy(normed_buf, grad_one_hbm, store_sem.at[1])
    grad_one_copy.start()
    grad_ref[...] = dot_nn(grad_one.astype(jnp.bfloat16), out_buf[...]).astype(jnp.bfloat16)

    attend_backward(
        lengths_ref, q_ref, k_ref, v_ref, ctx_ref, lse_ref, grad_ref, first_buf, gk_acc, gv_acc
    )
    gq_copy = pltpu.make_async_copy(first_buf, gq_hbm, store_sem.at[2])
    gq_copy.start()

    def grad_copies(block):
        window = kv_rows(block)
        return (
            pltpu.make_async_copy(gk_out.at[window], gk_hbm.at[window], grad_sem.at[0, block]),
            pltpu.make_async_copy(gv_out.at[window], gv_hbm.at[window], grad_sem.at[1, block]),
        )

    @pl.loop(0, kv_blocks)
    def _(block):
        window = kv_rows(block)

        @pl.when(touched(block))
        def _():
            gk_out[window, :] = (gk_acc[window, :] * SCORE_SCALE).astype(jnp.bfloat16)
            gv_out[window, :] = gv_acc[window, :].astype(jnp.bfloat16)

        @pl.when(jnp.logical_not(touched(block)))
        def _():
            gk_out[window, :] = jnp.zeros((KV_BLOCK, width), jnp.bfloat16)
            gv_out[window, :] = jnp.zeros((KV_BLOCK, width), jnp.bfloat16)

        for copy in grad_copies(block):
            copy.start()

    for copy in (mixed_copy, grad_one_copy, gq_copy):
        copy.wait()

    @pl.loop(0, kv_blocks)
    def _(block):
        for copy in grad_copies(block):
            copy.wait()


def middle(lengths, norms, q_own, k_all, v_all, tokens, cotangent, weights, full):
    rows, width = q_own.shape
    total_rows = k_all.shape[0]
    parts = full.shape[1]
    bf16, f32 = jnp.bfloat16, jnp.float32
    slots = rows // Q_BLOCK * (width // PAIR)
    kv_blocks = total_rows // KV_BLOCK
    dma = pltpu.SemaphoreType.DMA
    return pl.pallas_call(
        middle_kernel,
        out_shape=(
            jax.ShapeDtypeStruct((rows, width), bf16),
            jax.ShapeDtypeStruct((rows, width), f32),
            jax.ShapeDtypeStruct((rows, width), bf16),
            jax.ShapeDtypeStruct((total_rows, width), bf16),
            jax.ShapeDtypeStruct((total_rows, width), bf16),
        ),
        in_specs=[SMEM_SPEC] + [VMEM_SPEC] * 4 + [HBM_SPEC] * 7,
        out_specs=(HBM_SPEC,) * 5,
        scratch_shapes=[
            pltpu.VMEM((rows, width), bf16),
            pltpu.VMEM((total_rows, width), bf16),
            pltpu.VMEM((total_rows, width), bf16),
            pltpu.VMEM((rows, width), bf16),
            pltpu.VMEM((rows, width), bf16),
            pltpu.VMEM((width, width), bf16),
            pltpu.VMEM(full.shape[1:], bf16),
            pltpu.VMEM(full.shape[1:], bf16),
            pltpu.VMEM((parts, rows, full.shape[3]), f32),
            pltpu.VMEM((rows, width), bf16),
            pltpu.VMEM((rows, width), f32),
            pltpu.VMEM((rows, width), f32),
            pltpu.VMEM((rows, 1), f32),
            pltpu.VMEM((rows, width), bf16),
            pltpu.VMEM((slots, 1, 2 * Q_BLOCK), f32),
            pltpu.VMEM((rows, width), bf16),
            pltpu.VMEM((total_rows, width), f32),
            pltpu.VMEM((total_rows, width), f32),
            pltpu.VMEM((total_rows, width), bf16),
            pltpu.VMEM((total_rows, width), bf16),
            dma((4,)),
            dma((2, parts)),
            dma((2, kv_blocks)),
            dma((3,)),
            dma((2, kv_blocks)),
        ],
        compiler_params=pltpu.CompilerParams(vmem_limit_bytes=VMEM_LIMIT),
        name="middle",
    )(lengths, *norms, q_own, k_all, v_all, tokens, cotangent, weights, full)


def adapter_parts(rows_ref, grad_ref, down_t, up, total_ref, down_at, up_at):
    block = 512
    first = jnp.zeros(down_t.shape, jnp.float32)
    second = jnp.zeros(down_t.shape, jnp.float32)
    for at in range(rows_ref.shape[0] // block):
        window = pl.ds(at * block, block)
        rows, grads = rows_ref[window, :], grad_ref[window, :]
        lifted = (ADAPTER_SCALE * dot_nt(rows, down_t)).astype(jnp.bfloat16)
        grad_lifted = (ADAPTER_SCALE * dot_nt(grads, up)).astype(jnp.bfloat16)
        second = second + dot_tn(lifted, grads)
        first = first + dot_tn(grad_lifted, rows)
    total_ref[down_at : down_at + 8, :] = first
    total_ref[up_at : up_at + 8, :] = second


def final_kernel(
    gq_hbm,
    gk_hbm,
    gv_hbm,
    weights_hbm,
    rows_hbm,
    grad_one_hbm,
    ups_full,
    down_q_ref,
    down_v_ref,
    grad_tokens_ref,
    sums_ref,
    gq_ref,
    gk_ref,
    gv_ref,
    weights_ref,
    rows_ref,
    grad_one_ref,
    to_sib,
    from_sib,
    to_x,
    from_x,
    home_to,
    home_from,
    sums,
    sums_in,
    step_out,
    step_in,
    z_slots,
    final_in,
    load_sem,
    block_send,
    block_recv,
    sum_send,
    sum_recv,
):
    place = Place()
    x, y, z, core = place.x, place.y, place.z, place.core
    token_rows = gq_ref.shape[0]
    half_rows = token_rows // 2
    tensor = x * 2 + core

    def rows_of(block):
        return pl.ds(pl.multiple_of(block * token_rows, token_rows), token_rows)

    far_sib, far_same = (1 - x) * 2 + 1 - core, (1 - x) * 2 + core
    near_sib = x * 2 + 1 - core
    loads = {}

    def load(name, source, target):
        copy = pltpu.make_async_copy(source, target, load_sem.at[len(loads)])
        copy.start()
        loads[name] = copy

    for kind in (1, 2):
        load(("w", kind), weights_hbm.at[kind], weights_ref.at[kind])
    for block in range(4):
        owner = (far_sib, far_same, near_sib, tensor)[block]
        load(("k", block), gk_hbm.at[rows_of(owner)], gk_ref.at[rows_of(owner)])
        load(("v", block), gv_hbm.at[rows_of(owner)], gv_ref.at[rows_of(owner)])
    load("rows", rows_hbm, rows_ref)
    load("q", gq_hbm, gq_ref)
    load(("w", 0), weights_hbm.at[0], weights_ref.at[0])
    load("one", grad_one_hbm, grad_one_ref)

    barrier = pltpu.get_barrier_semaphore()
    others = [place.sibling(), place.step("x", 1), place.step("y", 1)]
    others += [place.device(z=lax.rem(z + i, DEPTH)) for i in range(1, DEPTH)]
    for target in others:
        pl.semaphore_signal(barrier, inc=1, device_id=target, device_id_type=MESH_ID)
    pl.semaphore_wait(barrier, len(others))

    def remote(source, target, send, recv, device):
        copy = pltpu.make_async_remote_copy(
            src_ref=source,
            dst_ref=target,
            send_sem=send,
            recv_sem=recv,
            device_id=device,
            device_id_type=MESH_ID,
        )
        copy.start()
        return copy


    def partial(owner, half):
        window = pl.ds(pl.multiple_of(owner * token_rows + half * half_rows, half_rows), half_rows)
        return dot_nt(gk_ref[window, :], weights_ref[1]) + dot_nt(gv_ref[window, :], weights_ref[2])

    def await_loads(*names):
        for name in names:
            loads[name].wait()

    await_loads(("w", 1), ("w", 2), ("k", 0), ("v", 0))
    sib_copies, x_copies, home_copies = [], [], []
    for half in range(2):
        to_sib[half] = partial(far_sib, half).astype(jnp.bfloat16)
        sib_copies.append(
            remote(
                to_sib.at[half],
                from_sib.at[half],
                block_send.at[0, half],
                block_recv.at[0, half],
                place.sibling(),
            )
        )
    await_loads(("k", 1), ("v", 1))
    for half in range(2):
        mine = partial(far_same, half)
        sib_copies[half].wait_recv()
        to_x[half] = (mine + from_sib[half].astype(jnp.float32)).astype(jnp.bfloat16)
        x_copies.append(
            remote(
                to_x.at[half],
                from_x.at[half],
                block_send.at[1, half],
                block_recv.at[1, half],
                place.step("x", 1),
            )
        )

    await_loads(("k", 2), ("v", 2), ("k", 3), ("v", 3), "rows", "q")
    own_rows = rows_ref.at[rows_of(tensor)]
    adapter_parts(own_rows, gq_ref, down_q_ref[...], ups_full[0:8, :], sums, 0, 16)
    adapter_parts(rows_ref, gv_ref, down_v_ref[...], ups_full[8:16, :], sums, 8, 24)
    kept = pl.ds(pl.multiple_of(core * 16, 16), 16)
    given = pl.ds(pl.multiple_of((1 - core) * 16, 16), 16)
    sum_copies = [
        remote(sums.at[given], sums_in, sum_send.at[0], sum_recv.at[0], place.sibling())
    ]
    for half in range(2):
        home_to[half] = partial(near_sib, half).astype(jnp.bfloat16)
        home_copies.append(
            remote(
                home_to.at[half],
                home_from.at[half],
                block_send.at[2, half],
                block_recv.at[2, half],
                place.sibling(),
            )
        )
    sum_copies[0].wait_recv()
    step_out[0] = sums[kept, :] + sums_in[...]
    sum_copies.append(
        remote(step_out.at[0], step_in.at[0], sum_send.at[1], sum_recv.at[1], place.step("y", 1))
    )
    await_loads(("w", 0), "one")
    for half in range(2):
        window = pl.ds(half * half_rows, half_rows)
        grad_one_ref[window, :] += partial(tensor, half) + dot_nt(gq_ref[window, :], weights_ref[0])
    sum_copies[1].wait_recv()
    z_slots[z] = step_out[0] + step_in[0]
    for i in range(1, DEPTH):
        there = lax.rem(z + i, DEPTH)
        sum_copies.append(
            remote(
                z_slots.at[z],
                z_slots.at[z],
                sum_send.at[1 + i],
                sum_recv.at[1 + i],
                place.device(z=there),
            )
        )
    for i in range(1, DEPTH):
        sum_copies[1 + i].wait_recv()
    column = z_slots[0]
    for i in range(1, DEPTH):
        column = column + z_slots[i]
    step_out[1] = column
    sum_copies.append(
        remote(
            step_out.at[1],
            step_in.at[1],
            sum_send.at[DEPTH + 1],
            sum_recv.at[DEPTH + 1],
            place.step("x", 1),
        )
    )
    sum_copies[-1].wait_recv()
    step_out[2] = step_out[1] + step_in[1]
    sum_copies.append(
        remote(
            step_out.at[2],
            final_in,
            sum_send.at[DEPTH + 2],
            sum_recv.at[DEPTH + 2],
            place.sibling(),
        )
    )

    for half in range(2):
        home_copies[half].wait_recv()
        x_copies[half].wait_recv()
        window = pl.ds(half * half_rows, half_rows)
        grad_tokens_ref[window, :] = (
            grad_one_ref[window, :]
            + home_from[half].astype(jnp.float32)
            + from_x[half].astype(jnp.float32)
        ).astype(jnp.bfloat16)
    sum_copies[-1].wait_recv()

    for sums_half, half in ((step_out.at[2], core), (final_in, 1 - core)):
        sums_ref[pl.ds(pl.multiple_of(half * 16, 16), 16), :] = sums_half[...]
    for copy in sib_copies + x_copies + home_copies + sum_copies:
        copy.wait_send()


def final_sums(grad_q, grad_k, grad_v, weights, rows_all, grad_one, ups_full, down_q_t, down_v_t):
    token_rows, width = grad_q.shape
    total_rows = grad_k.shape[0]
    bf16, f32 = jnp.bfloat16, jnp.float32
    half = (2, token_rows // 2, width)
    dma = pltpu.SemaphoreType.DMA
    return pl.pallas_call(
        final_kernel,
        out_shape=(
            jax.ShapeDtypeStruct((token_rows, width), bf16),
            jax.ShapeDtypeStruct((32, width), f32),
        ),
        in_specs=[HBM_SPEC] * 6 + [VMEM_SPEC] * 3,
        out_specs=(VMEM_SPEC,) * 2,
        scratch_shapes=[
            pltpu.VMEM((token_rows, width), bf16),
            pltpu.VMEM((total_rows, width), bf16),
            pltpu.VMEM((total_rows, width), bf16),
            pltpu.VMEM((3, width, width), bf16),
            pltpu.VMEM((total_rows, width), bf16),
            pltpu.VMEM((token_rows, width), f32),
        ]
        + [pltpu.VMEM(half, bf16)] * 6
        + [
            pltpu.VMEM((32, width), f32),
            pltpu.VMEM((16, width), f32),
            pltpu.VMEM((3, 16, width), f32),
            pltpu.VMEM((2, 16, width), f32),
            pltpu.VMEM((DEPTH, 16, width), f32),
            pltpu.VMEM((16, width), f32),
            dma((14,)),
            dma((3, 2)),
            dma((3, 2)),
            dma((DEPTH + 3,)),
            dma((DEPTH + 3,)),
        ],
        compiler_params=pltpu.CompilerParams(
            collective_id=2, has_side_effects=True, vmem_limit_bytes=VMEM_LIMIT
        ),
        name="final_sums",
    )(grad_q, grad_k, grad_v, weights, rows_all, grad_one, ups_full, down_q_t, down_v_t)


def hand_out_kernel(grad_ref, sums_ref, grad_out, aq_ref, av_ref, bq_ref, bv_ref):
    grad_out[...] = grad_ref[...]
    slim = bq_ref.shape[1]
    aq_ref[...] = sums_ref[0:8, :]
    av_ref[...] = sums_ref[8:16, :]
    for t in range(sums_ref.shape[1] // slim):

        @pl.when(lax.axis_index("tensor") == t)
        def _(t=t):
            bq_ref[...] = sums_ref[16:24, t * slim : (t + 1) * slim]
            bv_ref[...] = sums_ref[24:32, t * slim : (t + 1) * slim]


def hand_out(grad_tokens, sums, slim):
    f32, width = jnp.float32, sums.shape[1]
    return pl.pallas_call(
        hand_out_kernel,
        out_shape=(
            jax.ShapeDtypeStruct(grad_tokens.shape, grad_tokens.dtype),
            jax.ShapeDtypeStruct((8, width), f32),
            jax.ShapeDtypeStruct((8, width), f32),
            jax.ShapeDtypeStruct((8, slim), f32),
            jax.ShapeDtypeStruct((8, slim), f32),
        ),
        in_specs=[VMEM_SPEC] * 2,
        out_specs=(VMEM_SPEC,) * 5,
        name="hand_out",
    )(grad_tokens, sums)


def local(
    fast,
    tokens,
    query_weight,
    w_key,
    value_weight,
    w_out,
    w_in,
    w_down,
    gain_attn,
    shift_attn,
    gain_ffn,
    shift_ffn,
    query_down_factor,
    query_up_factor,
    value_down_factor,
    value_up_factor,
    lengths,
    cotangent,
):
    slim = query_weight.shape[1]
    width = tokens.shape[1]
    token_rows = tokens.shape[0]
    down_q_t, down_v_t = query_down_factor.T, value_down_factor.T
    if fast:
        full, weights, rows_all, q_own, k_all, v_all, ups_full = gather_all(
            query_weight,
            w_key,
            value_weight,
            w_out,
            w_in,
            w_down.T,
            tokens,
            query_up_factor,
            value_up_factor,
            down_q_t,
            down_v_t,
        )
        full = full.reshape(2, 4, width, width)
    else:
        attn_pack = jnp.concatenate([query_weight, w_key, value_weight, w_out.T], axis=1)
        full = jnp.stack([attn_pack, w_in, w_down.T])
        full = lax.all_gather(full, "dp", axis=1, tiled=True)
        full = lax.all_gather(full, "tensor", axis=1)
        rows_all = lax.all_gather(tokens, "tensor").reshape(-1, width)
        ups = jnp.concatenate([query_up_factor, value_up_factor], axis=0)
        ups = jnp.pad(ups, ((0, 0), (0, -slim % 128)))
        ups_all = lax.all_gather(ups, "tensor")
        downs = jnp.concatenate([down_q_t, down_v_t], axis=0)
        order = tuple(range(full.shape[1]))
        weights, q_own, k_all, v_all = project(order, full, rows_all, ups_all, downs, token_rows)

    norms = (gain_attn, shift_attn, gain_ffn, shift_ffn)
    mixed, grad_one, grad_q, grad_k, grad_v = middle(
        lengths, norms, q_own, k_all, v_all, tokens, cotangent, weights, full
    )
    if fast:
        grad_tokens, sums = final_sums(
            grad_q, grad_k, grad_v, weights, rows_all, grad_one, ups_full, down_q_t, down_v_t
        )
        grad_tokens, grad_aq, grad_av, grad_bq, grad_bv = hand_out(grad_tokens, sums, slim)
        return (mixed, grad_tokens, grad_aq.T, grad_bq, grad_av.T, grad_bv)

    query_up = ups_all[:, :8, :slim].transpose(1, 0, 2).reshape(8, width)
    value_up = ups_all[:, 8:, :slim].transpose(1, 0, 2).reshape(8, width)
    w_q, w_k, w_v = weights[0], weights[1], weights[2]
    u_query = dot_nn(tokens, query_down_factor).astype(jnp.bfloat16)
    u_value = dot_nn(rows_all, value_down_factor).astype(jnp.bfloat16)
    grad_uq = ADAPTER_SCALE * dot_nt(grad_q, query_up)
    grad_uv = ADAPTER_SCALE * dot_nt(grad_v, value_up)
    grad_bq = ADAPTER_SCALE * dot_tn(u_query, grad_q)
    grad_bv = ADAPTER_SCALE * dot_tn(u_value, grad_v)
    grad_aq = dot_tn(tokens, grad_uq.astype(jnp.bfloat16))
    grad_av = dot_tn(rows_all, grad_uv.astype(jnp.bfloat16))
    grad_rows = dot_nt(grad_k, w_k) + dot_nt(grad_v, w_v)
    own_rows = dot_nt(grad_q, w_q)
    shared = lax.psum_scatter(
        grad_rows.astype(jnp.bfloat16), "tensor", scatter_dimension=0, tiled=True
    )
    grad_tokens = (grad_one + own_rows + shared.astype(jnp.float32)).astype(jnp.bfloat16)
    grad_aq, grad_av, grad_bq, grad_bv = lax.psum(
        (grad_aq, grad_av, grad_bq, grad_bv), ("dp", "tensor")
    )
    at = lax.axis_index("tensor") * slim
    grad_bq = lax.dynamic_slice_in_dim(grad_bq, at, slim, 1)
    grad_bv = lax.dynamic_slice_in_dim(grad_bv, at, slim, 1)
    return (mixed, grad_tokens, grad_aq, grad_bq, grad_av, grad_bv)


def solution(mesh):
    fast = dict(mesh.shape) == {"dp": 2 * DEPTH, "tensor": 4}
    return jax.shard_map(
        functools.partial(local, fast),
        mesh=mesh,
        in_specs=(
            P(("dp", "tensor"), None),
            P("dp", "tensor"),
            P("dp", "tensor"),
            P("dp", "tensor"),
            P("tensor", "dp"),
            P("dp", "tensor"),
            P("tensor", "dp"),
            P(),
            P(),
            P(),
            P(),
            P(),
            P(None, "tensor"),
            P(),
            P(None, "tensor"),
            P("dp", None),
            P(("dp", "tensor"), None),
        ),
        out_specs=(
            P(("dp", "tensor"), None),
            P(("dp", "tensor"), None),
            P(),
            P(None, "tensor"),
            P(),
            P(None, "tensor"),
        ),
        check_vma=False,
    )
```

```python
import functools
import heapq

import jax
import jax.numpy as jnp
from jax import lax
from jax.experimental import pallas as pl
from jax.experimental.pallas import tpu as pltpu
from jax.sharding import PartitionSpec as P

HEAD_DIM = 64
PAIR = 2 * HEAD_DIM
Q_BLOCK = 256
K_BLOCK = 512
KV_BLOCK = 256
FAR_CHUNKS = 4
FORWARD_GROUP = 3
BACKWARD_GROUP = 3
ADAPTER_SCALE = 2.0
SCORE_SCALE = HEAD_DIM ** (-0.5)
LOG2_SCALE = SCORE_SCALE * 1.4426950408889634
NEG_FILL = -1e30
LN_EPS = 1e-05
VMEM_LIMIT = 60 * 1024 * 1024


def dot_nn(left, right):
    return jnp.dot(left, right, preferred_element_type=jnp.float32)


def dot_nt(left, right):
    return lax.dot_general(
        left, right, (((1,), (1,)), ((), ())), preferred_element_type=jnp.float32
    )


def dot_tn(left, right):
    return lax.dot_general(
        left, right, (((0,), (0,)), ((), ())), preferred_element_type=jnp.float32
    )


def norm_forward(row_vals, gain_vals, offset):
    middle = jnp.mean(row_vals, axis=-1, keepdims=True)
    centred = row_vals - middle
    inverse = lax.rsqrt(jnp.mean(centred * centred, axis=-1, keepdims=True) + LN_EPS)
    normed = centred * inverse
    return (normed * gain_vals + offset, normed, inverse)


def norm_backward(grad_out, normed, inverse, gain_vals):
    grad_n = grad_out * gain_vals
    return inverse * (
        grad_n
        - jnp.mean(grad_n, axis=-1, keepdims=True)
        - normed * jnp.mean(grad_n * normed, axis=-1, keepdims=True)
    )


def gelu_parts(hidden):
    cdf_part = 0.5 * (1.0 + lax.erf(hidden * 0.7071067811865476))
    density = jnp.exp(-0.5 * hidden * hidden) * 0.3989422804014327
    return (hidden * cdf_part, cdf_part + hidden * density)


def block_span(lengths_ref, first_row, rows, total_rows):
    last_row = first_row + rows - 1

    def slot_step(slot, carry):
        end, low, high = carry
        end = end + lengths_ref[0, slot]
        low = jnp.where(end <= first_row, jnp.maximum(low, end), low)
        high = jnp.where(end > last_row, jnp.minimum(high, end), high)
        return end, low, high

    start = (jnp.int32(0), jnp.int32(0), jnp.int32(total_rows))
    _, low, high = lax.fori_loop(0, lengths_ref.shape[1], slot_step, start, unroll=8)
    return low, high


def row_bounds(lengths_ref, first_row, rows, total_rows):
    place = first_row + lax.broadcasted_iota(jnp.int32, (1, rows), 1)

    def slot_step(slot, carry):
        end, begin, finish = carry
        end = end + lengths_ref[0, slot]
        done = place >= end
        begin = jnp.where(done, jnp.maximum(begin, end), begin)
        finish = jnp.where(done, finish, jnp.minimum(finish, end))
        return end, begin, finish

    start = (
        jnp.int32(0),
        jnp.zeros((1, rows), jnp.int32),
        jnp.full((1, rows), total_rows, jnp.int32),
    )
    _, begin, finish = lax.fori_loop(0, lengths_ref.shape[1], slot_step, start, unroll=8)
    return begin, finish


def stack_pair(block):
    lane = lax.broadcasted_iota(jnp.int32, block.shape, 1)
    zero = jnp.zeros_like(block)
    return jnp.concatenate(
        [jnp.where(lane < HEAD_DIM, block, zero), jnp.where(lane >= HEAD_DIM, block, zero)],
        axis=0,
    )


def unstack_pair(block, rows):
    joined = jnp.concatenate([block[:HEAD_DIM, :rows], block[HEAD_DIM:, rows:]], axis=0)
    return joined.T


def window_mask(step, low, begin, finish, total_rows):
    wanted = low + step * K_BLOCK
    start = pl.multiple_of(jnp.minimum(wanted, total_rows - K_BLOCK), 16)
    key_at = start + lax.broadcasted_iota(jnp.int32, (K_BLOCK, begin.shape[1]), 0)
    return start, (key_at >= jnp.maximum(begin, wanted)) & (key_at < finish)


def query_span(lengths_ref, first_row, total_rows):
    low, high = block_span(lengths_ref, first_row, Q_BLOCK, total_rows)
    low = (low // 16) * 16
    return low, (high - low + K_BLOCK - 1) // K_BLOCK


def each_q_block(lengths_ref, rows, total_rows, group, heads_width, block_step):
    base = lax.axis_index("tensor") * rows

    @pl.loop(0, rows // Q_BLOCK)
    def _(q_at):
        first_row = base + q_at * Q_BLOCK
        low, steps = query_span(lengths_ref, first_row, total_rows)
        begin, finish = row_bounds(lengths_ref, first_row, Q_BLOCK, total_rows)
        q_rows = pl.ds(pl.multiple_of(q_at * Q_BLOCK, Q_BLOCK), Q_BLOCK)

        @pl.loop(0, heads_width // PAIR // group)
        def _(at):
            pairs = [at * group + i for i in range(group)]
            lanes = [pl.ds(pl.multiple_of(pair * PAIR, PAIR), PAIR) for pair in pairs]
            slots = [q_at * (heads_width // PAIR) + pair for pair in pairs]
            block_step(q_rows, lanes, slots, low, steps, begin, finish)


def attend_forward(lengths_ref, q_ref, k_ref, v_ref, out_ref, lse_ref):
    total_rows = k_ref.shape[0]

    def block_step(q_rows, lanes, slots, low, steps, begin, finish):
        q_two = [stack_pair(q_ref[q_rows, lane]) for lane in lanes]

        def body(step, carry):
            start, allowed = window_mask(step, low, begin, finish, total_rows)
            window = pl.ds(start, K_BLOCK)
            both = jnp.concatenate([allowed, allowed], axis=1)
            result = []
            for (top, total, acc), q_pair, lane in zip(carry, q_two, lanes):
                scores = jnp.where(both, dot_nt(k_ref[window, lane], q_pair), NEG_FILL)
                new_top = jnp.maximum(top, jnp.max(scores, axis=0, keepdims=True))
                probs = jnp.exp2((scores - new_top) * LOG2_SCALE)
                shrink = jnp.exp2((top - new_top) * LOG2_SCALE)
                total = total * shrink + jnp.sum(probs, axis=0, keepdims=True)
                acc = acc * shrink + dot_tn(v_ref[window, lane], probs.astype(jnp.bfloat16))
                result.append((new_top, total, acc))
            return tuple(result)

        empty = (
            jnp.full((1, 2 * Q_BLOCK), NEG_FILL, jnp.float32),
            jnp.zeros((1, 2 * Q_BLOCK), jnp.float32),
            jnp.zeros((PAIR, 2 * Q_BLOCK), jnp.float32),
        )
        final = lax.fori_loop(0, steps, body, (empty,) * len(lanes))
        for (top, total, acc), lane, slot in zip(final, lanes, slots):
            out_ref[q_rows, lane] = unstack_pair(acc / total, Q_BLOCK).astype(jnp.bfloat16)
            lse_ref[slot] = top * LOG2_SCALE + jnp.log2(total)

    each_q_block(
        lengths_ref, q_ref.shape[0], total_rows, FORWARD_GROUP, q_ref.shape[1], block_step
    )


def attend_backward(
    lengths_ref, q_ref, k_ref, v_ref, ctx_ref, lse_ref, grad_ref, gq_ref, gk_acc, gv_acc
):
    total_rows = k_ref.shape[0]

    def block_step(q_rows, lanes, slots, low, steps, begin, finish):
        ready = []
        for lane, slot in zip(lanes, slots):
            grads = grad_ref[q_rows, lane]
            product = (grads.astype(jnp.float32) * ctx_ref[q_rows, lane].astype(jnp.float32)).T
            row_dot = jnp.concatenate(
                [
                    jnp.sum(product[:HEAD_DIM], axis=0, keepdims=True),
                    jnp.sum(product[HEAD_DIM:], axis=0, keepdims=True),
                ],
                axis=1,
            )
            ready.append((stack_pair(q_ref[q_rows, lane]), stack_pair(grads), row_dot, lse_ref[slot]))

        def body(step, carry):
            start, allowed = window_mask(step, low, begin, finish, total_rows)
            window = pl.ds(start, K_BLOCK)
            both = jnp.concatenate([allowed, allowed], axis=1)
            result = []
            for acc, (q_pair, grad_pair, row_dot, lse), lane in zip(carry, ready, lanes):
                keys = k_ref[window, lane]
                scores = jnp.where(both, dot_nt(keys, q_pair), NEG_FILL)
                probs = jnp.exp2(scores * LOG2_SCALE - lse)
                grad_probs = dot_nt(v_ref[window, lane], grad_pair)
                grad_scores = (probs * (grad_probs - row_dot)).astype(jnp.bfloat16)
                gk_acc[window, lane] += dot_nn(grad_scores, q_pair)
                gv_acc[window, lane] += dot_nn(probs.astype(jnp.bfloat16), grad_pair)
                result.append(acc + dot_tn(keys, grad_scores))
            return tuple(result)

        zero = jnp.zeros((PAIR, 2 * Q_BLOCK), jnp.float32)
        final = lax.fori_loop(0, steps, body, (zero,) * len(lanes))
        for acc, lane in zip(final, lanes):
            gq_ref[q_rows, lane] = (unstack_pair(acc, Q_BLOCK) * SCORE_SCALE).astype(jnp.bfloat16)

    each_q_block(
        lengths_ref, q_ref.shape[0], total_rows, BACKWARD_GROUP, q_ref.shape[1], block_step
    )


VMEM_SPEC = pl.BlockSpec(memory_space=pltpu.VMEM)
HBM_SPEC = pl.BlockSpec(memory_space=pltpu.HBM)
SMEM_SPEC = pl.BlockSpec(memory_space=pltpu.SMEM)


MESH_ID = pl.DeviceIdType.MESH
DEPTH = 4
FULL_ROWS = 96

FLOWS = (
    (0, 0, "zxy", 0.0),
    (0, 1, "zyx", 0.0),
    (1, 0, "xzy", 12.0),
    (1, 1, "zyx", 24.0),
    (2, 0, "xzy", 12.0),
    (2, 1, "yxz", 12.0),
)
OWN = (0, 0, 0)


def forwards(order, piece):
    used = [axis for axis in order if piece["xyz".index(axis)] != 0]
    at = order.index(used[-1]) if used else -1
    steps = []
    if used and used[-1] == "z":
        steps.append(("z", 1 if piece[2] < 0 else -1))
    for axis in order[at + 1 :]:
        steps += [("z", 1), ("z", -1)] if axis == "z" else [(axis, 1)]
    return steps


def passed(piece, axis, sign):
    x, y, z = piece
    if axis == "x":
        return (1 - x, y, z)
    return (x, 1 - y, z) if axis == "y" else (x, y, z - sign)


def event_order(token_time):
    per_piece = 1.7
    links, heap, times, count = {}, [], {}, 0
    for z in range(DEPTH):
        links[z, "x", 1] = token_time
        for flow, (_, _, _, start) in enumerate(FLOWS):
            heapq.heappush(heap, (start + 0.01 * flow, count, z, flow, OWN))
            count += 1
    while heap:
        now, _, z, flow, piece = heapq.heappop(heap)
        times.setdefault((flow, piece), []).append(now)
        for axis, sign in forwards(FLOWS[flow][2], piece):
            there = z + sign if axis == "z" else z
            if not 0 <= there < DEPTH:
                continue
            end = max(links.get((z, axis, sign), 0.0), now) + per_piece
            links[z, axis, sign] = end
            heapq.heappush(heap, (end + 3.0, count, there, flow, passed(piece, axis, sign)))
            count += 1
    return [key for _, key in sorted((sum(v) / len(v), key) for key, v in times.items())]


class Place:
    def __init__(self):
        dp, tensor = lax.axis_index("dp"), lax.axis_index("tensor")
        self.z, self.y = dp // 2, lax.rem(dp, 2)
        self.x, self.core = tensor // 2, lax.rem(tensor, 2)

    def device(self, x=None, y=None, z=None, core=None):
        x = self.x if x is None else x
        y = self.y if y is None else y
        z = self.z if z is None else z
        core = self.core if core is None else core
        return (z * 2 + y, x * 2 + core)

    def step(self, axis, sign):
        if axis == "x":
            return self.device(x=1 - self.x)
        return self.device(y=1 - self.y) if axis == "y" else self.device(z=self.z + sign)

    def sibling(self):
        return self.device(core=1 - self.core)


def gather_kernel(
    wq_ref,
    wk_ref,
    wv_ref,
    wo_ref,
    w_in_ref,
    w_down_ref,
    tokens_ref,
    up_q_ref,
    up_v_ref,
    down_q_ref,
    down_v_ref,
    lengths_ref,
    full_ref,
    weights_hbm,
    rows_hbm,
    q_hbm,
    k_hbm,
    v_hbm,
    ups_full,
    fewest_ref,
    pack_ref,
    packs_ref,
    rows_ref,
    ups_ref,
    ups_all_ref,
    weights_ref,
    q_ref,
    k_ref,
    v_ref,
    count_ref,
    counts_ref,
    count_send,
    count_recv,
    piece_recv,
    send_sem,
    sib_send,
    sib_recv,
    own_sem,
    rows_send,
    rows_recv,
    ups_send,
    ups_recv,
    out_sem,
):
    place = Place()
    x, y, z, core = place.x, place.y, place.z, place.core
    token_rows = tokens_ref.shape[0]
    part_rows = FULL_ROWS // 2
    half_rows = token_rows // 2

    barrier = pltpu.get_barrier_semaphore()
    others = (
        place.sibling(),
        place.step("x", 1),
        place.device(x=1 - x, core=1 - core),
        place.step("y", 1),
    )
    for target in others:
        pl.semaphore_signal(barrier, inc=1, device_id=target, device_id_type=MESH_ID)
    column = [place.device(z=lax.rem(z + i, DEPTH)) for i in range(1, DEPTH)]
    for target in column:
        pl.semaphore_signal(barrier, inc=1, device_id=target, device_id_type=MESH_ID)

    slim = wq_ref.shape[1]
    for kind, ref in enumerate((wq_ref, wk_ref, wv_ref)):
        pack_ref[:, kind * slim : (kind + 1) * slim] = ref[...]
    pack_ref[:, 3 * slim : 4 * slim] = wo_ref[...].astype(jnp.float32).T.astype(jnp.bfloat16)
    ups_ref[...] = jnp.zeros_like(ups_ref)
    ups_ref[0:8, :slim] = up_q_ref[...].astype(jnp.float32)
    ups_ref[8:16, :slim] = up_v_ref[...].astype(jnp.float32)
    count_ref[...] = jnp.broadcast_to(
        jnp.sum(lengths_ref[...].astype(jnp.float32), axis=1, keepdims=True), count_ref.shape
    )
    shards = (pack_ref, w_in_ref, w_down_ref)
    pl.semaphore_wait(barrier, len(others) + len(column))

    def remote(source, target, send, recv, device):
        return pltpu.make_async_remote_copy(
            src_ref=source,
            dst_ref=target,
            send_sem=send,
            recv_sem=recv,
            device_id=device,
            device_id_type=MESH_ID,
        )

    def rows_at(owner_x, owner_core, half):
        return rows_ref.at[owner_x * 2 + owner_core, pl.ds(half * half_rows, half_rows)]

    own_copies = [
        pltpu.make_async_copy(pack_ref, packs_ref.at[core, x, z, y], own_sem.at[0]),
        pltpu.make_async_copy(tokens_ref, rows_ref.at[x * 2 + core], own_sem.at[1]),
        pltpu.make_async_copy(ups_ref, ups_all_ref.at[x * 2 + core], own_sem.at[2]),
        pltpu.make_async_copy(w_in_ref, full_ref.at[0, core, x, z, y], own_sem.at[3]),
        pltpu.make_async_copy(w_down_ref, full_ref.at[1, core, x, z, y], own_sem.at[4]),
    ]
    row_copies = []
    for half in range(2):
        source = tokens_ref.at[pl.ds(half * half_rows, half_rows)]
        for slot, device in ((0, place.step("x", 1)), (1, place.sibling())):
            row_copies.append(
                remote(
                    source,
                    rows_at(x, core, half),
                    rows_send.at[slot, half],
                    rows_recv.at[slot, half],
                    device,
                )
            )
    up_copies = [
        remote(ups_ref, ups_all_ref.at[x * 2 + core], ups_send.at[i], ups_recv.at[i], device)
        for i, device in enumerate(others[:3])
    ]

    sends = {}

    def gathered(kind):
        return packs_ref if kind == 0 else full_ref.at[kind - 1]

    def half_of(kind, part):
        return pl.ds(part * part_rows, part_rows)

    def piece_at(flow, piece):
        kind, part, _, _ = FLOWS[flow]
        px, py = lax.rem(x + piece[0], 2), lax.rem(y + piece[1], 2)
        return (
            gathered(kind).at[core, px, z + piece[2], py, half_of(kind, part)],
            (px * 2 + py) * DEPTH + z + piece[2],
        )

    def handle(flow, piece):
        kind, part, order, _ = FLOWS[flow]
        landed, index = piece_at(flow, piece)
        source = landed
        if piece == OWN:
            source = shards[kind].at[half_of(kind, part)]
        else:
            remote(landed, landed, send_sem.at[flow, 0], piece_recv.at[flow, index], place.sibling()).wait_recv()
        for axis, sign in forwards(order, piece):
            slot = {"x": 0, "y": 1, "z": 2 if sign > 0 else 3}[axis]
            copy = remote(
                source,
                landed,
                send_sem.at[flow, slot],
                piece_recv.at[flow, index],
                place.step(axis, sign),
            )
            if axis == "z":
                pl.when((z + sign >= 0) & (z + sign < DEPTH))(copy.start)
            else:
                copy.start()
                sends[flow, slot] = sends.get((flow, slot), 0) + 1
        remote(source, landed, sib_send.at[flow], sib_recv.at[flow], place.sibling()).start()

    def block_of(flow, pieces, plane):
        kind, part, _, _ = FLOWS[flow]
        nx = 2 if pieces % 2 == 0 else 1
        ny = 2 if pieces % 4 == 0 else 1
        return gathered(kind).at[
            plane,
            pl.ds(0, nx),
            pl.ds(0, pieces // (nx * ny)),
            pl.ds(0, ny),
            half_of(kind, part),
        ]

    def finish_flow(flow):
        order = FLOWS[flow][2]
        everything = block_of(flow, 4 * DEPTH, 1 - core)
        remote(everything, everything, sib_send.at[flow], sib_recv.at[flow], place.sibling()).wait()

    def finish_sends(flow):
        order = FLOWS[flow][2]
        for axis, slot in (("x", 0), ("y", 1)):
            block = block_of(flow, 2 ** order.index(axis) * (DEPTH // 2 if "z" in order[: order.index(axis)] else 1), core)
            remote(block, block, send_sem.at[flow, slot], sib_recv.at[flow], place.sibling()).wait_send()
        each = 2 ** order.index("z")
        for at in range(DEPTH):
            for slot, sets in ((2, at + 1 if at < DEPTH - 1 else 0), (3, DEPTH - at if at > 0 else 0)):
                if sets:

                    @pl.when(z == at)
                    def _(slot=slot, sets=sets):
                        nx = 2 if each > 1 else 1
                        ny = 2 if each > 2 else 1
                        kind, part, _, _ = FLOWS[flow]
                        block = gathered(kind).at[
                            core,
                            pl.ds(0, nx),
                            pl.ds(0, sets),
                            pl.ds(0, ny),
                            half_of(kind, part),
                        ]
                        remote(
                            block, block, send_sem.at[flow, slot], sib_recv.at[flow], place.sibling()
                        ).wait_send()

    for copy in row_copies + up_copies + own_copies:
        copy.start()

    count_copies = [
        remote(
            count_ref, counts_ref.at[DEPTH], count_send.at[0], count_recv.at[0], place.step("y", 1)
        )
    ]
    count_copies[0].start()

    def pass_count():
        count_copies[0].wait_recv()
        counts_ref[z] = jnp.minimum(count_ref[...], counts_ref[DEPTH])
        for i, target in enumerate(column):
            copy = remote(
                counts_ref.at[z], counts_ref.at[z], count_send.at[1 + i], count_recv.at[1 + i], target
            )
            copy.start()
            count_copies.append(copy)

    def pass_rows(half):
        row_copies[2 * half].wait_recv()
        landed = rows_at(1 - x, core, half)
        copy = remote(landed, landed, rows_send.at[2, half], rows_recv.at[2, half], place.sibling())
        copy.start()
        return copy

    outs = []

    def write(source, target):
        copy = pltpu.make_async_copy(source, target, out_sem.at[len(outs)])
        copy.start()
        outs.append(copy)

    def assemble(t):
        if t == 0:
            for copy in up_copies + own_copies[:3]:
                copy.wait()
            for half in range(2):
                row_copies[2 * half + 1].wait_recv()
                passed_rows[half].wait_recv()
            for owner in range(4):
                write(rows_ref.at[owner], rows_hbm.at[pl.ds(owner * token_rows, token_rows)])
            finish_flow(0)
            finish_flow(1)
            for owner in range(4):
                ups_full[:, owner * slim : (owner + 1) * slim] = ups_all_ref[owner, :, :slim].astype(jnp.bfloat16)
        lanes = slice(t * slim, (t + 1) * slim)
        source = packs_ref.at[t % 2, t // 2]
        for kind, down_ref, first in ((0, down_q_ref, 0), (1, None, 0), (2, down_v_ref, 8), (3, None, 0)):
            part = source[:, :, :, kind * slim : (kind + 1) * slim].reshape(-1, slim)
            if down_ref is not None:
                up = ups_all_ref[t, first : first + 8, :slim].astype(jnp.bfloat16)
                product = dot_tn(down_ref[...], up)
                part = (part.astype(jnp.float32) + ADAPTER_SCALE * product).astype(jnp.bfloat16)
            weights_ref[kind, :, lanes] = part
        if t == 3:
            write(weights_ref, weights_hbm)

    def own_queries():
        q_ref[...] = dot_nn(rows_ref[x * 2 + core], weights_ref[0]).astype(jnp.bfloat16)
        write(q_ref, q_hbm)

    def keys_values(ref, hbm, kind, owner):
        ref[owner] = dot_nn(rows_ref[owner], weights_ref[kind]).astype(jnp.bfloat16)
        write(ref.at[owner], hbm.at[pl.ds(owner * token_rows, token_rows)])

    steps = [functools.partial(assemble, t) for t in range(4)] + [own_queries]
    for owner in range(4):
        steps.append(functools.partial(keys_values, k_ref, k_hbm, 1, owner))
        steps.append(functools.partial(keys_values, v_ref, v_hbm, 2, owner))

    passed_rows = []
    events = event_order(17.0)
    last_pack = max(i for i, (flow, _) in enumerate(events) if FLOWS[flow][0] == 0)
    between = max(1, (len(events) - last_pack) // (len(steps) + 1))
    arrivals = 0
    for at, (flow, piece) in enumerate(events):
        if piece[2] == 0:
            handle(flow, piece)
        else:
            pl.when((z + piece[2] >= 0) & (z + piece[2] < DEPTH))(
                functools.partial(handle, flow, piece)
            )
        if piece != OWN:
            arrivals += 1
            if arrivals in (8, 16):
                passed_rows.append(pass_rows(len(passed_rows)))
            if arrivals == 24:
                pass_count()
        if at >= last_pack and (at - last_pack) % between == between - 1 and steps:
            steps.pop(0)()
    for step in steps:
        step()

    for half in range(2):
        row_copies[2 * half].wait_send()
        row_copies[2 * half + 1].wait_send()
        passed_rows[half].wait_send()
    for copy in own_copies[3:] + outs:
        copy.wait()
    for flow in range(len(FLOWS)):
        if flow > 1:
            finish_flow(flow)
        finish_sends(flow)
    for copy in count_copies[1:]:
        copy.wait()
    count_copies[0].wait_send()
    fewest_ref[0, 0] = jnp.min(counts_ref[0:DEPTH])


def gather_all(
    w_q, w_k, w_v, w_out, w_in, w_down_t, tokens, up_q, up_v, down_q_t, down_v_t, lengths
):
    shard_rows, width = w_in.shape
    token_rows = tokens.shape[0]
    bf16, f32 = jnp.bfloat16, jnp.float32
    slim = w_q.shape[1]
    padded = slim + -slim % 128
    flows = len(FLOWS)
    dma = pltpu.SemaphoreType.DMA
    grid = (2, 2, DEPTH, 2, shard_rows, width)
    return pl.pallas_call(
        gather_kernel,
        out_shape=(
            jax.ShapeDtypeStruct((2,) + grid, bf16),
            jax.ShapeDtypeStruct((4, width, width), bf16),
            jax.ShapeDtypeStruct((4 * token_rows, width), bf16),
            jax.ShapeDtypeStruct((token_rows, width), bf16),
            jax.ShapeDtypeStruct((4 * token_rows, width), bf16),
            jax.ShapeDtypeStruct((4 * token_rows, width), bf16),
            jax.ShapeDtypeStruct((16, width), bf16),
            jax.ShapeDtypeStruct((1, 1), f32),
        ),
        in_specs=[VMEM_SPEC] * 4 + [HBM_SPEC] * 3 + [VMEM_SPEC] * 5,
        out_specs=(HBM_SPEC,) * 6 + (VMEM_SPEC, SMEM_SPEC),
        scratch_shapes=[
            pltpu.VMEM((shard_rows, width), bf16),
            pltpu.VMEM(grid, bf16),
            pltpu.VMEM((4, token_rows, width), bf16),
            pltpu.VMEM((16, padded), f32),
            pltpu.VMEM((4, 16, padded), f32),
            pltpu.VMEM((4, width, width), bf16),
            pltpu.VMEM((token_rows, width), bf16),
            pltpu.VMEM((4, token_rows, width), bf16),
            pltpu.VMEM((4, token_rows, width), bf16),
            pltpu.VMEM((8, 128), f32),
            pltpu.VMEM((DEPTH + 1, 8, 128), f32),
            dma((DEPTH,)),
            dma((DEPTH,)),
            dma((flows, 4 * DEPTH)),
            dma((flows, 4)),
            dma((flows,)),
            dma((flows,)),
            dma((5,)),
            dma((3, 2)),
            dma((3, 2)),
            dma((3,)),
            dma((3,)),
            dma((14,)),
        ],
        compiler_params=pltpu.CompilerParams(
            collective_id=1, has_side_effects=True, vmem_limit_bytes=VMEM_LIMIT
        ),
        name="gather_all",
    )(
        w_q,
        w_k,
        w_v,
        w_out,
        w_in,
        w_down_t,
        tokens,
        up_q,
        up_v,
        down_q_t,
        down_v_t,
        lengths,
    )


def project_kernel(
    order,
    full_hbm,
    rows_ref,
    ups_ref,
    downs_ref,
    weights_ref,
    q_ref,
    k_ref,
    v_ref,
    packs_ref,
    sems,
):
    token_rows = q_ref.shape[0]
    slim = packs_ref.shape[2] // 4
    tensor = lax.axis_index("tensor")
    copies = [
        pltpu.make_async_copy(full_hbm.at[0, i], packs_ref.at[i], sems.at[i])
        for i in range(len(order))
    ]
    for copy in copies:
        copy.start()
    for i, t in enumerate(order):
        copies[i].wait()
        lanes = slice(t * slim, (t + 1) * slim)
        for kind, first in ((0, 0), (1, None), (2, 8), (3, None)):
            part = packs_ref[i, :, kind * slim : (kind + 1) * slim]
            if first is not None:
                up = ups_ref[t, first : first + 8, :slim]
                product = dot_tn(downs_ref[first : first + 8, :], up)
                part = (part.astype(jnp.float32) + ADAPTER_SCALE * product).astype(jnp.bfloat16)
            weights_ref[kind, :, lanes] = part
    own = rows_ref[pl.ds(pl.multiple_of(tensor * token_rows, token_rows), token_rows), :]
    q_ref[...] = dot_nn(own, weights_ref[0]).astype(jnp.bfloat16)

    @pl.loop(0, rows_ref.shape[0] // token_rows)
    def _(at):
        window = pl.ds(pl.multiple_of(at * token_rows, token_rows), token_rows)
        block = rows_ref[window, :]
        k_ref[window, :] = dot_nn(block, weights_ref[1]).astype(jnp.bfloat16)
        v_ref[window, :] = dot_nn(block, weights_ref[2]).astype(jnp.bfloat16)


def project(order, full, rows_all, ups_all, downs, token_rows):
    total_rows, width = rows_all.shape
    bf16 = jnp.bfloat16
    return pl.pallas_call(
        functools.partial(project_kernel, order),
        out_shape=(
            jax.ShapeDtypeStruct((4, width, width), bf16),
            jax.ShapeDtypeStruct((token_rows, width), bf16),
            jax.ShapeDtypeStruct((total_rows, width), bf16),
            jax.ShapeDtypeStruct((total_rows, width), bf16),
        ),
        in_specs=[HBM_SPEC] + [VMEM_SPEC] * 3,
        out_specs=(VMEM_SPEC,) * 4,
        scratch_shapes=[
            pltpu.VMEM(full.shape[1:], bf16),
            pltpu.SemaphoreType.DMA((len(order),)),
        ],
        compiler_params=pltpu.CompilerParams(vmem_limit_bytes=VMEM_LIMIT),
        name="project",
    )(full, rows_all, ups_all, downs)


def middle_kernel(
    lengths_ref,
    gain_attn_ref,
    shift_attn_ref,
    gain_ffn_ref,
    shift_ffn_ref,
    q_hbm,
    k_hbm,
    v_hbm,
    tokens_hbm,
    cot_hbm,
    weights_hbm,
    full_hbm,
    rows_hbm,
    ups_ref,
    down_q_ref,
    down_v_ref,
    mixed_hbm,
    grad_one_hbm,
    gq_hbm,
    gk_hbm,
    gv_hbm,
    far_hbm,
    sums_hbm,
    q_ref,
    k_ref,
    v_ref,
    tokens_ref,
    cot_ref,
    out_buf,
    in_buf,
    down_buf,
    slope_buf,
    first_buf,
    sum_buf,
    normed_buf,
    inverse_buf,
    ctx_ref,
    lse_ref,
    grad_ref,
    gk_acc,
    gv_acc,
    gk_out,
    gv_out,
    far_out,
    pair_buf,
    sums_ref,
    load_sem,
    part_sem,
    kv_sem,
    store_sem,
    grad_sem,
    far_sem,
):
    rows, width = q_ref.shape
    total_rows = k_ref.shape[0]
    parts, kinds = in_buf.shape[0], full_hbm.shape[0]
    kv_blocks = total_rows // KV_BLOCK
    base = lax.axis_index("tensor") * rows

    span_low, span_high = jnp.int32(total_rows), jnp.int32(0)
    for at in range(rows // Q_BLOCK):
        low, steps = query_span(lengths_ref, base + at * Q_BLOCK, total_rows)
        span_low = jnp.minimum(span_low, jnp.minimum(low, total_rows - K_BLOCK))
        span_high = jnp.maximum(span_high, jnp.minimum(low + steps * K_BLOCK, total_rows))

    def kv_rows(block):
        return pl.ds(pl.multiple_of(block * KV_BLOCK, KV_BLOCK), KV_BLOCK)

    def touched(block):
        return (block * KV_BLOCK < span_high) & ((block + 1) * KV_BLOCK > span_low)

    def kv_copies(block):
        window = kv_rows(block)
        return (
            pltpu.make_async_copy(k_hbm.at[window], k_ref.at[window], kv_sem.at[0, block]),
            pltpu.make_async_copy(v_hbm.at[window], v_ref.at[window], kv_sem.at[1, block]),
        )

    def part_copies(part):
        return (
            pltpu.make_async_copy(
                full_hbm.at[kinds - 2, part], in_buf.at[part], part_sem.at[0, part]
            ),
            pltpu.make_async_copy(
                full_hbm.at[kinds - 1, part], down_buf.at[part], part_sem.at[1, part]
            ),
        )

    q_copy = pltpu.make_async_copy(q_hbm, q_ref, load_sem.at[0])
    tokens_copy = pltpu.make_async_copy(tokens_hbm, tokens_ref, load_sem.at[1])
    out_copy = pltpu.make_async_copy(weights_hbm.at[3], out_buf, load_sem.at[2])
    cot_copy = pltpu.make_async_copy(cot_hbm, cot_ref, load_sem.at[3])
    pair_copy = pltpu.make_async_copy(weights_hbm.at[pl.ds(1, 2)], pair_buf, load_sem.at[4])
    q_copy.start()

    @pl.loop(0, kv_blocks)
    def _(block):
        @pl.when(touched(block))
        def _():
            for copy in kv_copies(block):
                copy.start()

    tokens_copy.start()
    out_copy.start()
    cot_copy.start()
    for part in range(parts):
        for copy in part_copies(part):
            copy.start()
    pair_copy.start()

    gk_acc[...] = jnp.zeros_like(gk_acc)
    gv_acc[...] = jnp.zeros_like(gv_acc)
    q_copy.wait()

    @pl.loop(0, kv_blocks)
    def _(block):
        @pl.when(touched(block))
        def _():
            for copy in kv_copies(block):
                copy.wait()

    attend_forward(lengths_ref, q_ref, k_ref, v_ref, ctx_ref, lse_ref)

    gain_attn, shift_attn, gain_ffn, shift_ffn = (
        ref[...].reshape(1, -1) for ref in (gain_attn_ref, shift_attn_ref, gain_ffn_ref, shift_ffn_ref)
    )
    tokens_copy.wait()
    out_copy.wait()
    residual = tokens_ref[...].astype(jnp.float32) + dot_nt(ctx_ref[...], out_buf[...])
    first, normed, inverse = norm_forward(residual, gain_attn, shift_attn)
    first_buf[...] = first.astype(jnp.bfloat16)
    sum_buf[...] = first.astype(jnp.bfloat16).astype(jnp.float32)
    normed_buf[...] = normed
    inverse_buf[...] = inverse

    @pl.loop(0, parts)
    def _(part):
        for copy in part_copies(part):
            copy.wait()
        acted, slope = gelu_parts(dot_nn(first_buf[...], in_buf[part]))
        slope_buf[part] = slope
        sum_buf[...] += dot_nt(acted.astype(jnp.bfloat16), down_buf[part])

    cot_copy.wait()
    mixed, normed, inverse = norm_forward(sum_buf[...], gain_ffn, shift_ffn)
    tokens_ref[...] = mixed.astype(jnp.bfloat16)
    mixed_copy = pltpu.make_async_copy(tokens_ref, mixed_hbm, store_sem.at[0])
    mixed_copy.start()
    grad_two = norm_backward(cot_ref[...].astype(jnp.float32), normed, inverse, gain_ffn)
    first_buf[...] = grad_two.astype(jnp.bfloat16)
    sum_buf[...] = grad_two

    @pl.loop(0, parts)
    def _(part):
        grad_hidden = dot_nn(first_buf[...], down_buf[part]) * slope_buf[part]
        sum_buf[...] += dot_nt(grad_hidden.astype(jnp.bfloat16), in_buf[part])

    grad_one = norm_backward(sum_buf[...], normed_buf[...], inverse_buf[...], gain_attn)
    normed_buf[...] = grad_one
    grad_one_copy = pltpu.make_async_copy(normed_buf, grad_one_hbm, store_sem.at[1])
    grad_one_copy.start()
    grad_ref[...] = dot_nn(grad_one.astype(jnp.bfloat16), out_buf[...]).astype(jnp.bfloat16)

    attend_backward(
        lengths_ref, q_ref, k_ref, v_ref, ctx_ref, lse_ref, grad_ref, first_buf, gk_acc, gv_acc
    )
    gq_copy = pltpu.make_async_copy(first_buf, gq_hbm, store_sem.at[2])
    gq_copy.start()

    def rows_copy(block):
        window = kv_rows(block)
        return pltpu.make_async_copy(rows_hbm.at[window], k_ref.at[window], kv_sem.at[0, block])

    @pl.loop(0, kv_blocks)
    def _(block):
        @pl.when(touched(block))
        def _():
            rows_copy(block).start()

    def grad_copies(block):
        window = kv_rows(block)
        return (
            pltpu.make_async_copy(gk_out.at[window], gk_hbm.at[window], grad_sem.at[0, block]),
            pltpu.make_async_copy(gv_out.at[window], gv_hbm.at[window], grad_sem.at[1, block]),
        )

    @pl.loop(0, kv_blocks)
    def _(block):
        window = kv_rows(block)

        @pl.when(touched(block))
        def _():
            gk_out[window, :] = (gk_acc[window, :] * SCORE_SCALE).astype(jnp.bfloat16)
            gv_out[window, :] = gv_acc[window, :].astype(jnp.bfloat16)

        @pl.when(jnp.logical_not(touched(block)))
        def _():
            gk_out[window, :] = jnp.zeros((KV_BLOCK, width), jnp.bfloat16)
            gv_out[window, :] = jnp.zeros((KV_BLOCK, width), jnp.bfloat16)

        for copy in grad_copies(block):
            copy.start()

    def far_copy(at):
        window = kv_rows(at)
        return pltpu.make_async_copy(far_out.at[window], far_hbm.at[window], far_sem.at[at])

    pair_copy.wait()
    tensor = lax.axis_index("tensor")
    near = tensor // 2
    per_owner = rows // KV_BLOCK

    @pl.loop(0, kv_blocks // 2)
    def _(at):
        owner = (1 - near) * 2 + lax.rem(tensor + 1 + at // per_owner, 2)
        block = owner * per_owner + lax.rem(at, per_owner)
        source, target = kv_rows(block), kv_rows(at)

        @pl.when(touched(block))
        def _():
            far_out[target, :] = (
                dot_nt(gk_out[source, :], pair_buf[0]) + dot_nt(gv_out[source, :], pair_buf[1])
            ).astype(jnp.bfloat16)

        @pl.when(jnp.logical_not(touched(block)))
        def _():
            far_out[target, :] = jnp.zeros((KV_BLOCK, width), jnp.bfloat16)

        far_copy(at).start()

    def add_adapter(row_vals, grads, down, up, first_at, second_at):
        lifted = (ADAPTER_SCALE * dot_nt(row_vals, down)).astype(jnp.bfloat16)
        grad_lifted = (ADAPTER_SCALE * dot_nt(grads, up)).astype(jnp.bfloat16)
        sums_ref[first_at : first_at + 8, :] += dot_tn(grad_lifted, row_vals)
        sums_ref[second_at : second_at + 8, :] += dot_tn(lifted, grads)

    sums_ref[...] = jnp.zeros_like(sums_ref)

    @pl.loop(0, kv_blocks)
    def _(block):
        window = kv_rows(block)

        @pl.when(touched(block))
        def _():
            rows_copy(block).wait()
            add_adapter(k_ref[window, :], gv_out[window, :], down_v_ref[...], ups_ref[8:16, :], 8, 24)

    own = pl.ds(pl.multiple_of(base, rows), rows)
    add_adapter(k_ref[own, :], first_buf[...], down_q_ref[...], ups_ref[0:8, :], 0, 16)
    sums_copy = pltpu.make_async_copy(sums_ref, sums_hbm, store_sem.at[3])
    sums_copy.start()
    sums_copy.wait()

    @pl.loop(0, kv_blocks // 2)
    def _(at):
        far_copy(at).wait()

    for copy in (mixed_copy, grad_one_copy, gq_copy):
        copy.wait()

    @pl.loop(0, kv_blocks)
    def _(block):
        for copy in grad_copies(block):
            copy.wait()


def middle(
    lengths, norms, q_own, k_all, v_all, tokens, cotangent, weights, full, rows_all, ups, downs
):
    rows, width = q_own.shape
    total_rows = k_all.shape[0]
    parts = full.shape[1]
    bf16, f32 = jnp.bfloat16, jnp.float32
    slots = rows // Q_BLOCK * (width // PAIR)
    kv_blocks = total_rows // KV_BLOCK
    dma = pltpu.SemaphoreType.DMA
    return pl.pallas_call(
        middle_kernel,
        out_shape=(
            jax.ShapeDtypeStruct((rows, width), bf16),
            jax.ShapeDtypeStruct((rows, width), f32),
            jax.ShapeDtypeStruct((rows, width), bf16),
            jax.ShapeDtypeStruct((total_rows, width), bf16),
            jax.ShapeDtypeStruct((total_rows, width), bf16),
            jax.ShapeDtypeStruct((total_rows // 2, width), bf16),
            jax.ShapeDtypeStruct((32, width), f32),
        ),
        in_specs=[SMEM_SPEC] + [VMEM_SPEC] * 4 + [HBM_SPEC] * 8 + [VMEM_SPEC] * 3,
        out_specs=(HBM_SPEC,) * 7,
        scratch_shapes=[
            pltpu.VMEM((rows, width), bf16),
            pltpu.VMEM((total_rows, width), bf16),
            pltpu.VMEM((total_rows, width), bf16),
            pltpu.VMEM((rows, width), bf16),
            pltpu.VMEM((rows, width), bf16),
            pltpu.VMEM((width, width), bf16),
            pltpu.VMEM(full.shape[1:], bf16),
            pltpu.VMEM(full.shape[1:], bf16),
            pltpu.VMEM((parts, rows, full.shape[3]), f32),
            pltpu.VMEM((rows, width), bf16),
            pltpu.VMEM((rows, width), f32),
            pltpu.VMEM((rows, width), f32),
            pltpu.VMEM((rows, 1), f32),
            pltpu.VMEM((rows, width), bf16),
            pltpu.VMEM((slots, 1, 2 * Q_BLOCK), f32),
            pltpu.VMEM((rows, width), bf16),
            pltpu.VMEM((total_rows, width), f32),
            pltpu.VMEM((total_rows, width), f32),
            pltpu.VMEM((total_rows, width), bf16),
            pltpu.VMEM((total_rows, width), bf16),
            pltpu.VMEM((total_rows // 2, width), bf16),
            pltpu.VMEM((2, width, width), bf16),
            pltpu.VMEM((32, width), f32),
            dma((5,)),
            dma((2, parts)),
            dma((2, kv_blocks)),
            dma((4,)),
            dma((2, kv_blocks)),
            dma((kv_blocks // 2,)),
        ],
        compiler_params=pltpu.CompilerParams(vmem_limit_bytes=VMEM_LIMIT),
        name="middle",
    )(
        lengths,
        *norms,
        q_own,
        k_all,
        v_all,
        tokens,
        cotangent,
        weights,
        full,
        rows_all,
        ups,
        *downs,
    )


def final_kernel(
    reach,
    gq_hbm,
    gk_hbm,
    gv_hbm,
    far_hbm,
    weights_hbm,
    grad_one_hbm,
    part_sums,
    grad_tokens_ref,
    sums_ref,
    gq_ref,
    gk_ref,
    gv_ref,
    far_ref,
    weights_ref,
    grad_one_ref,
    from_sib,
    to_x,
    from_x,
    home_to,
    home_from,
    sums_in,
    total,
    total_in,
    step_out,
    step_in,
    z_slots,
    load_sem,
    far_send,
    far_recv,
    block_send,
    block_recv,
    sum_send,
    sum_recv,
):
    place = Place()
    x, y, z, core = place.x, place.y, place.z, place.core
    token_rows = gq_ref.shape[0]
    half_rows = token_rows // 2
    chunk_rows = token_rows // FAR_CHUNKS
    bf16, f32 = jnp.bfloat16, jnp.float32
    loads = {}

    def load(name, source, target):
        copy = pltpu.make_async_copy(source, target, load_sem.at[len(loads)])
        copy.start()
        loads[name] = copy

    if reach:
        load("far", far_hbm.at[pl.ds(token_rows, token_rows)], far_ref)
    near_rows = pl.ds(pl.multiple_of(x * 2 * token_rows, token_rows), 2 * token_rows)
    load("k", gk_hbm.at[near_rows], gk_ref)
    load("v", gv_hbm.at[near_rows], gv_ref)
    load("w", weights_hbm.at[pl.ds(0, 3)], weights_ref)
    load("q", gq_hbm, gq_ref)
    load("one", grad_one_hbm, grad_one_ref)

    across = place.device(x=1 - x, core=1 - core)
    middle_device = x != core
    barrier = pltpu.get_barrier_semaphore()
    others = [place.sibling(), place.step("x", 1), place.step("y", 1)]
    others += [place.device(z=lax.rem(z + i, DEPTH)) for i in range(1, DEPTH)]
    for target in others:
        pl.semaphore_signal(barrier, inc=1, device_id=target, device_id_type=MESH_ID)
    greeted = len(others)
    if not reach:

        @pl.when(middle_device)
        def _():
            pl.semaphore_signal(barrier, inc=1, device_id=across, device_id_type=MESH_ID)

        greeted = greeted + middle_device.astype(jnp.int32)
    pl.semaphore_wait(barrier, greeted)

    def remote(source, target, send, recv, device):
        return pltpu.make_async_remote_copy(
            src_ref=source,
            dst_ref=target,
            send_sem=send,
            recv_sem=recv,
            device_id=device,
            device_id_type=MESH_ID,
        )

    def started(*operands):
        copy = remote(*operands)
        copy.start()
        return copy

    chunks = [pl.ds(at * chunk_rows, chunk_rows) for at in range(FAR_CHUNKS)]
    kept = pl.ds(pl.multiple_of(core * 16, 16), 16)
    given = pl.ds(pl.multiple_of((1 - core) * 16, 16), 16)
    sum_copies = [
        started(part_sums.at[given], sums_in, sum_send.at[0], sum_recv.at[0], place.sibling())
    ]
    sib_copies, x_copies = [], []
    if reach:
        for at, chunk in enumerate(chunks):
            sib_copies.append(
                started(
                    far_hbm.at[chunk],
                    from_sib.at[chunk],
                    far_send.at[0, at],
                    far_recv.at[0, at],
                    place.sibling(),
                )
            )
    else:
        for at, chunk in enumerate(chunks):
            x_copies.append(
                remote(
                    far_hbm.at[chunk],
                    from_x.at[chunk],
                    far_send.at[1, at],
                    far_recv.at[1, at],
                    across,
                )
            )

        @pl.when(middle_device)
        def _():
            for copy in x_copies:
                copy.start()

        @pl.when(jnp.logical_not(middle_device))
        def _():
            from_x[...] = jnp.zeros_like(from_x)

    sum_copies[0].wait_recv()
    step_out[0] = (part_sums[kept, :] + sums_in[...]).astype(bf16)
    sum_copies.append(
        started(step_out.at[0], step_in.at[0], sum_send.at[1], sum_recv.at[1], place.step("y", 1))
    )
    if reach:
        loads["far"].wait()
        for at, chunk in enumerate(chunks):
            sib_copies[at].wait_recv()
            to_x[chunk, :] = (far_ref[chunk, :].astype(f32) + from_sib[chunk, :].astype(f32)).astype(
                bf16
            )
            x_copies.append(
                started(
                    to_x.at[chunk],
                    from_x.at[chunk],
                    far_send.at[1, at],
                    far_recv.at[1, at],
                    place.step("x", 1),
                )
            )

    sum_copies[1].wait_recv()
    z_slots[z] = (step_out[0].astype(f32) + step_in[0].astype(f32)).astype(bf16)
    for i in range(1, DEPTH):
        sum_copies.append(
            started(
                z_slots.at[z],
                z_slots.at[z],
                sum_send.at[1 + i],
                sum_recv.at[1 + i],
                place.device(z=lax.rem(z + i, DEPTH)),
            )
        )

    def partial(owner, half):
        window = pl.ds(pl.multiple_of(owner * token_rows + half * half_rows, half_rows), half_rows)
        return dot_nt(gk_ref[window, :], weights_ref[1]) + dot_nt(gv_ref[window, :], weights_ref[2])

    for name in ("k", "v", "w"):
        loads[name].wait()
    home_copies = []
    for half in range(2):
        window = pl.ds(half * half_rows, half_rows)
        home_to[window, :] = partial(1 - core, half).astype(bf16)
        home_copies.append(
            started(
                home_to.at[window],
                home_from.at[window],
                block_send.at[half],
                block_recv.at[half],
                place.sibling(),
            )
        )

    for i in range(1, DEPTH):
        sum_copies[1 + i].wait_recv()
    column = z_slots[0].astype(f32)
    for i in range(1, DEPTH):
        column = column + z_slots[i].astype(f32)
    step_out[1] = column.astype(bf16)
    sum_copies.append(
        started(
            step_out.at[1],
            step_in.at[1],
            sum_send.at[DEPTH + 1],
            sum_recv.at[DEPTH + 1],
            place.step("x", 1),
        )
    )
    for name in ("q", "one"):
        loads[name].wait()
    for half in range(2):
        window = pl.ds(half * half_rows, half_rows)
        grad_one_ref[window, :] += partial(core, half) + dot_nt(gq_ref[window, :], weights_ref[0])
    sum_copies[-1].wait_recv()
    total[...] = step_out[1].astype(f32) + step_in[1].astype(f32)
    sum_copies.append(
        started(total, total_in, sum_send.at[DEPTH + 2], sum_recv.at[DEPTH + 2], place.sibling())
    )

    for copy in home_copies:
        copy.wait_recv()
    for at, chunk in enumerate(chunks):
        if reach:
            x_copies[at].wait_recv()
        else:
            pl.when(middle_device)(x_copies[at].wait_recv)
        grad_tokens_ref[chunk, :] = (
            grad_one_ref[chunk, :] + home_from[chunk, :].astype(f32) + from_x[chunk, :].astype(f32)
        ).astype(bf16)
    sum_copies[-1].wait_recv()
    sums_ref[kept, :] = total[...]
    sums_ref[given, :] = total_in[...]

    for copy in sib_copies + home_copies + sum_copies:
        copy.wait_send()
    for copy in x_copies:
        if reach:
            copy.wait_send()
        else:
            pl.when(middle_device)(copy.wait_send)


def final_sums(reach, grad_q, grad_k, grad_v, far_rows, weights, grad_one, sums):
    token_rows, width = grad_q.shape
    bf16, f32 = jnp.bfloat16, jnp.float32
    dma = pltpu.SemaphoreType.DMA
    block = pltpu.VMEM((token_rows, width), bf16)
    return pl.pallas_call(
        functools.partial(final_kernel, reach),
        out_shape=(
            jax.ShapeDtypeStruct((token_rows, width), bf16),
            jax.ShapeDtypeStruct((32, width), f32),
        ),
        in_specs=[HBM_SPEC] * 6 + [VMEM_SPEC],
        out_specs=(VMEM_SPEC,) * 2,
        scratch_shapes=[
            block,
            pltpu.VMEM((2 * token_rows, width), bf16),
            pltpu.VMEM((2 * token_rows, width), bf16),
            block,
            pltpu.VMEM((3, width, width), bf16),
            pltpu.VMEM((token_rows, width), f32),
            block,
            block,
            block,
            block,
            block,
            pltpu.VMEM((16, width), f32),
            pltpu.VMEM((16, width), f32),
            pltpu.VMEM((16, width), f32),
            pltpu.VMEM((2, 16, width), bf16),
            pltpu.VMEM((2, 16, width), bf16),
            pltpu.VMEM((DEPTH, 16, width), bf16),
            dma((6,)),
            dma((2, FAR_CHUNKS)),
            dma((2, FAR_CHUNKS)),
            dma((2,)),
            dma((2,)),
            dma((DEPTH + 3,)),
            dma((DEPTH + 3,)),
        ],
        compiler_params=pltpu.CompilerParams(
            collective_id=2 if reach else 3, has_side_effects=True, vmem_limit_bytes=VMEM_LIMIT
        ),
        name="final_sums_wide" if reach else "final_sums",
    )(grad_q, grad_k, grad_v, far_rows, weights, grad_one, sums)


def hand_out_kernel(grad_ref, sums_ref, grad_out, aq_ref, av_ref, bq_ref, bv_ref):
    grad_out[...] = grad_ref[...]
    slim = bq_ref.shape[1]
    aq_ref[...] = sums_ref[0:8, :]
    av_ref[...] = sums_ref[8:16, :]
    for t in range(sums_ref.shape[1] // slim):

        @pl.when(lax.axis_index("tensor") == t)
        def _(t=t):
            bq_ref[...] = sums_ref[16:24, t * slim : (t + 1) * slim]
            bv_ref[...] = sums_ref[24:32, t * slim : (t + 1) * slim]


def hand_out(grad_tokens, sums, slim):
    f32, width = jnp.float32, sums.shape[1]
    return pl.pallas_call(
        hand_out_kernel,
        out_shape=(
            jax.ShapeDtypeStruct(grad_tokens.shape, grad_tokens.dtype),
            jax.ShapeDtypeStruct((8, width), f32),
            jax.ShapeDtypeStruct((8, width), f32),
            jax.ShapeDtypeStruct((8, slim), f32),
            jax.ShapeDtypeStruct((8, slim), f32),
        ),
        in_specs=[VMEM_SPEC] * 2,
        out_specs=(VMEM_SPEC,) * 5,
        name="hand_out",
    )(grad_tokens, sums)


def local(
    fast,
    tokens,
    query_weight,
    w_key,
    value_weight,
    w_out,
    w_in,
    w_down,
    gain_attn,
    shift_attn,
    gain_ffn,
    shift_ffn,
    query_down_factor,
    query_up_factor,
    value_down_factor,
    value_up_factor,
    lengths,
    cotangent,
):
    slim = query_weight.shape[1]
    width = tokens.shape[1]
    token_rows = tokens.shape[0]
    down_q_t, down_v_t = query_down_factor.T, value_down_factor.T
    if fast:
        full, weights, rows_all, q_own, k_all, v_all, ups_full, fewest = gather_all(
            query_weight,
            w_key,
            value_weight,
            w_out,
            w_in,
            w_down.T,
            tokens,
            query_up_factor,
            value_up_factor,
            down_q_t,
            down_v_t,
            lengths,
        )
        full = full.reshape(2, 4, width, width)
    else:
        attn_pack = jnp.concatenate([query_weight, w_key, value_weight, w_out.T], axis=1)
        full = jnp.stack([attn_pack, w_in, w_down.T])
        full = lax.all_gather(full, "dp", axis=1, tiled=True)
        full = lax.all_gather(full, "tensor", axis=1)
        rows_all = lax.all_gather(tokens, "tensor").reshape(-1, width)
        ups = jnp.concatenate([query_up_factor, value_up_factor], axis=0)
        ups = jnp.pad(ups, ((0, 0), (0, -slim % 128)))
        ups_all = lax.all_gather(ups, "tensor")
        downs = jnp.concatenate([down_q_t, down_v_t], axis=0)
        ups_full = ups_all[:, :, :slim].transpose(1, 0, 2).reshape(16, width)
        order = tuple(range(full.shape[1]))
        weights, q_own, k_all, v_all = project(order, full, rows_all, ups_all, downs, token_rows)

    norms = (gain_attn, shift_attn, gain_ffn, shift_ffn)
    mixed, grad_one, grad_q, grad_k, grad_v, far_rows, sums = middle(
        lengths,
        norms,
        q_own,
        k_all,
        v_all,
        tokens,
        cotangent,
        weights,
        full,
        rows_all,
        ups_full,
        (down_q_t, down_v_t),
    )
    if fast:
        operands = (grad_q, grad_k, grad_v, far_rows, weights, grad_one, sums)
        grad_tokens, sums = lax.cond(
            fewest[0, 0] >= rows_all.shape[0] // 2,
            functools.partial(final_sums, False),
            functools.partial(final_sums, True),
            *operands,
        )
        grad_tokens, grad_aq, grad_av, grad_bq, grad_bv = hand_out(grad_tokens, sums, slim)
        return (mixed, grad_tokens, grad_aq.T, grad_bq, grad_av.T, grad_bv)

    grad_rows = dot_nt(grad_k, weights[1]) + dot_nt(grad_v, weights[2])
    shared = lax.psum_scatter(
        grad_rows.astype(jnp.bfloat16), "tensor", scatter_dimension=0, tiled=True
    )
    own_rows = dot_nt(grad_q, weights[0])
    grad_tokens = (grad_one + own_rows + shared.astype(jnp.float32)).astype(jnp.bfloat16)
    sums = lax.psum(sums, ("dp", "tensor"))
    at = lax.axis_index("tensor") * slim
    grad_bq = lax.dynamic_slice_in_dim(sums[16:24], at, slim, 1)
    grad_bv = lax.dynamic_slice_in_dim(sums[24:32], at, slim, 1)
    return (mixed, grad_tokens, sums[0:8].T, grad_bq, sums[8:16].T, grad_bv)


def solution(mesh):
    fast = dict(mesh.shape) == {"dp": 2 * DEPTH, "tensor": 4}
    return jax.shard_map(
        functools.partial(local, fast),
        mesh=mesh,
        in_specs=(
            P(("dp", "tensor"), None),
            P("dp", "tensor"),
            P("dp", "tensor"),
            P("dp", "tensor"),
            P("tensor", "dp"),
            P("dp", "tensor"),
            P("tensor", "dp"),
            P(),
            P(),
            P(),
            P(),
            P(),
            P(None, "tensor"),
            P(),
            P(None, "tensor"),
            P("dp", None),
            P(("dp", "tensor"), None),
        ),
        out_specs=(
            P(("dp", "tensor"), None),
            P(("dp", "tensor"), None),
            P(),
            P(None, "tensor"),
            P(),
            P(None, "tensor"),
        ),
        check_vma=False,
    )
```

```python
import functools
import heapq

import jax
import jax.numpy as jnp
from jax import lax
from jax.experimental import pallas as pl
from jax.experimental.pallas import tpu as pltpu
from jax.sharding import PartitionSpec as P

HEAD_DIM = 64
PAIR = 2 * HEAD_DIM
Q_BLOCK = 256
K_BLOCK = 512
KV_BLOCK = 256
NORM_BLOCK = 512
FAR_CHUNKS = 4
FORWARD_GROUP = 6
BACKWARD_GROUP = 3
ADAPTER_SCALE = 2.0
SCORE_SCALE = HEAD_DIM ** (-0.5)
LOG2_SCALE = SCORE_SCALE * 1.4426950408889634
NEG_FILL = -1e30
LN_EPS = 1e-05
VMEM_LIMIT = 60 * 1024 * 1024


def dot_nn(left, right):
    return jnp.dot(left, right, preferred_element_type=jnp.float32)


def dot_nt(left, right):
    return lax.dot_general(
        left, right, (((1,), (1,)), ((), ())), preferred_element_type=jnp.float32
    )


def dot_tn(left, right):
    return lax.dot_general(
        left, right, (((0,), (0,)), ((), ())), preferred_element_type=jnp.float32
    )


def norm_forward(row_vals, gain_vals, offset):
    middle = jnp.mean(row_vals, axis=-1, keepdims=True)
    centred = row_vals - middle
    inverse = lax.rsqrt(jnp.mean(centred * centred, axis=-1, keepdims=True) + LN_EPS)
    normed = centred * inverse
    return (normed * gain_vals + offset, normed, inverse)


def norm_backward(grad_out, normed, inverse, gain_vals):
    grad_n = grad_out * gain_vals
    return inverse * (
        grad_n
        - jnp.mean(grad_n, axis=-1, keepdims=True)
        - normed * jnp.mean(grad_n * normed, axis=-1, keepdims=True)
    )


def gelu_parts(hidden):
    cdf_part = 0.5 * (1.0 + lax.erf(hidden * 0.7071067811865476))
    density = jnp.exp(-0.5 * hidden * hidden) * 0.3989422804014327
    return (hidden * cdf_part, cdf_part + hidden * density)


def block_span(lengths_ref, first_row, rows, total_rows):
    last_row = first_row + rows - 1

    def slot_step(slot, carry):
        end, low, high = carry
        end = end + lengths_ref[0, slot]
        low = jnp.where(end <= first_row, jnp.maximum(low, end), low)
        high = jnp.where(end > last_row, jnp.minimum(high, end), high)
        return end, low, high

    start = (jnp.int32(0), jnp.int32(0), jnp.int32(total_rows))
    _, low, high = lax.fori_loop(0, lengths_ref.shape[1], slot_step, start, unroll=8)
    return low, high


def row_bounds(lengths_ref, first_row, rows, total_rows):
    place = first_row + lax.broadcasted_iota(jnp.int32, (1, rows), 1)

    def slot_step(slot, carry):
        end, begin, finish = carry
        end = end + lengths_ref[0, slot]
        done = place >= end
        begin = jnp.where(done, jnp.maximum(begin, end), begin)
        finish = jnp.where(done, finish, jnp.minimum(finish, end))
        return end, begin, finish

    start = (
        jnp.int32(0),
        jnp.zeros((1, rows), jnp.int32),
        jnp.full((1, rows), total_rows, jnp.int32),
    )
    _, begin, finish = lax.fori_loop(0, lengths_ref.shape[1], slot_step, start, unroll=8)
    return begin, finish


def stack_pair(block):
    lane = lax.broadcasted_iota(jnp.int32, block.shape, 1)
    zero = jnp.zeros_like(block)
    return jnp.concatenate(
        [jnp.where(lane < HEAD_DIM, block, zero), jnp.where(lane >= HEAD_DIM, block, zero)],
        axis=0,
    )


def unstack_pair(block, rows):
    joined = jnp.concatenate([block[:HEAD_DIM, :rows], block[HEAD_DIM:, rows:]], axis=0)
    return joined.T


def window_mask(step, low, begin, finish, total_rows):
    wanted = low + step * K_BLOCK
    start = pl.multiple_of(jnp.minimum(wanted, total_rows - K_BLOCK), 16)
    key_at = start + lax.broadcasted_iota(jnp.int32, (K_BLOCK, begin.shape[1]), 0)
    return start, (key_at >= jnp.maximum(begin, wanted)) & (key_at < finish)


def query_span(lengths_ref, first_row, total_rows):
    low, high = block_span(lengths_ref, first_row, Q_BLOCK, total_rows)
    low = (low // 16) * 16
    return low, (high - low + K_BLOCK - 1) // K_BLOCK


def each_q_block(lengths_ref, rows, total_rows, group, heads_width, block_step):
    base = lax.axis_index("tensor") * rows

    @pl.loop(0, rows // Q_BLOCK)
    def _(q_at):
        first_row = base + q_at * Q_BLOCK
        low, steps = query_span(lengths_ref, first_row, total_rows)
        begin, finish = row_bounds(lengths_ref, first_row, Q_BLOCK, total_rows)
        q_rows = pl.ds(pl.multiple_of(q_at * Q_BLOCK, Q_BLOCK), Q_BLOCK)

        @pl.loop(0, heads_width // PAIR // group)
        def _(at):
            pairs = [at * group + i for i in range(group)]
            lanes = [pl.ds(pl.multiple_of(pair * PAIR, PAIR), PAIR) for pair in pairs]
            slots = [q_at * (heads_width // PAIR) + pair for pair in pairs]
            block_step(q_rows, lanes, slots, low, steps, begin, finish)


def attend_forward(lengths_ref, q_ref, k_ref, v_ref, out_ref, lse_ref):
    total_rows = k_ref.shape[0]

    def block_step(q_rows, lanes, slots, low, steps, begin, finish):
        q_two = [stack_pair(q_ref[q_rows, lane]) for lane in lanes]

        def body(step, carry):
            start, allowed = window_mask(step, low, begin, finish, total_rows)
            window = pl.ds(start, K_BLOCK)
            both = jnp.concatenate([allowed, allowed], axis=1)
            result = []
            for (top, total, acc), q_pair, lane in zip(carry, q_two, lanes):
                scores = jnp.where(both, dot_nt(k_ref[window, lane], q_pair), NEG_FILL)
                new_top = jnp.maximum(top, jnp.max(scores, axis=0, keepdims=True))
                probs = jnp.exp2((scores - new_top) * LOG2_SCALE)
                shrink = jnp.exp2((top - new_top) * LOG2_SCALE)
                total = total * shrink + jnp.sum(probs, axis=0, keepdims=True)
                acc = acc * shrink + dot_tn(v_ref[window, lane], probs.astype(jnp.bfloat16))
                result.append((new_top, total, acc))
            return tuple(result)

        empty = (
            jnp.full((1, 2 * Q_BLOCK), NEG_FILL, jnp.float32),
            jnp.zeros((1, 2 * Q_BLOCK), jnp.float32),
            jnp.zeros((PAIR, 2 * Q_BLOCK), jnp.float32),
        )
        final = lax.fori_loop(0, steps, body, (empty,) * len(lanes))
        for (top, total, acc), lane, slot in zip(final, lanes, slots):
            out_ref[q_rows, lane] = unstack_pair(acc / total, Q_BLOCK).astype(jnp.bfloat16)
            lse_ref[slot] = top * LOG2_SCALE + jnp.log2(total)

    each_q_block(
        lengths_ref, q_ref.shape[0], total_rows, FORWARD_GROUP, q_ref.shape[1], block_step
    )


def attend_backward(
    lengths_ref, q_ref, k_ref, v_ref, ctx_ref, lse_ref, grad_ref, gq_ref, gk_acc, gv_acc
):
    total_rows = k_ref.shape[0]

    def block_step(q_rows, lanes, slots, low, steps, begin, finish):
        ready = []
        for lane, slot in zip(lanes, slots):
            grads = grad_ref[q_rows, lane]
            product = (grads.astype(jnp.float32) * ctx_ref[q_rows, lane].astype(jnp.float32)).T
            row_dot = jnp.concatenate(
                [
                    jnp.sum(product[:HEAD_DIM], axis=0, keepdims=True),
                    jnp.sum(product[HEAD_DIM:], axis=0, keepdims=True),
                ],
                axis=1,
            )
            ready.append((stack_pair(q_ref[q_rows, lane]), stack_pair(grads), row_dot, lse_ref[slot]))

        def body(step, carry):
            start, allowed = window_mask(step, low, begin, finish, total_rows)
            window = pl.ds(start, K_BLOCK)
            both = jnp.concatenate([allowed, allowed], axis=1)
            result = []
            for acc, (q_pair, grad_pair, row_dot, lse), lane in zip(carry, ready, lanes):
                keys = k_ref[window, lane]
                scores = jnp.where(both, dot_nt(keys, q_pair), NEG_FILL)
                probs = jnp.exp2(scores * LOG2_SCALE - lse)
                grad_probs = dot_nt(v_ref[window, lane], grad_pair)
                grad_scores = (probs * (grad_probs - row_dot)).astype(jnp.bfloat16)
                gk_acc[window, lane] += dot_nn(grad_scores, q_pair)
                gv_acc[window, lane] += dot_nn(probs.astype(jnp.bfloat16), grad_pair)
                result.append(acc + dot_tn(keys, grad_scores))
            return tuple(result)

        zero = jnp.zeros((PAIR, 2 * Q_BLOCK), jnp.float32)
        final = lax.fori_loop(0, steps, body, (zero,) * len(lanes))
        for acc, lane in zip(final, lanes):
            gq_ref[q_rows, lane] = (unstack_pair(acc, Q_BLOCK) * SCORE_SCALE).astype(jnp.bfloat16)

    each_q_block(
        lengths_ref, q_ref.shape[0], total_rows, BACKWARD_GROUP, q_ref.shape[1], block_step
    )


VMEM_SPEC = pl.BlockSpec(memory_space=pltpu.VMEM)
HBM_SPEC = pl.BlockSpec(memory_space=pltpu.HBM)
SMEM_SPEC = pl.BlockSpec(memory_space=pltpu.SMEM)


MESH_ID = pl.DeviceIdType.MESH
DEPTH = 4
FULL_ROWS = 96

FLOWS = (
    (0, 0, "zxy", 0.0),
    (0, 1, "zyx", 0.0),
    (1, 0, "xzy", 12.0),
    (1, 1, "zyx", 24.0),
    (2, 0, "xzy", 12.0),
    (2, 1, "yxz", 12.0),
)
OWN = (0, 0, 0)


def forwards(order, piece):
    used = [axis for axis in order if piece["xyz".index(axis)] != 0]
    at = order.index(used[-1]) if used else -1
    steps = []
    if used and used[-1] == "z":
        steps.append(("z", 1 if piece[2] < 0 else -1))
    for axis in order[at + 1 :]:
        steps += [("z", 1), ("z", -1)] if axis == "z" else [(axis, 1)]
    return steps


def passed(piece, axis, sign):
    x, y, z = piece
    if axis == "x":
        return (1 - x, y, z)
    return (x, 1 - y, z) if axis == "y" else (x, y, z - sign)


def event_order(token_time):
    per_piece = 1.7
    links, heap, times, count = {}, [], {}, 0
    for z in range(DEPTH):
        links[z, "x", 1] = token_time
        for flow, (_, _, _, start) in enumerate(FLOWS):
            heapq.heappush(heap, (start + 0.01 * flow, count, z, flow, OWN))
            count += 1
    while heap:
        now, _, z, flow, piece = heapq.heappop(heap)
        times.setdefault((flow, piece), []).append(now)
        for axis, sign in forwards(FLOWS[flow][2], piece):
            there = z + sign if axis == "z" else z
            if not 0 <= there < DEPTH:
                continue
            end = max(links.get((z, axis, sign), 0.0), now) + per_piece
            links[z, axis, sign] = end
            heapq.heappush(heap, (end + 3.0, count, there, flow, passed(piece, axis, sign)))
            count += 1
    return [key for _, key in sorted((sum(v) / len(v), key) for key, v in times.items())]


class Place:
    def __init__(self):
        dp, tensor = lax.axis_index("dp"), lax.axis_index("tensor")
        self.z, self.y = dp // 2, lax.rem(dp, 2)
        self.x, self.core = tensor // 2, lax.rem(tensor, 2)

    def device(self, x=None, y=None, z=None, core=None):
        x = self.x if x is None else x
        y = self.y if y is None else y
        z = self.z if z is None else z
        core = self.core if core is None else core
        return (z * 2 + y, x * 2 + core)

    def step(self, axis, sign):
        if axis == "x":
            return self.device(x=1 - self.x)
        return self.device(y=1 - self.y) if axis == "y" else self.device(z=self.z + sign)

    def sibling(self):
        return self.device(core=1 - self.core)


def gather_kernel(
    wq_ref,
    wk_ref,
    wv_ref,
    wo_ref,
    w_in_ref,
    w_down_ref,
    tokens_ref,
    up_q_ref,
    up_v_ref,
    down_q_ref,
    down_v_ref,
    lengths_ref,
    full_ref,
    weights_hbm,
    rows_hbm,
    q_hbm,
    k_hbm,
    v_hbm,
    ups_full,
    fewest_ref,
    pack_ref,
    packs_ref,
    rows_ref,
    ups_ref,
    ups_all_ref,
    weights_ref,
    q_ref,
    k_ref,
    v_ref,
    count_ref,
    counts_ref,
    count_send,
    count_recv,
    piece_recv,
    send_sem,
    sib_send,
    sib_recv,
    own_sem,
    rows_send,
    rows_recv,
    ups_send,
    ups_recv,
    out_sem,
):
    place = Place()
    x, y, z, core = place.x, place.y, place.z, place.core
    token_rows = tokens_ref.shape[0]
    part_rows = FULL_ROWS // 2
    half_rows = token_rows // 2

    barrier = pltpu.get_barrier_semaphore()
    others = (
        place.sibling(),
        place.step("x", 1),
        place.device(x=1 - x, core=1 - core),
        place.step("y", 1),
    )
    for target in others:
        pl.semaphore_signal(barrier, inc=1, device_id=target, device_id_type=MESH_ID)
    column = [place.device(z=lax.rem(z + i, DEPTH)) for i in range(1, DEPTH)]
    for target in column:
        pl.semaphore_signal(barrier, inc=1, device_id=target, device_id_type=MESH_ID)

    slim = wq_ref.shape[1]
    for kind, ref in enumerate((wq_ref, wk_ref, wv_ref)):
        pack_ref[:, kind * slim : (kind + 1) * slim] = ref[...]
    pack_ref[:, 3 * slim : 4 * slim] = wo_ref[...].astype(jnp.float32).T.astype(jnp.bfloat16)
    ups_ref[...] = jnp.zeros_like(ups_ref)
    ups_ref[0:8, :slim] = up_q_ref[...].astype(jnp.float32)
    ups_ref[8:16, :slim] = up_v_ref[...].astype(jnp.float32)
    count_ref[...] = jnp.broadcast_to(
        jnp.sum(lengths_ref[...].astype(jnp.float32), axis=1, keepdims=True), count_ref.shape
    )
    shards = (pack_ref, w_in_ref, w_down_ref)
    pl.semaphore_wait(barrier, len(others) + len(column))

    def remote(source, target, send, recv, device):
        return pltpu.make_async_remote_copy(
            src_ref=source,
            dst_ref=target,
            send_sem=send,
            recv_sem=recv,
            device_id=device,
            device_id_type=MESH_ID,
        )

    def rows_at(owner_x, owner_core, half):
        return rows_ref.at[owner_x * 2 + owner_core, pl.ds(half * half_rows, half_rows)]

    own_copies = [
        pltpu.make_async_copy(pack_ref, packs_ref.at[core, x, z, y], own_sem.at[0]),
        pltpu.make_async_copy(tokens_ref, rows_ref.at[x * 2 + core], own_sem.at[1]),
        pltpu.make_async_copy(ups_ref, ups_all_ref.at[x * 2 + core], own_sem.at[2]),
        pltpu.make_async_copy(w_in_ref, full_ref.at[0, core, x, z, y], own_sem.at[3]),
        pltpu.make_async_copy(w_down_ref, full_ref.at[1, core, x, z, y], own_sem.at[4]),
    ]
    row_copies = []
    for half in range(2):
        source = tokens_ref.at[pl.ds(half * half_rows, half_rows)]
        for slot, device in ((0, place.step("x", 1)), (1, place.sibling())):
            row_copies.append(
                remote(
                    source,
                    rows_at(x, core, half),
                    rows_send.at[slot, half],
                    rows_recv.at[slot, half],
                    device,
                )
            )
    up_copies = [
        remote(ups_ref, ups_all_ref.at[x * 2 + core], ups_send.at[i], ups_recv.at[i], device)
        for i, device in enumerate(others[:3])
    ]

    sends = {}

    def gathered(kind):
        return packs_ref if kind == 0 else full_ref.at[kind - 1]

    def half_of(kind, part):
        return pl.ds(part * part_rows, part_rows)

    def piece_at(flow, piece):
        kind, part, _, _ = FLOWS[flow]
        px, py = lax.rem(x + piece[0], 2), lax.rem(y + piece[1], 2)
        return (
            gathered(kind).at[core, px, z + piece[2], py, half_of(kind, part)],
            (px * 2 + py) * DEPTH + z + piece[2],
        )

    def handle(flow, piece):
        kind, part, order, _ = FLOWS[flow]
        landed, index = piece_at(flow, piece)
        source = landed
        if piece == OWN:
            source = shards[kind].at[half_of(kind, part)]
        else:
            remote(landed, landed, send_sem.at[flow, 0], piece_recv.at[flow, index], place.sibling()).wait_recv()
        for axis, sign in forwards(order, piece):
            slot = {"x": 0, "y": 1, "z": 2 if sign > 0 else 3}[axis]
            copy = remote(
                source,
                landed,
                send_sem.at[flow, slot],
                piece_recv.at[flow, index],
                place.step(axis, sign),
            )
            if axis == "z":
                pl.when((z + sign >= 0) & (z + sign < DEPTH))(copy.start)
            else:
                copy.start()
                sends[flow, slot] = sends.get((flow, slot), 0) + 1
        remote(source, landed, sib_send.at[flow], sib_recv.at[flow], place.sibling()).start()

    def block_of(flow, pieces, plane):
        kind, part, _, _ = FLOWS[flow]
        nx = 2 if pieces % 2 == 0 else 1
        ny = 2 if pieces % 4 == 0 else 1
        return gathered(kind).at[
            plane,
            pl.ds(0, nx),
            pl.ds(0, pieces // (nx * ny)),
            pl.ds(0, ny),
            half_of(kind, part),
        ]

    def finish_flow(flow):
        order = FLOWS[flow][2]
        everything = block_of(flow, 4 * DEPTH, 1 - core)
        remote(everything, everything, sib_send.at[flow], sib_recv.at[flow], place.sibling()).wait()

    def finish_sends(flow):
        order = FLOWS[flow][2]
        for axis, slot in (("x", 0), ("y", 1)):
            block = block_of(flow, 2 ** order.index(axis) * (DEPTH // 2 if "z" in order[: order.index(axis)] else 1), core)
            remote(block, block, send_sem.at[flow, slot], sib_recv.at[flow], place.sibling()).wait_send()
        each = 2 ** order.index("z")
        for at in range(DEPTH):
            for slot, sets in ((2, at + 1 if at < DEPTH - 1 else 0), (3, DEPTH - at if at > 0 else 0)):
                if sets:

                    @pl.when(z == at)
                    def _(slot=slot, sets=sets):
                        nx = 2 if each > 1 else 1
                        ny = 2 if each > 2 else 1
                        kind, part, _, _ = FLOWS[flow]
                        block = gathered(kind).at[
                            core,
                            pl.ds(0, nx),
                            pl.ds(0, sets),
                            pl.ds(0, ny),
                            half_of(kind, part),
                        ]
                        remote(
                            block, block, send_sem.at[flow, slot], sib_recv.at[flow], place.sibling()
                        ).wait_send()

    for copy in row_copies + up_copies + own_copies:
        copy.start()

    count_copies = [
        remote(
            count_ref, counts_ref.at[DEPTH], count_send.at[0], count_recv.at[0], place.step("y", 1)
        )
    ]
    count_copies[0].start()

    def pass_count():
        count_copies[0].wait_recv()
        counts_ref[z] = jnp.minimum(count_ref[...], counts_ref[DEPTH])
        for i, target in enumerate(column):
            copy = remote(
                counts_ref.at[z], counts_ref.at[z], count_send.at[1 + i], count_recv.at[1 + i], target
            )
            copy.start()
            count_copies.append(copy)

    def pass_rows(half):
        row_copies[2 * half].wait_recv()
        landed = rows_at(1 - x, core, half)
        copy = remote(landed, landed, rows_send.at[2, half], rows_recv.at[2, half], place.sibling())
        copy.start()
        return copy

    outs = []

    def write(source, target):
        copy = pltpu.make_async_copy(source, target, out_sem.at[len(outs)])
        copy.start()
        outs.append(copy)

    def assemble(t):
        if t == 0:
            for copy in up_copies + own_copies[:3]:
                copy.wait()
            for half in range(2):
                row_copies[2 * half + 1].wait_recv()
                passed_rows[half].wait_recv()
            for owner in range(4):
                write(rows_ref.at[owner], rows_hbm.at[pl.ds(owner * token_rows, token_rows)])
            finish_flow(0)
            finish_flow(1)
            for owner in range(4):
                ups_full[:, owner * slim : (owner + 1) * slim] = ups_all_ref[owner, :, :slim].astype(jnp.bfloat16)
        lanes = slice(t * slim, (t + 1) * slim)
        source = packs_ref.at[t % 2, t // 2]
        for kind, down_ref, first in ((0, down_q_ref, 0), (1, None, 0), (2, down_v_ref, 8), (3, None, 0)):
            part = source[:, :, :, kind * slim : (kind + 1) * slim].reshape(-1, slim)
            if down_ref is not None:
                up = ups_all_ref[t, first : first + 8, :slim].astype(jnp.bfloat16)
                product = dot_tn(down_ref[...], up)
                part = (part.astype(jnp.float32) + ADAPTER_SCALE * product).astype(jnp.bfloat16)
            weights_ref[kind, :, lanes] = part
        if t == 3:
            write(weights_ref, weights_hbm)

    def own_queries():
        q_ref[...] = dot_nn(rows_ref[x * 2 + core], weights_ref[0]).astype(jnp.bfloat16)
        write(q_ref, q_hbm)

    def keys_values(ref, hbm, kind, owner):
        ref[owner] = dot_nn(rows_ref[owner], weights_ref[kind]).astype(jnp.bfloat16)
        write(ref.at[owner], hbm.at[pl.ds(owner * token_rows, token_rows)])

    steps = [functools.partial(assemble, t) for t in range(4)] + [own_queries]
    for owner in range(4):
        steps.append(functools.partial(keys_values, k_ref, k_hbm, 1, owner))
        steps.append(functools.partial(keys_values, v_ref, v_hbm, 2, owner))

    passed_rows = []
    events = event_order(17.0)
    last_pack = max(i for i, (flow, _) in enumerate(events) if FLOWS[flow][0] == 0)
    between = max(1, (len(events) - last_pack) // (len(steps) + 1))
    arrivals = 0
    for at, (flow, piece) in enumerate(events):
        if piece[2] == 0:
            handle(flow, piece)
        else:
            pl.when((z + piece[2] >= 0) & (z + piece[2] < DEPTH))(
                functools.partial(handle, flow, piece)
            )
        if piece != OWN:
            arrivals += 1
            if arrivals in (8, 16):
                passed_rows.append(pass_rows(len(passed_rows)))
            if arrivals == 24:
                pass_count()
        if at >= last_pack and (at - last_pack) % between == between - 1 and steps:
            steps.pop(0)()
    for step in steps:
        step()

    for half in range(2):
        row_copies[2 * half].wait_send()
        row_copies[2 * half + 1].wait_send()
        passed_rows[half].wait_send()
    for copy in own_copies[3:] + outs:
        copy.wait()
    for flow in range(len(FLOWS)):
        if flow > 1:
            finish_flow(flow)
        finish_sends(flow)
    for copy in count_copies[1:]:
        copy.wait()
    count_copies[0].wait_send()
    fewest_ref[0, 0] = jnp.min(counts_ref[0:DEPTH])


def gather_all(
    w_q, w_k, w_v, w_out, w_in, w_down_t, tokens, up_q, up_v, down_q_t, down_v_t, lengths
):
    shard_rows, width = w_in.shape
    token_rows = tokens.shape[0]
    bf16, f32 = jnp.bfloat16, jnp.float32
    slim = w_q.shape[1]
    padded = slim + -slim % 128
    flows = len(FLOWS)
    dma = pltpu.SemaphoreType.DMA
    grid = (2, 2, DEPTH, 2, shard_rows, width)
    return pl.pallas_call(
        gather_kernel,
        out_shape=(
            jax.ShapeDtypeStruct((2,) + grid, bf16),
            jax.ShapeDtypeStruct((4, width, width), bf16),
            jax.ShapeDtypeStruct((4 * token_rows, width), bf16),
            jax.ShapeDtypeStruct((token_rows, width), bf16),
            jax.ShapeDtypeStruct((4 * token_rows, width), bf16),
            jax.ShapeDtypeStruct((4 * token_rows, width), bf16),
            jax.ShapeDtypeStruct((16, width), bf16),
            jax.ShapeDtypeStruct((1, 1), f32),
        ),
        in_specs=[VMEM_SPEC] * 4 + [HBM_SPEC] * 3 + [VMEM_SPEC] * 5,
        out_specs=(HBM_SPEC,) * 6 + (VMEM_SPEC, SMEM_SPEC),
        scratch_shapes=[
            pltpu.VMEM((shard_rows, width), bf16),
            pltpu.VMEM(grid, bf16),
            pltpu.VMEM((4, token_rows, width), bf16),
            pltpu.VMEM((16, padded), f32),
            pltpu.VMEM((4, 16, padded), f32),
            pltpu.VMEM((4, width, width), bf16),
            pltpu.VMEM((token_rows, width), bf16),
            pltpu.VMEM((4, token_rows, width), bf16),
            pltpu.VMEM((4, token_rows, width), bf16),
            pltpu.VMEM((8, 128), f32),
            pltpu.VMEM((DEPTH + 1, 8, 128), f32),
            dma((DEPTH,)),
            dma((DEPTH,)),
            dma((flows, 4 * DEPTH)),
            dma((flows, 4)),
            dma((flows,)),
            dma((flows,)),
            dma((5,)),
            dma((3, 2)),
            dma((3, 2)),
            dma((3,)),
            dma((3,)),
            dma((14,)),
        ],
        compiler_params=pltpu.CompilerParams(
            collective_id=1, has_side_effects=True, vmem_limit_bytes=VMEM_LIMIT
        ),
        name="gather_all",
    )(
        w_q,
        w_k,
        w_v,
        w_out,
        w_in,
        w_down_t,
        tokens,
        up_q,
        up_v,
        down_q_t,
        down_v_t,
        lengths,
    )


def project_kernel(
    order,
    full_hbm,
    rows_ref,
    ups_ref,
    downs_ref,
    weights_ref,
    q_ref,
    k_ref,
    v_ref,
    packs_ref,
    sems,
):
    token_rows = q_ref.shape[0]
    slim = packs_ref.shape[2] // 4
    tensor = lax.axis_index("tensor")
    copies = [
        pltpu.make_async_copy(full_hbm.at[0, i], packs_ref.at[i], sems.at[i])
        for i in range(len(order))
    ]
    for copy in copies:
        copy.start()
    for i, t in enumerate(order):
        copies[i].wait()
        lanes = slice(t * slim, (t + 1) * slim)
        for kind, first in ((0, 0), (1, None), (2, 8), (3, None)):
            part = packs_ref[i, :, kind * slim : (kind + 1) * slim]
            if first is not None:
                up = ups_ref[t, first : first + 8, :slim]
                product = dot_tn(downs_ref[first : first + 8, :], up)
                part = (part.astype(jnp.float32) + ADAPTER_SCALE * product).astype(jnp.bfloat16)
            weights_ref[kind, :, lanes] = part
    own = rows_ref[pl.ds(pl.multiple_of(tensor * token_rows, token_rows), token_rows), :]
    q_ref[...] = dot_nn(own, weights_ref[0]).astype(jnp.bfloat16)

    @pl.loop(0, rows_ref.shape[0] // token_rows)
    def _(at):
        window = pl.ds(pl.multiple_of(at * token_rows, token_rows), token_rows)
        block = rows_ref[window, :]
        k_ref[window, :] = dot_nn(block, weights_ref[1]).astype(jnp.bfloat16)
        v_ref[window, :] = dot_nn(block, weights_ref[2]).astype(jnp.bfloat16)


def project(order, full, rows_all, ups_all, downs, token_rows):
    total_rows, width = rows_all.shape
    bf16 = jnp.bfloat16
    return pl.pallas_call(
        functools.partial(project_kernel, order),
        out_shape=(
            jax.ShapeDtypeStruct((4, width, width), bf16),
            jax.ShapeDtypeStruct((token_rows, width), bf16),
            jax.ShapeDtypeStruct((total_rows, width), bf16),
            jax.ShapeDtypeStruct((total_rows, width), bf16),
        ),
        in_specs=[HBM_SPEC] + [VMEM_SPEC] * 3,
        out_specs=(VMEM_SPEC,) * 4,
        scratch_shapes=[
            pltpu.VMEM(full.shape[1:], bf16),
            pltpu.SemaphoreType.DMA((len(order),)),
        ],
        compiler_params=pltpu.CompilerParams(vmem_limit_bytes=VMEM_LIMIT),
        name="project",
    )(full, rows_all, ups_all, downs)


def middle_kernel(
    near_only,
    lengths_ref,
    gain_attn_ref,
    shift_attn_ref,
    gain_ffn_ref,
    shift_ffn_ref,
    q_hbm,
    k_hbm,
    v_hbm,
    tokens_hbm,
    cot_hbm,
    weights_hbm,
    full_hbm,
    rows_hbm,
    ups_ref,
    down_q_ref,
    down_v_ref,
    mixed_hbm,
    grad_one_hbm,
    gq_hbm,
    gk_hbm,
    gv_hbm,
    far_hbm,
    sums_hbm,
    q_ref,
    k_ref,
    v_ref,
    tokens_ref,
    cot_ref,
    out_buf,
    in_buf,
    down_buf,
    slope_buf,
    first_buf,
    sum_buf,
    normed_buf,
    inverse_buf,
    ctx_ref,
    lse_ref,
    grad_ref,
    gk_acc,
    gv_acc,
    gk_out,
    gv_out,
    far_out,
    pair_buf,
    sums_ref,
    sums_low,
    load_sem,
    part_sem,
    kv_sem,
    store_sem,
    grad_sem,
    far_sem,
):
    rows, width = q_ref.shape
    total_rows = k_ref.shape[0]
    parts, kinds = in_buf.shape[0], full_hbm.shape[0]
    kv_blocks = total_rows // KV_BLOCK
    base = lax.axis_index("tensor") * rows

    span_low, span_high = jnp.int32(total_rows), jnp.int32(0)
    for at in range(rows // Q_BLOCK):
        low, steps = query_span(lengths_ref, base + at * Q_BLOCK, total_rows)
        span_low = jnp.minimum(span_low, jnp.minimum(low, total_rows - K_BLOCK))
        span_high = jnp.maximum(span_high, jnp.minimum(low + steps * K_BLOCK, total_rows))

    def kv_rows(block):
        return pl.ds(pl.multiple_of(block * KV_BLOCK, KV_BLOCK), KV_BLOCK)

    def touched(block):
        return (block * KV_BLOCK < span_high) & ((block + 1) * KV_BLOCK > span_low)

    def kv_copies(block):
        window = kv_rows(block)
        return (
            pltpu.make_async_copy(k_hbm.at[window], k_ref.at[window], kv_sem.at[0, block]),
            pltpu.make_async_copy(v_hbm.at[window], v_ref.at[window], kv_sem.at[1, block]),
        )

    def part_copies(part):
        return (
            pltpu.make_async_copy(
                full_hbm.at[kinds - 2, part], in_buf.at[part], part_sem.at[0, part]
            ),
            pltpu.make_async_copy(
                full_hbm.at[kinds - 1, part], down_buf.at[part], part_sem.at[1, part]
            ),
        )

    q_copy = pltpu.make_async_copy(q_hbm, q_ref, load_sem.at[0])
    tokens_copy = pltpu.make_async_copy(tokens_hbm, tokens_ref, load_sem.at[1])
    out_copy = pltpu.make_async_copy(weights_hbm.at[3], out_buf, load_sem.at[2])
    cot_copy = pltpu.make_async_copy(cot_hbm, cot_ref, load_sem.at[3])
    pair_copy = pltpu.make_async_copy(weights_hbm.at[pl.ds(1, 2)], pair_buf, load_sem.at[4])
    q_copy.start()

    @pl.loop(0, kv_blocks)
    def _(block):
        @pl.when(touched(block))
        def _():
            for copy in kv_copies(block):
                copy.start()

    gk_acc[...] = jnp.zeros_like(gk_acc)
    gv_acc[...] = jnp.zeros_like(gv_acc)
    q_copy.wait()

    @pl.loop(0, kv_blocks)
    def _(block):
        @pl.when(touched(block))
        def _():
            for copy in kv_copies(block):
                copy.wait()

    tokens_copy.start()
    out_copy.start()
    cot_copy.start()
    for part in range(parts):
        for copy in part_copies(part):
            copy.start()
    pair_copy.start()

    attend_forward(lengths_ref, q_ref, k_ref, v_ref, ctx_ref, lse_ref)

    gain_attn, shift_attn, gain_ffn, shift_ffn = (
        ref[...].reshape(1, -1) for ref in (gain_attn_ref, shift_attn_ref, gain_ffn_ref, shift_ffn_ref)
    )
    tokens_copy.wait()
    out_copy.wait()
    sum_buf[...] = dot_nt(ctx_ref[...], out_buf[...])

    def each_norm_block(step):
        @pl.loop(0, rows // NORM_BLOCK)
        def _(at):
            step(pl.ds(pl.multiple_of(at * NORM_BLOCK, NORM_BLOCK), NORM_BLOCK))

    @each_norm_block
    def _(block):
        residual = tokens_ref[block, :].astype(jnp.float32) + sum_buf[block, :]
        first, normed, inverse = norm_forward(residual, gain_attn, shift_attn)
        first_buf[block, :] = first.astype(jnp.bfloat16)
        sum_buf[block, :] = first.astype(jnp.bfloat16).astype(jnp.float32)
        normed_buf[block, :] = normed
        inverse_buf[block, :] = inverse

    @pl.loop(0, parts)
    def _(part):
        for copy in part_copies(part):
            copy.wait()
        acted, slope = gelu_parts(dot_nn(first_buf[...], in_buf[part]))
        slope_buf[part] = slope
        sum_buf[...] += dot_nt(acted.astype(jnp.bfloat16), down_buf[part])

    cot_copy.wait()

    @each_norm_block
    def _(block):
        mixed, normed, inverse = norm_forward(sum_buf[block, :], gain_ffn, shift_ffn)
        tokens_ref[block, :] = mixed.astype(jnp.bfloat16)
        cotangents = cot_ref[block, :].astype(jnp.float32)
        grad_two = norm_backward(cotangents, normed, inverse, gain_ffn)
        first_buf[block, :] = grad_two.astype(jnp.bfloat16)
        sum_buf[block, :] = grad_two

    mixed_copy = pltpu.make_async_copy(tokens_ref, mixed_hbm, store_sem.at[0])
    mixed_copy.start()

    @pl.loop(0, parts)
    def _(part):
        grad_hidden = dot_nn(first_buf[...], down_buf[part]) * slope_buf[part]
        sum_buf[...] += dot_nt(grad_hidden.astype(jnp.bfloat16), in_buf[part])

    @each_norm_block
    def _(block):
        grad_one = norm_backward(
            sum_buf[block, :], normed_buf[block, :], inverse_buf[block, :], gain_attn
        )
        normed_buf[block, :] = grad_one
        first_buf[block, :] = grad_one.astype(jnp.bfloat16)

    grad_one_copy = pltpu.make_async_copy(normed_buf, grad_one_hbm, store_sem.at[1])
    grad_one_copy.start()
    grad_ref[...] = dot_nn(first_buf[...], out_buf[...]).astype(jnp.bfloat16)

    attend_backward(
        lengths_ref, q_ref, k_ref, v_ref, ctx_ref, lse_ref, grad_ref, first_buf, gk_acc, gv_acc
    )
    gq_copy = pltpu.make_async_copy(first_buf, gq_hbm, store_sem.at[2])
    gq_copy.start()

    def rows_copy(block):
        window = kv_rows(block)
        return pltpu.make_async_copy(rows_hbm.at[window], k_ref.at[window], kv_sem.at[0, block])

    @pl.loop(0, kv_blocks)
    def _(block):
        @pl.when(touched(block))
        def _():
            rows_copy(block).start()

    def wanted(block):
        if not near_only:
            return block >= 0
        return block // (kv_blocks // 2) == lax.axis_index("tensor") // 2

    def grad_copies(block):
        window = kv_rows(block)
        return (
            pltpu.make_async_copy(gk_out.at[window], gk_hbm.at[window], grad_sem.at[0, block]),
            pltpu.make_async_copy(gv_out.at[window], gv_hbm.at[window], grad_sem.at[1, block]),
        )

    @pl.loop(0, kv_blocks)
    def _(block):
        window = kv_rows(block)

        @pl.when(touched(block))
        def _():
            gk_out[window, :] = (gk_acc[window, :] * SCORE_SCALE).astype(jnp.bfloat16)
            gv_out[window, :] = gv_acc[window, :].astype(jnp.bfloat16)

        @pl.when(jnp.logical_not(touched(block)))
        def _():
            gk_out[window, :] = jnp.zeros((KV_BLOCK, width), jnp.bfloat16)
            gv_out[window, :] = jnp.zeros((KV_BLOCK, width), jnp.bfloat16)

        @pl.when(wanted(block))
        def _():
            for copy in grad_copies(block):
                copy.start()

    def far_copy(at):
        window = kv_rows(at)
        return pltpu.make_async_copy(far_out.at[window], far_hbm.at[window], far_sem.at[at])

    pair_copy.wait()
    tensor = lax.axis_index("tensor")
    near = tensor // 2
    per_owner = rows // KV_BLOCK

    @pl.loop(0, kv_blocks // 2)
    def _(at):
        owner = (1 - near) * 2 + lax.rem(tensor + 1 + at // per_owner, 2)
        block = owner * per_owner + lax.rem(at, per_owner)
        source, target = kv_rows(block), kv_rows(at)

        @pl.when(touched(block))
        def _():
            far_out[target, :] = (
                dot_nt(gk_out[source, :], pair_buf[0]) + dot_nt(gv_out[source, :], pair_buf[1])
            ).astype(jnp.bfloat16)

        @pl.when(jnp.logical_not(touched(block)))
        def _():
            far_out[target, :] = jnp.zeros((KV_BLOCK, width), jnp.bfloat16)

        far_copy(at).start()

    def add_adapter(row_vals, grads, down, up, first_at, second_at):
        lifted = (ADAPTER_SCALE * dot_nt(row_vals, down)).astype(jnp.bfloat16)
        grad_lifted = (ADAPTER_SCALE * dot_nt(grads, up)).astype(jnp.bfloat16)
        sums_ref[first_at : first_at + 8, :] += dot_tn(grad_lifted, row_vals)
        sums_ref[second_at : second_at + 8, :] += dot_tn(lifted, grads)

    sums_ref[...] = jnp.zeros_like(sums_ref)

    @pl.loop(0, kv_blocks)
    def _(block):
        window = kv_rows(block)

        @pl.when(touched(block))
        def _():
            rows_copy(block).wait()
            add_adapter(k_ref[window, :], gv_out[window, :], down_v_ref[...], ups_ref[8:16, :], 8, 24)

    own = pl.ds(pl.multiple_of(base, rows), rows)
    add_adapter(k_ref[own, :], first_buf[...], down_q_ref[...], ups_ref[0:8, :], 0, 16)
    sums_low[...] = sums_ref[...].astype(jnp.bfloat16)
    sums_copy = pltpu.make_async_copy(sums_low, sums_hbm, store_sem.at[3])
    sums_copy.start()
    sums_copy.wait()

    @pl.loop(0, kv_blocks // 2)
    def _(at):
        far_copy(at).wait()

    for copy in (mixed_copy, grad_one_copy, gq_copy):
        copy.wait()

    @pl.loop(0, kv_blocks)
    def _(block):
        @pl.when(wanted(block))
        def _():
            for copy in grad_copies(block):
                copy.wait()


def middle(
    near_only, lengths, norms, q_own, k_all, v_all, tokens, cotangent, weights, full, rows_all, ups, downs
):
    rows, width = q_own.shape
    total_rows = k_all.shape[0]
    parts = full.shape[1]
    bf16, f32 = jnp.bfloat16, jnp.float32
    slots = rows // Q_BLOCK * (width // PAIR)
    kv_blocks = total_rows // KV_BLOCK
    dma = pltpu.SemaphoreType.DMA
    return pl.pallas_call(
        functools.partial(middle_kernel, near_only),
        out_shape=(
            jax.ShapeDtypeStruct((rows, width), bf16),
            jax.ShapeDtypeStruct((rows, width), f32),
            jax.ShapeDtypeStruct((rows, width), bf16),
            jax.ShapeDtypeStruct((total_rows, width), bf16),
            jax.ShapeDtypeStruct((total_rows, width), bf16),
            jax.ShapeDtypeStruct((total_rows // 2, width), bf16),
            jax.ShapeDtypeStruct((32, width), bf16),
        ),
        in_specs=[SMEM_SPEC] + [VMEM_SPEC] * 4 + [HBM_SPEC] * 8 + [VMEM_SPEC] * 3,
        out_specs=(HBM_SPEC,) * 7,
        scratch_shapes=[
            pltpu.VMEM((rows, width), bf16),
            pltpu.VMEM((total_rows, width), bf16),
            pltpu.VMEM((total_rows, width), bf16),
            pltpu.VMEM((rows, width), bf16),
            pltpu.VMEM((rows, width), bf16),
            pltpu.VMEM((width, width), bf16),
            pltpu.VMEM(full.shape[1:], bf16),
            pltpu.VMEM(full.shape[1:], bf16),
            pltpu.VMEM((parts, rows, full.shape[3]), f32),
            pltpu.VMEM((rows, width), bf16),
            pltpu.VMEM((rows, width), f32),
            pltpu.VMEM((rows, width), f32),
            pltpu.VMEM((rows, 1), f32),
            pltpu.VMEM((rows, width), bf16),
            pltpu.VMEM((slots, 1, 2 * Q_BLOCK), f32),
            pltpu.VMEM((rows, width), bf16),
            pltpu.VMEM((total_rows, width), f32),
            pltpu.VMEM((total_rows, width), f32),
            pltpu.VMEM((total_rows, width), bf16),
            pltpu.VMEM((total_rows, width), bf16),
            pltpu.VMEM((total_rows // 2, width), bf16),
            pltpu.VMEM((2, width, width), bf16),
            pltpu.VMEM((32, width), f32),
            pltpu.VMEM((32, width), bf16),
            dma((5,)),
            dma((2, parts)),
            dma((2, kv_blocks)),
            dma((4,)),
            dma((2, kv_blocks)),
            dma((kv_blocks // 2,)),
        ],
        compiler_params=pltpu.CompilerParams(vmem_limit_bytes=VMEM_LIMIT),
        name="middle",
    )(
        lengths,
        *norms,
        q_own,
        k_all,
        v_all,
        tokens,
        cotangent,
        weights,
        full,
        rows_all,
        ups,
        *downs,
    )


def final_kernel(
    reach,
    gq_hbm,
    gk_hbm,
    gv_hbm,
    far_hbm,
    weights_hbm,
    grad_one_hbm,
    part_sums,
    grad_tokens_ref,
    sums_ref,
    gq_ref,
    gk_ref,
    gv_ref,
    far_ref,
    weights_ref,
    grad_one_ref,
    from_sib,
    to_x,
    from_x,
    home_to,
    home_from,
    yc_slots,
    z_slots,
    xc_slots,
    load_sem,
    far_send,
    far_recv,
    block_send,
    block_recv,
    sum_send,
    sum_recv,
):
    place = Place()
    x, y, z, core = place.x, place.y, place.z, place.core
    token_rows = gq_ref.shape[0]
    half_rows = token_rows // 2
    chunk_rows = token_rows // FAR_CHUNKS
    bf16, f32 = jnp.bfloat16, jnp.float32
    loads = {}

    def load(name, source, target):
        copy = pltpu.make_async_copy(source, target, load_sem.at[len(loads)])
        copy.start()
        loads[name] = copy

    if reach:
        load("far", far_hbm.at[pl.ds(token_rows, token_rows)], far_ref)
    near_rows = pl.ds(pl.multiple_of(x * 2 * token_rows, token_rows), 2 * token_rows)
    load("k", gk_hbm.at[near_rows], gk_ref)
    load("v", gv_hbm.at[near_rows], gv_ref)
    load("w", weights_hbm.at[pl.ds(0, 3)], weights_ref)
    load("q", gq_hbm, gq_ref)
    load("one", grad_one_hbm, grad_one_ref)

    across = place.device(x=1 - x, core=1 - core)
    middle_device = x != core
    barrier = pltpu.get_barrier_semaphore()
    around = [place.step("y", 1), place.sibling(), place.device(y=1 - y, core=1 - core)]
    column = [place.device(z=lax.rem(z + i, DEPTH)) for i in range(1, DEPTH)]
    beside = [place.step("x", 1), across]
    for target in around + column + beside:
        pl.semaphore_signal(barrier, inc=1, device_id=target, device_id_type=MESH_ID)
    pl.semaphore_wait(barrier, len(around + column + beside))

    def remote(source, target, send, recv, device):
        return pltpu.make_async_remote_copy(
            src_ref=source,
            dst_ref=target,
            send_sem=send,
            recv_sem=recv,
            device_id=device,
            device_id_type=MESH_ID,
        )

    def started(*operands):
        copy = remote(*operands)
        copy.start()
        return copy

    chunks = [pl.ds(at * chunk_rows, chunk_rows) for at in range(FAR_CHUNKS)]
    kept = pl.ds(pl.multiple_of(core * 16, 16), 16)
    given = pl.ds(pl.multiple_of((1 - core) * 16, 16), 16)
    sum_copies = []

    def send_sum(source, target, device):
        at = len(sum_copies)
        sum_copies.append(started(source, target, sum_send.at[at], sum_recv.at[at], device))

    for source, device in zip((kept, given, given), around):
        send_sum(part_sums.at[source], yc_slots.at[y * 2 + core], device)
    yc_slots[y * 2 + core] = part_sums[kept, :]
    sib_copies, x_copies = [], []
    if reach:
        for at, chunk in enumerate(chunks):
            sib_copies.append(
                started(
                    far_hbm.at[chunk],
                    from_sib.at[chunk],
                    far_send.at[0, at],
                    far_recv.at[0, at],
                    place.sibling(),
                )
            )
    else:
        for at, chunk in enumerate(chunks):
            x_copies.append(
                remote(
                    far_hbm.at[chunk],
                    from_x.at[chunk],
                    far_send.at[1, at],
                    far_recv.at[1, at],
                    across,
                )
            )

        @pl.when(middle_device)
        def _():
            for copy in x_copies:
                copy.start()

        @pl.when(jnp.logical_not(middle_device))
        def _():
            from_x[...] = jnp.zeros_like(from_x)

    def slot_sum(slots, indices):
        result = slots[indices[0]].astype(f32)
        for i in indices[1:]:
            result = result + slots[i].astype(f32)
        return result

    if reach:
        loads["far"].wait()
        for at, chunk in enumerate(chunks):
            sib_copies[at].wait_recv()
            to_x[chunk, :] = (far_ref[chunk, :].astype(f32) + from_sib[chunk, :].astype(f32)).astype(
                bf16
            )
            x_copies.append(
                started(
                    to_x.at[chunk],
                    from_x.at[chunk],
                    far_send.at[1, at],
                    far_recv.at[1, at],
                    place.step("x", 1),
                )
            )

    for copy in sum_copies[0:3]:
        copy.wait_recv()
    z_slots[z] = slot_sum(yc_slots, range(4)).astype(bf16)
    for device in column:
        send_sum(z_slots.at[z], z_slots.at[z], device)

    def partial(owner, half):
        window = pl.ds(pl.multiple_of(owner * token_rows + half * half_rows, half_rows), half_rows)
        return dot_nt(gk_ref[window, :], weights_ref[1]) + dot_nt(gv_ref[window, :], weights_ref[2])

    for name in ("k", "v", "w"):
        loads[name].wait()
    home_copies = []
    for half in range(2):
        window = pl.ds(half * half_rows, half_rows)
        home_to[window, :] = partial(1 - core, half).astype(bf16)
        home_copies.append(
            started(
                home_to.at[window],
                home_from.at[window],
                block_send.at[half],
                block_recv.at[half],
                place.sibling(),
            )
        )

    for copy in sum_copies[3:]:
        copy.wait_recv()
    xc_slots[x * 2 + core] = slot_sum(z_slots, range(DEPTH)).astype(bf16)
    own_slot = xc_slots.at[x * 2 + core]
    for device in [place.sibling()] + beside:
        send_sum(own_slot, own_slot, device)
    for name in ("q", "one"):
        loads[name].wait()
    for half in range(2):
        window = pl.ds(half * half_rows, half_rows)
        grad_one_ref[window, :] += partial(core, half) + dot_nt(gq_ref[window, :], weights_ref[0])
    for copy in home_copies:
        copy.wait_recv()
    for at, chunk in enumerate(chunks):
        if reach:
            x_copies[at].wait_recv()
        else:
            pl.when(middle_device)(x_copies[at].wait_recv)
        grad_tokens_ref[chunk, :] = (
            grad_one_ref[chunk, :] + home_from[chunk, :].astype(f32) + from_x[chunk, :].astype(f32)
        ).astype(bf16)
    for copy in sum_copies[2 + DEPTH :]:
        copy.wait_recv()
    for half in range(2):
        sums_ref[half * 16 : half * 16 + 16, :] = slot_sum(xc_slots, (half, 2 + half))

    for copy in sib_copies + home_copies + sum_copies:
        copy.wait_send()
    for copy in x_copies:
        if reach:
            copy.wait_send()
        else:
            pl.when(middle_device)(copy.wait_send)


def final_sums(reach, grad_q, grad_k, grad_v, far_rows, weights, grad_one, sums):
    token_rows, width = grad_q.shape
    bf16, f32 = jnp.bfloat16, jnp.float32
    dma = pltpu.SemaphoreType.DMA
    block = pltpu.VMEM((token_rows, width), bf16)
    return pl.pallas_call(
        functools.partial(final_kernel, reach),
        out_shape=(
            jax.ShapeDtypeStruct((token_rows, width), bf16),
            jax.ShapeDtypeStruct((32, width), f32),
        ),
        in_specs=[HBM_SPEC] * 6 + [VMEM_SPEC],
        out_specs=(VMEM_SPEC,) * 2,
        scratch_shapes=[
            block,
            pltpu.VMEM((2 * token_rows, width), bf16),
            pltpu.VMEM((2 * token_rows, width), bf16),
            block,
            pltpu.VMEM((3, width, width), bf16),
            pltpu.VMEM((token_rows, width), f32),
            block,
            block,
            block,
            block,
            block,
            pltpu.VMEM((4, 16, width), bf16),
            pltpu.VMEM((DEPTH, 16, width), bf16),
            pltpu.VMEM((4, 16, width), bf16),
            dma((6,)),
            dma((2, FAR_CHUNKS)),
            dma((2, FAR_CHUNKS)),
            dma((2,)),
            dma((2,)),
            dma((DEPTH + 5,)),
            dma((DEPTH + 5,)),
        ],
        compiler_params=pltpu.CompilerParams(
            collective_id=2 if reach else 3, has_side_effects=True, vmem_limit_bytes=VMEM_LIMIT
        ),
        name="final_sums_wide" if reach else "final_sums",
    )(grad_q, grad_k, grad_v, far_rows, weights, grad_one, sums)


def hand_out_kernel(grad_ref, sums_ref, grad_out, aq_ref, av_ref, bq_ref, bv_ref):
    grad_out[...] = grad_ref[...]
    slim = bq_ref.shape[1]
    aq_ref[...] = sums_ref[0:8, :]
    av_ref[...] = sums_ref[8:16, :]
    for t in range(sums_ref.shape[1] // slim):

        @pl.when(lax.axis_index("tensor") == t)
        def _(t=t):
            bq_ref[...] = sums_ref[16:24, t * slim : (t + 1) * slim]
            bv_ref[...] = sums_ref[24:32, t * slim : (t + 1) * slim]


def hand_out(grad_tokens, sums, slim):
    f32, width = jnp.float32, sums.shape[1]
    return pl.pallas_call(
        hand_out_kernel,
        out_shape=(
            jax.ShapeDtypeStruct(grad_tokens.shape, grad_tokens.dtype),
            jax.ShapeDtypeStruct((8, width), f32),
            jax.ShapeDtypeStruct((8, width), f32),
            jax.ShapeDtypeStruct((8, slim), f32),
            jax.ShapeDtypeStruct((8, slim), f32),
        ),
        in_specs=[VMEM_SPEC] * 2,
        out_specs=(VMEM_SPEC,) * 5,
        name="hand_out",
    )(grad_tokens, sums)


def local(
    fast,
    tokens,
    query_weight,
    w_key,
    value_weight,
    w_out,
    w_in,
    w_down,
    gain_attn,
    shift_attn,
    gain_ffn,
    shift_ffn,
    query_down_factor,
    query_up_factor,
    value_down_factor,
    value_up_factor,
    lengths,
    cotangent,
):
    slim = query_weight.shape[1]
    width = tokens.shape[1]
    token_rows = tokens.shape[0]
    down_q_t, down_v_t = query_down_factor.T, value_down_factor.T
    if fast:
        full, weights, rows_all, q_own, k_all, v_all, ups_full, fewest = gather_all(
            query_weight,
            w_key,
            value_weight,
            w_out,
            w_in,
            w_down.T,
            tokens,
            query_up_factor,
            value_up_factor,
            down_q_t,
            down_v_t,
            lengths,
        )
        full = full.reshape(2, 4, width, width)
    else:
        attn_pack = jnp.concatenate([query_weight, w_key, value_weight, w_out.T], axis=1)
        full = jnp.stack([attn_pack, w_in, w_down.T])
        full = lax.all_gather(full, "dp", axis=1, tiled=True)
        full = lax.all_gather(full, "tensor", axis=1)
        rows_all = lax.all_gather(tokens, "tensor").reshape(-1, width)
        ups = jnp.concatenate([query_up_factor, value_up_factor], axis=0)
        ups = jnp.pad(ups, ((0, 0), (0, -slim % 128)))
        ups_all = lax.all_gather(ups, "tensor")
        downs = jnp.concatenate([down_q_t, down_v_t], axis=0)
        ups_full = ups_all[:, :, :slim].transpose(1, 0, 2).reshape(16, width)
        order = tuple(range(full.shape[1]))
        weights, q_own, k_all, v_all = project(order, full, rows_all, ups_all, downs, token_rows)

    norms = (gain_attn, shift_attn, gain_ffn, shift_ffn)
    mixed, grad_one, grad_q, grad_k, grad_v, far_rows, sums = middle(
        fast,
        lengths,
        norms,
        q_own,
        k_all,
        v_all,
        tokens,
        cotangent,
        weights,
        full,
        rows_all,
        ups_full,
        (down_q_t, down_v_t),
    )
    if fast:
        operands = (grad_q, grad_k, grad_v, far_rows, weights, grad_one, sums)
        grad_tokens, sums = lax.cond(
            fewest[0, 0] >= rows_all.shape[0] // 2,
            functools.partial(final_sums, False),
            functools.partial(final_sums, True),
            *operands,
        )
        grad_tokens, grad_aq, grad_av, grad_bq, grad_bv = hand_out(grad_tokens, sums, slim)
        return (mixed, grad_tokens, grad_aq.T, grad_bq, grad_av.T, grad_bv)

    grad_rows = dot_nt(grad_k, weights[1]) + dot_nt(grad_v, weights[2])
    shared = lax.psum_scatter(
        grad_rows.astype(jnp.bfloat16), "tensor", scatter_dimension=0, tiled=True
    )
    own_rows = dot_nt(grad_q, weights[0])
    grad_tokens = (grad_one + own_rows + shared.astype(jnp.float32)).astype(jnp.bfloat16)
    sums = lax.psum(sums.astype(jnp.float32), ("dp", "tensor"))
    at = lax.axis_index("tensor") * slim
    grad_bq = lax.dynamic_slice_in_dim(sums[16:24], at, slim, 1)
    grad_bv = lax.dynamic_slice_in_dim(sums[24:32], at, slim, 1)
    return (mixed, grad_tokens, sums[0:8].T, grad_bq, sums[8:16].T, grad_bv)


def solution(mesh):
    fast = dict(mesh.shape) == {"dp": 2 * DEPTH, "tensor": 4}
    return jax.shard_map(
        functools.partial(local, fast),
        mesh=mesh,
        in_specs=(
            P(("dp", "tensor"), None),
            P("dp", "tensor"),
            P("dp", "tensor"),
            P("dp", "tensor"),
            P("tensor", "dp"),
            P("dp", "tensor"),
            P("tensor", "dp"),
            P(),
            P(),
            P(),
            P(),
            P(),
            P(None, "tensor"),
            P(),
            P(None, "tensor"),
            P("dp", None),
            P(("dp", "tensor"), None),
        ),
        out_specs=(
            P(("dp", "tensor"), None),
            P(("dp", "tensor"), None),
            P(),
            P(None, "tensor"),
            P(),
            P(None, "tensor"),
        ),
        check_vma=False,
    )
```

```python
import functools
import heapq

import jax
import jax.numpy as jnp
from jax import lax
from jax.experimental import pallas as pl
from jax.experimental.pallas import tpu as pltpu
from jax.sharding import PartitionSpec as P

HEAD_DIM = 64
PAIR = 2 * HEAD_DIM
Q_BLOCK = 256
K_BLOCK = 512
KV_BLOCK = 256
NORM_BLOCK = 512
FAR_CHUNKS = 4
FORWARD_GROUP = 6
BACKWARD_GROUP = 3
ADAPTER_SCALE = 2.0
SCORE_SCALE = HEAD_DIM ** (-0.5)
LOG2_SCALE = SCORE_SCALE * 1.4426950408889634
NEG_FILL = -1e30
LN_EPS = 1e-05
VMEM_LIMIT = 60 * 1024 * 1024


def dot_nn(left, right):
    return jnp.dot(left, right, preferred_element_type=jnp.float32)


def dot_nt(left, right):
    return lax.dot_general(
        left, right, (((1,), (1,)), ((), ())), preferred_element_type=jnp.float32
    )


def dot_tn(left, right):
    return lax.dot_general(
        left, right, (((0,), (0,)), ((), ())), preferred_element_type=jnp.float32
    )


def norm_forward(row_vals, gain_vals, offset):
    middle = jnp.mean(row_vals, axis=-1, keepdims=True)
    centred = row_vals - middle
    inverse = lax.rsqrt(jnp.mean(centred * centred, axis=-1, keepdims=True) + LN_EPS)
    normed = centred * inverse
    return (normed * gain_vals + offset, normed, inverse)


def norm_backward(grad_out, normed, inverse, gain_vals):
    grad_n = grad_out * gain_vals
    return inverse * (
        grad_n
        - jnp.mean(grad_n, axis=-1, keepdims=True)
        - normed * jnp.mean(grad_n * normed, axis=-1, keepdims=True)
    )


def gelu_parts(hidden):
    cdf_part = 0.5 * (1.0 + lax.erf(hidden * 0.7071067811865476))
    density = jnp.exp(-0.5 * hidden * hidden) * 0.3989422804014327
    return (hidden * cdf_part, cdf_part + hidden * density)


def block_span(lengths_ref, first_row, rows, total_rows):
    last_row = first_row + rows - 1

    def slot_step(slot, carry):
        end, low, high = carry
        end = end + lengths_ref[0, slot]
        low = jnp.where(end <= first_row, jnp.maximum(low, end), low)
        high = jnp.where(end > last_row, jnp.minimum(high, end), high)
        return end, low, high

    start = (jnp.int32(0), jnp.int32(0), jnp.int32(total_rows))
    _, low, high = lax.fori_loop(0, lengths_ref.shape[1], slot_step, start, unroll=8)
    return low, high


def row_bounds(lengths_ref, first_row, rows, total_rows):
    place = first_row + lax.broadcasted_iota(jnp.int32, (1, rows), 1)

    def slot_step(slot, carry):
        end, begin, finish = carry
        end = end + lengths_ref[0, slot]
        done = place >= end
        begin = jnp.where(done, jnp.maximum(begin, end), begin)
        finish = jnp.where(done, finish, jnp.minimum(finish, end))
        return end, begin, finish

    start = (
        jnp.int32(0),
        jnp.zeros((1, rows), jnp.int32),
        jnp.full((1, rows), total_rows, jnp.int32),
    )
    _, begin, finish = lax.fori_loop(0, lengths_ref.shape[1], slot_step, start, unroll=8)
    return begin, finish


def stack_pair(block):
    lane = lax.broadcasted_iota(jnp.int32, block.shape, 1)
    zero = jnp.zeros_like(block)
    return jnp.concatenate(
        [jnp.where(lane < HEAD_DIM, block, zero), jnp.where(lane >= HEAD_DIM, block, zero)],
        axis=0,
    )


def unstack_pair(block, rows):
    joined = jnp.concatenate([block[:HEAD_DIM, :rows], block[HEAD_DIM:, rows:]], axis=0)
    return joined.T


def window_mask(step, low, begin, finish, limit):
    wanted = low + step * K_BLOCK
    start = pl.multiple_of(jnp.minimum(wanted, limit - K_BLOCK), 16)
    key_at = start + lax.broadcasted_iota(jnp.int32, (K_BLOCK, begin.shape[1]), 0)
    return start, (key_at >= jnp.maximum(begin, wanted)) & (key_at < finish)


def query_span(lengths_ref, first_row, total_rows):
    low, high = block_span(lengths_ref, first_row, Q_BLOCK, total_rows)
    low = (low // 16) * 16
    return low, (high - low + K_BLOCK - 1) // K_BLOCK


def each_q_block(lengths_ref, rows, total_rows, group, heads_width, block_step):
    base = lax.axis_index("tensor") * rows

    @pl.loop(0, rows // Q_BLOCK)
    def _(q_at):
        first_row = base + q_at * Q_BLOCK
        low, steps = query_span(lengths_ref, first_row, total_rows)
        begin, finish = row_bounds(lengths_ref, first_row, Q_BLOCK, total_rows)
        q_rows = pl.ds(pl.multiple_of(q_at * Q_BLOCK, Q_BLOCK), Q_BLOCK)

        @pl.loop(0, heads_width // PAIR // group)
        def _(at):
            pairs = [at * group + i for i in range(group)]
            lanes = [pl.ds(pl.multiple_of(pair * PAIR, PAIR), PAIR) for pair in pairs]
            slots = [q_at * (heads_width // PAIR) + pair for pair in pairs]
            block_step(q_rows, lanes, slots, low, steps, begin, finish)


def attend_forward(limit, lengths_ref, q_ref, k_ref, v_ref, out_ref, lse_ref):
    total_rows = k_ref.shape[0]

    def block_step(q_rows, lanes, slots, low, steps, begin, finish):
        q_two = [stack_pair(q_ref[q_rows, lane]) for lane in lanes]

        def body(step, carry):
            start, allowed = window_mask(step, low, begin, finish, limit)
            window = pl.ds(start, K_BLOCK)
            both = jnp.concatenate([allowed, allowed], axis=1)
            result = []
            for (top, total, acc), q_pair, lane in zip(carry, q_two, lanes):
                scores = jnp.where(both, dot_nt(k_ref[window, lane], q_pair), NEG_FILL)
                new_top = jnp.maximum(top, jnp.max(scores, axis=0, keepdims=True))
                probs = jnp.exp2((scores - new_top) * LOG2_SCALE)
                shrink = jnp.exp2((top - new_top) * LOG2_SCALE)
                total = total * shrink + jnp.sum(probs, axis=0, keepdims=True)
                acc = acc * shrink + dot_tn(v_ref[window, lane], probs.astype(jnp.bfloat16))
                result.append((new_top, total, acc))
            return tuple(result)

        empty = (
            jnp.full((1, 2 * Q_BLOCK), NEG_FILL, jnp.float32),
            jnp.zeros((1, 2 * Q_BLOCK), jnp.float32),
            jnp.zeros((PAIR, 2 * Q_BLOCK), jnp.float32),
        )
        final = lax.fori_loop(0, steps, body, (empty,) * len(lanes))
        for (top, total, acc), lane, slot in zip(final, lanes, slots):
            out_ref[q_rows, lane] = unstack_pair(acc / total, Q_BLOCK).astype(jnp.bfloat16)
            lse_ref[slot] = top * LOG2_SCALE + jnp.log2(total)

    each_q_block(
        lengths_ref, q_ref.shape[0], total_rows, FORWARD_GROUP, q_ref.shape[1], block_step
    )


def attend_backward(
    limit, lengths_ref, q_ref, k_ref, v_ref, ctx_ref, lse_ref, grad_ref, gq_ref, gk_acc, gv_acc
):
    total_rows = k_ref.shape[0]

    def block_step(q_rows, lanes, slots, low, steps, begin, finish):
        ready = []
        for lane, slot in zip(lanes, slots):
            grads = grad_ref[q_rows, lane]
            product = (grads.astype(jnp.float32) * ctx_ref[q_rows, lane].astype(jnp.float32)).T
            row_dot = jnp.concatenate(
                [
                    jnp.sum(product[:HEAD_DIM], axis=0, keepdims=True),
                    jnp.sum(product[HEAD_DIM:], axis=0, keepdims=True),
                ],
                axis=1,
            )
            ready.append((stack_pair(q_ref[q_rows, lane]), stack_pair(grads), row_dot, lse_ref[slot]))

        def body(step, carry):
            start, allowed = window_mask(step, low, begin, finish, limit)
            window = pl.ds(start, K_BLOCK)
            both = jnp.concatenate([allowed, allowed], axis=1)
            result = []
            for acc, (q_pair, grad_pair, row_dot, lse), lane in zip(carry, ready, lanes):
                keys = k_ref[window, lane]
                scores = jnp.where(both, dot_nt(keys, q_pair), NEG_FILL)
                probs = jnp.exp2(scores * LOG2_SCALE - lse)
                grad_probs = dot_nt(v_ref[window, lane], grad_pair)
                grad_scores = (probs * (grad_probs - row_dot)).astype(jnp.bfloat16)
                gk_acc[window, lane] += dot_nn(grad_scores, q_pair)
                gv_acc[window, lane] += dot_nn(probs.astype(jnp.bfloat16), grad_pair)
                result.append(acc + dot_tn(keys, grad_scores))
            return tuple(result)

        zero = jnp.zeros((PAIR, 2 * Q_BLOCK), jnp.float32)
        final = lax.fori_loop(0, steps, body, (zero,) * len(lanes))
        for acc, lane in zip(final, lanes):
            gq_ref[q_rows, lane] = (unstack_pair(acc, Q_BLOCK) * SCORE_SCALE).astype(jnp.bfloat16)

    each_q_block(
        lengths_ref, q_ref.shape[0], total_rows, BACKWARD_GROUP, q_ref.shape[1], block_step
    )


VMEM_SPEC = pl.BlockSpec(memory_space=pltpu.VMEM)
HBM_SPEC = pl.BlockSpec(memory_space=pltpu.HBM)
SMEM_SPEC = pl.BlockSpec(memory_space=pltpu.SMEM)


MESH_ID = pl.DeviceIdType.MESH
DEPTH = 4
FULL_ROWS = 96

FLOWS = (
    (0, 0, "zxy", 0.0),
    (0, 1, "zyx", 0.0),
    (1, 0, "xzy", 12.0),
    (1, 1, "zyx", 24.0),
    (2, 0, "xzy", 12.0),
    (2, 1, "yxz", 12.0),
)
OWN = (0, 0, 0)


def forwards(order, piece):
    used = [axis for axis in order if piece["xyz".index(axis)] != 0]
    at = order.index(used[-1]) if used else -1
    steps = []
    if used and used[-1] == "z":
        steps.append(("z", 1 if piece[2] < 0 else -1))
    for axis in order[at + 1 :]:
        steps += [("z", 1), ("z", -1)] if axis == "z" else [(axis, 1)]
    return steps


def passed(piece, axis, sign):
    x, y, z = piece
    if axis == "x":
        return (1 - x, y, z)
    return (x, 1 - y, z) if axis == "y" else (x, y, z - sign)


def event_order(token_time):
    per_piece = 1.7
    links, heap, times, count = {}, [], {}, 0
    for z in range(DEPTH):
        links[z, "x", 1] = token_time
        for flow, (_, _, _, start) in enumerate(FLOWS):
            heapq.heappush(heap, (start + 0.01 * flow, count, z, flow, OWN))
            count += 1
    while heap:
        now, _, z, flow, piece = heapq.heappop(heap)
        times.setdefault((flow, piece), []).append(now)
        for axis, sign in forwards(FLOWS[flow][2], piece):
            there = z + sign if axis == "z" else z
            if not 0 <= there < DEPTH:
                continue
            end = max(links.get((z, axis, sign), 0.0), now) + per_piece
            links[z, axis, sign] = end
            heapq.heappush(heap, (end + 3.0, count, there, flow, passed(piece, axis, sign)))
            count += 1
    return [key for _, key in sorted((sum(v) / len(v), key) for key, v in times.items())]


class Place:
    def __init__(self):
        dp, tensor = lax.axis_index("dp"), lax.axis_index("tensor")
        self.z, self.y = dp // 2, lax.rem(dp, 2)
        self.x, self.core = tensor // 2, lax.rem(tensor, 2)

    def device(self, x=None, y=None, z=None, core=None):
        x = self.x if x is None else x
        y = self.y if y is None else y
        z = self.z if z is None else z
        core = self.core if core is None else core
        return (z * 2 + y, x * 2 + core)

    def step(self, axis, sign):
        if axis == "x":
            return self.device(x=1 - self.x)
        return self.device(y=1 - self.y) if axis == "y" else self.device(z=self.z + sign)

    def sibling(self):
        return self.device(core=1 - self.core)


def gather_kernel(
    wq_ref,
    wk_ref,
    wv_ref,
    wo_ref,
    w_in_ref,
    w_down_ref,
    tokens_ref,
    up_q_ref,
    up_v_ref,
    down_q_ref,
    down_v_ref,
    lengths_ref,
    full_ref,
    weights_hbm,
    rows_hbm,
    q_hbm,
    k_hbm,
    v_hbm,
    ups_full,
    fewest_ref,
    pack_ref,
    packs_ref,
    rows_ref,
    ups_ref,
    ups_all_ref,
    weights_ref,
    q_ref,
    k_ref,
    v_ref,
    count_ref,
    counts_ref,
    count_send,
    count_recv,
    piece_recv,
    send_sem,
    sib_send,
    sib_recv,
    own_sem,
    rows_send,
    rows_recv,
    ups_send,
    ups_recv,
    out_sem,
    far_sem,
):
    place = Place()
    x, y, z, core = place.x, place.y, place.z, place.core
    token_rows = tokens_ref.shape[0]
    part_rows = FULL_ROWS // 2
    half_rows = token_rows // 2

    across = place.device(x=1 - x, core=1 - core)
    middle_device = x != core
    barrier = pltpu.get_barrier_semaphore()
    others = (
        place.sibling(),
        place.step("x", 1),
        across,
        place.step("y", 1),
    )
    for target in others:
        pl.semaphore_signal(barrier, inc=1, device_id=target, device_id_type=MESH_ID)
    column = [place.device(z=lax.rem(z + i, DEPTH)) for i in range(1, DEPTH)]
    for target in column:
        pl.semaphore_signal(barrier, inc=1, device_id=target, device_id_type=MESH_ID)

    slim = wq_ref.shape[1]
    for kind, ref in enumerate((wq_ref, wk_ref, wv_ref)):
        pack_ref[:, kind * slim : (kind + 1) * slim] = ref[...]
    pack_ref[:, 3 * slim : 4 * slim] = wo_ref[...].astype(jnp.float32).T.astype(jnp.bfloat16)
    ups_ref[...] = jnp.zeros_like(ups_ref)
    ups_ref[0:8, :slim] = up_q_ref[...].astype(jnp.float32)
    ups_ref[8:16, :slim] = up_v_ref[...].astype(jnp.float32)
    count_ref[...] = jnp.broadcast_to(
        jnp.sum(lengths_ref[...].astype(jnp.float32), axis=1, keepdims=True), count_ref.shape
    )
    shards = (pack_ref, w_in_ref, w_down_ref)
    pl.semaphore_wait(barrier, len(others) + len(column))

    def remote(source, target, send, recv, device):
        return pltpu.make_async_remote_copy(
            src_ref=source,
            dst_ref=target,
            send_sem=send,
            recv_sem=recv,
            device_id=device,
            device_id_type=MESH_ID,
        )

    def rows_at(owner_x, owner_core, half):
        return rows_ref.at[owner_x * 2 + owner_core, pl.ds(half * half_rows, half_rows)]

    own_copies = [
        pltpu.make_async_copy(pack_ref, packs_ref.at[core, x, z, y], own_sem.at[0]),
        pltpu.make_async_copy(tokens_ref, rows_ref.at[x * 2 + core], own_sem.at[1]),
        pltpu.make_async_copy(ups_ref, ups_all_ref.at[x * 2 + core], own_sem.at[2]),
        pltpu.make_async_copy(w_in_ref, full_ref.at[0, core, x, z, y], own_sem.at[3]),
        pltpu.make_async_copy(w_down_ref, full_ref.at[1, core, x, z, y], own_sem.at[4]),
    ]
    row_copies = []
    for half in range(2):
        source = tokens_ref.at[pl.ds(half * half_rows, half_rows)]
        for slot, device in ((0, across), (1, place.sibling())):
            row_copies.append(
                remote(
                    source,
                    rows_at(x, core, half),
                    rows_send.at[slot, half],
                    rows_recv.at[slot, half],
                    device,
                )
            )
    up_copies = [
        remote(ups_ref, ups_all_ref.at[x * 2 + core], ups_send.at[i], ups_recv.at[i], device)
        for i, device in enumerate(others[:3])
    ]

    sends = {}

    def gathered(kind):
        return packs_ref if kind == 0 else full_ref.at[kind - 1]

    def half_of(kind, part):
        return pl.ds(part * part_rows, part_rows)

    def piece_at(flow, piece):
        kind, part, _, _ = FLOWS[flow]
        px, py = lax.rem(x + piece[0], 2), lax.rem(y + piece[1], 2)
        return (
            gathered(kind).at[core, px, z + piece[2], py, half_of(kind, part)],
            (px * 2 + py) * DEPTH + z + piece[2],
        )

    def handle(flow, piece):
        kind, part, order, _ = FLOWS[flow]
        landed, index = piece_at(flow, piece)
        source = landed
        if piece == OWN:
            source = shards[kind].at[half_of(kind, part)]
        else:
            remote(landed, landed, send_sem.at[flow, 0], piece_recv.at[flow, index], place.sibling()).wait_recv()
        for axis, sign in forwards(order, piece):
            slot = {"x": 0, "y": 1, "z": 2 if sign > 0 else 3}[axis]
            copy = remote(
                source,
                landed,
                send_sem.at[flow, slot],
                piece_recv.at[flow, index],
                place.step(axis, sign),
            )
            if axis == "z":
                pl.when((z + sign >= 0) & (z + sign < DEPTH))(copy.start)
            else:
                copy.start()
                sends[flow, slot] = sends.get((flow, slot), 0) + 1
        remote(source, landed, sib_send.at[flow], sib_recv.at[flow], place.sibling()).start()

    def block_of(flow, pieces, plane):
        kind, part, _, _ = FLOWS[flow]
        nx = 2 if pieces % 2 == 0 else 1
        ny = 2 if pieces % 4 == 0 else 1
        return gathered(kind).at[
            plane,
            pl.ds(0, nx),
            pl.ds(0, pieces // (nx * ny)),
            pl.ds(0, ny),
            half_of(kind, part),
        ]

    def finish_flow(flow):
        order = FLOWS[flow][2]
        everything = block_of(flow, 4 * DEPTH, 1 - core)
        remote(everything, everything, sib_send.at[flow], sib_recv.at[flow], place.sibling()).wait()

    def finish_sends(flow):
        order = FLOWS[flow][2]
        for axis, slot in (("x", 0), ("y", 1)):
            block = block_of(flow, 2 ** order.index(axis) * (DEPTH // 2 if "z" in order[: order.index(axis)] else 1), core)
            remote(block, block, send_sem.at[flow, slot], sib_recv.at[flow], place.sibling()).wait_send()
        each = 2 ** order.index("z")
        for at in range(DEPTH):
            for slot, sets in ((2, at + 1 if at < DEPTH - 1 else 0), (3, DEPTH - at if at > 0 else 0)):
                if sets:

                    @pl.when(z == at)
                    def _(slot=slot, sets=sets):
                        nx = 2 if each > 1 else 1
                        ny = 2 if each > 2 else 1
                        kind, part, _, _ = FLOWS[flow]
                        block = gathered(kind).at[
                            core,
                            pl.ds(0, nx),
                            pl.ds(0, sets),
                            pl.ds(0, ny),
                            half_of(kind, part),
                        ]
                        remote(
                            block, block, send_sem.at[flow, slot], sib_recv.at[flow], place.sibling()
                        ).wait_send()

    across_copies, sibling_copies = row_copies[0::2], row_copies[1::2]
    for copy in sibling_copies + up_copies + own_copies:
        copy.start()

    def middle_devices(step):
        pl.when(middle_device)(step)

    @middle_devices
    def _():
        for copy in across_copies:
            copy.start()

    count_copies = [
        remote(
            count_ref, counts_ref.at[DEPTH], count_send.at[0], count_recv.at[0], place.step("y", 1)
        )
    ]
    count_copies[0].start()

    def pass_count():
        count_copies[0].wait_recv()
        counts_ref[z] = jnp.minimum(count_ref[...], counts_ref[DEPTH])
        for i, target in enumerate(column):
            copy = remote(
                counts_ref.at[z], counts_ref.at[z], count_send.at[1 + i], count_recv.at[1 + i], target
            )
            copy.start()
            count_copies.append(copy)

    outs = []

    far_owner = (1 - x) * 2 + 1 - core
    far_writes = []

    def write(source, target):
        copy = pltpu.make_async_copy(source, target, out_sem.at[len(outs)])
        copy.start()
        outs.append(copy)

    def block_of_rows(hbm, owner):
        return hbm.at[pl.ds(pl.multiple_of(owner * token_rows, token_rows), token_rows)]

    def write_rows(source, hbm, owner):
        write(source, block_of_rows(hbm, owner))

    def far_write(source, hbm):
        return pltpu.make_async_copy(
            source, block_of_rows(hbm, far_owner), far_sem.at[len(far_writes)]
        )

    def assemble(t):
        if t == 0:
            for copy in up_copies + own_copies[:3]:
                copy.wait()
            for copy in sibling_copies:
                copy.wait_recv()
            for at in range(2):
                write_rows(rows_ref.at[x * 2 + at], rows_hbm, x * 2 + at)
            far_writes.append(far_write(rows_ref.at[far_owner], rows_hbm))

            @middle_devices
            def _():
                for copy in across_copies:
                    copy.wait_recv()
                far_writes[0].start()

            finish_flow(0)
            finish_flow(1)
            for owner in range(4):
                ups_full[:, owner * slim : (owner + 1) * slim] = ups_all_ref[owner, :, :slim].astype(jnp.bfloat16)
        lanes = slice(t * slim, (t + 1) * slim)
        source = packs_ref.at[t % 2, t // 2]
        for kind, down_ref, first in ((0, down_q_ref, 0), (1, None, 0), (2, down_v_ref, 8), (3, None, 0)):
            part = source[:, :, :, kind * slim : (kind + 1) * slim].reshape(-1, slim)
            if down_ref is not None:
                up = ups_all_ref[t, first : first + 8, :slim].astype(jnp.bfloat16)
                product = dot_tn(down_ref[...], up)
                part = (part.astype(jnp.float32) + ADAPTER_SCALE * product).astype(jnp.bfloat16)
            weights_ref[kind, :, lanes] = part
        if t == 3:
            write(weights_ref, weights_hbm)

    def own_queries():
        q_ref[...] = dot_nn(rows_ref[x * 2 + core], weights_ref[0]).astype(jnp.bfloat16)
        write(q_ref, q_hbm)

    def keys_values(ref, hbm, kind, at):
        owner = x * 2 + at
        ref[at] = dot_nn(rows_ref[owner], weights_ref[kind]).astype(jnp.bfloat16)
        write_rows(ref.at[at], hbm, owner)

    def far_keys_values(ref, hbm, kind):
        far_writes.append(far_write(ref.at[2], hbm))
        at = len(far_writes) - 1

        @middle_devices
        def _():
            ref[2] = dot_nn(rows_ref[far_owner], weights_ref[kind]).astype(jnp.bfloat16)
            far_writes[at].start()

    steps = [functools.partial(assemble, t) for t in range(4)] + [own_queries]
    for at in range(2):
        steps.append(functools.partial(keys_values, k_ref, k_hbm, 1, at))
        steps.append(functools.partial(keys_values, v_ref, v_hbm, 2, at))
    steps.append(functools.partial(far_keys_values, k_ref, k_hbm, 1))
    steps.append(functools.partial(far_keys_values, v_ref, v_hbm, 2))

    events = event_order(8.5)
    last_pack = max(i for i, (flow, _) in enumerate(events) if FLOWS[flow][0] == 0)
    between = max(1, (len(events) - last_pack) // (len(steps) + 1))
    arrivals = 0
    for at, (flow, piece) in enumerate(events):
        if piece[2] == 0:
            handle(flow, piece)
        else:
            pl.when((z + piece[2] >= 0) & (z + piece[2] < DEPTH))(
                functools.partial(handle, flow, piece)
            )
        if piece != OWN:
            arrivals += 1
            if arrivals == 24:
                pass_count()
        if at >= last_pack and (at - last_pack) % between == between - 1 and steps:
            steps.pop(0)()
    for step in steps:
        step()

    for copy in sibling_copies:
        copy.wait_send()

    @middle_devices
    def _():
        for copy in across_copies:
            copy.wait_send()
        for copy in far_writes:
            copy.wait()

    for copy in own_copies[3:] + outs:
        copy.wait()
    for flow in range(len(FLOWS)):
        if flow > 1:
            finish_flow(flow)
        finish_sends(flow)
    for copy in count_copies[1:]:
        copy.wait()
    count_copies[0].wait_send()
    fewest_ref[0, 0] = jnp.min(counts_ref[0:DEPTH])


def gather_all(
    w_q, w_k, w_v, w_out, w_in, w_down_t, tokens, up_q, up_v, down_q_t, down_v_t, lengths
):
    shard_rows, width = w_in.shape
    token_rows = tokens.shape[0]
    bf16, f32 = jnp.bfloat16, jnp.float32
    slim = w_q.shape[1]
    padded = slim + -slim % 128
    flows = len(FLOWS)
    dma = pltpu.SemaphoreType.DMA
    grid = (2, 2, DEPTH, 2, shard_rows, width)
    return pl.pallas_call(
        gather_kernel,
        out_shape=(
            jax.ShapeDtypeStruct((2,) + grid, bf16),
            jax.ShapeDtypeStruct((4, width, width), bf16),
            jax.ShapeDtypeStruct((4 * token_rows, width), bf16),
            jax.ShapeDtypeStruct((token_rows, width), bf16),
            jax.ShapeDtypeStruct((4 * token_rows, width), bf16),
            jax.ShapeDtypeStruct((4 * token_rows, width), bf16),
            jax.ShapeDtypeStruct((16, width), bf16),
            jax.ShapeDtypeStruct((1, 1), f32),
        ),
        in_specs=[VMEM_SPEC] * 4 + [HBM_SPEC] * 3 + [VMEM_SPEC] * 5,
        out_specs=(HBM_SPEC,) * 6 + (VMEM_SPEC, SMEM_SPEC),
        scratch_shapes=[
            pltpu.VMEM((shard_rows, width), bf16),
            pltpu.VMEM(grid, bf16),
            pltpu.VMEM((4, token_rows, width), bf16),
            pltpu.VMEM((16, padded), f32),
            pltpu.VMEM((4, 16, padded), f32),
            pltpu.VMEM((4, width, width), bf16),
            pltpu.VMEM((token_rows, width), bf16),
            pltpu.VMEM((3, token_rows, width), bf16),
            pltpu.VMEM((3, token_rows, width), bf16),
            pltpu.VMEM((8, 128), f32),
            pltpu.VMEM((DEPTH + 1, 8, 128), f32),
            dma((DEPTH,)),
            dma((DEPTH,)),
            dma((flows, 4 * DEPTH)),
            dma((flows, 4)),
            dma((flows,)),
            dma((flows,)),
            dma((5,)),
            dma((3, 2)),
            dma((3, 2)),
            dma((3,)),
            dma((3,)),
            dma((14,)),
            dma((3,)),
        ],
        compiler_params=pltpu.CompilerParams(
            collective_id=1, has_side_effects=True, vmem_limit_bytes=VMEM_LIMIT
        ),
        name="gather_all",
    )(
        w_q,
        w_k,
        w_v,
        w_out,
        w_in,
        w_down_t,
        tokens,
        up_q,
        up_v,
        down_q_t,
        down_v_t,
        lengths,
    )


def project_kernel(
    order,
    full_hbm,
    rows_ref,
    ups_ref,
    downs_ref,
    weights_ref,
    q_ref,
    k_ref,
    v_ref,
    packs_ref,
    sems,
):
    token_rows = q_ref.shape[0]
    slim = packs_ref.shape[2] // 4
    tensor = lax.axis_index("tensor")
    copies = [
        pltpu.make_async_copy(full_hbm.at[0, i], packs_ref.at[i], sems.at[i])
        for i in range(len(order))
    ]
    for copy in copies:
        copy.start()
    for i, t in enumerate(order):
        copies[i].wait()
        lanes = slice(t * slim, (t + 1) * slim)
        for kind, first in ((0, 0), (1, None), (2, 8), (3, None)):
            part = packs_ref[i, :, kind * slim : (kind + 1) * slim]
            if first is not None:
                up = ups_ref[t, first : first + 8, :slim]
                product = dot_tn(downs_ref[first : first + 8, :], up)
                part = (part.astype(jnp.float32) + ADAPTER_SCALE * product).astype(jnp.bfloat16)
            weights_ref[kind, :, lanes] = part
    own = rows_ref[pl.ds(pl.multiple_of(tensor * token_rows, token_rows), token_rows), :]
    q_ref[...] = dot_nn(own, weights_ref[0]).astype(jnp.bfloat16)

    @pl.loop(0, rows_ref.shape[0] // token_rows)
    def _(at):
        window = pl.ds(pl.multiple_of(at * token_rows, token_rows), token_rows)
        block = rows_ref[window, :]
        k_ref[window, :] = dot_nn(block, weights_ref[1]).astype(jnp.bfloat16)
        v_ref[window, :] = dot_nn(block, weights_ref[2]).astype(jnp.bfloat16)


def project(order, full, rows_all, ups_all, downs, token_rows):
    total_rows, width = rows_all.shape
    bf16 = jnp.bfloat16
    return pl.pallas_call(
        functools.partial(project_kernel, order),
        out_shape=(
            jax.ShapeDtypeStruct((4, width, width), bf16),
            jax.ShapeDtypeStruct((token_rows, width), bf16),
            jax.ShapeDtypeStruct((total_rows, width), bf16),
            jax.ShapeDtypeStruct((total_rows, width), bf16),
        ),
        in_specs=[HBM_SPEC] + [VMEM_SPEC] * 3,
        out_specs=(VMEM_SPEC,) * 4,
        scratch_shapes=[
            pltpu.VMEM(full.shape[1:], bf16),
            pltpu.SemaphoreType.DMA((len(order),)),
        ],
        compiler_params=pltpu.CompilerParams(vmem_limit_bytes=VMEM_LIMIT),
        name="project",
    )(full, rows_all, ups_all, downs)


def middle_kernel(
    near_only,
    lengths_ref,
    fewest_ref,
    gain_attn_ref,
    shift_attn_ref,
    gain_ffn_ref,
    shift_ffn_ref,
    q_hbm,
    k_hbm,
    v_hbm,
    tokens_hbm,
    cot_hbm,
    weights_hbm,
    full_hbm,
    rows_hbm,
    wide_k_hbm,
    wide_v_hbm,
    wide_rows_hbm,
    ups_ref,
    down_q_ref,
    down_v_ref,
    mixed_hbm,
    grad_one_hbm,
    gq_hbm,
    gk_hbm,
    gv_hbm,
    far_hbm,
    sums_hbm,
    q_ref,
    k_ref,
    v_ref,
    tokens_ref,
    cot_ref,
    out_buf,
    in_buf,
    down_buf,
    slope_buf,
    first_buf,
    sum_buf,
    normed_buf,
    inverse_buf,
    ctx_ref,
    lse_ref,
    grad_ref,
    gk_acc,
    gv_acc,
    gk_out,
    gv_out,
    far_out,
    pair_buf,
    sums_ref,
    sums_low,
    load_sem,
    part_sem,
    kv_sem,
    store_sem,
    grad_sem,
    far_sem,
):
    rows, width = q_ref.shape
    total_rows = k_ref.shape[0]
    parts, kinds = in_buf.shape[0], full_hbm.shape[0]
    kv_blocks = total_rows // KV_BLOCK
    base = lax.axis_index("tensor") * rows
    wide = fewest_ref[0, 0] < total_rows // 2
    limit = jnp.where(wide, total_rows, jnp.minimum(base + 2 * rows, total_rows))

    span_low, span_high = jnp.int32(total_rows), jnp.int32(0)
    for at in range(rows // Q_BLOCK):
        low, steps = query_span(lengths_ref, base + at * Q_BLOCK, total_rows)
        span_low = jnp.minimum(span_low, jnp.minimum(low, limit - K_BLOCK))
        span_high = jnp.maximum(span_high, jnp.minimum(low + steps * K_BLOCK, limit))

    def kv_rows(block):
        return pl.ds(pl.multiple_of(block * KV_BLOCK, KV_BLOCK), KV_BLOCK)

    def touched(block):
        return (block * KV_BLOCK < span_high) & ((block + 1) * KV_BLOCK > span_low)

    def kv_copies(block, k_source=k_hbm, v_source=v_hbm):
        window = kv_rows(block)
        return (
            pltpu.make_async_copy(k_source.at[window], k_ref.at[window], kv_sem.at[0, block]),
            pltpu.make_async_copy(v_source.at[window], v_ref.at[window], kv_sem.at[1, block]),
        )

    def part_copies(part):
        return (
            pltpu.make_async_copy(
                full_hbm.at[kinds - 2, part], in_buf.at[part], part_sem.at[0, part]
            ),
            pltpu.make_async_copy(
                full_hbm.at[kinds - 1, part], down_buf.at[part], part_sem.at[1, part]
            ),
        )

    q_copy = pltpu.make_async_copy(q_hbm, q_ref, load_sem.at[0])
    tokens_copy = pltpu.make_async_copy(tokens_hbm, tokens_ref, load_sem.at[1])
    out_copy = pltpu.make_async_copy(weights_hbm.at[3], out_buf, load_sem.at[2])
    cot_copy = pltpu.make_async_copy(cot_hbm, cot_ref, load_sem.at[3])
    pair_copy = pltpu.make_async_copy(weights_hbm.at[pl.ds(1, 2)], pair_buf, load_sem.at[4])
    q_copy.start()

    @pl.loop(0, kv_blocks)
    def _(block):
        @pl.when(touched(block) & jnp.logical_not(wide))
        def _():
            for copy in kv_copies(block):
                copy.start()

        @pl.when(touched(block) & wide)
        def _():
            for copy in kv_copies(block, wide_k_hbm, wide_v_hbm):
                copy.start()

    gk_acc[...] = jnp.zeros_like(gk_acc)
    gv_acc[...] = jnp.zeros_like(gv_acc)
    q_copy.wait()

    @pl.loop(0, kv_blocks)
    def _(block):
        @pl.when(touched(block))
        def _():
            for copy in kv_copies(block):
                copy.wait()

    tokens_copy.start()
    out_copy.start()
    cot_copy.start()
    for part in range(parts):
        for copy in part_copies(part):
            copy.start()
    pair_copy.start()

    attend_forward(limit, lengths_ref, q_ref, k_ref, v_ref, ctx_ref, lse_ref)

    gain_attn, shift_attn, gain_ffn, shift_ffn = (
        ref[...].reshape(1, -1) for ref in (gain_attn_ref, shift_attn_ref, gain_ffn_ref, shift_ffn_ref)
    )
    tokens_copy.wait()
    out_copy.wait()
    sum_buf[...] = dot_nt(ctx_ref[...], out_buf[...])

    def each_norm_block(step):
        @pl.loop(0, rows // NORM_BLOCK)
        def _(at):
            step(pl.ds(pl.multiple_of(at * NORM_BLOCK, NORM_BLOCK), NORM_BLOCK))

    @each_norm_block
    def _(block):
        residual = tokens_ref[block, :].astype(jnp.float32) + sum_buf[block, :]
        first, normed, inverse = norm_forward(residual, gain_attn, shift_attn)
        first_buf[block, :] = first.astype(jnp.bfloat16)
        sum_buf[block, :] = first.astype(jnp.bfloat16).astype(jnp.float32)
        normed_buf[block, :] = normed
        inverse_buf[block, :] = inverse

    @pl.loop(0, parts)
    def _(part):
        for copy in part_copies(part):
            copy.wait()
        acted, slope = gelu_parts(dot_nn(first_buf[...], in_buf[part]))
        slope_buf[part] = slope
        sum_buf[...] += dot_nt(acted.astype(jnp.bfloat16), down_buf[part])

    cot_copy.wait()

    @each_norm_block
    def _(block):
        mixed, normed, inverse = norm_forward(sum_buf[block, :], gain_ffn, shift_ffn)
        tokens_ref[block, :] = mixed.astype(jnp.bfloat16)
        cotangents = cot_ref[block, :].astype(jnp.float32)
        grad_two = norm_backward(cotangents, normed, inverse, gain_ffn)
        first_buf[block, :] = grad_two.astype(jnp.bfloat16)
        sum_buf[block, :] = grad_two

    mixed_copy = pltpu.make_async_copy(tokens_ref, mixed_hbm, store_sem.at[0])
    mixed_copy.start()

    @pl.loop(0, parts)
    def _(part):
        grad_hidden = dot_nn(first_buf[...], down_buf[part]) * slope_buf[part]
        sum_buf[...] += dot_nt(grad_hidden.astype(jnp.bfloat16), in_buf[part])

    @each_norm_block
    def _(block):
        grad_one = norm_backward(
            sum_buf[block, :], normed_buf[block, :], inverse_buf[block, :], gain_attn
        )
        normed_buf[block, :] = grad_one
        first_buf[block, :] = grad_one.astype(jnp.bfloat16)

    grad_one_copy = pltpu.make_async_copy(normed_buf, grad_one_hbm, store_sem.at[1])
    grad_one_copy.start()
    grad_ref[...] = dot_nn(first_buf[...], out_buf[...]).astype(jnp.bfloat16)

    attend_backward(
        limit,
        lengths_ref,
        q_ref,
        k_ref,
        v_ref,
        ctx_ref,
        lse_ref,
        grad_ref,
        first_buf,
        gk_acc,
        gv_acc,
    )
    gq_copy = pltpu.make_async_copy(first_buf, gq_hbm, store_sem.at[2])
    gq_copy.start()

    def rows_copy(block, source=rows_hbm):
        window = kv_rows(block)
        return pltpu.make_async_copy(source.at[window], k_ref.at[window], kv_sem.at[0, block])

    @pl.loop(0, kv_blocks)
    def _(block):
        @pl.when(touched(block) & jnp.logical_not(wide))
        def _():
            rows_copy(block).start()

        @pl.when(touched(block) & wide)
        def _():
            rows_copy(block, wide_rows_hbm).start()

    def wanted(block):
        if not near_only:
            return block >= 0
        return block // (kv_blocks // 2) == lax.axis_index("tensor") // 2

    def grad_copies(block):
        window = kv_rows(block)
        return (
            pltpu.make_async_copy(gk_out.at[window], gk_hbm.at[window], grad_sem.at[0, block]),
            pltpu.make_async_copy(gv_out.at[window], gv_hbm.at[window], grad_sem.at[1, block]),
        )

    @pl.loop(0, kv_blocks)
    def _(block):
        window = kv_rows(block)

        @pl.when(touched(block))
        def _():
            gk_out[window, :] = (gk_acc[window, :] * SCORE_SCALE).astype(jnp.bfloat16)
            gv_out[window, :] = gv_acc[window, :].astype(jnp.bfloat16)

        @pl.when(jnp.logical_not(touched(block)))
        def _():
            gk_out[window, :] = jnp.zeros((KV_BLOCK, width), jnp.bfloat16)
            gv_out[window, :] = jnp.zeros((KV_BLOCK, width), jnp.bfloat16)

        @pl.when(wanted(block))
        def _():
            for copy in grad_copies(block):
                copy.start()

    def far_copy(at):
        window = kv_rows(at)
        return pltpu.make_async_copy(far_out.at[window], far_hbm.at[window], far_sem.at[at])

    pair_copy.wait()
    tensor = lax.axis_index("tensor")
    near = tensor // 2
    per_owner = rows // KV_BLOCK

    @pl.loop(0, kv_blocks // 2)
    def _(at):
        owner = (1 - near) * 2 + lax.rem(tensor + 1 + at // per_owner, 2)
        block = owner * per_owner + lax.rem(at, per_owner)
        source, target = kv_rows(block), kv_rows(at)

        @pl.when(touched(block))
        def _():
            far_out[target, :] = (
                dot_nt(gk_out[source, :], pair_buf[0]) + dot_nt(gv_out[source, :], pair_buf[1])
            ).astype(jnp.bfloat16)

        @pl.when(jnp.logical_not(touched(block)))
        def _():
            far_out[target, :] = jnp.zeros((KV_BLOCK, width), jnp.bfloat16)

        far_copy(at).start()

    def add_adapter(row_vals, grads, down, up, first_at, second_at):
        lifted = (ADAPTER_SCALE * dot_nt(row_vals, down)).astype(jnp.bfloat16)
        grad_lifted = (ADAPTER_SCALE * dot_nt(grads, up)).astype(jnp.bfloat16)
        sums_ref[first_at : first_at + 8, :] += dot_tn(grad_lifted, row_vals)
        sums_ref[second_at : second_at + 8, :] += dot_tn(lifted, grads)

    sums_ref[...] = jnp.zeros_like(sums_ref)

    @pl.loop(0, kv_blocks)
    def _(block):
        window = kv_rows(block)

        @pl.when(touched(block))
        def _():
            rows_copy(block).wait()
            add_adapter(k_ref[window, :], gv_out[window, :], down_v_ref[...], ups_ref[8:16, :], 8, 24)

    own = pl.ds(pl.multiple_of(base, rows), rows)
    add_adapter(k_ref[own, :], first_buf[...], down_q_ref[...], ups_ref[0:8, :], 0, 16)
    sums_low[...] = sums_ref[...].astype(jnp.bfloat16)
    sums_copy = pltpu.make_async_copy(sums_low, sums_hbm, store_sem.at[3])
    sums_copy.start()
    sums_copy.wait()

    @pl.loop(0, kv_blocks // 2)
    def _(at):
        far_copy(at).wait()

    for copy in (mixed_copy, grad_one_copy, gq_copy):
        copy.wait()

    @pl.loop(0, kv_blocks)
    def _(block):
        @pl.when(wanted(block))
        def _():
            for copy in grad_copies(block):
                copy.wait()


def middle(
    near_only,
    lengths,
    fewest,
    norms,
    q_own,
    k_all,
    v_all,
    wide_rows,
    tokens,
    cotangent,
    weights,
    full,
    rows_all,
    ups,
    downs,
):
    rows, width = q_own.shape
    total_rows = k_all.shape[0]
    parts = full.shape[1]
    bf16, f32 = jnp.bfloat16, jnp.float32
    slots = rows // Q_BLOCK * (width // PAIR)
    kv_blocks = total_rows // KV_BLOCK
    dma = pltpu.SemaphoreType.DMA
    return pl.pallas_call(
        functools.partial(middle_kernel, near_only),
        out_shape=(
            jax.ShapeDtypeStruct((rows, width), bf16),
            jax.ShapeDtypeStruct((rows, width), f32),
            jax.ShapeDtypeStruct((rows, width), bf16),
            jax.ShapeDtypeStruct((total_rows, width), bf16),
            jax.ShapeDtypeStruct((total_rows, width), bf16),
            jax.ShapeDtypeStruct((total_rows // 2, width), bf16),
            jax.ShapeDtypeStruct((32, width), bf16),
        ),
        in_specs=[SMEM_SPEC] * 2 + [VMEM_SPEC] * 4 + [HBM_SPEC] * 11 + [VMEM_SPEC] * 3,
        out_specs=(HBM_SPEC,) * 7,
        scratch_shapes=[
            pltpu.VMEM((rows, width), bf16),
            pltpu.VMEM((total_rows, width), bf16),
            pltpu.VMEM((total_rows, width), bf16),
            pltpu.VMEM((rows, width), bf16),
            pltpu.VMEM((rows, width), bf16),
            pltpu.VMEM((width, width), bf16),
            pltpu.VMEM(full.shape[1:], bf16),
            pltpu.VMEM(full.shape[1:], bf16),
            pltpu.VMEM((parts, rows, full.shape[3]), f32),
            pltpu.VMEM((rows, width), bf16),
            pltpu.VMEM((rows, width), f32),
            pltpu.VMEM((rows, width), f32),
            pltpu.VMEM((rows, 1), f32),
            pltpu.VMEM((rows, width), bf16),
            pltpu.VMEM((slots, 1, 2 * Q_BLOCK), f32),
            pltpu.VMEM((rows, width), bf16),
            pltpu.VMEM((total_rows, width), f32),
            pltpu.VMEM((total_rows, width), f32),
            pltpu.VMEM((total_rows, width), bf16),
            pltpu.VMEM((total_rows, width), bf16),
            pltpu.VMEM((total_rows // 2, width), bf16),
            pltpu.VMEM((2, width, width), bf16),
            pltpu.VMEM((32, width), f32),
            pltpu.VMEM((32, width), bf16),
            dma((5,)),
            dma((2, parts)),
            dma((2, kv_blocks)),
            dma((4,)),
            dma((2, kv_blocks)),
            dma((kv_blocks // 2,)),
        ],
        compiler_params=pltpu.CompilerParams(vmem_limit_bytes=VMEM_LIMIT),
        name="middle",
    )(
        lengths,
        fewest,
        *norms,
        q_own,
        k_all,
        v_all,
        tokens,
        cotangent,
        weights,
        full,
        rows_all,
        *wide_rows,
        ups,
        *downs,
    )


def final_kernel(
    reach,
    gq_hbm,
    gk_hbm,
    gv_hbm,
    far_hbm,
    weights_hbm,
    grad_one_hbm,
    part_sums,
    grad_tokens_ref,
    sums_ref,
    gq_ref,
    gk_ref,
    gv_ref,
    far_ref,
    weights_ref,
    grad_one_ref,
    from_sib,
    to_x,
    from_x,
    home_to,
    home_from,
    yc_slots,
    z_slots,
    xc_slots,
    load_sem,
    far_send,
    far_recv,
    block_send,
    block_recv,
    sum_send,
    sum_recv,
):
    place = Place()
    x, y, z, core = place.x, place.y, place.z, place.core
    token_rows = gq_ref.shape[0]
    half_rows = token_rows // 2
    chunk_rows = token_rows // FAR_CHUNKS
    bf16, f32 = jnp.bfloat16, jnp.float32
    loads = {}

    def load(name, source, target):
        copy = pltpu.make_async_copy(source, target, load_sem.at[len(loads)])
        copy.start()
        loads[name] = copy

    if reach:
        load("far", far_hbm.at[pl.ds(token_rows, token_rows)], far_ref)
    near_rows = pl.ds(pl.multiple_of(x * 2 * token_rows, token_rows), 2 * token_rows)
    load("k", gk_hbm.at[near_rows], gk_ref)
    load("v", gv_hbm.at[near_rows], gv_ref)
    load("w", weights_hbm.at[pl.ds(0, 3)], weights_ref)
    load("q", gq_hbm, gq_ref)
    load("one", grad_one_hbm, grad_one_ref)

    across = place.device(x=1 - x, core=1 - core)
    middle_device = x != core
    barrier = pltpu.get_barrier_semaphore()
    around = [place.step("y", 1), place.sibling(), place.device(y=1 - y, core=1 - core)]
    column = [place.device(z=lax.rem(z + i, DEPTH)) for i in range(1, DEPTH)]
    beside = [place.step("x", 1), across]
    for target in around + column + beside:
        pl.semaphore_signal(barrier, inc=1, device_id=target, device_id_type=MESH_ID)
    pl.semaphore_wait(barrier, len(around + column + beside))

    def remote(source, target, send, recv, device):
        return pltpu.make_async_remote_copy(
            src_ref=source,
            dst_ref=target,
            send_sem=send,
            recv_sem=recv,
            device_id=device,
            device_id_type=MESH_ID,
        )

    def started(*operands):
        copy = remote(*operands)
        copy.start()
        return copy

    chunks = [pl.ds(at * chunk_rows, chunk_rows) for at in range(FAR_CHUNKS)]
    kept = pl.ds(pl.multiple_of(core * 16, 16), 16)
    given = pl.ds(pl.multiple_of((1 - core) * 16, 16), 16)
    sum_copies = []

    def send_sum(source, target, device):
        at = len(sum_copies)
        sum_copies.append(started(source, target, sum_send.at[at], sum_recv.at[at], device))

    for source, device in zip((kept, given, given), around):
        send_sum(part_sums.at[source], yc_slots.at[y * 2 + core], device)
    yc_slots[y * 2 + core] = part_sums[kept, :]
    sib_copies, x_copies = [], []
    if reach:
        for at, chunk in enumerate(chunks):
            sib_copies.append(
                started(
                    far_hbm.at[chunk],
                    from_sib.at[chunk],
                    far_send.at[0, at],
                    far_recv.at[0, at],
                    place.sibling(),
                )
            )
    else:
        for at, chunk in enumerate(chunks):
            x_copies.append(
                remote(
                    far_hbm.at[chunk],
                    from_x.at[chunk],
                    far_send.at[1, at],
                    far_recv.at[1, at],
                    across,
                )
            )

        @pl.when(middle_device)
        def _():
            for copy in x_copies:
                copy.start()

        @pl.when(jnp.logical_not(middle_device))
        def _():
            from_x[...] = jnp.zeros_like(from_x)

    def slot_sum(slots, indices):
        result = slots[indices[0]].astype(f32)
        for i in indices[1:]:
            result = result + slots[i].astype(f32)
        return result

    if reach:
        loads["far"].wait()
        for at, chunk in enumerate(chunks):
            sib_copies[at].wait_recv()
            to_x[chunk, :] = (far_ref[chunk, :].astype(f32) + from_sib[chunk, :].astype(f32)).astype(
                bf16
            )
            x_copies.append(
                started(
                    to_x.at[chunk],
                    from_x.at[chunk],
                    far_send.at[1, at],
                    far_recv.at[1, at],
                    place.step("x", 1),
                )
            )

    for copy in sum_copies[0:3]:
        copy.wait_recv()
    z_slots[z] = slot_sum(yc_slots, range(4)).astype(bf16)
    for device in column:
        send_sum(z_slots.at[z], z_slots.at[z], device)

    def partial(owner, half):
        window = pl.ds(pl.multiple_of(owner * token_rows + half * half_rows, half_rows), half_rows)
        return dot_nt(gk_ref[window, :], weights_ref[1]) + dot_nt(gv_ref[window, :], weights_ref[2])

    for name in ("k", "v", "w"):
        loads[name].wait()
    home_copies = []
    for half in range(2):
        window = pl.ds(half * half_rows, half_rows)
        home_to[window, :] = partial(1 - core, half).astype(bf16)
        home_copies.append(
            started(
                home_to.at[window],
                home_from.at[window],
                block_send.at[half],
                block_recv.at[half],
                place.sibling(),
            )
        )

    for copy in sum_copies[3:]:
        copy.wait_recv()
    xc_slots[x * 2 + core] = slot_sum(z_slots, range(DEPTH)).astype(bf16)
    own_slot = xc_slots.at[x * 2 + core]
    for device in [place.sibling()] + beside:
        send_sum(own_slot, own_slot, device)
    for name in ("q", "one"):
        loads[name].wait()
    for half in range(2):
        window = pl.ds(half * half_rows, half_rows)
        grad_one_ref[window, :] += partial(core, half) + dot_nt(gq_ref[window, :], weights_ref[0])
    for copy in home_copies:
        copy.wait_recv()
    for at, chunk in enumerate(chunks):
        if reach:
            x_copies[at].wait_recv()
        else:
            pl.when(middle_device)(x_copies[at].wait_recv)
        grad_tokens_ref[chunk, :] = (
            grad_one_ref[chunk, :] + home_from[chunk, :].astype(f32) + from_x[chunk, :].astype(f32)
        ).astype(bf16)
    for copy in sum_copies[2 + DEPTH :]:
        copy.wait_recv()
    for half in range(2):
        sums_ref[half * 16 : half * 16 + 16, :] = slot_sum(xc_slots, (half, 2 + half))

    for copy in sib_copies + home_copies + sum_copies:
        copy.wait_send()
    for copy in x_copies:
        if reach:
            copy.wait_send()
        else:
            pl.when(middle_device)(copy.wait_send)


def final_sums(reach, grad_q, grad_k, grad_v, far_rows, weights, grad_one, sums):
    token_rows, width = grad_q.shape
    bf16, f32 = jnp.bfloat16, jnp.float32
    dma = pltpu.SemaphoreType.DMA
    block = pltpu.VMEM((token_rows, width), bf16)
    return pl.pallas_call(
        functools.partial(final_kernel, reach),
        out_shape=(
            jax.ShapeDtypeStruct((token_rows, width), bf16),
            jax.ShapeDtypeStruct((32, width), f32),
        ),
        in_specs=[HBM_SPEC] * 6 + [VMEM_SPEC],
        out_specs=(VMEM_SPEC,) * 2,
        scratch_shapes=[
            block,
            pltpu.VMEM((2 * token_rows, width), bf16),
            pltpu.VMEM((2 * token_rows, width), bf16),
            block,
            pltpu.VMEM((3, width, width), bf16),
            pltpu.VMEM((token_rows, width), f32),
            block,
            block,
            block,
            block,
            block,
            pltpu.VMEM((4, 16, width), bf16),
            pltpu.VMEM((DEPTH, 16, width), bf16),
            pltpu.VMEM((4, 16, width), bf16),
            dma((6,)),
            dma((2, FAR_CHUNKS)),
            dma((2, FAR_CHUNKS)),
            dma((2,)),
            dma((2,)),
            dma((DEPTH + 5,)),
            dma((DEPTH + 5,)),
        ],
        compiler_params=pltpu.CompilerParams(
            collective_id=2 if reach else 3, has_side_effects=True, vmem_limit_bytes=VMEM_LIMIT
        ),
        name="final_sums_wide" if reach else "final_sums",
    )(grad_q, grad_k, grad_v, far_rows, weights, grad_one, sums)


def no_rows_kernel(*refs):
    del refs


def no_rows(tokens, weights):
    shape = jax.ShapeDtypeStruct((4 * tokens.shape[0], tokens.shape[1]), tokens.dtype)
    return pl.pallas_call(
        no_rows_kernel, out_shape=(shape,) * 3, out_specs=(HBM_SPEC,) * 3, name="no_rows"
    )()


def hand_out_kernel(grad_ref, sums_ref, grad_out, aq_ref, av_ref, bq_ref, bv_ref):
    grad_out[...] = grad_ref[...]
    slim = bq_ref.shape[1]
    aq_ref[...] = sums_ref[0:8, :]
    av_ref[...] = sums_ref[8:16, :]
    for t in range(sums_ref.shape[1] // slim):

        @pl.when(lax.axis_index("tensor") == t)
        def _(t=t):
            bq_ref[...] = sums_ref[16:24, t * slim : (t + 1) * slim]
            bv_ref[...] = sums_ref[24:32, t * slim : (t + 1) * slim]


def hand_out(grad_tokens, sums, slim):
    f32, width = jnp.float32, sums.shape[1]
    return pl.pallas_call(
        hand_out_kernel,
        out_shape=(
            jax.ShapeDtypeStruct(grad_tokens.shape, grad_tokens.dtype),
            jax.ShapeDtypeStruct((8, width), f32),
            jax.ShapeDtypeStruct((8, width), f32),
            jax.ShapeDtypeStruct((8, slim), f32),
            jax.ShapeDtypeStruct((8, slim), f32),
        ),
        in_specs=[VMEM_SPEC] * 2,
        out_specs=(VMEM_SPEC,) * 5,
        name="hand_out",
    )(grad_tokens, sums)


def local(
    fast,
    tokens,
    query_weight,
    w_key,
    value_weight,
    w_out,
    w_in,
    w_down,
    gain_attn,
    shift_attn,
    gain_ffn,
    shift_ffn,
    query_down_factor,
    query_up_factor,
    value_down_factor,
    value_up_factor,
    lengths,
    cotangent,
):
    slim = query_weight.shape[1]
    width = tokens.shape[1]
    token_rows = tokens.shape[0]
    down_q_t, down_v_t = query_down_factor.T, value_down_factor.T
    if fast:
        full, weights, rows_all, q_own, k_all, v_all, ups_full, fewest = gather_all(
            query_weight,
            w_key,
            value_weight,
            w_out,
            w_in,
            w_down.T,
            tokens,
            query_up_factor,
            value_up_factor,
            down_q_t,
            down_v_t,
            lengths,
        )
        full = full.reshape(2, 4, width, width)
    else:
        attn_pack = jnp.concatenate([query_weight, w_key, value_weight, w_out.T], axis=1)
        full = jnp.stack([attn_pack, w_in, w_down.T])
        full = lax.all_gather(full, "dp", axis=1, tiled=True)
        full = lax.all_gather(full, "tensor", axis=1)
        rows_all = lax.all_gather(tokens, "tensor").reshape(-1, width)
        ups = jnp.concatenate([query_up_factor, value_up_factor], axis=0)
        ups = jnp.pad(ups, ((0, 0), (0, -slim % 128)))
        ups_all = lax.all_gather(ups, "tensor")
        downs = jnp.concatenate([down_q_t, down_v_t], axis=0)
        ups_full = ups_all[:, :, :slim].transpose(1, 0, 2).reshape(16, width)
        order = tuple(range(full.shape[1]))
        weights, q_own, k_all, v_all = project(order, full, rows_all, ups_all, downs, token_rows)

    norms = (gain_attn, shift_attn, gain_ffn, shift_ffn)
    downs_t = (down_q_t, down_v_t)
    if fast:

        def either(near, wide, *operands):
            return lax.cond(fewest[0, 0] >= rows_all.shape[0] // 2, near, wide, *operands)

        def wide_rows(tokens, weights):
            me = lax.axis_index("tensor")
            rows_all = jnp.zeros((4 * token_rows, width), tokens.dtype)
            for away in range(4):
                block = tokens
                if away:
                    block = lax.ppermute(tokens, "tensor", [(i, i ^ away) for i in range(4)])
                first_row = (me ^ away) * token_rows
                rows_all = lax.dynamic_update_slice_in_dim(rows_all, block, first_row, 0)
            k_all = dot_nn(rows_all, weights[1]).astype(jnp.bfloat16)
            v_all = dot_nn(rows_all, weights[2]).astype(jnp.bfloat16)
            return (k_all, v_all, rows_all)

        mixed, grad_one, grad_q, grad_k, grad_v, far_rows, sums = middle(
            True,
            lengths,
            fewest,
            norms,
            q_own,
            k_all,
            v_all,
            either(no_rows, wide_rows, tokens, weights),
            tokens,
            cotangent,
            weights,
            full,
            rows_all,
            ups_full,
            downs_t,
        )
        grad_tokens, sums = either(
            functools.partial(final_sums, False),
            functools.partial(final_sums, True),
            *(grad_q, grad_k, grad_v, far_rows, weights, grad_one, sums),
        )
        grad_tokens, grad_aq, grad_av, grad_bq, grad_bv = hand_out(grad_tokens, sums, slim)
        return (mixed, grad_tokens, grad_aq.T, grad_bq, grad_av.T, grad_bv)

    mixed, grad_one, grad_q, grad_k, grad_v, far_rows, sums = middle(
        False,
        lengths,
        jnp.zeros((1, 1), jnp.float32),
        norms,
        q_own,
        k_all,
        v_all,
        (k_all, v_all, rows_all),
        tokens,
        cotangent,
        weights,
        full,
        rows_all,
        ups_full,
        downs_t,
    )
    grad_rows = dot_nt(grad_k, weights[1]) + dot_nt(grad_v, weights[2])
    shared = lax.psum_scatter(
        grad_rows.astype(jnp.bfloat16), "tensor", scatter_dimension=0, tiled=True
    )
    own_rows = dot_nt(grad_q, weights[0])
    grad_tokens = (grad_one + own_rows + shared.astype(jnp.float32)).astype(jnp.bfloat16)
    sums = lax.psum(sums.astype(jnp.float32), ("dp", "tensor"))
    at = lax.axis_index("tensor") * slim
    grad_bq = lax.dynamic_slice_in_dim(sums[16:24], at, slim, 1)
    grad_bv = lax.dynamic_slice_in_dim(sums[24:32], at, slim, 1)
    return (mixed, grad_tokens, sums[0:8].T, grad_bq, sums[8:16].T, grad_bv)


def solution(mesh):
    fast = dict(mesh.shape) == {"dp": 2 * DEPTH, "tensor": 4}
    return jax.shard_map(
        functools.partial(local, fast),
        mesh=mesh,
        in_specs=(
            P(("dp", "tensor"), None),
            P("dp", "tensor"),
            P("dp", "tensor"),
            P("dp", "tensor"),
            P("tensor", "dp"),
            P("dp", "tensor"),
            P("tensor", "dp"),
            P(),
            P(),
            P(),
            P(),
            P(),
            P(None, "tensor"),
            P(),
            P(None, "tensor"),
            P("dp", None),
            P(("dp", "tensor"), None),
        ),
        out_specs=(
            P(("dp", "tensor"), None),
            P(("dp", "tensor"), None),
            P(),
            P(None, "tensor"),
            P(),
            P(None, "tensor"),
        ),
        check_vma=False,
    )
```

```python
import functools
import heapq

import jax
import jax.numpy as jnp
from jax import lax
from jax.experimental import pallas as pl
from jax.experimental.pallas import tpu as pltpu
from jax.sharding import PartitionSpec as P

HEAD_DIM = 64
PAIR = 2 * HEAD_DIM
Q_BLOCK = 256
K_BLOCK = 512
KV_BLOCK = 256
NORM_BLOCK = 512
FAR_CHUNKS = 4
FORWARD_GROUP = 6
BACKWARD_GROUP = 3
ADAPTER_SCALE = 2.0
SCORE_SCALE = HEAD_DIM ** (-0.5)
LOG2_SCALE = SCORE_SCALE * 1.4426950408889634
NEG_FILL = -1e30
LN_EPS = 1e-05
VMEM_LIMIT = 60 * 1024 * 1024


def dot_nn(left, right):
    return jnp.dot(left, right, preferred_element_type=jnp.float32)


def dot_nt(left, right):
    return lax.dot_general(
        left, right, (((1,), (1,)), ((), ())), preferred_element_type=jnp.float32
    )


def dot_tn(left, right):
    return lax.dot_general(
        left, right, (((0,), (0,)), ((), ())), preferred_element_type=jnp.float32
    )


def norm_forward(row_vals, gain_vals, offset):
    middle = jnp.mean(row_vals, axis=-1, keepdims=True)
    centred = row_vals - middle
    inverse = lax.rsqrt(jnp.mean(centred * centred, axis=-1, keepdims=True) + LN_EPS)
    normed = centred * inverse
    return (normed * gain_vals + offset, normed, inverse)


def norm_backward(grad_out, normed, inverse, gain_vals):
    grad_n = grad_out * gain_vals
    return inverse * (
        grad_n
        - jnp.mean(grad_n, axis=-1, keepdims=True)
        - normed * jnp.mean(grad_n * normed, axis=-1, keepdims=True)
    )


def gelu_parts(hidden):
    cdf_part = 0.5 * (1.0 + lax.erf(hidden * 0.7071067811865476))
    density = jnp.exp(-0.5 * hidden * hidden) * 0.3989422804014327
    return (hidden * cdf_part, cdf_part + hidden * density)


def block_span(lengths_ref, first_row, rows, total_rows):
    last_row = first_row + rows - 1

    def slot_step(slot, carry):
        end, low, high = carry
        end = end + lengths_ref[0, slot]
        low = jnp.where(end <= first_row, jnp.maximum(low, end), low)
        high = jnp.where(end > last_row, jnp.minimum(high, end), high)
        return end, low, high

    start = (jnp.int32(0), jnp.int32(0), jnp.int32(total_rows))
    _, low, high = lax.fori_loop(0, lengths_ref.shape[1], slot_step, start, unroll=8)
    return low, high


def row_bounds(lengths_ref, first_row, rows, total_rows):
    place = first_row + lax.broadcasted_iota(jnp.int32, (1, rows), 1)

    def slot_step(slot, carry):
        end, begin, finish = carry
        end = end + lengths_ref[0, slot]
        done = place >= end
        begin = jnp.where(done, jnp.maximum(begin, end), begin)
        finish = jnp.where(done, finish, jnp.minimum(finish, end))
        return end, begin, finish

    start = (
        jnp.int32(0),
        jnp.zeros((1, rows), jnp.int32),
        jnp.full((1, rows), total_rows, jnp.int32),
    )
    _, begin, finish = lax.fori_loop(0, lengths_ref.shape[1], slot_step, start, unroll=8)
    return begin, finish


def stack_pair(block):
    lane = lax.broadcasted_iota(jnp.int32, block.shape, 1)
    zero = jnp.zeros_like(block)
    return jnp.concatenate(
        [jnp.where(lane < HEAD_DIM, block, zero), jnp.where(lane >= HEAD_DIM, block, zero)],
        axis=0,
    )


def unstack_pair(block, rows):
    joined = jnp.concatenate([block[:HEAD_DIM, :rows], block[HEAD_DIM:, rows:]], axis=0)
    return joined.T


def window_mask(step, low, begin, finish, limit):
    wanted = low + step * K_BLOCK
    start = pl.multiple_of(jnp.minimum(wanted, limit - K_BLOCK), 16)
    key_at = start + lax.broadcasted_iota(jnp.int32, (K_BLOCK, begin.shape[1]), 0)
    return start, (key_at >= jnp.maximum(begin, wanted)) & (key_at < finish)


def query_span(lengths_ref, first_row, total_rows):
    low, high = block_span(lengths_ref, first_row, Q_BLOCK, total_rows)
    low = (low // 16) * 16
    return low, (high - low + K_BLOCK - 1) // K_BLOCK


def each_q_block(lengths_ref, rows, total_rows, group, heads_width, block_step):
    base = lax.axis_index("tensor") * rows

    @pl.loop(0, rows // Q_BLOCK)
    def _(q_at):
        first_row = base + q_at * Q_BLOCK
        low, steps = query_span(lengths_ref, first_row, total_rows)
        begin, finish = row_bounds(lengths_ref, first_row, Q_BLOCK, total_rows)
        q_rows = pl.ds(pl.multiple_of(q_at * Q_BLOCK, Q_BLOCK), Q_BLOCK)

        @pl.loop(0, heads_width // PAIR // group)
        def _(at):
            pairs = [at * group + i for i in range(group)]
            lanes = [pl.ds(pl.multiple_of(pair * PAIR, PAIR), PAIR) for pair in pairs]
            slots = [q_at * (heads_width // PAIR) + pair for pair in pairs]
            block_step(q_rows, lanes, slots, low, steps, begin, finish)


def attend_forward(limit, lengths_ref, q_ref, k_ref, v_ref, out_ref, lse_ref):
    total_rows = k_ref.shape[0]

    def block_step(q_rows, lanes, slots, low, steps, begin, finish):
        q_two = [stack_pair(q_ref[q_rows, lane]) for lane in lanes]

        def body(step, carry):
            start, allowed = window_mask(step, low, begin, finish, limit)
            window = pl.ds(start, K_BLOCK)
            both = jnp.concatenate([allowed, allowed], axis=1)
            result = []
            for (top, total, acc), q_pair, lane in zip(carry, q_two, lanes):
                scores = jnp.where(both, dot_nt(k_ref[window, lane], q_pair), NEG_FILL)
                new_top = jnp.maximum(top, jnp.max(scores, axis=0, keepdims=True))
                probs = jnp.exp2((scores - new_top) * LOG2_SCALE)
                shrink = jnp.exp2((top - new_top) * LOG2_SCALE)
                total = total * shrink + jnp.sum(probs, axis=0, keepdims=True)
                acc = acc * shrink + dot_tn(v_ref[window, lane], probs.astype(jnp.bfloat16))
                result.append((new_top, total, acc))
            return tuple(result)

        empty = (
            jnp.full((1, 2 * Q_BLOCK), NEG_FILL, jnp.float32),
            jnp.zeros((1, 2 * Q_BLOCK), jnp.float32),
            jnp.zeros((PAIR, 2 * Q_BLOCK), jnp.float32),
        )
        final = lax.fori_loop(0, steps, body, (empty,) * len(lanes))
        for (top, total, acc), lane, slot in zip(final, lanes, slots):
            out_ref[q_rows, lane] = unstack_pair(acc / total, Q_BLOCK).astype(jnp.bfloat16)
            lse_ref[slot] = top * LOG2_SCALE + jnp.log2(total)

    each_q_block(
        lengths_ref, q_ref.shape[0], total_rows, FORWARD_GROUP, q_ref.shape[1], block_step
    )


def attend_backward(
    limit, lengths_ref, q_ref, k_ref, v_ref, ctx_ref, lse_ref, grad_ref, gq_ref, gk_acc, gv_acc
):
    total_rows = k_ref.shape[0]

    def block_step(q_rows, lanes, slots, low, steps, begin, finish):
        ready = []
        for lane, slot in zip(lanes, slots):
            grads = grad_ref[q_rows, lane]
            product = (grads.astype(jnp.float32) * ctx_ref[q_rows, lane].astype(jnp.float32)).T
            row_dot = jnp.concatenate(
                [
                    jnp.sum(product[:HEAD_DIM], axis=0, keepdims=True),
                    jnp.sum(product[HEAD_DIM:], axis=0, keepdims=True),
                ],
                axis=1,
            )
            ready.append((stack_pair(q_ref[q_rows, lane]), stack_pair(grads), row_dot, lse_ref[slot]))

        def body(step, carry):
            start, allowed = window_mask(step, low, begin, finish, limit)
            window = pl.ds(start, K_BLOCK)
            both = jnp.concatenate([allowed, allowed], axis=1)
            result = []
            for acc, (q_pair, grad_pair, row_dot, lse), lane in zip(carry, ready, lanes):
                keys = k_ref[window, lane]
                scores = jnp.where(both, dot_nt(keys, q_pair), NEG_FILL)
                probs = jnp.exp2(scores * LOG2_SCALE - lse)
                grad_probs = dot_nt(v_ref[window, lane], grad_pair)
                grad_scores = (probs * (grad_probs - row_dot)).astype(jnp.bfloat16)
                gk_acc[window, lane] += dot_nn(grad_scores, q_pair)
                gv_acc[window, lane] += dot_nn(probs.astype(jnp.bfloat16), grad_pair)
                result.append(acc + dot_tn(keys, grad_scores))
            return tuple(result)

        zero = jnp.zeros((PAIR, 2 * Q_BLOCK), jnp.float32)
        final = lax.fori_loop(0, steps, body, (zero,) * len(lanes))
        for acc, lane in zip(final, lanes):
            gq_ref[q_rows, lane] = (unstack_pair(acc, Q_BLOCK) * SCORE_SCALE).astype(jnp.bfloat16)

    each_q_block(
        lengths_ref, q_ref.shape[0], total_rows, BACKWARD_GROUP, q_ref.shape[1], block_step
    )


VMEM_SPEC = pl.BlockSpec(memory_space=pltpu.VMEM)
HBM_SPEC = pl.BlockSpec(memory_space=pltpu.HBM)
SMEM_SPEC = pl.BlockSpec(memory_space=pltpu.SMEM)


MESH_ID = pl.DeviceIdType.MESH
DEPTH = 4
FULL_ROWS = 96

FLOWS = (
    (0, 0, "zyx", 0.0),
    (0, 1, "zxy", 0.0),
    (1, 0, "zxy", 16.0),
    (1, 1, "xyz", 12.0),
    (2, 0, "yzx", 12.0),
    (2, 1, "xzy", 4.0),
)
OWN = (0, 0, 0)


def forwards(order, piece):
    used = [axis for axis in order if piece["xyz".index(axis)] != 0]
    at = order.index(used[-1]) if used else -1
    steps = []
    if used and used[-1] == "z":
        steps.append(("z", 1 if piece[2] < 0 else -1))
    for axis in order[at + 1 :]:
        steps += [("z", 1), ("z", -1)] if axis == "z" else [(axis, 1)]
    return steps


def passed(piece, axis, sign):
    x, y, z = piece
    if axis == "x":
        return (1 - x, y, z)
    return (x, 1 - y, z) if axis == "y" else (x, y, z - sign)


def event_order(token_time):
    per_piece = 1.7
    links, heap, times, count = {}, [], {}, 0
    for z in range(DEPTH):
        links[z, "x", 1] = token_time
        for flow, (_, _, _, start) in enumerate(FLOWS):
            heapq.heappush(heap, (start + 0.01 * flow, count, z, flow, OWN))
            count += 1
    while heap:
        now, _, z, flow, piece = heapq.heappop(heap)
        times.setdefault((flow, piece), []).append(now)
        for axis, sign in forwards(FLOWS[flow][2], piece):
            there = z + sign if axis == "z" else z
            if not 0 <= there < DEPTH:
                continue
            end = max(links.get((z, axis, sign), 0.0), now) + per_piece
            links[z, axis, sign] = end
            heapq.heappush(heap, (end + 3.0, count, there, flow, passed(piece, axis, sign)))
            count += 1
    return [key for _, key in sorted((sum(v) / len(v), key) for key, v in times.items())]


class Place:
    def __init__(self):
        dp, tensor = lax.axis_index("dp"), lax.axis_index("tensor")
        self.z, self.y = dp // 2, lax.rem(dp, 2)
        self.x, self.core = tensor // 2, lax.rem(tensor, 2)

    def device(self, x=None, y=None, z=None, core=None):
        x = self.x if x is None else x
        y = self.y if y is None else y
        z = self.z if z is None else z
        core = self.core if core is None else core
        return (z * 2 + y, x * 2 + core)

    def step(self, axis, sign):
        if axis == "x":
            return self.device(x=1 - self.x)
        return self.device(y=1 - self.y) if axis == "y" else self.device(z=self.z + sign)

    def sibling(self):
        return self.device(core=1 - self.core)


def gather_kernel(
    wq_ref,
    wk_ref,
    wv_ref,
    wo_ref,
    w_in_ref,
    w_down_ref,
    tokens_ref,
    up_q_ref,
    up_v_ref,
    down_q_ref,
    down_v_ref,
    lengths_ref,
    full_ref,
    weights_hbm,
    rows_hbm,
    q_hbm,
    k_hbm,
    v_hbm,
    ups_full,
    fewest_ref,
    pack_ref,
    packs_ref,
    rows_ref,
    ups_ref,
    ups_all_ref,
    weights_ref,
    q_ref,
    k_ref,
    v_ref,
    count_ref,
    counts_ref,
    count_send,
    count_recv,
    piece_recv,
    send_sem,
    sib_send,
    sib_recv,
    own_sem,
    rows_send,
    rows_recv,
    ups_send,
    ups_recv,
    out_sem,
    far_sem,
):
    place = Place()
    x, y, z, core = place.x, place.y, place.z, place.core
    token_rows = tokens_ref.shape[0]
    part_rows = FULL_ROWS // 2
    half_rows = token_rows // 2

    across = place.device(x=1 - x, core=1 - core)
    middle_device = x != core
    barrier = pltpu.get_barrier_semaphore()
    others = (
        place.sibling(),
        place.step("x", 1),
        across,
        place.step("y", 1),
    )
    for target in others:
        pl.semaphore_signal(barrier, inc=1, device_id=target, device_id_type=MESH_ID)
    column = [place.device(z=lax.rem(z + i, DEPTH)) for i in range(1, DEPTH)]
    for target in column:
        pl.semaphore_signal(barrier, inc=1, device_id=target, device_id_type=MESH_ID)

    slim = wq_ref.shape[1]
    for kind, ref in enumerate((wq_ref, wk_ref, wv_ref)):
        pack_ref[:, kind * slim : (kind + 1) * slim] = ref[...]
    pack_ref[:, 3 * slim : 4 * slim] = wo_ref[...].astype(jnp.float32).T.astype(jnp.bfloat16)
    ups_ref[...] = jnp.zeros_like(ups_ref)
    ups_ref[0:8, :slim] = up_q_ref[...].astype(jnp.float32)
    ups_ref[8:16, :slim] = up_v_ref[...].astype(jnp.float32)
    count_ref[...] = jnp.broadcast_to(
        jnp.sum(lengths_ref[...].astype(jnp.float32), axis=1, keepdims=True), count_ref.shape
    )
    shards = (pack_ref, w_in_ref, w_down_ref)
    pl.semaphore_wait(barrier, len(others) + len(column))

    def remote(source, target, send, recv, device):
        return pltpu.make_async_remote_copy(
            src_ref=source,
            dst_ref=target,
            send_sem=send,
            recv_sem=recv,
            device_id=device,
            device_id_type=MESH_ID,
        )

    def rows_at(owner_x, owner_core, half):
        return rows_ref.at[owner_x * 2 + owner_core, pl.ds(half * half_rows, half_rows)]

    own_copies = [
        pltpu.make_async_copy(pack_ref, packs_ref.at[core, x, z, y], own_sem.at[0]),
        pltpu.make_async_copy(tokens_ref, rows_ref.at[x * 2 + core], own_sem.at[1]),
        pltpu.make_async_copy(ups_ref, ups_all_ref.at[x * 2 + core], own_sem.at[2]),
        pltpu.make_async_copy(w_in_ref, full_ref.at[0, core, x, z, y], own_sem.at[3]),
        pltpu.make_async_copy(w_down_ref, full_ref.at[1, core, x, z, y], own_sem.at[4]),
    ]
    row_copies = []
    for half in range(2):
        source = tokens_ref.at[pl.ds(half * half_rows, half_rows)]
        for slot, device in ((0, across), (1, place.sibling())):
            row_copies.append(
                remote(
                    source,
                    rows_at(x, core, half),
                    rows_send.at[slot, half],
                    rows_recv.at[slot, half],
                    device,
                )
            )
    up_copies = [
        remote(ups_ref, ups_all_ref.at[x * 2 + core], ups_send.at[i], ups_recv.at[i], device)
        for i, device in enumerate(others[:3])
    ]

    sends = {}

    def gathered(kind):
        return packs_ref if kind == 0 else full_ref.at[kind - 1]

    def half_of(kind, part):
        return pl.ds(part * part_rows, part_rows)

    def piece_at(flow, piece):
        kind, part, _, _ = FLOWS[flow]
        px, py = lax.rem(x + piece[0], 2), lax.rem(y + piece[1], 2)
        return (
            gathered(kind).at[core, px, z + piece[2], py, half_of(kind, part)],
            (px * 2 + py) * DEPTH + z + piece[2],
        )

    def handle(flow, piece):
        kind, part, order, _ = FLOWS[flow]
        landed, index = piece_at(flow, piece)
        source = landed
        if piece == OWN:
            source = shards[kind].at[half_of(kind, part)]
        else:
            remote(landed, landed, send_sem.at[flow, 0], piece_recv.at[flow, index], place.sibling()).wait_recv()
        for axis, sign in forwards(order, piece):
            slot = {"x": 0, "y": 1, "z": 2 if sign > 0 else 3}[axis]
            copy = remote(
                source,
                landed,
                send_sem.at[flow, slot],
                piece_recv.at[flow, index],
                place.step(axis, sign),
            )
            if axis == "z":
                pl.when((z + sign >= 0) & (z + sign < DEPTH))(copy.start)
            else:
                copy.start()
                sends[flow, slot] = sends.get((flow, slot), 0) + 1
        remote(source, landed, sib_send.at[flow], sib_recv.at[flow], place.sibling()).start()

    def block_of(flow, pieces, plane):
        kind, part, _, _ = FLOWS[flow]
        nx = 2 if pieces % 2 == 0 else 1
        ny = 2 if pieces % 4 == 0 else 1
        return gathered(kind).at[
            plane,
            pl.ds(0, nx),
            pl.ds(0, pieces // (nx * ny)),
            pl.ds(0, ny),
            half_of(kind, part),
        ]

    def finish_flow(flow):
        order = FLOWS[flow][2]
        everything = block_of(flow, 4 * DEPTH, 1 - core)
        remote(everything, everything, sib_send.at[flow], sib_recv.at[flow], place.sibling()).wait()

    def finish_sends(flow):
        order = FLOWS[flow][2]
        for axis, slot in (("x", 0), ("y", 1)):
            block = block_of(flow, 2 ** order.index(axis) * (DEPTH // 2 if "z" in order[: order.index(axis)] else 1), core)
            remote(block, block, send_sem.at[flow, slot], sib_recv.at[flow], place.sibling()).wait_send()
        each = 2 ** order.index("z")
        for at in range(DEPTH):
            for slot, sets in ((2, at + 1 if at < DEPTH - 1 else 0), (3, DEPTH - at if at > 0 else 0)):
                if sets:

                    @pl.when(z == at)
                    def _(slot=slot, sets=sets):
                        nx = 2 if each > 1 else 1
                        ny = 2 if each > 2 else 1
                        kind, part, _, _ = FLOWS[flow]
                        block = gathered(kind).at[
                            core,
                            pl.ds(0, nx),
                            pl.ds(0, sets),
                            pl.ds(0, ny),
                            half_of(kind, part),
                        ]
                        remote(
                            block, block, send_sem.at[flow, slot], sib_recv.at[flow], place.sibling()
                        ).wait_send()

    across_copies, sibling_copies = row_copies[0::2], row_copies[1::2]
    for copy in sibling_copies + up_copies + own_copies:
        copy.start()

    def middle_devices(step):
        pl.when(middle_device)(step)

    @middle_devices
    def _():
        for copy in across_copies:
            copy.start()

    count_copies = [
        remote(
            count_ref, counts_ref.at[DEPTH], count_send.at[0], count_recv.at[0], place.step("y", 1)
        )
    ]
    count_copies[0].start()

    def pass_count():
        count_copies[0].wait_recv()
        counts_ref[z] = jnp.minimum(count_ref[...], counts_ref[DEPTH])
        for i, target in enumerate(column):
            copy = remote(
                counts_ref.at[z], counts_ref.at[z], count_send.at[1 + i], count_recv.at[1 + i], target
            )
            copy.start()
            count_copies.append(copy)

    outs = []

    far_owner = (1 - x) * 2 + 1 - core
    far_writes = []

    def write(source, target):
        copy = pltpu.make_async_copy(source, target, out_sem.at[len(outs)])
        copy.start()
        outs.append(copy)

    def block_of_rows(hbm, owner):
        return hbm.at[pl.ds(pl.multiple_of(owner * token_rows, token_rows), token_rows)]

    def write_rows(source, hbm, owner):
        write(source, block_of_rows(hbm, owner))

    def far_write(source, hbm):
        return pltpu.make_async_copy(
            source, block_of_rows(hbm, far_owner), far_sem.at[len(far_writes)]
        )

    def assemble(t):
        if t == 0:
            for copy in up_copies + own_copies[:3]:
                copy.wait()
            for copy in sibling_copies:
                copy.wait_recv()
            for at in range(2):
                write_rows(rows_ref.at[x * 2 + at], rows_hbm, x * 2 + at)
            far_writes.append(far_write(rows_ref.at[far_owner], rows_hbm))

            @middle_devices
            def _():
                for copy in across_copies:
                    copy.wait_recv()
                far_writes[0].start()

            finish_flow(0)
            finish_flow(1)
            for owner in range(4):
                ups_full[:, owner * slim : (owner + 1) * slim] = ups_all_ref[owner, :, :slim].astype(jnp.bfloat16)
        lanes = slice(t * slim, (t + 1) * slim)
        source = packs_ref.at[t % 2, t // 2]
        for kind, down_ref, first in ((0, down_q_ref, 0), (1, None, 0), (2, down_v_ref, 8), (3, None, 0)):
            part = source[:, :, :, kind * slim : (kind + 1) * slim].reshape(-1, slim)
            if down_ref is not None:
                up = ups_all_ref[t, first : first + 8, :slim].astype(jnp.bfloat16)
                product = dot_tn(down_ref[...], up)
                part = (part.astype(jnp.float32) + ADAPTER_SCALE * product).astype(jnp.bfloat16)
            weights_ref[kind, :, lanes] = part
        if t == 3:
            write(weights_ref, weights_hbm)

    def own_queries():
        q_ref[...] = dot_nn(rows_ref[x * 2 + core], weights_ref[0]).astype(jnp.bfloat16)
        write(q_ref, q_hbm)

    def keys_values(ref, hbm, kind, at):
        owner = x * 2 + at
        ref[at] = dot_nn(rows_ref[owner], weights_ref[kind]).astype(jnp.bfloat16)
        write_rows(ref.at[at], hbm, owner)

    def far_keys_values(ref, hbm, kind):
        far_writes.append(far_write(ref.at[2], hbm))
        at = len(far_writes) - 1

        @middle_devices
        def _():
            ref[2] = dot_nn(rows_ref[far_owner], weights_ref[kind]).astype(jnp.bfloat16)
            far_writes[at].start()

    steps = [functools.partial(assemble, t) for t in range(4)] + [own_queries]
    for at in range(2):
        steps.append(functools.partial(keys_values, k_ref, k_hbm, 1, at))
        steps.append(functools.partial(keys_values, v_ref, v_hbm, 2, at))
    steps.append(functools.partial(far_keys_values, k_ref, k_hbm, 1))
    steps.append(functools.partial(far_keys_values, v_ref, v_hbm, 2))

    events = event_order(8.5)
    last_pack = max(i for i, (flow, _) in enumerate(events) if FLOWS[flow][0] == 0)
    between = max(1, (len(events) - last_pack) // (len(steps) + 1))
    arrivals = 0
    for at, (flow, piece) in enumerate(events):
        if piece[2] == 0:
            handle(flow, piece)
        else:
            pl.when((z + piece[2] >= 0) & (z + piece[2] < DEPTH))(
                functools.partial(handle, flow, piece)
            )
        if piece != OWN:
            arrivals += 1
            if arrivals == 24:
                pass_count()
        if at >= last_pack and (at - last_pack) % between == between - 1 and steps:
            steps.pop(0)()
    for step in steps:
        step()

    for copy in sibling_copies:
        copy.wait_send()

    @middle_devices
    def _():
        for copy in across_copies:
            copy.wait_send()
        for copy in far_writes:
            copy.wait()

    for copy in own_copies[3:] + outs:
        copy.wait()
    for flow in range(len(FLOWS)):
        if flow > 1:
            finish_flow(flow)
        finish_sends(flow)
    for copy in count_copies[1:]:
        copy.wait()
    count_copies[0].wait_send()
    fewest_ref[0, 0] = jnp.min(counts_ref[0:DEPTH])


def gather_all(
    w_q, w_k, w_v, w_out, w_in, w_down_t, tokens, up_q, up_v, down_q_t, down_v_t, lengths
):
    shard_rows, width = w_in.shape
    token_rows = tokens.shape[0]
    bf16, f32 = jnp.bfloat16, jnp.float32
    slim = w_q.shape[1]
    padded = slim + -slim % 128
    flows = len(FLOWS)
    dma = pltpu.SemaphoreType.DMA
    grid = (2, 2, DEPTH, 2, shard_rows, width)
    return pl.pallas_call(
        gather_kernel,
        out_shape=(
            jax.ShapeDtypeStruct((2,) + grid, bf16),
            jax.ShapeDtypeStruct((4, width, width), bf16),
            jax.ShapeDtypeStruct((4 * token_rows, width), bf16),
            jax.ShapeDtypeStruct((token_rows, width), bf16),
            jax.ShapeDtypeStruct((4 * token_rows, width), bf16),
            jax.ShapeDtypeStruct((4 * token_rows, width), bf16),
            jax.ShapeDtypeStruct((16, width), bf16),
            jax.ShapeDtypeStruct((1, 1), f32),
        ),
        in_specs=[VMEM_SPEC] * 4 + [HBM_SPEC] * 3 + [VMEM_SPEC] * 5,
        out_specs=(HBM_SPEC,) * 6 + (VMEM_SPEC, SMEM_SPEC),
        scratch_shapes=[
            pltpu.VMEM((shard_rows, width), bf16),
            pltpu.VMEM(grid, bf16),
            pltpu.VMEM((4, token_rows, width), bf16),
            pltpu.VMEM((16, padded), f32),
            pltpu.VMEM((4, 16, padded), f32),
            pltpu.VMEM((4, width, width), bf16),
            pltpu.VMEM((token_rows, width), bf16),
            pltpu.VMEM((3, token_rows, width), bf16),
            pltpu.VMEM((3, token_rows, width), bf16),
            pltpu.VMEM((8, 128), f32),
            pltpu.VMEM((DEPTH + 1, 8, 128), f32),
            dma((DEPTH,)),
            dma((DEPTH,)),
            dma((flows, 4 * DEPTH)),
            dma((flows, 4)),
            dma((flows,)),
            dma((flows,)),
            dma((5,)),
            dma((3, 2)),
            dma((3, 2)),
            dma((3,)),
            dma((3,)),
            dma((14,)),
            dma((3,)),
        ],
        compiler_params=pltpu.CompilerParams(
            collective_id=1, has_side_effects=True, vmem_limit_bytes=VMEM_LIMIT
        ),
        name="gather_all",
    )(
        w_q,
        w_k,
        w_v,
        w_out,
        w_in,
        w_down_t,
        tokens,
        up_q,
        up_v,
        down_q_t,
        down_v_t,
        lengths,
    )


def project_kernel(
    order,
    full_hbm,
    rows_ref,
    ups_ref,
    downs_ref,
    weights_ref,
    q_ref,
    k_ref,
    v_ref,
    packs_ref,
    sems,
):
    token_rows = q_ref.shape[0]
    slim = packs_ref.shape[2] // 4
    tensor = lax.axis_index("tensor")
    copies = [
        pltpu.make_async_copy(full_hbm.at[0, i], packs_ref.at[i], sems.at[i])
        for i in range(len(order))
    ]
    for copy in copies:
        copy.start()
    for i, t in enumerate(order):
        copies[i].wait()
        lanes = slice(t * slim, (t + 1) * slim)
        for kind, first in ((0, 0), (1, None), (2, 8), (3, None)):
            part = packs_ref[i, :, kind * slim : (kind + 1) * slim]
            if first is not None:
                up = ups_ref[t, first : first + 8, :slim]
                product = dot_tn(downs_ref[first : first + 8, :], up)
                part = (part.astype(jnp.float32) + ADAPTER_SCALE * product).astype(jnp.bfloat16)
            weights_ref[kind, :, lanes] = part
    own = rows_ref[pl.ds(pl.multiple_of(tensor * token_rows, token_rows), token_rows), :]
    q_ref[...] = dot_nn(own, weights_ref[0]).astype(jnp.bfloat16)

    @pl.loop(0, rows_ref.shape[0] // token_rows)
    def _(at):
        window = pl.ds(pl.multiple_of(at * token_rows, token_rows), token_rows)
        block = rows_ref[window, :]
        k_ref[window, :] = dot_nn(block, weights_ref[1]).astype(jnp.bfloat16)
        v_ref[window, :] = dot_nn(block, weights_ref[2]).astype(jnp.bfloat16)


def project(order, full, rows_all, ups_all, downs, token_rows):
    total_rows, width = rows_all.shape
    bf16 = jnp.bfloat16
    return pl.pallas_call(
        functools.partial(project_kernel, order),
        out_shape=(
            jax.ShapeDtypeStruct((4, width, width), bf16),
            jax.ShapeDtypeStruct((token_rows, width), bf16),
            jax.ShapeDtypeStruct((total_rows, width), bf16),
            jax.ShapeDtypeStruct((total_rows, width), bf16),
        ),
        in_specs=[HBM_SPEC] + [VMEM_SPEC] * 3,
        out_specs=(VMEM_SPEC,) * 4,
        scratch_shapes=[
            pltpu.VMEM(full.shape[1:], bf16),
            pltpu.SemaphoreType.DMA((len(order),)),
        ],
        compiler_params=pltpu.CompilerParams(vmem_limit_bytes=VMEM_LIMIT),
        name="project",
    )(full, rows_all, ups_all, downs)


def middle_kernel(
    near_only,
    lengths_ref,
    fewest_ref,
    gain_attn_ref,
    shift_attn_ref,
    gain_ffn_ref,
    shift_ffn_ref,
    q_hbm,
    k_hbm,
    v_hbm,
    tokens_hbm,
    cot_hbm,
    weights_hbm,
    full_hbm,
    rows_hbm,
    wide_k_hbm,
    wide_v_hbm,
    wide_rows_hbm,
    ups_ref,
    down_q_ref,
    down_v_ref,
    mixed_hbm,
    grad_one_hbm,
    gq_hbm,
    gk_hbm,
    gv_hbm,
    far_hbm,
    sums_hbm,
    q_ref,
    k_ref,
    v_ref,
    tokens_ref,
    cot_ref,
    out_buf,
    in_buf,
    down_buf,
    slope_buf,
    first_buf,
    sum_buf,
    normed_buf,
    inverse_buf,
    ctx_ref,
    lse_ref,
    grad_ref,
    gk_acc,
    gv_acc,
    gk_out,
    gv_out,
    far_out,
    pair_buf,
    sums_ref,
    sums_low,
    load_sem,
    part_sem,
    kv_sem,
    store_sem,
    grad_sem,
    far_sem,
):
    rows, width = q_ref.shape
    total_rows = k_ref.shape[0]
    parts, kinds = in_buf.shape[0], full_hbm.shape[0]
    kv_blocks = total_rows // KV_BLOCK
    base = lax.axis_index("tensor") * rows
    wide = fewest_ref[0, 0] < total_rows // 2
    limit = jnp.where(wide, total_rows, jnp.minimum(base + 2 * rows, total_rows))

    span_low, span_high = jnp.int32(total_rows), jnp.int32(0)
    for at in range(rows // Q_BLOCK):
        low, steps = query_span(lengths_ref, base + at * Q_BLOCK, total_rows)
        span_low = jnp.minimum(span_low, jnp.minimum(low, limit - K_BLOCK))
        span_high = jnp.maximum(span_high, jnp.minimum(low + steps * K_BLOCK, limit))

    def kv_rows(block):
        return pl.ds(pl.multiple_of(block * KV_BLOCK, KV_BLOCK), KV_BLOCK)

    def touched(block):
        return (block * KV_BLOCK < span_high) & ((block + 1) * KV_BLOCK > span_low)

    def kv_copies(block, k_source=k_hbm, v_source=v_hbm):
        window = kv_rows(block)
        return (
            pltpu.make_async_copy(k_source.at[window], k_ref.at[window], kv_sem.at[0, block]),
            pltpu.make_async_copy(v_source.at[window], v_ref.at[window], kv_sem.at[1, block]),
        )

    def part_copies(part):
        return (
            pltpu.make_async_copy(
                full_hbm.at[kinds - 2, part], in_buf.at[part], part_sem.at[0, part]
            ),
            pltpu.make_async_copy(
                full_hbm.at[kinds - 1, part], down_buf.at[part], part_sem.at[1, part]
            ),
        )

    q_copy = pltpu.make_async_copy(q_hbm, q_ref, load_sem.at[0])
    tokens_copy = pltpu.make_async_copy(tokens_hbm, tokens_ref, load_sem.at[1])
    out_copy = pltpu.make_async_copy(weights_hbm.at[3], out_buf, load_sem.at[2])
    cot_copy = pltpu.make_async_copy(cot_hbm, cot_ref, load_sem.at[3])
    pair_copy = pltpu.make_async_copy(weights_hbm.at[pl.ds(1, 2)], pair_buf, load_sem.at[4])
    q_copy.start()

    @pl.loop(0, kv_blocks)
    def _(block):
        @pl.when(touched(block) & jnp.logical_not(wide))
        def _():
            for copy in kv_copies(block):
                copy.start()

        @pl.when(touched(block) & wide)
        def _():
            for copy in kv_copies(block, wide_k_hbm, wide_v_hbm):
                copy.start()

    gk_acc[...] = jnp.zeros_like(gk_acc)
    gv_acc[...] = jnp.zeros_like(gv_acc)
    q_copy.wait()

    @pl.loop(0, kv_blocks)
    def _(block):
        @pl.when(touched(block))
        def _():
            for copy in kv_copies(block):
                copy.wait()

    tokens_copy.start()
    out_copy.start()
    cot_copy.start()
    for part in range(parts):
        for copy in part_copies(part):
            copy.start()
    pair_copy.start()

    attend_forward(limit, lengths_ref, q_ref, k_ref, v_ref, ctx_ref, lse_ref)

    gain_attn, shift_attn, gain_ffn, shift_ffn = (
        ref[...].reshape(1, -1) for ref in (gain_attn_ref, shift_attn_ref, gain_ffn_ref, shift_ffn_ref)
    )
    tokens_copy.wait()
    out_copy.wait()
    sum_buf[...] = dot_nt(ctx_ref[...], out_buf[...])

    def each_norm_block(step):
        @pl.loop(0, rows // NORM_BLOCK)
        def _(at):
            step(pl.ds(pl.multiple_of(at * NORM_BLOCK, NORM_BLOCK), NORM_BLOCK))

    @each_norm_block
    def _(block):
        residual = tokens_ref[block, :].astype(jnp.float32) + sum_buf[block, :]
        first, normed, inverse = norm_forward(residual, gain_attn, shift_attn)
        first_buf[block, :] = first.astype(jnp.bfloat16)
        sum_buf[block, :] = first.astype(jnp.bfloat16).astype(jnp.float32)
        normed_buf[block, :] = normed
        inverse_buf[block, :] = inverse

    @pl.loop(0, parts)
    def _(part):
        for copy in part_copies(part):
            copy.wait()
        acted, slope = gelu_parts(dot_nn(first_buf[...], in_buf[part]))
        slope_buf[part] = slope
        sum_buf[...] += dot_nt(acted.astype(jnp.bfloat16), down_buf[part])

    cot_copy.wait()

    @each_norm_block
    def _(block):
        mixed, normed, inverse = norm_forward(sum_buf[block, :], gain_ffn, shift_ffn)
        tokens_ref[block, :] = mixed.astype(jnp.bfloat16)
        cotangents = cot_ref[block, :].astype(jnp.float32)
        grad_two = norm_backward(cotangents, normed, inverse, gain_ffn)
        first_buf[block, :] = grad_two.astype(jnp.bfloat16)
        sum_buf[block, :] = grad_two

    mixed_copy = pltpu.make_async_copy(tokens_ref, mixed_hbm, store_sem.at[0])
    mixed_copy.start()

    @pl.loop(0, parts)
    def _(part):
        grad_hidden = dot_nn(first_buf[...], down_buf[part]) * slope_buf[part]
        sum_buf[...] += dot_nt(grad_hidden.astype(jnp.bfloat16), in_buf[part])

    @each_norm_block
    def _(block):
        grad_one = norm_backward(
            sum_buf[block, :], normed_buf[block, :], inverse_buf[block, :], gain_attn
        )
        normed_buf[block, :] = grad_one
        first_buf[block, :] = grad_one.astype(jnp.bfloat16)

    grad_one_copy = pltpu.make_async_copy(normed_buf, grad_one_hbm, store_sem.at[1])
    grad_one_copy.start()
    grad_ref[...] = dot_nn(first_buf[...], out_buf[...]).astype(jnp.bfloat16)

    attend_backward(
        limit,
        lengths_ref,
        q_ref,
        k_ref,
        v_ref,
        ctx_ref,
        lse_ref,
        grad_ref,
        first_buf,
        gk_acc,
        gv_acc,
    )
    gq_copy = pltpu.make_async_copy(first_buf, gq_hbm, store_sem.at[2])
    gq_copy.start()

    def rows_copy(block, source=rows_hbm):
        window = kv_rows(block)
        return pltpu.make_async_copy(source.at[window], k_ref.at[window], kv_sem.at[0, block])

    @pl.loop(0, kv_blocks)
    def _(block):
        @pl.when(touched(block) & jnp.logical_not(wide))
        def _():
            rows_copy(block).start()

        @pl.when(touched(block) & wide)
        def _():
            rows_copy(block, wide_rows_hbm).start()

    def wanted(block):
        if not near_only:
            return block >= 0
        return block // (kv_blocks // 2) == lax.axis_index("tensor") // 2

    def grad_copies(block):
        window = kv_rows(block)
        return (
            pltpu.make_async_copy(gk_out.at[window], gk_hbm.at[window], grad_sem.at[0, block]),
            pltpu.make_async_copy(gv_out.at[window], gv_hbm.at[window], grad_sem.at[1, block]),
        )

    @pl.loop(0, kv_blocks)
    def _(block):
        window = kv_rows(block)

        @pl.when(touched(block))
        def _():
            gk_out[window, :] = (gk_acc[window, :] * SCORE_SCALE).astype(jnp.bfloat16)
            gv_out[window, :] = gv_acc[window, :].astype(jnp.bfloat16)

        @pl.when(jnp.logical_not(touched(block)))
        def _():
            gk_out[window, :] = jnp.zeros((KV_BLOCK, width), jnp.bfloat16)
            gv_out[window, :] = jnp.zeros((KV_BLOCK, width), jnp.bfloat16)

        @pl.when(wanted(block))
        def _():
            for copy in grad_copies(block):
                copy.start()

    def far_copy(at):
        window = kv_rows(at)
        return pltpu.make_async_copy(far_out.at[window], far_hbm.at[window], far_sem.at[at])

    pair_copy.wait()
    tensor = lax.axis_index("tensor")
    near = tensor // 2
    per_owner = rows // KV_BLOCK

    @pl.loop(0, kv_blocks // 2)
    def _(at):
        owner = (1 - near) * 2 + lax.rem(tensor + 1 + at // per_owner, 2)
        block = owner * per_owner + lax.rem(at, per_owner)
        source, target = kv_rows(block), kv_rows(at)

        @pl.when(touched(block))
        def _():
            far_out[target, :] = (
                dot_nt(gk_out[source, :], pair_buf[0]) + dot_nt(gv_out[source, :], pair_buf[1])
            ).astype(jnp.bfloat16)

        @pl.when(jnp.logical_not(touched(block)))
        def _():
            far_out[target, :] = jnp.zeros((KV_BLOCK, width), jnp.bfloat16)

        far_copy(at).start()

    def add_adapter(row_vals, grads, down, up, first_at, second_at):
        lifted = (ADAPTER_SCALE * dot_nt(row_vals, down)).astype(jnp.bfloat16)
        grad_lifted = (ADAPTER_SCALE * dot_nt(grads, up)).astype(jnp.bfloat16)
        sums_ref[first_at : first_at + 8, :] += dot_tn(grad_lifted, row_vals)
        sums_ref[second_at : second_at + 8, :] += dot_tn(lifted, grads)

    sums_ref[...] = jnp.zeros_like(sums_ref)

    @pl.loop(0, kv_blocks)
    def _(block):
        window = kv_rows(block)

        @pl.when(touched(block))
        def _():
            rows_copy(block).wait()
            add_adapter(k_ref[window, :], gv_out[window, :], down_v_ref[...], ups_ref[8:16, :], 8, 24)

    own = pl.ds(pl.multiple_of(base, rows), rows)
    add_adapter(k_ref[own, :], first_buf[...], down_q_ref[...], ups_ref[0:8, :], 0, 16)
    sums_low[...] = sums_ref[...].astype(jnp.bfloat16)
    sums_copy = pltpu.make_async_copy(sums_low, sums_hbm, store_sem.at[3])
    sums_copy.start()
    sums_copy.wait()

    @pl.loop(0, kv_blocks // 2)
    def _(at):
        far_copy(at).wait()

    for copy in (mixed_copy, grad_one_copy, gq_copy):
        copy.wait()

    @pl.loop(0, kv_blocks)
    def _(block):
        @pl.when(wanted(block))
        def _():
            for copy in grad_copies(block):
                copy.wait()


def middle(
    near_only,
    lengths,
    fewest,
    norms,
    q_own,
    k_all,
    v_all,
    wide_rows,
    tokens,
    cotangent,
    weights,
    full,
    rows_all,
    ups,
    downs,
):
    rows, width = q_own.shape
    total_rows = k_all.shape[0]
    parts = full.shape[1]
    bf16, f32 = jnp.bfloat16, jnp.float32
    slots = rows // Q_BLOCK * (width // PAIR)
    kv_blocks = total_rows // KV_BLOCK
    dma = pltpu.SemaphoreType.DMA
    return pl.pallas_call(
        functools.partial(middle_kernel, near_only),
        out_shape=(
            jax.ShapeDtypeStruct((rows, width), bf16),
            jax.ShapeDtypeStruct((rows, width), f32),
            jax.ShapeDtypeStruct((rows, width), bf16),
            jax.ShapeDtypeStruct((total_rows, width), bf16),
            jax.ShapeDtypeStruct((total_rows, width), bf16),
            jax.ShapeDtypeStruct((total_rows // 2, width), bf16),
            jax.ShapeDtypeStruct((32, width), bf16),
        ),
        in_specs=[SMEM_SPEC] * 2 + [VMEM_SPEC] * 4 + [HBM_SPEC] * 11 + [VMEM_SPEC] * 3,
        out_specs=(HBM_SPEC,) * 7,
        scratch_shapes=[
            pltpu.VMEM((rows, width), bf16),
            pltpu.VMEM((total_rows, width), bf16),
            pltpu.VMEM((total_rows, width), bf16),
            pltpu.VMEM((rows, width), bf16),
            pltpu.VMEM((rows, width), bf16),
            pltpu.VMEM((width, width), bf16),
            pltpu.VMEM(full.shape[1:], bf16),
            pltpu.VMEM(full.shape[1:], bf16),
            pltpu.VMEM((parts, rows, full.shape[3]), f32),
            pltpu.VMEM((rows, width), bf16),
            pltpu.VMEM((rows, width), f32),
            pltpu.VMEM((rows, width), f32),
            pltpu.VMEM((rows, 1), f32),
            pltpu.VMEM((rows, width), bf16),
            pltpu.VMEM((slots, 1, 2 * Q_BLOCK), f32),
            pltpu.VMEM((rows, width), bf16),
            pltpu.VMEM((total_rows, width), f32),
            pltpu.VMEM((total_rows, width), f32),
            pltpu.VMEM((total_rows, width), bf16),
            pltpu.VMEM((total_rows, width), bf16),
            pltpu.VMEM((total_rows // 2, width), bf16),
            pltpu.VMEM((2, width, width), bf16),
            pltpu.VMEM((32, width), f32),
            pltpu.VMEM((32, width), bf16),
            dma((5,)),
            dma((2, parts)),
            dma((2, kv_blocks)),
            dma((4,)),
            dma((2, kv_blocks)),
            dma((kv_blocks // 2,)),
        ],
        compiler_params=pltpu.CompilerParams(vmem_limit_bytes=VMEM_LIMIT),
        name="middle",
    )(
        lengths,
        fewest,
        *norms,
        q_own,
        k_all,
        v_all,
        tokens,
        cotangent,
        weights,
        full,
        rows_all,
        *wide_rows,
        ups,
        *downs,
    )


def final_kernel(
    reach,
    gq_hbm,
    gk_hbm,
    gv_hbm,
    far_hbm,
    weights_hbm,
    grad_one_hbm,
    part_sums,
    grad_tokens_ref,
    sums_ref,
    gq_ref,
    gk_ref,
    gv_ref,
    far_ref,
    weights_ref,
    grad_one_ref,
    from_sib,
    to_x,
    from_x,
    home_to,
    home_from,
    yc_slots,
    z_slots,
    xc_slots,
    load_sem,
    far_send,
    far_recv,
    block_send,
    block_recv,
    sum_send,
    sum_recv,
):
    place = Place()
    x, y, z, core = place.x, place.y, place.z, place.core
    token_rows = gq_ref.shape[0]
    half_rows = token_rows // 2
    chunk_rows = token_rows // FAR_CHUNKS
    bf16, f32 = jnp.bfloat16, jnp.float32
    loads = {}

    def load(name, source, target):
        copy = pltpu.make_async_copy(source, target, load_sem.at[len(loads)])
        copy.start()
        loads[name] = copy

    if reach:
        load("far", far_hbm.at[pl.ds(token_rows, token_rows)], far_ref)
    near_rows = pl.ds(pl.multiple_of(x * 2 * token_rows, token_rows), 2 * token_rows)
    load("k", gk_hbm.at[near_rows], gk_ref)
    load("v", gv_hbm.at[near_rows], gv_ref)
    load("w", weights_hbm.at[pl.ds(0, 3)], weights_ref)
    load("q", gq_hbm, gq_ref)
    load("one", grad_one_hbm, grad_one_ref)

    across = place.device(x=1 - x, core=1 - core)
    middle_device = x != core
    barrier = pltpu.get_barrier_semaphore()
    around = [place.step("y", 1), place.sibling(), place.device(y=1 - y, core=1 - core)]
    column = [place.device(z=lax.rem(z + i, DEPTH)) for i in range(1, DEPTH)]
    beside = [place.step("x", 1), across]
    for target in around + column + beside:
        pl.semaphore_signal(barrier, inc=1, device_id=target, device_id_type=MESH_ID)
    pl.semaphore_wait(barrier, len(around + column + beside))

    def remote(source, target, send, recv, device):
        return pltpu.make_async_remote_copy(
            src_ref=source,
            dst_ref=target,
            send_sem=send,
            recv_sem=recv,
            device_id=device,
            device_id_type=MESH_ID,
        )

    def started(*operands):
        copy = remote(*operands)
        copy.start()
        return copy

    chunks = [pl.ds(at * chunk_rows, chunk_rows) for at in range(FAR_CHUNKS)]
    kept = pl.ds(pl.multiple_of(core * 16, 16), 16)
    given = pl.ds(pl.multiple_of((1 - core) * 16, 16), 16)
    sum_copies = []

    def send_sum(source, target, device):
        at = len(sum_copies)
        sum_copies.append(started(source, target, sum_send.at[at], sum_recv.at[at], device))

    for source, device in zip((kept, given, given), around):
        send_sum(part_sums.at[source], yc_slots.at[y * 2 + core], device)
    yc_slots[y * 2 + core] = part_sums[kept, :]
    sib_copies, x_copies = [], []
    if reach:
        for at, chunk in enumerate(chunks):
            sib_copies.append(
                started(
                    far_hbm.at[chunk],
                    from_sib.at[chunk],
                    far_send.at[0, at],
                    far_recv.at[0, at],
                    place.sibling(),
                )
            )
    else:
        for at, chunk in enumerate(chunks):
            x_copies.append(
                remote(
                    far_hbm.at[chunk],
                    from_x.at[chunk],
                    far_send.at[1, at],
                    far_recv.at[1, at],
                    across,
                )
            )

        @pl.when(middle_device)
        def _():
            for copy in x_copies:
                copy.start()

        @pl.when(jnp.logical_not(middle_device))
        def _():
            from_x[...] = jnp.zeros_like(from_x)

    def slot_sum(slots, indices):
        result = slots[indices[0]].astype(f32)
        for i in indices[1:]:
            result = result + slots[i].astype(f32)
        return result

    if reach:
        loads["far"].wait()
        for at, chunk in enumerate(chunks):
            sib_copies[at].wait_recv()
            to_x[chunk, :] = (far_ref[chunk, :].astype(f32) + from_sib[chunk, :].astype(f32)).astype(
                bf16
            )
            x_copies.append(
                started(
                    to_x.at[chunk],
                    from_x.at[chunk],
                    far_send.at[1, at],
                    far_recv.at[1, at],
                    place.step("x", 1),
                )
            )

    for copy in sum_copies[0:3]:
        copy.wait_recv()
    z_slots[z] = slot_sum(yc_slots, range(4)).astype(bf16)
    for device in column:
        send_sum(z_slots.at[z], z_slots.at[z], device)

    def partial(owner, half):
        window = pl.ds(pl.multiple_of(owner * token_rows + half * half_rows, half_rows), half_rows)
        return dot_nt(gk_ref[window, :], weights_ref[1]) + dot_nt(gv_ref[window, :], weights_ref[2])

    for name in ("k", "v", "w"):
        loads[name].wait()
    home_copies = []
    for half in range(2):
        window = pl.ds(half * half_rows, half_rows)
        home_to[window, :] = partial(1 - core, half).astype(bf16)
        home_copies.append(
            started(
                home_to.at[window],
                home_from.at[window],
                block_send.at[half],
                block_recv.at[half],
                place.sibling(),
            )
        )

    for copy in sum_copies[3:]:
        copy.wait_recv()
    xc_slots[x * 2 + core] = slot_sum(z_slots, range(DEPTH)).astype(bf16)
    own_slot = xc_slots.at[x * 2 + core]
    for device in [place.sibling()] + beside:
        send_sum(own_slot, own_slot, device)
    for name in ("q", "one"):
        loads[name].wait()
    for half in range(2):
        window = pl.ds(half * half_rows, half_rows)
        grad_one_ref[window, :] += partial(core, half) + dot_nt(gq_ref[window, :], weights_ref[0])
    for copy in home_copies:
        copy.wait_recv()
    for at, chunk in enumerate(chunks):
        if reach:
            x_copies[at].wait_recv()
        else:
            pl.when(middle_device)(x_copies[at].wait_recv)
        grad_tokens_ref[chunk, :] = (
            grad_one_ref[chunk, :] + home_from[chunk, :].astype(f32) + from_x[chunk, :].astype(f32)
        ).astype(bf16)
    for copy in sum_copies[2 + DEPTH :]:
        copy.wait_recv()
    for half in range(2):
        sums_ref[half * 16 : half * 16 + 16, :] = slot_sum(xc_slots, (half, 2 + half))

    for copy in sib_copies + home_copies + sum_copies:
        copy.wait_send()
    for copy in x_copies:
        if reach:
            copy.wait_send()
        else:
            pl.when(middle_device)(copy.wait_send)


def final_sums(reach, grad_q, grad_k, grad_v, far_rows, weights, grad_one, sums):
    token_rows, width = grad_q.shape
    bf16, f32 = jnp.bfloat16, jnp.float32
    dma = pltpu.SemaphoreType.DMA
    block = pltpu.VMEM((token_rows, width), bf16)
    return pl.pallas_call(
        functools.partial(final_kernel, reach),
        out_shape=(
            jax.ShapeDtypeStruct((token_rows, width), bf16),
            jax.ShapeDtypeStruct((32, width), f32),
        ),
        in_specs=[HBM_SPEC] * 6 + [VMEM_SPEC],
        out_specs=(VMEM_SPEC,) * 2,
        scratch_shapes=[
            block,
            pltpu.VMEM((2 * token_rows, width), bf16),
            pltpu.VMEM((2 * token_rows, width), bf16),
            block,
            pltpu.VMEM((3, width, width), bf16),
            pltpu.VMEM((token_rows, width), f32),
            block,
            block,
            block,
            block,
            block,
            pltpu.VMEM((4, 16, width), bf16),
            pltpu.VMEM((DEPTH, 16, width), bf16),
            pltpu.VMEM((4, 16, width), bf16),
            dma((6,)),
            dma((2, FAR_CHUNKS)),
            dma((2, FAR_CHUNKS)),
            dma((2,)),
            dma((2,)),
            dma((DEPTH + 5,)),
            dma((DEPTH + 5,)),
        ],
        compiler_params=pltpu.CompilerParams(
            collective_id=2 if reach else 3, has_side_effects=True, vmem_limit_bytes=VMEM_LIMIT
        ),
        name="final_sums_wide" if reach else "final_sums",
    )(grad_q, grad_k, grad_v, far_rows, weights, grad_one, sums)


def no_rows_kernel(*refs):
    del refs


def no_rows(tokens, weights):
    shape = jax.ShapeDtypeStruct((4 * tokens.shape[0], tokens.shape[1]), tokens.dtype)
    return pl.pallas_call(
        no_rows_kernel, out_shape=(shape,) * 3, out_specs=(HBM_SPEC,) * 3, name="no_rows"
    )()


def hand_out_kernel(grad_ref, sums_ref, grad_out, aq_ref, av_ref, bq_ref, bv_ref):
    grad_out[...] = grad_ref[...]
    slim = bq_ref.shape[1]
    aq_ref[...] = sums_ref[0:8, :]
    av_ref[...] = sums_ref[8:16, :]
    for t in range(sums_ref.shape[1] // slim):

        @pl.when(lax.axis_index("tensor") == t)
        def _(t=t):
            bq_ref[...] = sums_ref[16:24, t * slim : (t + 1) * slim]
            bv_ref[...] = sums_ref[24:32, t * slim : (t + 1) * slim]


def hand_out(grad_tokens, sums, slim):
    f32, width = jnp.float32, sums.shape[1]
    return pl.pallas_call(
        hand_out_kernel,
        out_shape=(
            jax.ShapeDtypeStruct(grad_tokens.shape, grad_tokens.dtype),
            jax.ShapeDtypeStruct((8, width), f32),
            jax.ShapeDtypeStruct((8, width), f32),
            jax.ShapeDtypeStruct((8, slim), f32),
            jax.ShapeDtypeStruct((8, slim), f32),
        ),
        in_specs=[VMEM_SPEC] * 2,
        out_specs=(VMEM_SPEC,) * 5,
        name="hand_out",
    )(grad_tokens, sums)


def local(
    fast,
    tokens,
    query_weight,
    w_key,
    value_weight,
    w_out,
    w_in,
    w_down,
    gain_attn,
    shift_attn,
    gain_ffn,
    shift_ffn,
    query_down_factor,
    query_up_factor,
    value_down_factor,
    value_up_factor,
    lengths,
    cotangent,
):
    slim = query_weight.shape[1]
    width = tokens.shape[1]
    token_rows = tokens.shape[0]
    down_q_t, down_v_t = query_down_factor.T, value_down_factor.T
    if fast:
        full, weights, rows_all, q_own, k_all, v_all, ups_full, fewest = gather_all(
            query_weight,
            w_key,
            value_weight,
            w_out,
            w_in,
            w_down.T,
            tokens,
            query_up_factor,
            value_up_factor,
            down_q_t,
            down_v_t,
            lengths,
        )
        full = full.reshape(2, 4, width, width)
    else:
        attn_pack = jnp.concatenate([query_weight, w_key, value_weight, w_out.T], axis=1)
        full = jnp.stack([attn_pack, w_in, w_down.T])
        full = lax.all_gather(full, "dp", axis=1, tiled=True)
        full = lax.all_gather(full, "tensor", axis=1)
        rows_all = lax.all_gather(tokens, "tensor").reshape(-1, width)
        ups = jnp.concatenate([query_up_factor, value_up_factor], axis=0)
        ups = jnp.pad(ups, ((0, 0), (0, -slim % 128)))
        ups_all = lax.all_gather(ups, "tensor")
        downs = jnp.concatenate([down_q_t, down_v_t], axis=0)
        ups_full = ups_all[:, :, :slim].transpose(1, 0, 2).reshape(16, width)
        order = tuple(range(full.shape[1]))
        weights, q_own, k_all, v_all = project(order, full, rows_all, ups_all, downs, token_rows)

    norms = (gain_attn, shift_attn, gain_ffn, shift_ffn)
    downs_t = (down_q_t, down_v_t)
    if fast:

        def either(near, wide, *operands):
            return lax.cond(fewest[0, 0] >= rows_all.shape[0] // 2, near, wide, *operands)

        def wide_rows(tokens, weights):
            me = lax.axis_index("tensor")
            rows_all = jnp.zeros((4 * token_rows, width), tokens.dtype)
            for away in range(4):
                block = tokens
                if away:
                    block = lax.ppermute(tokens, "tensor", [(i, i ^ away) for i in range(4)])
                first_row = (me ^ away) * token_rows
                rows_all = lax.dynamic_update_slice_in_dim(rows_all, block, first_row, 0)
            k_all = dot_nn(rows_all, weights[1]).astype(jnp.bfloat16)
            v_all = dot_nn(rows_all, weights[2]).astype(jnp.bfloat16)
            return (k_all, v_all, rows_all)

        mixed, grad_one, grad_q, grad_k, grad_v, far_rows, sums = middle(
            True,
            lengths,
            fewest,
            norms,
            q_own,
            k_all,
            v_all,
            either(no_rows, wide_rows, tokens, weights),
            tokens,
            cotangent,
            weights,
            full,
            rows_all,
            ups_full,
            downs_t,
        )
        grad_tokens, sums = either(
            functools.partial(final_sums, False),
            functools.partial(final_sums, True),
            *(grad_q, grad_k, grad_v, far_rows, weights, grad_one, sums),
        )
        grad_tokens, grad_aq, grad_av, grad_bq, grad_bv = hand_out(grad_tokens, sums, slim)
        return (mixed, grad_tokens, grad_aq.T, grad_bq, grad_av.T, grad_bv)

    mixed, grad_one, grad_q, grad_k, grad_v, far_rows, sums = middle(
        False,
        lengths,
        jnp.zeros((1, 1), jnp.float32),
        norms,
        q_own,
        k_all,
        v_all,
        (k_all, v_all, rows_all),
        tokens,
        cotangent,
        weights,
        full,
        rows_all,
        ups_full,
        downs_t,
    )
    grad_rows = dot_nt(grad_k, weights[1]) + dot_nt(grad_v, weights[2])
    shared = lax.psum_scatter(
        grad_rows.astype(jnp.bfloat16), "tensor", scatter_dimension=0, tiled=True
    )
    own_rows = dot_nt(grad_q, weights[0])
    grad_tokens = (grad_one + own_rows + shared.astype(jnp.float32)).astype(jnp.bfloat16)
    sums = lax.psum(sums.astype(jnp.float32), ("dp", "tensor"))
    at = lax.axis_index("tensor") * slim
    grad_bq = lax.dynamic_slice_in_dim(sums[16:24], at, slim, 1)
    grad_bv = lax.dynamic_slice_in_dim(sums[24:32], at, slim, 1)
    return (mixed, grad_tokens, sums[0:8].T, grad_bq, sums[8:16].T, grad_bv)


def solution(mesh):
    fast = dict(mesh.shape) == {"dp": 2 * DEPTH, "tensor": 4}
    return jax.shard_map(
        functools.partial(local, fast),
        mesh=mesh,
        in_specs=(
            P(("dp", "tensor"), None),
            P("dp", "tensor"),
            P("dp", "tensor"),
            P("dp", "tensor"),
            P("tensor", "dp"),
            P("dp", "tensor"),
            P("tensor", "dp"),
            P(),
            P(),
            P(),
            P(),
            P(),
            P(None, "tensor"),
            P(),
            P(None, "tensor"),
            P("dp", None),
            P(("dp", "tensor"), None),
        ),
        out_specs=(
            P(("dp", "tensor"), None),
            P(("dp", "tensor"), None),
            P(),
            P(None, "tensor"),
            P(),
            P(None, "tensor"),
        ),
        check_vma=False,
    )
```

```python
import functools
import heapq

import jax
import jax.numpy as jnp
from jax import lax
from jax.experimental import pallas as pl
from jax.experimental.pallas import tpu as pltpu
from jax.sharding import PartitionSpec as P

HEAD_DIM = 64
PAIR = 2 * HEAD_DIM
Q_BLOCK = 256
K_BLOCK = 512
KV_BLOCK = 256
NORM_BLOCK = 512
FAR_CHUNKS = 2
FORWARD_GROUP = 6
BACKWARD_GROUP = 3
ADAPTER_SCALE = 2.0
SCORE_SCALE = HEAD_DIM ** (-0.5)
LOG2_SCALE = SCORE_SCALE * 1.4426950408889634
NEG_FILL = -1e30
LN_EPS = 1e-05
VMEM_LIMIT = 60 * 1024 * 1024


def dot_nn(left, right):
    return jnp.dot(left, right, preferred_element_type=jnp.float32)


def dot_nt(left, right):
    return lax.dot_general(
        left, right, (((1,), (1,)), ((), ())), preferred_element_type=jnp.float32
    )


def dot_tn(left, right):
    return lax.dot_general(
        left, right, (((0,), (0,)), ((), ())), preferred_element_type=jnp.float32
    )


def norm_forward(row_vals, gain_vals, offset):
    middle = jnp.mean(row_vals, axis=-1, keepdims=True)
    centred = row_vals - middle
    inverse = lax.rsqrt(jnp.mean(centred * centred, axis=-1, keepdims=True) + LN_EPS)
    normed = centred * inverse
    return (normed * gain_vals + offset, normed, inverse)


def norm_backward(grad_out, normed, inverse, gain_vals):
    grad_n = grad_out * gain_vals
    return inverse * (
        grad_n
        - jnp.mean(grad_n, axis=-1, keepdims=True)
        - normed * jnp.mean(grad_n * normed, axis=-1, keepdims=True)
    )


def gelu_parts(hidden):
    cdf_part = 0.5 * (1.0 + lax.erf(hidden * 0.7071067811865476))
    density = jnp.exp(-0.5 * hidden * hidden) * 0.3989422804014327
    return (hidden * cdf_part, cdf_part + hidden * density)


def block_span(lengths_ref, first_row, rows, total_rows):
    last_row = first_row + rows - 1

    def slot_step(slot, carry):
        end, low, high = carry
        end = end + lengths_ref[0, slot]
        low = jnp.where(end <= first_row, jnp.maximum(low, end), low)
        high = jnp.where(end > last_row, jnp.minimum(high, end), high)
        return end, low, high

    start = (jnp.int32(0), jnp.int32(0), jnp.int32(total_rows))
    _, low, high = lax.fori_loop(0, lengths_ref.shape[1], slot_step, start, unroll=8)
    return low, high


def row_bounds(lengths_ref, first_row, rows, total_rows):
    place = first_row + lax.broadcasted_iota(jnp.int32, (1, rows), 1)

    def slot_step(slot, carry):
        end, begin, finish = carry
        end = end + lengths_ref[0, slot]
        done = place >= end
        begin = jnp.where(done, jnp.maximum(begin, end), begin)
        finish = jnp.where(done, finish, jnp.minimum(finish, end))
        return end, begin, finish

    start = (
        jnp.int32(0),
        jnp.zeros((1, rows), jnp.int32),
        jnp.full((1, rows), total_rows, jnp.int32),
    )
    _, begin, finish = lax.fori_loop(0, lengths_ref.shape[1], slot_step, start, unroll=8)
    return begin, finish


def stack_pair(block):
    lane = lax.broadcasted_iota(jnp.int32, block.shape, 1)
    zero = jnp.zeros_like(block)
    return jnp.concatenate(
        [jnp.where(lane < HEAD_DIM, block, zero), jnp.where(lane >= HEAD_DIM, block, zero)],
        axis=0,
    )


def unstack_pair(block, rows):
    joined = jnp.concatenate([block[:HEAD_DIM, :rows], block[HEAD_DIM:, rows:]], axis=0)
    return joined.T


def window_mask(step, low, begin, finish, limit):
    wanted = low + step * K_BLOCK
    start = pl.multiple_of(jnp.minimum(wanted, limit - K_BLOCK), 16)
    key_at = start + lax.broadcasted_iota(jnp.int32, (K_BLOCK, begin.shape[1]), 0)
    return start, (key_at >= jnp.maximum(begin, wanted)) & (key_at < finish)


def query_span(lengths_ref, first_row, total_rows):
    low, high = block_span(lengths_ref, first_row, Q_BLOCK, total_rows)
    low = (low // 16) * 16
    return low, (high - low + K_BLOCK - 1) // K_BLOCK


def each_q_block(lengths_ref, rows, total_rows, group, heads_width, block_step):
    base = lax.axis_index("tensor") * rows

    @pl.loop(0, rows // Q_BLOCK)
    def _(q_at):
        first_row = base + q_at * Q_BLOCK
        low, steps = query_span(lengths_ref, first_row, total_rows)
        begin, finish = row_bounds(lengths_ref, first_row, Q_BLOCK, total_rows)
        q_rows = pl.ds(pl.multiple_of(q_at * Q_BLOCK, Q_BLOCK), Q_BLOCK)

        @pl.loop(0, heads_width // PAIR // group)
        def _(at):
            pairs = [at * group + i for i in range(group)]
            lanes = [pl.ds(pl.multiple_of(pair * PAIR, PAIR), PAIR) for pair in pairs]
            slots = [q_at * (heads_width // PAIR) + pair for pair in pairs]
            block_step(q_rows, lanes, slots, low, steps, begin, finish)


def attend_forward(limit, lengths_ref, q_ref, k_ref, v_ref, out_ref, lse_ref):
    total_rows = k_ref.shape[0]

    def block_step(q_rows, lanes, slots, low, steps, begin, finish):
        q_two = [stack_pair(q_ref[q_rows, lane]) for lane in lanes]

        def body(step, carry):
            start, allowed = window_mask(step, low, begin, finish, limit)
            window = pl.ds(start, K_BLOCK)
            both = jnp.concatenate([allowed, allowed], axis=1)
            result = []
            for (top, total, acc), q_pair, lane in zip(carry, q_two, lanes):
                scores = jnp.where(both, dot_nt(k_ref[window, lane], q_pair), NEG_FILL)
                new_top = jnp.maximum(top, jnp.max(scores, axis=0, keepdims=True))
                probs = jnp.exp2((scores - new_top) * LOG2_SCALE)
                shrink = jnp.exp2((top - new_top) * LOG2_SCALE)
                total = total * shrink + jnp.sum(probs, axis=0, keepdims=True)
                acc = acc * shrink + dot_tn(v_ref[window, lane], probs.astype(jnp.bfloat16))
                result.append((new_top, total, acc))
            return tuple(result)

        empty = (
            jnp.full((1, 2 * Q_BLOCK), NEG_FILL, jnp.float32),
            jnp.zeros((1, 2 * Q_BLOCK), jnp.float32),
            jnp.zeros((PAIR, 2 * Q_BLOCK), jnp.float32),
        )
        final = lax.fori_loop(0, steps, body, (empty,) * len(lanes))
        for (top, total, acc), lane, slot in zip(final, lanes, slots):
            out_ref[q_rows, lane] = unstack_pair(acc / total, Q_BLOCK).astype(jnp.bfloat16)
            lse_ref[slot] = top * LOG2_SCALE + jnp.log2(total)

    each_q_block(
        lengths_ref, q_ref.shape[0], total_rows, FORWARD_GROUP, q_ref.shape[1], block_step
    )


def attend_backward(
    limit, lengths_ref, q_ref, k_ref, v_ref, ctx_ref, lse_ref, grad_ref, gq_ref, gk_acc, gv_acc
):
    total_rows = k_ref.shape[0]

    def block_step(q_rows, lanes, slots, low, steps, begin, finish):
        ready = []
        for lane, slot in zip(lanes, slots):
            grads = grad_ref[q_rows, lane]
            product = (grads.astype(jnp.float32) * ctx_ref[q_rows, lane].astype(jnp.float32)).T
            row_dot = jnp.concatenate(
                [
                    jnp.sum(product[:HEAD_DIM], axis=0, keepdims=True),
                    jnp.sum(product[HEAD_DIM:], axis=0, keepdims=True),
                ],
                axis=1,
            )
            ready.append((stack_pair(q_ref[q_rows, lane]), stack_pair(grads), row_dot, lse_ref[slot]))

        def body(step, carry):
            start, allowed = window_mask(step, low, begin, finish, limit)
            window = pl.ds(start, K_BLOCK)
            both = jnp.concatenate([allowed, allowed], axis=1)
            result = []
            for acc, (q_pair, grad_pair, row_dot, lse), lane in zip(carry, ready, lanes):
                keys = k_ref[window, lane]
                scores = jnp.where(both, dot_nt(keys, q_pair), NEG_FILL)
                probs = jnp.exp2(scores * LOG2_SCALE - lse)
                grad_probs = dot_nt(v_ref[window, lane], grad_pair)
                grad_scores = (probs * (grad_probs - row_dot)).astype(jnp.bfloat16)
                gk_acc[window, lane] += dot_nn(grad_scores, q_pair)
                gv_acc[window, lane] += dot_nn(probs.astype(jnp.bfloat16), grad_pair)
                result.append(acc + dot_tn(keys, grad_scores))
            return tuple(result)

        zero = jnp.zeros((PAIR, 2 * Q_BLOCK), jnp.float32)
        final = lax.fori_loop(0, steps, body, (zero,) * len(lanes))
        for acc, lane in zip(final, lanes):
            gq_ref[q_rows, lane] = (unstack_pair(acc, Q_BLOCK) * SCORE_SCALE).astype(jnp.bfloat16)

    each_q_block(
        lengths_ref, q_ref.shape[0], total_rows, BACKWARD_GROUP, q_ref.shape[1], block_step
    )


VMEM_SPEC = pl.BlockSpec(memory_space=pltpu.VMEM)
HBM_SPEC = pl.BlockSpec(memory_space=pltpu.HBM)
SMEM_SPEC = pl.BlockSpec(memory_space=pltpu.SMEM)


MESH_ID = pl.DeviceIdType.MESH
DEPTH = 4
FULL_ROWS = 96

FLOWS = (
    (0, 0, "zyx", 0.0),
    (0, 1, "zxy", 0.0),
    (1, 0, "zxy", 16.0),
    (1, 1, "xyz", 12.0),
    (2, 0, "yzx", 12.0),
    (2, 1, "xzy", 4.0),
)
OWN = (0, 0, 0)


def forwards(order, piece):
    used = [axis for axis in order if piece["xyz".index(axis)] != 0]
    at = order.index(used[-1]) if used else -1
    steps = []
    if used and used[-1] == "z":
        steps.append(("z", 1 if piece[2] < 0 else -1))
    for axis in order[at + 1 :]:
        steps += [("z", 1), ("z", -1)] if axis == "z" else [(axis, 1)]
    return steps


def passed(piece, axis, sign):
    x, y, z = piece
    if axis == "x":
        return (1 - x, y, z)
    return (x, 1 - y, z) if axis == "y" else (x, y, z - sign)


def event_order(token_time):
    per_piece = 1.7
    links, heap, times, count = {}, [], {}, 0
    for z in range(DEPTH):
        links[z, "x", 1] = token_time
        for flow, (_, _, _, start) in enumerate(FLOWS):
            heapq.heappush(heap, (start + 0.01 * flow, count, z, flow, OWN))
            count += 1
    while heap:
        now, _, z, flow, piece = heapq.heappop(heap)
        times.setdefault((flow, piece), []).append(now)
        for axis, sign in forwards(FLOWS[flow][2], piece):
            there = z + sign if axis == "z" else z
            if not 0 <= there < DEPTH:
                continue
            end = max(links.get((z, axis, sign), 0.0), now) + per_piece
            links[z, axis, sign] = end
            heapq.heappush(heap, (end + 3.0, count, there, flow, passed(piece, axis, sign)))
            count += 1
    return [key for _, key in sorted((sum(v) / len(v), key) for key, v in times.items())]


class Place:
    def __init__(self):
        dp, tensor = lax.axis_index("dp"), lax.axis_index("tensor")
        self.z, self.y = dp // 2, lax.rem(dp, 2)
        self.x, self.core = tensor // 2, lax.rem(tensor, 2)

    def device(self, x=None, y=None, z=None, core=None):
        x = self.x if x is None else x
        y = self.y if y is None else y
        z = self.z if z is None else z
        core = self.core if core is None else core
        return (z * 2 + y, x * 2 + core)

    def step(self, axis, sign):
        if axis == "x":
            return self.device(x=1 - self.x)
        return self.device(y=1 - self.y) if axis == "y" else self.device(z=self.z + sign)

    def sibling(self):
        return self.device(core=1 - self.core)


def gather_kernel(
    wq_ref,
    wk_ref,
    wv_ref,
    wo_ref,
    w_in_ref,
    w_down_ref,
    tokens_ref,
    up_q_ref,
    up_v_ref,
    down_q_ref,
    down_v_ref,
    lengths_ref,
    full_ref,
    weights_hbm,
    rows_hbm,
    q_hbm,
    k_hbm,
    v_hbm,
    ups_full,
    fewest_ref,
    pack_ref,
    packs_ref,
    rows_ref,
    ups_ref,
    ups_all_ref,
    weights_ref,
    q_ref,
    k_ref,
    v_ref,
    count_ref,
    counts_ref,
    count_send,
    count_recv,
    piece_recv,
    send_sem,
    sib_send,
    sib_recv,
    own_sem,
    rows_send,
    rows_recv,
    ups_send,
    ups_recv,
    out_sem,
    far_sem,
):
    place = Place()
    x, y, z, core = place.x, place.y, place.z, place.core
    token_rows = tokens_ref.shape[0]
    part_rows = FULL_ROWS // 2
    half_rows = token_rows // 2

    across = place.device(x=1 - x, core=1 - core)
    middle_device = x != core
    barrier = pltpu.get_barrier_semaphore()
    others = (
        place.sibling(),
        place.step("x", 1),
        across,
        place.step("y", 1),
    )
    for target in others:
        pl.semaphore_signal(barrier, inc=1, device_id=target, device_id_type=MESH_ID)
    column = [place.device(z=lax.rem(z + i, DEPTH)) for i in range(1, DEPTH)]
    for target in column:
        pl.semaphore_signal(barrier, inc=1, device_id=target, device_id_type=MESH_ID)

    slim = wq_ref.shape[1]
    for kind, ref in enumerate((wq_ref, wk_ref, wv_ref)):
        pack_ref[:, kind * slim : (kind + 1) * slim] = ref[...]
    pack_ref[:, 3 * slim : 4 * slim] = wo_ref[...].astype(jnp.float32).T.astype(jnp.bfloat16)
    ups_ref[...] = jnp.zeros_like(ups_ref)
    ups_ref[0:8, :slim] = up_q_ref[...].astype(jnp.float32)
    ups_ref[8:16, :slim] = up_v_ref[...].astype(jnp.float32)
    count_ref[...] = jnp.broadcast_to(
        jnp.sum(lengths_ref[...].astype(jnp.float32), axis=1, keepdims=True), count_ref.shape
    )
    shards = (pack_ref, w_in_ref, w_down_ref)
    pl.semaphore_wait(barrier, len(others) + len(column))

    def remote(source, target, send, recv, device):
        return pltpu.make_async_remote_copy(
            src_ref=source,
            dst_ref=target,
            send_sem=send,
            recv_sem=recv,
            device_id=device,
            device_id_type=MESH_ID,
        )

    def rows_at(owner_x, owner_core, half):
        return rows_ref.at[owner_x * 2 + owner_core, pl.ds(half * half_rows, half_rows)]

    own_copies = [
        pltpu.make_async_copy(pack_ref, packs_ref.at[core, x, z, y], own_sem.at[0]),
        pltpu.make_async_copy(tokens_ref, rows_ref.at[x * 2 + core], own_sem.at[1]),
        pltpu.make_async_copy(ups_ref, ups_all_ref.at[x * 2 + core], own_sem.at[2]),
        pltpu.make_async_copy(w_in_ref, full_ref.at[0, core, x, z, y], own_sem.at[3]),
        pltpu.make_async_copy(w_down_ref, full_ref.at[1, core, x, z, y], own_sem.at[4]),
    ]
    row_copies = []
    for half in range(2):
        source = tokens_ref.at[pl.ds(half * half_rows, half_rows)]
        for slot, device in ((0, across), (1, place.sibling())):
            row_copies.append(
                remote(
                    source,
                    rows_at(x, core, half),
                    rows_send.at[slot, half],
                    rows_recv.at[slot, half],
                    device,
                )
            )
    up_copies = [
        remote(ups_ref, ups_all_ref.at[x * 2 + core], ups_send.at[i], ups_recv.at[i], device)
        for i, device in enumerate(others[:3])
    ]

    sends = {}

    def gathered(kind):
        return packs_ref if kind == 0 else full_ref.at[kind - 1]

    def half_of(kind, part):
        return pl.ds(part * part_rows, part_rows)

    def piece_at(flow, piece):
        kind, part, _, _ = FLOWS[flow]
        px, py = lax.rem(x + piece[0], 2), lax.rem(y + piece[1], 2)
        return (
            gathered(kind).at[core, px, z + piece[2], py, half_of(kind, part)],
            (px * 2 + py) * DEPTH + z + piece[2],
        )

    def handle(flow, piece):
        kind, part, order, _ = FLOWS[flow]
        landed, index = piece_at(flow, piece)
        source = landed
        if piece == OWN:
            source = shards[kind].at[half_of(kind, part)]
        else:
            remote(landed, landed, send_sem.at[flow, 0], piece_recv.at[flow, index], place.sibling()).wait_recv()
        for axis, sign in forwards(order, piece):
            slot = {"x": 0, "y": 1, "z": 2 if sign > 0 else 3}[axis]
            copy = remote(
                source,
                landed,
                send_sem.at[flow, slot],
                piece_recv.at[flow, index],
                place.step(axis, sign),
            )
            if axis == "z":
                pl.when((z + sign >= 0) & (z + sign < DEPTH))(copy.start)
            else:
                copy.start()
                sends[flow, slot] = sends.get((flow, slot), 0) + 1
        remote(source, landed, sib_send.at[flow], sib_recv.at[flow], place.sibling()).start()

    def block_of(flow, pieces, plane):
        kind, part, _, _ = FLOWS[flow]
        nx = 2 if pieces % 2 == 0 else 1
        ny = 2 if pieces % 4 == 0 else 1
        return gathered(kind).at[
            plane,
            pl.ds(0, nx),
            pl.ds(0, pieces // (nx * ny)),
            pl.ds(0, ny),
            half_of(kind, part),
        ]

    def finish_flow(flow):
        order = FLOWS[flow][2]
        everything = block_of(flow, 4 * DEPTH, 1 - core)
        remote(everything, everything, sib_send.at[flow], sib_recv.at[flow], place.sibling()).wait()

    def finish_sends(flow):
        order = FLOWS[flow][2]
        for axis, slot in (("x", 0), ("y", 1)):
            block = block_of(flow, 2 ** order.index(axis) * (DEPTH // 2 if "z" in order[: order.index(axis)] else 1), core)
            remote(block, block, send_sem.at[flow, slot], sib_recv.at[flow], place.sibling()).wait_send()
        each = 2 ** order.index("z")
        for at in range(DEPTH):
            for slot, sets in ((2, at + 1 if at < DEPTH - 1 else 0), (3, DEPTH - at if at > 0 else 0)):
                if sets:

                    @pl.when(z == at)
                    def _(slot=slot, sets=sets):
                        nx = 2 if each > 1 else 1
                        ny = 2 if each > 2 else 1
                        kind, part, _, _ = FLOWS[flow]
                        block = gathered(kind).at[
                            core,
                            pl.ds(0, nx),
                            pl.ds(0, sets),
                            pl.ds(0, ny),
                            half_of(kind, part),
                        ]
                        remote(
                            block, block, send_sem.at[flow, slot], sib_recv.at[flow], place.sibling()
                        ).wait_send()

    across_copies, sibling_copies = row_copies[0::2], row_copies[1::2]
    for copy in sibling_copies + up_copies + own_copies:
        copy.start()

    def middle_devices(step):
        pl.when(middle_device)(step)

    @middle_devices
    def _():
        for copy in across_copies:
            copy.start()

    count_copies = [
        remote(
            count_ref, counts_ref.at[DEPTH], count_send.at[0], count_recv.at[0], place.step("y", 1)
        )
    ]
    count_copies[0].start()

    def pass_count():
        count_copies[0].wait_recv()
        counts_ref[z] = jnp.minimum(count_ref[...], counts_ref[DEPTH])
        for i, target in enumerate(column):
            copy = remote(
                counts_ref.at[z], counts_ref.at[z], count_send.at[1 + i], count_recv.at[1 + i], target
            )
            copy.start()
            count_copies.append(copy)

    outs = []

    far_owner = (1 - x) * 2 + 1 - core
    far_writes = []

    def write(source, target):
        copy = pltpu.make_async_copy(source, target, out_sem.at[len(outs)])
        copy.start()
        outs.append(copy)

    def block_of_rows(hbm, owner):
        return hbm.at[pl.ds(pl.multiple_of(owner * token_rows, token_rows), token_rows)]

    def write_rows(source, hbm, owner):
        write(source, block_of_rows(hbm, owner))

    def far_write(source, hbm):
        return pltpu.make_async_copy(
            source, block_of_rows(hbm, far_owner), far_sem.at[len(far_writes)]
        )

    def assemble(t):
        if t == 0:
            for copy in up_copies + own_copies[:3]:
                copy.wait()
            for copy in sibling_copies:
                copy.wait_recv()
            for at in range(2):
                write_rows(rows_ref.at[x * 2 + at], rows_hbm, x * 2 + at)
            far_writes.append(far_write(rows_ref.at[far_owner], rows_hbm))

            @middle_devices
            def _():
                for copy in across_copies:
                    copy.wait_recv()
                far_writes[0].start()

            finish_flow(0)
            finish_flow(1)
            for owner in range(4):
                ups_full[:, owner * slim : (owner + 1) * slim] = ups_all_ref[owner, :, :slim].astype(jnp.bfloat16)
        lanes = slice(t * slim, (t + 1) * slim)
        source = packs_ref.at[t % 2, t // 2]
        for kind, down_ref, first in ((0, down_q_ref, 0), (1, None, 0), (2, down_v_ref, 8), (3, None, 0)):
            part = source[:, :, :, kind * slim : (kind + 1) * slim].reshape(-1, slim)
            if down_ref is not None:
                up = ups_all_ref[t, first : first + 8, :slim].astype(jnp.bfloat16)
                product = dot_tn(down_ref[...], up)
                part = (part.astype(jnp.float32) + ADAPTER_SCALE * product).astype(jnp.bfloat16)
            weights_ref[kind, :, lanes] = part
        if t == 3:
            write(weights_ref, weights_hbm)

    def own_queries():
        q_ref[...] = dot_nn(rows_ref[x * 2 + core], weights_ref[0]).astype(jnp.bfloat16)
        write(q_ref, q_hbm)

    def keys_values(ref, hbm, kind, at):
        owner = x * 2 + at
        ref[at] = dot_nn(rows_ref[owner], weights_ref[kind]).astype(jnp.bfloat16)
        write_rows(ref.at[at], hbm, owner)

    def far_keys_values(ref, hbm, kind):
        far_writes.append(far_write(ref.at[2], hbm))
        at = len(far_writes) - 1

        @middle_devices
        def _():
            ref[2] = dot_nn(rows_ref[far_owner], weights_ref[kind]).astype(jnp.bfloat16)
            far_writes[at].start()

    steps = [functools.partial(assemble, t) for t in range(4)] + [own_queries]
    for at in range(2):
        steps.append(functools.partial(keys_values, k_ref, k_hbm, 1, at))
        steps.append(functools.partial(keys_values, v_ref, v_hbm, 2, at))
    steps.append(functools.partial(far_keys_values, k_ref, k_hbm, 1))
    steps.append(functools.partial(far_keys_values, v_ref, v_hbm, 2))

    events = event_order(8.5)
    last_pack = max(i for i, (flow, _) in enumerate(events) if FLOWS[flow][0] == 0)
    between = max(1, (len(events) - last_pack) // (len(steps) + 1))
    arrivals = 0
    for at, (flow, piece) in enumerate(events):
        if piece[2] == 0:
            handle(flow, piece)
        else:
            pl.when((z + piece[2] >= 0) & (z + piece[2] < DEPTH))(
                functools.partial(handle, flow, piece)
            )
        if piece != OWN:
            arrivals += 1
            if arrivals == 24:
                pass_count()
        if at >= last_pack and (at - last_pack) % between == between - 1 and steps:
            steps.pop(0)()
    for step in steps:
        step()

    for copy in sibling_copies:
        copy.wait_send()

    @middle_devices
    def _():
        for copy in across_copies:
            copy.wait_send()
        for copy in far_writes:
            copy.wait()

    for copy in own_copies[3:] + outs:
        copy.wait()
    for flow in range(len(FLOWS)):
        if flow > 1:
            finish_flow(flow)
        finish_sends(flow)
    for copy in count_copies[1:]:
        copy.wait()
    count_copies[0].wait_send()
    fewest_ref[0, 0] = jnp.min(counts_ref[0:DEPTH])


def gather_all(
    w_q, w_k, w_v, w_out, w_in, w_down_t, tokens, up_q, up_v, down_q_t, down_v_t, lengths
):
    shard_rows, width = w_in.shape
    token_rows = tokens.shape[0]
    bf16, f32 = jnp.bfloat16, jnp.float32
    slim = w_q.shape[1]
    padded = slim + -slim % 128
    flows = len(FLOWS)
    dma = pltpu.SemaphoreType.DMA
    grid = (2, 2, DEPTH, 2, shard_rows, width)
    return pl.pallas_call(
        gather_kernel,
        out_shape=(
            jax.ShapeDtypeStruct((2,) + grid, bf16),
            jax.ShapeDtypeStruct((4, width, width), bf16),
            jax.ShapeDtypeStruct((4 * token_rows, width), bf16),
            jax.ShapeDtypeStruct((token_rows, width), bf16),
            jax.ShapeDtypeStruct((4 * token_rows, width), bf16),
            jax.ShapeDtypeStruct((4 * token_rows, width), bf16),
            jax.ShapeDtypeStruct((16, width), bf16),
            jax.ShapeDtypeStruct((1, 1), f32),
        ),
        in_specs=[VMEM_SPEC] * 4 + [HBM_SPEC] * 3 + [VMEM_SPEC] * 5,
        out_specs=(HBM_SPEC,) * 6 + (VMEM_SPEC, SMEM_SPEC),
        scratch_shapes=[
            pltpu.VMEM((shard_rows, width), bf16),
            pltpu.VMEM(grid, bf16),
            pltpu.VMEM((4, token_rows, width), bf16),
            pltpu.VMEM((16, padded), f32),
            pltpu.VMEM((4, 16, padded), f32),
            pltpu.VMEM((4, width, width), bf16),
            pltpu.VMEM((token_rows, width), bf16),
            pltpu.VMEM((3, token_rows, width), bf16),
            pltpu.VMEM((3, token_rows, width), bf16),
            pltpu.VMEM((8, 128), f32),
            pltpu.VMEM((DEPTH + 1, 8, 128), f32),
            dma((DEPTH,)),
            dma((DEPTH,)),
            dma((flows, 4 * DEPTH)),
            dma((flows, 4)),
            dma((flows,)),
            dma((flows,)),
            dma((5,)),
            dma((3, 2)),
            dma((3, 2)),
            dma((3,)),
            dma((3,)),
            dma((14,)),
            dma((3,)),
        ],
        compiler_params=pltpu.CompilerParams(
            collective_id=1, has_side_effects=True, vmem_limit_bytes=VMEM_LIMIT
        ),
        name="gather_all",
    )(
        w_q,
        w_k,
        w_v,
        w_out,
        w_in,
        w_down_t,
        tokens,
        up_q,
        up_v,
        down_q_t,
        down_v_t,
        lengths,
    )


def project_kernel(
    order,
    full_hbm,
    rows_ref,
    ups_ref,
    downs_ref,
    weights_ref,
    q_ref,
    k_ref,
    v_ref,
    packs_ref,
    sems,
):
    token_rows = q_ref.shape[0]
    slim = packs_ref.shape[2] // 4
    tensor = lax.axis_index("tensor")
    copies = [
        pltpu.make_async_copy(full_hbm.at[0, i], packs_ref.at[i], sems.at[i])
        for i in range(len(order))
    ]
    for copy in copies:
        copy.start()
    for i, t in enumerate(order):
        copies[i].wait()
        lanes = slice(t * slim, (t + 1) * slim)
        for kind, first in ((0, 0), (1, None), (2, 8), (3, None)):
            part = packs_ref[i, :, kind * slim : (kind + 1) * slim]
            if first is not None:
                up = ups_ref[t, first : first + 8, :slim]
                product = dot_tn(downs_ref[first : first + 8, :], up)
                part = (part.astype(jnp.float32) + ADAPTER_SCALE * product).astype(jnp.bfloat16)
            weights_ref[kind, :, lanes] = part
    own = rows_ref[pl.ds(pl.multiple_of(tensor * token_rows, token_rows), token_rows), :]
    q_ref[...] = dot_nn(own, weights_ref[0]).astype(jnp.bfloat16)

    @pl.loop(0, rows_ref.shape[0] // token_rows)
    def _(at):
        window = pl.ds(pl.multiple_of(at * token_rows, token_rows), token_rows)
        block = rows_ref[window, :]
        k_ref[window, :] = dot_nn(block, weights_ref[1]).astype(jnp.bfloat16)
        v_ref[window, :] = dot_nn(block, weights_ref[2]).astype(jnp.bfloat16)


def project(order, full, rows_all, ups_all, downs, token_rows):
    total_rows, width = rows_all.shape
    bf16 = jnp.bfloat16
    return pl.pallas_call(
        functools.partial(project_kernel, order),
        out_shape=(
            jax.ShapeDtypeStruct((4, width, width), bf16),
            jax.ShapeDtypeStruct((token_rows, width), bf16),
            jax.ShapeDtypeStruct((total_rows, width), bf16),
            jax.ShapeDtypeStruct((total_rows, width), bf16),
        ),
        in_specs=[HBM_SPEC] + [VMEM_SPEC] * 3,
        out_specs=(VMEM_SPEC,) * 4,
        scratch_shapes=[
            pltpu.VMEM(full.shape[1:], bf16),
            pltpu.SemaphoreType.DMA((len(order),)),
        ],
        compiler_params=pltpu.CompilerParams(vmem_limit_bytes=VMEM_LIMIT),
        name="project",
    )(full, rows_all, ups_all, downs)


def middle_kernel(
    near_only,
    lengths_ref,
    fewest_ref,
    gain_attn_ref,
    shift_attn_ref,
    gain_ffn_ref,
    shift_ffn_ref,
    q_hbm,
    k_hbm,
    v_hbm,
    tokens_hbm,
    cot_hbm,
    weights_hbm,
    full_hbm,
    rows_hbm,
    wide_k_hbm,
    wide_v_hbm,
    wide_rows_hbm,
    ups_ref,
    down_q_ref,
    down_v_ref,
    mixed_hbm,
    grad_one_hbm,
    gq_hbm,
    gk_hbm,
    gv_hbm,
    far_hbm,
    sums_hbm,
    q_ref,
    k_ref,
    v_ref,
    tokens_ref,
    cot_ref,
    out_buf,
    in_buf,
    down_buf,
    slope_buf,
    first_buf,
    sum_buf,
    normed_buf,
    inverse_buf,
    ctx_ref,
    lse_ref,
    grad_ref,
    gk_acc,
    gv_acc,
    gk_out,
    gv_out,
    far_out,
    pair_buf,
    sums_ref,
    sums_low,
    load_sem,
    part_sem,
    kv_sem,
    store_sem,
    grad_sem,
    far_sem,
):
    rows, width = q_ref.shape
    total_rows = k_ref.shape[0]
    parts, kinds = in_buf.shape[0], full_hbm.shape[0]
    kv_blocks = total_rows // KV_BLOCK
    base = lax.axis_index("tensor") * rows
    wide = fewest_ref[0, 0] < total_rows // 2
    limit = jnp.where(wide, total_rows, jnp.minimum(base + 2 * rows, total_rows))

    span_low, span_high = jnp.int32(total_rows), jnp.int32(0)
    for at in range(rows // Q_BLOCK):
        low, steps = query_span(lengths_ref, base + at * Q_BLOCK, total_rows)
        span_low = jnp.minimum(span_low, jnp.minimum(low, limit - K_BLOCK))
        span_high = jnp.maximum(span_high, jnp.minimum(low + steps * K_BLOCK, limit))

    def kv_rows(block):
        return pl.ds(pl.multiple_of(block * KV_BLOCK, KV_BLOCK), KV_BLOCK)

    def touched(block):
        return (block * KV_BLOCK < span_high) & ((block + 1) * KV_BLOCK > span_low)

    def kv_copies(block, k_source=k_hbm, v_source=v_hbm):
        window = kv_rows(block)
        return (
            pltpu.make_async_copy(k_source.at[window], k_ref.at[window], kv_sem.at[0, block]),
            pltpu.make_async_copy(v_source.at[window], v_ref.at[window], kv_sem.at[1, block]),
        )

    def part_copies(part):
        return (
            pltpu.make_async_copy(
                full_hbm.at[kinds - 2, part], in_buf.at[part], part_sem.at[0, part]
            ),
            pltpu.make_async_copy(
                full_hbm.at[kinds - 1, part], down_buf.at[part], part_sem.at[1, part]
            ),
        )

    q_copy = pltpu.make_async_copy(q_hbm, q_ref, load_sem.at[0])
    tokens_copy = pltpu.make_async_copy(tokens_hbm, tokens_ref, load_sem.at[1])
    out_copy = pltpu.make_async_copy(weights_hbm.at[3], out_buf, load_sem.at[2])
    cot_copy = pltpu.make_async_copy(cot_hbm, cot_ref, load_sem.at[3])
    pair_copy = pltpu.make_async_copy(weights_hbm.at[pl.ds(1, 2)], pair_buf, load_sem.at[4])
    q_copy.start()

    @pl.loop(0, kv_blocks)
    def _(block):
        @pl.when(touched(block) & jnp.logical_not(wide))
        def _():
            for copy in kv_copies(block):
                copy.start()

        @pl.when(touched(block) & wide)
        def _():
            for copy in kv_copies(block, wide_k_hbm, wide_v_hbm):
                copy.start()

    gk_acc[...] = jnp.zeros_like(gk_acc)
    gv_acc[...] = jnp.zeros_like(gv_acc)
    q_copy.wait()

    @pl.loop(0, kv_blocks)
    def _(block):
        @pl.when(touched(block))
        def _():
            for copy in kv_copies(block):
                copy.wait()

    tokens_copy.start()
    out_copy.start()
    cot_copy.start()
    for part in range(parts):
        for copy in part_copies(part):
            copy.start()
    pair_copy.start()

    attend_forward(limit, lengths_ref, q_ref, k_ref, v_ref, ctx_ref, lse_ref)

    gain_attn, shift_attn, gain_ffn, shift_ffn = (
        ref[...].reshape(1, -1) for ref in (gain_attn_ref, shift_attn_ref, gain_ffn_ref, shift_ffn_ref)
    )
    tokens_copy.wait()
    out_copy.wait()
    sum_buf[...] = dot_nt(ctx_ref[...], out_buf[...])

    def each_norm_block(step):
        @pl.loop(0, rows // NORM_BLOCK)
        def _(at):
            step(pl.ds(pl.multiple_of(at * NORM_BLOCK, NORM_BLOCK), NORM_BLOCK))

    @each_norm_block
    def _(block):
        residual = tokens_ref[block, :].astype(jnp.float32) + sum_buf[block, :]
        first, normed, inverse = norm_forward(residual, gain_attn, shift_attn)
        first_buf[block, :] = first.astype(jnp.bfloat16)
        sum_buf[block, :] = first.astype(jnp.bfloat16).astype(jnp.float32)
        normed_buf[block, :] = normed
        inverse_buf[block, :] = inverse

    @pl.loop(0, parts)
    def _(part):
        for copy in part_copies(part):
            copy.wait()
        acted, slope = gelu_parts(dot_nn(first_buf[...], in_buf[part]))
        slope_buf[part] = slope
        sum_buf[...] += dot_nt(acted.astype(jnp.bfloat16), down_buf[part])

    cot_copy.wait()

    @each_norm_block
    def _(block):
        mixed, normed, inverse = norm_forward(sum_buf[block, :], gain_ffn, shift_ffn)
        tokens_ref[block, :] = mixed.astype(jnp.bfloat16)
        cotangents = cot_ref[block, :].astype(jnp.float32)
        grad_two = norm_backward(cotangents, normed, inverse, gain_ffn)
        first_buf[block, :] = grad_two.astype(jnp.bfloat16)
        sum_buf[block, :] = grad_two

    mixed_copy = pltpu.make_async_copy(tokens_ref, mixed_hbm, store_sem.at[0])
    mixed_copy.start()

    @pl.loop(0, parts)
    def _(part):
        grad_hidden = dot_nn(first_buf[...], down_buf[part]) * slope_buf[part]
        sum_buf[...] += dot_nt(grad_hidden.astype(jnp.bfloat16), in_buf[part])

    @each_norm_block
    def _(block):
        grad_one = norm_backward(
            sum_buf[block, :], normed_buf[block, :], inverse_buf[block, :], gain_attn
        )
        normed_buf[block, :] = grad_one
        first_buf[block, :] = grad_one.astype(jnp.bfloat16)

    grad_one_copy = pltpu.make_async_copy(normed_buf, grad_one_hbm, store_sem.at[1])
    grad_one_copy.start()
    grad_ref[...] = dot_nn(first_buf[...], out_buf[...]).astype(jnp.bfloat16)

    attend_backward(
        limit,
        lengths_ref,
        q_ref,
        k_ref,
        v_ref,
        ctx_ref,
        lse_ref,
        grad_ref,
        first_buf,
        gk_acc,
        gv_acc,
    )
    gq_copy = pltpu.make_async_copy(first_buf, gq_hbm, store_sem.at[2])
    gq_copy.start()

    def rows_copy(block, source=rows_hbm):
        window = kv_rows(block)
        return pltpu.make_async_copy(source.at[window], k_ref.at[window], kv_sem.at[0, block])

    @pl.loop(0, kv_blocks)
    def _(block):
        @pl.when(touched(block) & jnp.logical_not(wide))
        def _():
            rows_copy(block).start()

        @pl.when(touched(block) & wide)
        def _():
            rows_copy(block, wide_rows_hbm).start()

    def wanted(block):
        if not near_only:
            return block >= 0
        return block // (kv_blocks // 2) == lax.axis_index("tensor") // 2

    def grad_copies(block):
        window = kv_rows(block)
        return (
            pltpu.make_async_copy(gk_out.at[window], gk_hbm.at[window], grad_sem.at[0, block]),
            pltpu.make_async_copy(gv_out.at[window], gv_hbm.at[window], grad_sem.at[1, block]),
        )

    @pl.loop(0, kv_blocks)
    def _(block):
        window = kv_rows(block)

        @pl.when(touched(block))
        def _():
            gk_out[window, :] = (gk_acc[window, :] * SCORE_SCALE).astype(jnp.bfloat16)
            gv_out[window, :] = gv_acc[window, :].astype(jnp.bfloat16)

        @pl.when(jnp.logical_not(touched(block)))
        def _():
            gk_out[window, :] = jnp.zeros((KV_BLOCK, width), jnp.bfloat16)
            gv_out[window, :] = jnp.zeros((KV_BLOCK, width), jnp.bfloat16)

        @pl.when(wanted(block))
        def _():
            for copy in grad_copies(block):
                copy.start()

    def far_copy(at):
        window = kv_rows(at)
        return pltpu.make_async_copy(far_out.at[window], far_hbm.at[window], far_sem.at[at])

    pair_copy.wait()
    tensor = lax.axis_index("tensor")
    near = tensor // 2
    per_owner = rows // KV_BLOCK

    @pl.loop(0, kv_blocks // 2)
    def _(at):
        owner = (1 - near) * 2 + lax.rem(tensor + 1 + at // per_owner, 2)
        block = owner * per_owner + lax.rem(at, per_owner)
        source, target = kv_rows(block), kv_rows(at)

        @pl.when(touched(block))
        def _():
            far_out[target, :] = (
                dot_nt(gk_out[source, :], pair_buf[0]) + dot_nt(gv_out[source, :], pair_buf[1])
            ).astype(jnp.bfloat16)

        @pl.when(jnp.logical_not(touched(block)))
        def _():
            far_out[target, :] = jnp.zeros((KV_BLOCK, width), jnp.bfloat16)

        far_copy(at).start()

    def add_adapter(row_vals, grads, down, up, first_at, second_at):
        lifted = (ADAPTER_SCALE * dot_nt(row_vals, down)).astype(jnp.bfloat16)
        grad_lifted = (ADAPTER_SCALE * dot_nt(grads, up)).astype(jnp.bfloat16)
        sums_ref[first_at : first_at + 8, :] += dot_tn(grad_lifted, row_vals)
        sums_ref[second_at : second_at + 8, :] += dot_tn(lifted, grads)

    sums_ref[...] = jnp.zeros_like(sums_ref)

    @pl.loop(0, kv_blocks)
    def _(block):
        window = kv_rows(block)

        @pl.when(touched(block))
        def _():
            rows_copy(block).wait()
            add_adapter(k_ref[window, :], gv_out[window, :], down_v_ref[...], ups_ref[8:16, :], 8, 24)

    own = pl.ds(pl.multiple_of(base, rows), rows)
    add_adapter(k_ref[own, :], first_buf[...], down_q_ref[...], ups_ref[0:8, :], 0, 16)
    sums_low[...] = sums_ref[...].astype(jnp.bfloat16)
    sums_copy = pltpu.make_async_copy(sums_low, sums_hbm, store_sem.at[3])
    sums_copy.start()
    sums_copy.wait()

    @pl.loop(0, kv_blocks // 2)
    def _(at):
        far_copy(at).wait()

    for copy in (mixed_copy, grad_one_copy, gq_copy):
        copy.wait()

    @pl.loop(0, kv_blocks)
    def _(block):
        @pl.when(wanted(block))
        def _():
            for copy in grad_copies(block):
                copy.wait()


def middle(
    near_only,
    lengths,
    fewest,
    norms,
    q_own,
    k_all,
    v_all,
    wide_rows,
    tokens,
    cotangent,
    weights,
    full,
    rows_all,
    ups,
    downs,
):
    rows, width = q_own.shape
    total_rows = k_all.shape[0]
    parts = full.shape[1]
    bf16, f32 = jnp.bfloat16, jnp.float32
    slots = rows // Q_BLOCK * (width // PAIR)
    kv_blocks = total_rows // KV_BLOCK
    dma = pltpu.SemaphoreType.DMA
    return pl.pallas_call(
        functools.partial(middle_kernel, near_only),
        out_shape=(
            jax.ShapeDtypeStruct((rows, width), bf16),
            jax.ShapeDtypeStruct((rows, width), f32),
            jax.ShapeDtypeStruct((rows, width), bf16),
            jax.ShapeDtypeStruct((total_rows, width), bf16),
            jax.ShapeDtypeStruct((total_rows, width), bf16),
            jax.ShapeDtypeStruct((total_rows // 2, width), bf16),
            jax.ShapeDtypeStruct((32, width), bf16),
        ),
        in_specs=[SMEM_SPEC] * 2 + [VMEM_SPEC] * 4 + [HBM_SPEC] * 11 + [VMEM_SPEC] * 3,
        out_specs=(HBM_SPEC,) * 7,
        scratch_shapes=[
            pltpu.VMEM((rows, width), bf16),
            pltpu.VMEM((total_rows, width), bf16),
            pltpu.VMEM((total_rows, width), bf16),
            pltpu.VMEM((rows, width), bf16),
            pltpu.VMEM((rows, width), bf16),
            pltpu.VMEM((width, width), bf16),
            pltpu.VMEM(full.shape[1:], bf16),
            pltpu.VMEM(full.shape[1:], bf16),
            pltpu.VMEM((parts, rows, full.shape[3]), f32),
            pltpu.VMEM((rows, width), bf16),
            pltpu.VMEM((rows, width), f32),
            pltpu.VMEM((rows, width), f32),
            pltpu.VMEM((rows, 1), f32),
            pltpu.VMEM((rows, width), bf16),
            pltpu.VMEM((slots, 1, 2 * Q_BLOCK), f32),
            pltpu.VMEM((rows, width), bf16),
            pltpu.VMEM((total_rows, width), f32),
            pltpu.VMEM((total_rows, width), f32),
            pltpu.VMEM((total_rows, width), bf16),
            pltpu.VMEM((total_rows, width), bf16),
            pltpu.VMEM((total_rows // 2, width), bf16),
            pltpu.VMEM((2, width, width), bf16),
            pltpu.VMEM((32, width), f32),
            pltpu.VMEM((32, width), bf16),
            dma((5,)),
            dma((2, parts)),
            dma((2, kv_blocks)),
            dma((4,)),
            dma((2, kv_blocks)),
            dma((kv_blocks // 2,)),
        ],
        compiler_params=pltpu.CompilerParams(vmem_limit_bytes=VMEM_LIMIT),
        name="middle",
    )(
        lengths,
        fewest,
        *norms,
        q_own,
        k_all,
        v_all,
        tokens,
        cotangent,
        weights,
        full,
        rows_all,
        *wide_rows,
        ups,
        *downs,
    )


def final_kernel(
    reach,
    gq_hbm,
    gk_hbm,
    gv_hbm,
    far_hbm,
    weights_hbm,
    grad_one_hbm,
    part_sums,
    grad_tokens_ref,
    sums_ref,
    gq_ref,
    gk_ref,
    gv_ref,
    far_ref,
    weights_ref,
    grad_one_ref,
    from_sib,
    to_x,
    from_x,
    home_to,
    home_from,
    yc_slots,
    z_slots,
    xc_slots,
    load_sem,
    far_send,
    far_recv,
    block_send,
    block_recv,
    sum_send,
    sum_recv,
):
    place = Place()
    x, y, z, core = place.x, place.y, place.z, place.core
    token_rows = gq_ref.shape[0]
    half_rows = token_rows // 2
    chunk_rows = token_rows // FAR_CHUNKS
    bf16, f32 = jnp.bfloat16, jnp.float32
    loads = {}

    def load(name, source, target):
        copy = pltpu.make_async_copy(source, target, load_sem.at[len(loads)])
        copy.start()
        loads[name] = copy

    if reach:
        load("far", far_hbm.at[pl.ds(token_rows, token_rows)], far_ref)
    near_rows = pl.ds(pl.multiple_of(x * 2 * token_rows, token_rows), 2 * token_rows)
    load("k", gk_hbm.at[near_rows], gk_ref)
    load("v", gv_hbm.at[near_rows], gv_ref)
    load("w", weights_hbm.at[pl.ds(0, 3)], weights_ref)
    load("q", gq_hbm, gq_ref)
    load("one", grad_one_hbm, grad_one_ref)

    across = place.device(x=1 - x, core=1 - core)
    middle_device = x != core
    barrier = pltpu.get_barrier_semaphore()
    around = [place.step("y", 1), place.sibling(), place.device(y=1 - y, core=1 - core)]
    column = [place.device(z=lax.rem(z + i, DEPTH)) for i in range(1, DEPTH)]
    beside = [place.step("x", 1), across]
    for target in around + column + beside:
        pl.semaphore_signal(barrier, inc=1, device_id=target, device_id_type=MESH_ID)
    pl.semaphore_wait(barrier, len(around + column + beside))

    def remote(source, target, send, recv, device):
        return pltpu.make_async_remote_copy(
            src_ref=source,
            dst_ref=target,
            send_sem=send,
            recv_sem=recv,
            device_id=device,
            device_id_type=MESH_ID,
        )

    def started(*operands):
        copy = remote(*operands)
        copy.start()
        return copy

    chunks = [pl.ds(at * chunk_rows, chunk_rows) for at in range(FAR_CHUNKS)]
    kept = pl.ds(pl.multiple_of(core * 16, 16), 16)
    given = pl.ds(pl.multiple_of((1 - core) * 16, 16), 16)
    sum_copies = []

    def send_sum(source, target, device):
        at = len(sum_copies)
        sum_copies.append(started(source, target, sum_send.at[at], sum_recv.at[at], device))

    for source, device in zip((kept, given, given), around):
        send_sum(part_sums.at[source], yc_slots.at[y * 2 + core], device)
    yc_slots[y * 2 + core] = part_sums[kept, :]
    sib_copies, x_copies = [], []
    if reach:
        for at, chunk in enumerate(chunks):
            sib_copies.append(
                started(
                    far_hbm.at[chunk],
                    from_sib.at[chunk],
                    far_send.at[0, at],
                    far_recv.at[0, at],
                    place.sibling(),
                )
            )
    else:
        for at, chunk in enumerate(chunks):
            x_copies.append(
                remote(
                    far_hbm.at[chunk],
                    from_x.at[chunk],
                    far_send.at[1, at],
                    far_recv.at[1, at],
                    across,
                )
            )

        @pl.when(middle_device)
        def _():
            for copy in x_copies:
                copy.start()

        @pl.when(jnp.logical_not(middle_device))
        def _():
            from_x[...] = jnp.zeros_like(from_x)

    def slot_sum(slots, indices):
        result = slots[indices[0]].astype(f32)
        for i in indices[1:]:
            result = result + slots[i].astype(f32)
        return result

    if reach:
        loads["far"].wait()
        for at, chunk in enumerate(chunks):
            sib_copies[at].wait_recv()
            to_x[chunk, :] = (far_ref[chunk, :].astype(f32) + from_sib[chunk, :].astype(f32)).astype(
                bf16
            )
            x_copies.append(
                started(
                    to_x.at[chunk],
                    from_x.at[chunk],
                    far_send.at[1, at],
                    far_recv.at[1, at],
                    place.step("x", 1),
                )
            )

    for copy in sum_copies[0:3]:
        copy.wait_recv()
    z_slots[z] = slot_sum(yc_slots, range(4)).astype(bf16)
    for device in column:
        send_sum(z_slots.at[z], z_slots.at[z], device)

    def partial(owner, half):
        window = pl.ds(pl.multiple_of(owner * token_rows + half * half_rows, half_rows), half_rows)
        return dot_nt(gk_ref[window, :], weights_ref[1]) + dot_nt(gv_ref[window, :], weights_ref[2])

    for name in ("k", "v", "w"):
        loads[name].wait()
    home_copies = []
    for half in range(2):
        window = pl.ds(half * half_rows, half_rows)
        home_to[window, :] = partial(1 - core, half).astype(bf16)
        home_copies.append(
            started(
                home_to.at[window],
                home_from.at[window],
                block_send.at[half],
                block_recv.at[half],
                place.sibling(),
            )
        )

    for copy in sum_copies[3:]:
        copy.wait_recv()
    xc_slots[x * 2 + core] = slot_sum(z_slots, range(DEPTH)).astype(bf16)
    own_slot = xc_slots.at[x * 2 + core]
    for device in [place.sibling()] + beside:
        send_sum(own_slot, own_slot, device)
    for name in ("q", "one"):
        loads[name].wait()
    for half in range(2):
        window = pl.ds(half * half_rows, half_rows)
        grad_one_ref[window, :] += partial(core, half) + dot_nt(gq_ref[window, :], weights_ref[0])
    for copy in home_copies:
        copy.wait_recv()
    for at, chunk in enumerate(chunks):
        if reach:
            x_copies[at].wait_recv()
        else:
            pl.when(middle_device)(x_copies[at].wait_recv)
        grad_tokens_ref[chunk, :] = (
            grad_one_ref[chunk, :] + home_from[chunk, :].astype(f32) + from_x[chunk, :].astype(f32)
        ).astype(bf16)
    for copy in sum_copies[2 + DEPTH :]:
        copy.wait_recv()
    for half in range(2):
        sums_ref[half * 16 : half * 16 + 16, :] = slot_sum(xc_slots, (half, 2 + half))

    for copy in sib_copies + home_copies + sum_copies:
        copy.wait_send()
    for copy in x_copies:
        if reach:
            copy.wait_send()
        else:
            pl.when(middle_device)(copy.wait_send)


def final_sums(reach, grad_q, grad_k, grad_v, far_rows, weights, grad_one, sums):
    token_rows, width = grad_q.shape
    bf16, f32 = jnp.bfloat16, jnp.float32
    dma = pltpu.SemaphoreType.DMA
    block = pltpu.VMEM((token_rows, width), bf16)
    return pl.pallas_call(
        functools.partial(final_kernel, reach),
        out_shape=(
            jax.ShapeDtypeStruct((token_rows, width), bf16),
            jax.ShapeDtypeStruct((32, width), f32),
        ),
        in_specs=[HBM_SPEC] * 6 + [VMEM_SPEC],
        out_specs=(VMEM_SPEC,) * 2,
        scratch_shapes=[
            block,
            pltpu.VMEM((2 * token_rows, width), bf16),
            pltpu.VMEM((2 * token_rows, width), bf16),
            block,
            pltpu.VMEM((3, width, width), bf16),
            pltpu.VMEM((token_rows, width), f32),
            block,
            block,
            block,
            block,
            block,
            pltpu.VMEM((4, 16, width), bf16),
            pltpu.VMEM((DEPTH, 16, width), bf16),
            pltpu.VMEM((4, 16, width), bf16),
            dma((6,)),
            dma((2, FAR_CHUNKS)),
            dma((2, FAR_CHUNKS)),
            dma((2,)),
            dma((2,)),
            dma((DEPTH + 5,)),
            dma((DEPTH + 5,)),
        ],
        compiler_params=pltpu.CompilerParams(
            collective_id=2 if reach else 3, has_side_effects=True, vmem_limit_bytes=VMEM_LIMIT
        ),
        name="final_sums_wide" if reach else "final_sums",
    )(grad_q, grad_k, grad_v, far_rows, weights, grad_one, sums)


def no_rows_kernel(*refs):
    del refs


def no_rows(tokens, weights):
    shape = jax.ShapeDtypeStruct((4 * tokens.shape[0], tokens.shape[1]), tokens.dtype)
    return pl.pallas_call(
        no_rows_kernel, out_shape=(shape,) * 3, out_specs=(HBM_SPEC,) * 3, name="no_rows"
    )()


def hand_out_kernel(grad_ref, sums_ref, grad_out, aq_ref, av_ref, bq_ref, bv_ref):
    grad_out[...] = grad_ref[...]
    slim = bq_ref.shape[1]
    aq_ref[...] = sums_ref[0:8, :]
    av_ref[...] = sums_ref[8:16, :]
    for t in range(sums_ref.shape[1] // slim):

        @pl.when(lax.axis_index("tensor") == t)
        def _(t=t):
            bq_ref[...] = sums_ref[16:24, t * slim : (t + 1) * slim]
            bv_ref[...] = sums_ref[24:32, t * slim : (t + 1) * slim]


def hand_out(grad_tokens, sums, slim):
    f32, width = jnp.float32, sums.shape[1]
    return pl.pallas_call(
        hand_out_kernel,
        out_shape=(
            jax.ShapeDtypeStruct(grad_tokens.shape, grad_tokens.dtype),
            jax.ShapeDtypeStruct((8, width), f32),
            jax.ShapeDtypeStruct((8, width), f32),
            jax.ShapeDtypeStruct((8, slim), f32),
            jax.ShapeDtypeStruct((8, slim), f32),
        ),
        in_specs=[VMEM_SPEC] * 2,
        out_specs=(VMEM_SPEC,) * 5,
        name="hand_out",
    )(grad_tokens, sums)


def local(
    fast,
    tokens,
    query_weight,
    w_key,
    value_weight,
    w_out,
    w_in,
    w_down,
    gain_attn,
    shift_attn,
    gain_ffn,
    shift_ffn,
    query_down_factor,
    query_up_factor,
    value_down_factor,
    value_up_factor,
    lengths,
    cotangent,
):
    slim = query_weight.shape[1]
    width = tokens.shape[1]
    token_rows = tokens.shape[0]
    down_q_t, down_v_t = query_down_factor.T, value_down_factor.T
    if fast:
        full, weights, rows_all, q_own, k_all, v_all, ups_full, fewest = gather_all(
            query_weight,
            w_key,
            value_weight,
            w_out,
            w_in,
            w_down.T,
            tokens,
            query_up_factor,
            value_up_factor,
            down_q_t,
            down_v_t,
            lengths,
        )
        full = full.reshape(2, 4, width, width)
    else:
        attn_pack = jnp.concatenate([query_weight, w_key, value_weight, w_out.T], axis=1)
        full = jnp.stack([attn_pack, w_in, w_down.T])
        full = lax.all_gather(full, "dp", axis=1, tiled=True)
        full = lax.all_gather(full, "tensor", axis=1)
        rows_all = lax.all_gather(tokens, "tensor").reshape(-1, width)
        ups = jnp.concatenate([query_up_factor, value_up_factor], axis=0)
        ups = jnp.pad(ups, ((0, 0), (0, -slim % 128)))
        ups_all = lax.all_gather(ups, "tensor")
        downs = jnp.concatenate([down_q_t, down_v_t], axis=0)
        ups_full = ups_all[:, :, :slim].transpose(1, 0, 2).reshape(16, width)
        order = tuple(range(full.shape[1]))
        weights, q_own, k_all, v_all = project(order, full, rows_all, ups_all, downs, token_rows)

    norms = (gain_attn, shift_attn, gain_ffn, shift_ffn)
    downs_t = (down_q_t, down_v_t)
    if fast:

        def either(near, wide, *operands):
            return lax.cond(fewest[0, 0] >= rows_all.shape[0] // 2, near, wide, *operands)

        def wide_rows(tokens, weights):
            me = lax.axis_index("tensor")
            rows_all = jnp.zeros((4 * token_rows, width), tokens.dtype)
            for away in range(4):
                block = tokens
                if away:
                    block = lax.ppermute(tokens, "tensor", [(i, i ^ away) for i in range(4)])
                first_row = (me ^ away) * token_rows
                rows_all = lax.dynamic_update_slice_in_dim(rows_all, block, first_row, 0)
            k_all = dot_nn(rows_all, weights[1]).astype(jnp.bfloat16)
            v_all = dot_nn(rows_all, weights[2]).astype(jnp.bfloat16)
            return (k_all, v_all, rows_all)

        mixed, grad_one, grad_q, grad_k, grad_v, far_rows, sums = middle(
            True,
            lengths,
            fewest,
            norms,
            q_own,
            k_all,
            v_all,
            either(no_rows, wide_rows, tokens, weights),
            tokens,
            cotangent,
            weights,
            full,
            rows_all,
            ups_full,
            downs_t,
        )
        grad_tokens, sums = either(
            functools.partial(final_sums, False),
            functools.partial(final_sums, True),
            *(grad_q, grad_k, grad_v, far_rows, weights, grad_one, sums),
        )
        grad_tokens, grad_aq, grad_av, grad_bq, grad_bv = hand_out(grad_tokens, sums, slim)
        return (mixed, grad_tokens, grad_aq.T, grad_bq, grad_av.T, grad_bv)

    mixed, grad_one, grad_q, grad_k, grad_v, far_rows, sums = middle(
        False,
        lengths,
        jnp.zeros((1, 1), jnp.float32),
        norms,
        q_own,
        k_all,
        v_all,
        (k_all, v_all, rows_all),
        tokens,
        cotangent,
        weights,
        full,
        rows_all,
        ups_full,
        downs_t,
    )
    grad_rows = dot_nt(grad_k, weights[1]) + dot_nt(grad_v, weights[2])
    shared = lax.psum_scatter(
        grad_rows.astype(jnp.bfloat16), "tensor", scatter_dimension=0, tiled=True
    )
    own_rows = dot_nt(grad_q, weights[0])
    grad_tokens = (grad_one + own_rows + shared.astype(jnp.float32)).astype(jnp.bfloat16)
    sums = lax.psum(sums.astype(jnp.float32), ("dp", "tensor"))
    at = lax.axis_index("tensor") * slim
    grad_bq = lax.dynamic_slice_in_dim(sums[16:24], at, slim, 1)
    grad_bv = lax.dynamic_slice_in_dim(sums[24:32], at, slim, 1)
    return (mixed, grad_tokens, sums[0:8].T, grad_bq, sums[8:16].T, grad_bv)


def solution(mesh):
    fast = dict(mesh.shape) == {"dp": 2 * DEPTH, "tensor": 4}
    return jax.shard_map(
        functools.partial(local, fast),
        mesh=mesh,
        in_specs=(
            P(("dp", "tensor"), None),
            P("dp", "tensor"),
            P("dp", "tensor"),
            P("dp", "tensor"),
            P("tensor", "dp"),
            P("dp", "tensor"),
            P("tensor", "dp"),
            P(),
            P(),
            P(),
            P(),
            P(),
            P(None, "tensor"),
            P(),
            P(None, "tensor"),
            P("dp", None),
            P(("dp", "tensor"), None),
        ),
        out_specs=(
            P(("dp", "tensor"), None),
            P(("dp", "tensor"), None),
            P(),
            P(None, "tensor"),
            P(),
            P(None, "tensor"),
        ),
        check_vma=False,
    )
```
